32 devices in a mesh: dp: 16 (over z, x, core), ctx: 2 (over y).
Axes of the slice: x: 2, y: 2, z: 4, core: 2. Of those that a mesh axis runs over, the one named last changes fastest.
Arguments:
- tokens: bfloat16 [16384, 1024], P(('dp', 'ctx')), may hold values from -6 to 6
- lengths: int32 [16, 7], P('dp'), may hold values from 1 to 640, as said below
- w_qkv: bfloat16 [1024, 3072], P(('dp', 'ctx')), may hold values from -0.1875 to 0.1875
- w_out: bfloat16 [1024, 1024], P(('dp', 'ctx')), may hold values from -0.1875 to 0.1875
- w_up: bfloat16 [1024, 4096], P(('dp', 'ctx')), may hold values from -0.1875 to 0.1875
- w_down: bfloat16 [4096, 1024], P(('dp', 'ctx')), may hold values from -0.09375 to 0.09375
- gains: bfloat16 [1024, 4], P(('dp', 'ctx')), may hold values from 0.25 to 1.75
- d_out: bfloat16 [16384, 1024], P(('dp', 'ctx')), may hold values from -6 to 6
Outputs:
- output: bfloat16 [16384, 1024], P(('dp', 'ctx'))
- d_tokens: bfloat16 [16384, 1024], P(('dp', 'ctx'))
- grad_qkv: float32 [1024, 3072], P(('dp', 'ctx'))
- grad_out: float32 [1024, 1024], P(('dp', 'ctx'))
- grad_up: float32 [1024, 4096], P(('dp', 'ctx'))
- grad_down: float32 [4096, 1024], P(('dp', 'ctx'))
- grad_gains: float32 [1024, 4], P(('dp', 'ctx'))
The draws below stay inside these ranges and needn't reach their ends.
Inputs may be any that keep to these rules, and one draw needn't show every extreme that they name: Each row holds 7 positive numbers that sum to 1024: the lengths of 6 documents packed from the row's start, then the length of the padding tail, whose slots hold no token.
All inputs are finite; a program needn't handle non-finite values.
Results may differ from the reference program's by a relative error of at most 0.018.
Values may be sent and summed in bfloat16 or wider, within the bound.
A program may use at most 256 MiB of HBM per device.

```python
import math
import jax
import jax.numpy as jnp
from jax import lax

D = 1024
HEADS = 16
HEAD = 64
FF = 4096
DOCS = 7
ROW_LEN = 1024
ROWS = 16
TOKENS = 16384


def draw_lengths(key, part):
    key = jax.random.fold_in(key, 7)
    subkeys = jax.random.split(key, 5)
    padding = jax.random.randint(subkeys[0], (ROWS,), ROW_LEN // 16, ROW_LEN // 8 + 1)
    valid_end = ROW_LEN - padding
    span_start = jax.random.randint(subkeys[1], (ROWS,), 2, ROW_LEN // 4 - 2)
    span_end = span_start + 5 * ROW_LEN // 8
    first_cut = jax.random.randint(subkeys[3], (ROWS,), 1, span_start)
    spare_room = jnp.maximum(valid_end - span_end - 2, 1)
    offsets = jax.random.randint(subkeys[4], (ROWS, 2), 0, spare_room[:, None])
    smaller = jnp.min(offsets, axis=-1)
    larger = jnp.max(offsets, axis=-1)
    mid_cut = span_end + 1 + smaller
    last_cut = span_end + 2 + larger
    lengths = jnp.stack([first_cut, span_start - first_cut, span_end - span_start, mid_cut - span_end, last_cut - mid_cut, valid_end - last_cut, padding], axis=-1)
    return lengths.astype(jnp.int32)


def block_scale(rng, dims, cuts, low, top_value):
    def one(dim, blocks):
        draws = jax.random.uniform(jax.random.fold_in(jax.random.fold_in(rng, 6), dim), (blocks,), jnp.float32, low / len(cuts), top_value / len(cuts))
        return jnp.repeat(jnp.exp(draws), dims[dim] // blocks).reshape((-1,) + (1,) * (len(dims) - dim - 1))

    factor_of = one(*cuts[0])
    for cut in cuts[1:]:
        factor_of = factor_of * one(*cut)
    return factor_of


def centred(rng, extent, scale, most, cuts=(), held_as=jnp.bfloat16):
    entries = scale * jax.random.normal(rng, extent, jnp.float32)
    if cuts:
        entries = entries * block_scale(rng, extent, cuts, -0.22, 0.18)
    return jnp.clip(entries, -most, most).astype(held_as)


def setup_inputs(seed: int = 0) -> dict:
    seeds = jax.random.split(jax.random.key(seed), 9)
    return {
        "tokens": centred(seeds[0], (TOKENS, D), 1.0, 6.0, ((0, 32),)),
        "lengths": draw_lengths(jax.random.fold_in(seeds[8], 71), 0),
        "w_qkv": centred(seeds[2], (D, 3 * D), D ** -0.5, 0.1875, ((0, 32),)),
        "w_out": centred(seeds[3], (D, D), D ** -0.5, 0.1875, ((0, 32),)),
        "w_up": centred(seeds[4], (D, FF), D ** -0.5, 0.1875, ((0, 32),)),
        "w_down": centred(seeds[5], (FF, D), FF ** -0.5, 0.09375, ((0, 32),)),
        "gains": jnp.clip(1.0 + 0.15 * jax.random.normal(seeds[6], (D, 4), jnp.float32), 0.25, 1.75).astype(jnp.bfloat16),
        "d_out": centred(seeds[7], (TOKENS, D), 1.0, 6.0, ((0, 32),)),
    }


epsilon = 1e-05
highest = lax.Precision.HIGHEST

@jax.custom_vjp
def low(v):
    return lax.optimization_barrier(v.astype(jnp.bfloat16)).astype(jnp.float32)

@jax.custom_vjp
def low_back(v):
    return v

def low_keep(v):
    return (low(v), None)

def low_pass(kept, grad):
    return (grad,)

def back_keep(v):
    return (v, None)

def back_low(kept, grad):
    return (low(grad),)
low.defvjp(low_keep, low_pass)
low_back.defvjp(back_keep, back_low)

def doc_layout(lengths):
    doc_ends = jnp.cumsum(lengths, axis=-1).astype(jnp.int32)
    places = jnp.arange(ROW_LEN, dtype=jnp.int32)
    passed = places[None, :, None] >= doc_ends[:, None, :]
    segment = lax.optimization_barrier(jnp.sum(passed.astype(jnp.int32), axis=-1)).astype(jnp.int32)
    starts = lax.optimization_barrier(jnp.sum(jnp.where(passed, lengths[:, None, :], 0), axis=-1)).astype(jnp.int32)
    position = places[None, :] - starts
    is_valid = places[None, :] < doc_ends[:, DOCS - 2][:, None]
    return (segment, position, is_valid)

def layer_norm(values, gain_vec):
    center = values - lax.optimization_barrier(jnp.mean(values, axis=-1, keepdims=True))
    spread = lax.optimization_barrier(jnp.mean(center * center, axis=-1, keepdims=True))
    return center * lax.rsqrt(spread + epsilon) * gain_vec

def rope_tables(position):
    freq_index = jnp.arange(HEAD // 2, dtype=jnp.float32)
    inverse = 10000.0 ** (-2.0 * freq_index / HEAD)
    angles = position.astype(jnp.float32)[..., None] * inverse
    return (jnp.cos(angles)[..., None, :], jnp.sin(angles)[..., None, :])

def rotate(values, cosine_table, sine_table, direction):
    half_dim = values.shape[-1] // 2
    first_half = values[..., :half_dim]
    second_half = values[..., half_dim:]
    return jnp.concatenate([first_half * cosine_table - direction * second_half * sine_table, second_half * cosine_table + direction * first_half * sine_table], axis=-1)

def row_attention(queries, keys_in, values, segment):
    scores = jnp.einsum('qhd,khd->hqk', queries, keys_in, precision=highest) * HEAD ** (-0.5)
    scores = low_back(scores)
    places = jnp.arange(ROW_LEN, dtype=jnp.int32)
    allowed = (segment[:, None] == segment[None, :]) & (places[None, :] <= places[:, None])
    scores = jnp.where(allowed[None], scores, -1e+30)
    row_max = lax.optimization_barrier(jnp.max(scores, axis=-1, keepdims=True))
    shifted = jnp.where(allowed[None], jnp.exp(scores - row_max), 0.0)
    attn_prob = low(shifted / lax.optimization_barrier(jnp.sum(shifted, axis=-1, keepdims=True)))
    return jnp.einsum('hqk,khd->qhd', attn_prob, values, precision=highest)

def layer_forward(stream, qkv_w, out_w, up_w, down_w, gain_w, segment, cosine_table, sine_table, is_valid):
    head_shape = stream.shape[:2] + (HEADS, HEAD)
    normed = low(layer_norm(stream, gain_w[:, 0]))
    qkv_raw = low_back(jnp.einsum('gtd,de->gte', normed, qkv_w, precision=highest))
    queries = low(rotate(qkv_raw[..., :D].reshape(head_shape), cosine_table, sine_table, 1.0))
    key_heads = low(rotate(qkv_raw[..., D:2 * D].reshape(head_shape), cosine_table, sine_table, 1.0))
    value_heads = low(qkv_raw[..., 2 * D:].reshape(head_shape))
    checked = jax.checkpoint(row_attention)

    def per_row(items):
        return checked(items[0], items[1], items[2], items[3])
    attended = lax.map(per_row, (queries, key_heads, value_heads, segment))
    attended = low(low_back(attended.reshape(stream.shape[:2] + (D,))))
    attn_raw = low_back(jnp.einsum('gtd,de->gte', attended, out_w, precision=highest))
    hidden = stream + layer_norm(attn_raw, gain_w[:, 1])
    mlp_in = low(layer_norm(hidden, gain_w[:, 2]))
    up_proj = low_back(jnp.einsum('gtd,df->gtf', mlp_in, up_w, precision=highest))
    activated = low(jax.nn.gelu(up_proj))
    mlp_raw = low_back(jnp.einsum('gtf,fd->gtd', activated, down_w, precision=highest))
    result = hidden + layer_norm(mlp_raw, gain_w[:, 3])
    return jnp.where(is_valid[..., None], result, 0.0)

def reference(tokens, lengths, w_qkv, w_out, w_up, w_down, gains, d_out):
    segment, position, is_valid = doc_layout(lengths)
    cosine_table, sine_table = rope_tables(position)
    group_rows = math.gcd(ROWS, max(1, 4096 // ROW_LEN))
    steps_count = ROWS // group_rows

    def grouped(whole_array):
        return whole_array.reshape((steps_count, group_rows) + whole_array.shape[1:])
    stream = grouped(tokens.astype(jnp.float32).reshape(ROWS, ROW_LEN, D))
    cotangent = grouped(d_out.astype(jnp.float32).reshape(ROWS, ROW_LEN, D))
    weights = (w_qkv.astype(jnp.float32), w_out.astype(jnp.float32), w_up.astype(jnp.float32), w_down.astype(jnp.float32), gains.astype(jnp.float32))

    def one_group(totals, items):
        group_stream, group_cotangent, group_segment, group_cosine, group_sine, group_valid = items

        def forward(stream_in, qkv_w, out_w, up_w, down_w, gain_w):
            return layer_forward(stream_in, qkv_w, out_w, up_w, down_w, gain_w, group_segment, group_cosine, group_sine, group_valid)
        output, pullback = jax.vjp(forward, group_stream, weights[0], weights[1], weights[2], weights[3], weights[4])
        gradients = pullback(group_cotangent)
        totals = tuple((running_sum + new_term for running_sum, new_term in zip(totals, gradients[1:])))
        return (totals, (output.astype(jnp.bfloat16), gradients[0].astype(jnp.bfloat16)))
    start_totals = tuple((jnp.zeros_like(weight) for weight in weights))
    totals, (outputs, d_tokens) = lax.scan(one_group, start_totals, (stream, cotangent, grouped(segment), grouped(cosine_table), grouped(sine_table), grouped(is_valid)))
    return (outputs.reshape(TOKENS, D), d_tokens.reshape(TOKENS, D), totals[0], totals[1], totals[2], totals[3], totals[4])
```

```python
import math

import jax
import jax.numpy as jnp
from jax import lax
from jax.sharding import PartitionSpec as P

import functools
from jax.experimental import pallas as pl
from jax.experimental.pallas import tpu as pltpu

MESH = pl.DeviceIdType.MESH


class Place:
    def __init__(self, dp_size):
        dp = lax.axis_index("dp")
        self.Z = dp_size // 4
        self.z = lax.div(dp, 4)
        self.x = lax.rem(lax.div(dp, 2), 2)
        self.c = lax.rem(dp, 2)
        self.y = lax.axis_index("ctx")
        c, x, y = self.c, self.x, self.y
        self.i2 = y * (1 - c) + x * c
        self.i3 = x * (1 - c) + y * c
        self.sib = self.device(self.z, x, 1 - c, y)
        self.p2 = self.device(self.z, x * (1 - c) + (1 - x) * c, c, (1 - y) * (1 - c) + y * c)
        self.p3 = self.device(self.z, (1 - x) * (1 - c) + x * c, c, y * (1 - c) + (1 - y) * c)

    def device(self, z, x, c, y):
        return ((z * 2 + x) * 2 + c, y)

    def at_z(self, z):
        return self.device(z, self.x, self.c, self.y)

    def block(self, z, a2, a3):
        c = self.c
        return (z * 2 + a3 * (1 - c) + a2 * c) * 2 + a2 * (1 - c) + a3 * c

    def row_block(self, z, a2, a3, core):
        c = self.c
        xx = a3 * (1 - c) + a2 * c
        yy = a2 * (1 - c) + a3 * c
        return ((z * 2 + xx) * 2 + core) * 2 + yy

    def barrier(self):
        bar = pltpu.get_barrier_semaphore()
        for device in (self.sib, self.p2, self.p3):
            pl.semaphore_signal(bar, 1, device_id=device, device_id_type=MESH)
        for k in range(1, self.Z):
            pl.semaphore_signal(
                bar, 1, device_id=self.at_z(lax.rem(self.z + k, self.Z)), device_id_type=MESH
            )
        pl.semaphore_wait(bar, 3 + self.Z - 1)


class Gather:
    def __init__(self, place, shard, full, send, recv, by_z):
        self.g, self.shard, self.full = place, shard, full
        self.send, self.recv = send, recv
        self.rows = shard.shape[0]
        self.by_z = by_z
        Z = place.Z
        self.n_z = 0
        self.n_p2 = 2 * (Z - 1)
        self.n_p3 = self.n_p2 + Z
        self.n_sib = self.n_p3 + 2 * Z
        self.n_own = self.n_sib + 4 * Z
        self.count = self.n_own + 1

    @staticmethod
    def sems(Z):
        return 2 * (Z - 1) + Z + 2 * Z + 4 * Z + 1

    def at(self, index):
        return self.full.at[pl.ds(pl.multiple_of(index * self.rows, self.rows), self.rows)]

    def copy(self, index, number, device, src=None):
        return pltpu.make_async_remote_copy(
            src_ref=self.at(index) if src is None else src,
            dst_ref=self.at(index),
            send_sem=self.send.at[number],
            recv_sem=self.recv.at[number],
            device_id=device,
            device_id_type=MESH,
        )

    def own_copy(self):
        g = self.g
        index = g.row_block(g.z, g.i2, g.i3, g.c)
        return pltpu.make_async_copy(self.shard, self.at(index), self.recv.at[self.n_own])

    def z_copy(self, z, a2_is_other, k, src=None):
        g = self.g
        a2 = (1 - g.i2) if a2_is_other else g.i2
        index = g.row_block(z, a2, g.i3, g.c)
        to = lax.rem(g.z + k, g.Z)
        return self.copy(index, self.n_z + (k - 1) * 2 + int(a2_is_other), g.at_z(to), src)

    def p2_copy(self, z, src=None):
        g = self.g
        return self.copy(g.row_block(z, g.i2, g.i3, g.c), self.n_p2 + z, g.p2, src)

    def p3_copy(self, z, a2, src=None):
        g = self.g
        return self.copy(g.row_block(z, a2, g.i3, g.c), self.n_p3 + z * 2 + a2, g.p3, src)

    def sib_copy(self, z, a2, a3, src=None):
        g = self.g
        number = self.n_sib + g.block(z, a2, a3)
        return self.copy(g.row_block(z, a2, a3, g.c), number, g.sib, src)

    def wait(self, number, index):
        self.copy(index, number, self.g.sib).wait_recv()

    def start(self):
        g, src = self.g, self.shard
        self.own_copy().start()
        self.p2_copy(g.z, src).start()
        self.p3_copy(g.z, g.i2, src).start()
        for k in range(1, g.Z):
            self.z_copy(g.z, False, k, src).start()
        self.sib_copy(g.z, g.i2, g.i3, src).start()

    def arrived_p2(self, z):
        g = self.g
        o2 = 1 - g.i2
        self.wait(self.n_p2 + z, g.row_block(z, o2, g.i3, g.c))
        self.p3_copy(z, o2).start()
        self.sib_copy(z, o2, g.i3).start()

    def first_p2(self):
        g = self.g
        self.arrived_p2(g.z)
        if self.by_z:
            for k in range(1, g.Z):
                self.z_copy(g.z, True, k).start()

    def arrived_z(self, k):
        g = self.g
        z = lax.rem(g.z - k + g.Z, g.Z)
        for other in ((False, True) if self.by_z else (False,)):
            a2 = (1 - g.i2) if other else g.i2
            self.wait(self.n_z + (k - 1) * 2 + int(other), g.row_block(z, a2, g.i3, g.c))
            if not self.by_z:
                self.p2_copy(z).start()
            self.p3_copy(z, a2).start()
            self.sib_copy(z, a2, g.i3).start()

    def later_p2(self, k):
        if not self.by_z:
            self.arrived_p2(lax.rem(self.g.z + k, self.g.Z))

    def arrived_p3(self, k):
        g = self.g
        z = lax.rem(g.z + k, g.Z)
        for a2 in (0, 1):
            self.wait(self.n_p3 + z * 2 + a2, g.row_block(z, a2, 1 - g.i3, g.c))
            self.sib_copy(z, a2, 1 - g.i3).start()

    def arrived_sib(self, z):
        g = self.g
        for xx in (0, 1):
            for yy in (0, 1):
                number = self.n_sib + (z * 2 + xx) * 2 + yy
                self.wait(number, ((z * 2 + xx) * 2 + 1 - g.c) * 2 + yy)

    def own_here(self):
        self.own_copy().wait()

    def sent(self):
        g, src = self.g, self.shard
        self.p2_copy(g.z, src).wait_send()
        self.p3_copy(g.z, g.i2, src).wait_send()
        self.sib_copy(g.z, g.i2, g.i3, src).wait_send()
        for k in range(1, g.Z):
            self.z_copy(g.z, False, k, src).wait_send()
            if self.by_z:
                self.z_copy(g.z, True, k).wait_send()
            z = lax.rem(g.z + k, g.Z)
            if not self.by_z:
                self.p2_copy(z).wait_send()
            self.p3_copy(z, g.i2).wait_send()
            self.sib_copy(z, g.i2, g.i3).wait_send()
        for k in range(g.Z):
            z = lax.rem(g.z + k, g.Z)
            self.p3_copy(z, 1 - g.i2).wait_send()
            self.sib_copy(z, 1 - g.i2, g.i3).wait_send()
            for a2 in (0, 1):
                self.sib_copy(z, a2, 1 - g.i3).wait_send()


def gather_kernel(dp_size, by_z, n, *refs):
    shards, fulls = refs[:n], refs[n : 2 * n]
    sends, recvs = refs[2 * n : 3 * n], refs[3 * n : 4 * n]
    g = Place(dp_size)
    g.barrier()
    ms = [
        Gather(g, shards[i], fulls[i], sends[i], recvs[i], by_z[i]) for i in range(n)
    ]
    for m in ms:
        m.start()
    for m in ms:
        m.first_p2()
        for k in range(1, g.Z):
            m.arrived_z(k)
        for k in range(1, g.Z):
            m.later_p2(k)
        for k in range(g.Z):
            m.arrived_p3(k)
    for m in ms:
        for z in range(g.Z):
            m.arrived_sib(z)
        m.own_here()
    for m in ms:
        m.sent()


def gather_all(shards, by_z):
    dp_size = lax.axis_size("dp")
    devices = dp_size * lax.axis_size("ctx")
    n = len(shards)
    any_spec = pl.BlockSpec(memory_space=pl.ANY)
    return pl.pallas_call(
        functools.partial(gather_kernel, dp_size, by_z, n),
        out_shape=[jax.ShapeDtypeStruct((s.shape[0] * devices, s.shape[1]), s.dtype) for s in shards],
        in_specs=[any_spec] * n,
        out_specs=[any_spec] * n,
        scratch_shapes=[pltpu.SemaphoreType.DMA((Gather.sems(dp_size // 4),))] * (2 * n),
        compiler_params=pltpu.CompilerParams(
            collective_id=0, has_side_effects=True, vmem_limit_bytes=16 * 2**20
        ),
    )(*shards)


class Scatter:
    def __init__(self, place, part, rec3, rec2, recz, out, send, recv, by_z):
        self.g = place
        self.part, self.rec3, self.rec2, self.recz, self.out = part, rec3, rec2, recz, out
        self.send, self.recv, self.by_z = send, recv, by_z
        Z = place.Z
        self.n_p3, self.n_z, self.n_p2 = 0, 2 * Z, 2 * Z + 2 * (Z - 1)

    @staticmethod
    def sems(Z):
        return 2 * Z + 2 * (Z - 1) + Z

    def copy(self, src, dst, number, device):
        return pltpu.make_async_remote_copy(
            src_ref=src,
            dst_ref=dst,
            send_sem=self.send.at[number],
            recv_sem=self.recv.at[number],
            device_id=device,
            device_id_type=MESH,
        )

    def p3_copy(self, z, a2):
        g = self.g
        slot = z * 2 + a2
        return self.copy(
            self.part.at[g.block(z, a2, 1 - g.i3)], self.rec3.at[slot], self.n_p3 + slot, g.p3
        )

    def z_copy(self, k, a2):
        g = self.g
        z = lax.rem(g.z + k, g.Z)
        if self.by_z:
            slot = (k - 1) * 2 + a2
        else:
            slot = k - 1
        return self.copy(
            self.part.at[g.block(z, a2, g.i3)], self.recz.at[slot], self.n_z + slot, g.at_z(z)
        )

    def p2_copy(self, z):
        g = self.g
        slot = 0 if self.by_z else z
        return self.copy(
            self.part.at[g.block(z, 1 - g.i2, g.i3)], self.rec2.at[slot], self.n_p2 + slot, g.p2
        )

    def start(self, z, a2):
        self.p3_copy(z, a2).start()

    def add3(self, k, a2):
        g = self.g
        z = lax.rem(g.z + k, g.Z)
        self.p3_copy(z, a2).wait_recv()
        block = g.block(z, a2, g.i3)
        total = self.part[block].astype(jnp.float32) + self.rec3[z * 2 + a2].astype(jnp.float32)
        self.part[block] = total.astype(jnp.bfloat16)
        if self.by_z and k > 0:
            self.z_copy(k, a2).start()

    def stage3(self, k):
        g = self.g
        if self.by_z:
            for a2 in (0, 1):
                self.add3(k, a2)
        else:
            self.add3(k, 1 - g.i2)
            self.p2_copy(lax.rem(g.z + k, g.Z)).start()
            self.add3(k, g.i2)

    def stage2(self, k):
        g = self.g
        z = lax.rem(g.z + k, g.Z)
        self.p2_copy(z).wait_recv()
        block = g.block(z, g.i2, g.i3)
        total = self.part[block].astype(jnp.float32) + self.rec2[z].astype(jnp.float32)
        if k > 0:
            self.part[block] = total.astype(jnp.bfloat16)
            self.z_copy(k, g.i2).start()
        else:
            self.out[...] = total

    def last_z(self):
        g = self.g
        for k in range(1, g.Z):
            self.z_copy(k, g.i2).wait_recv()
            self.out[...] += self.recz[k - 1].astype(jnp.float32)

    def sum_z(self):
        g = self.g
        block = g.block(g.z, 1 - g.i2, g.i3)
        total = self.part[block].astype(jnp.float32)
        for k in range(1, g.Z):
            self.z_copy(k, 1 - g.i2).wait_recv()
            total += self.recz[(k - 1) * 2 + 1 - g.i2].astype(jnp.float32)
        self.part[block] = total.astype(jnp.bfloat16)
        self.p2_copy(g.z).start()
        total = self.part[g.block(g.z, g.i2, g.i3)].astype(jnp.float32)
        for k in range(1, g.Z):
            self.z_copy(k, g.i2).wait_recv()
            total += self.recz[(k - 1) * 2 + g.i2].astype(jnp.float32)
        self.out[...] = total

    def last_p2(self):
        self.p2_copy(self.g.z).wait_recv()
        self.out[...] += self.rec2[0].astype(jnp.float32)

    def sent(self):
        g = self.g
        for z in range(g.Z):
            for a2 in (0, 1):
                self.p3_copy(z, a2).wait_send()
        for k in range(1, g.Z):
            if self.by_z:
                self.z_copy(k, 0).wait_send()
                self.z_copy(k, 1).wait_send()
            else:
                self.z_copy(k, g.i2).wait_send()
        if self.by_z:
            self.p2_copy(g.z).wait_send()
        else:
            for z in range(g.Z):
                self.p2_copy(z).wait_send()


def scatter_kernel(dp_size, by_z, n, *refs):
    grads, outs = refs[:n], refs[n : 2 * n]
    scr = refs[2 * n :]
    g = Place(dp_size)
    Z = g.Z
    g.barrier()
    ms = []
    sibs = []
    for i in range(n):
        part, rsib, rec3, rec2, recz, send, recv, ssend, srecv, slocal = scr[10 * i : 10 * i + 10]
        ms.append(Scatter(g, part, rec3, rec2, recz, outs[i], send, recv, by_z[i]))
        sibs.append((grads[i], part, rsib, ssend, srecv, slocal))

    def sib_copy(s, q):
        grad, part, rsib, ssend, srecv, slocal = s
        return pltpu.make_async_remote_copy(
            src_ref=grad.at[2 * q + 1 - g.c],
            dst_ref=rsib.at[q],
            send_sem=ssend.at[q],
            recv_sem=srecv.at[q],
            device_id=g.sib,
            device_id_type=MESH,
        )

    def loc_copy(s, q):
        grad, part, rsib, ssend, srecv, slocal = s
        return pltpu.make_async_copy(grad.at[2 * q + g.c], part.at[pl.ds(2 * q, 2)], slocal.at[q])

    for s in sibs:
        for q in range(2 * Z):
            sib_copy(s, q).start()
            loc_copy(s, q).start()
    for s, m in zip(sibs, ms):
        for q in range(2 * Z):
            sib_copy(s, q).wait_recv()
            loc_copy(s, q).wait()
            for j in (0, 1):
                part, rsib = s[1], s[2]
                part[2 * q + j] = (
                    part[2 * q + j].astype(jnp.float32) + rsib[q, j].astype(jnp.float32)
                ).astype(jnp.bfloat16)
        for z in range(Z):
            for a2 in (0, 1):
                m.start(z, a2)
    for m in ms:
        for k in range(1, Z):
            m.stage3(k)
        m.stage3(0)
    for m in ms:
        if not m.by_z:
            for k in range(1, Z):
                m.stage2(k)
            m.stage2(0)
    for m in ms:
        if m.by_z:
            m.sum_z()
    for m in ms:
        if m.by_z:
            m.last_p2()
        else:
            m.last_z()
    for s, m in zip(sibs, ms):
        m.sent()
        for q in range(2 * Z):
            sib_copy(s, q).wait_send()


def scatter_all(grads, by_z):
    dp_size = lax.axis_size("dp")
    Z = dp_size // 4
    n = len(grads)
    scratch, outs, views = [], [], []
    for grad, z_first in zip(grads, by_z):
        rows, cols = grad.shape[0] // (8 * Z), grad.shape[1]
        bf = jnp.bfloat16
        scratch += [
            pltpu.VMEM((4 * Z, rows, cols), bf),
            pltpu.VMEM((2 * Z, 2, rows, cols), bf),
            pltpu.VMEM((2 * Z, rows, cols), bf),
            pltpu.VMEM((1 if z_first else Z, rows, cols), bf),
            pltpu.VMEM(((2 if z_first else 1) * (Z - 1), rows, cols), bf),
            pltpu.SemaphoreType.DMA((Scatter.sems(Z),)),
            pltpu.SemaphoreType.DMA((Scatter.sems(Z),)),
            pltpu.SemaphoreType.DMA((2 * Z,)),
            pltpu.SemaphoreType.DMA((2 * Z,)),
            pltpu.SemaphoreType.DMA((2 * Z,)),
        ]
        outs.append(jax.ShapeDtypeStruct((rows, cols), jnp.float32))
        views.append(grad.reshape(4 * Z, 2, rows, cols))
    return pl.pallas_call(
        functools.partial(scatter_kernel, dp_size, by_z, n),
        out_shape=outs,
        in_specs=[pl.BlockSpec(memory_space=pl.ANY)] * n,
        out_specs=[pl.BlockSpec(memory_space=pltpu.VMEM)] * n,
        scratch_shapes=scratch,
        compiler_params=pltpu.CompilerParams(
            collective_id=1, has_side_effects=True, vmem_limit_bytes=60 * 2**20
        ),
    )(*views)


HEADS = 16
DOCS = 7


epsilon = 1e-05
masked_score = -1e30


def layer_norm(values, gain_vec):
    center = values - jnp.mean(values, axis=-1, keepdims=True)
    spread = jnp.mean(center * center, axis=-1, keepdims=True)
    return center * lax.rsqrt(spread + epsilon) * gain_vec


def norm_back(values, gain_vec, upstream):
    unused, pullback = jax.vjp(layer_norm, values, gain_vec)
    return pullback(upstream)


def rotate(values, cosine_table, sine_table, direction):
    half_dim = values.shape[-1] // 2
    first_half = values[..., :half_dim]
    second_half = values[..., half_dim:]
    return jnp.concatenate(
        [
            first_half * cosine_table - direction * second_half * sine_table,
            second_half * cosine_table + direction * first_half * sine_table,
        ],
        axis=-1,
    )


def doc_layout(lengths, row_len):
    doc_ends = jnp.cumsum(lengths, axis=-1)
    places = jnp.arange(row_len, dtype=jnp.int32)
    passed = places[None, :, None] >= doc_ends[:, None, :]
    segment = jnp.sum(passed.astype(jnp.int32), axis=-1)
    starts = jnp.sum(jnp.where(passed, lengths[:, None, :], 0), axis=-1)
    position = places[None, :] - starts
    is_valid = places[None, :] < doc_ends[:, DOCS - 2][:, None]
    return (segment[0], position[0], is_valid[0])


def allowed_keys(own_seg, own_place, seg_full, first_key, block_rows):
    key_place = first_key + jnp.arange(block_rows, dtype=jnp.int32)
    key_seg = lax.dynamic_slice_in_dim(seg_full, first_key, block_rows)
    return (own_seg[:, None] == key_seg[None, :]) & (key_place[None, :] <= own_place[:, None])


def make_fold(queries, own_seg, own_place, seg_full, score_scale):

    def fold_piece(fold_state, piece, start):
        key_piece, value_piece = piece
        piece_rows = key_piece.shape[0]
        block_rows = math.gcd(piece_rows, 256)
        block_count = piece_rows // block_rows
        key_blocks = key_piece.reshape((block_count, block_rows) + key_piece.shape[1:])
        value_blocks = value_piece.reshape((block_count, block_rows) + value_piece.shape[1:])

        def step_block(carried, block_items):
            row_max, row_sum, weighted = carried
            key_block, value_block, block_id = block_items
            allowed = allowed_keys(own_seg, own_place, seg_full, block_id * block_rows, block_rows)
            scores = (
                jnp.einsum("qhd,khd->hqk", queries, key_block, preferred_element_type=jnp.float32)
                * score_scale
            )
            scores = jnp.where(allowed[None], scores, masked_score)
            new_max = jnp.maximum(row_max, jnp.max(scores, axis=-1))
            factor = jnp.exp(row_max - new_max)
            shifted = jnp.where(allowed[None], jnp.exp(scores - new_max[..., None]), 0.0)
            row_sum = row_sum * factor + jnp.sum(shifted, axis=-1)
            weighted = weighted * factor[..., None] + jnp.einsum(
                "hqk,khd->hqd",
                shifted.astype(jnp.bfloat16),
                value_block,
                preferred_element_type=jnp.float32,
            )
            return ((new_max, row_sum, weighted), None)

        block_ids = jnp.arange(block_count, dtype=jnp.int32)
        fold_state, unused = lax.scan(step_block, fold_state, (key_blocks, value_blocks, block_ids))
        return fold_state

    return fold_piece


def per_device(tokens, lengths, w_qkv, w_out, w_up, w_down, gains, d_out):
    tok_rows, model_width = tokens.shape
    row_len = tok_rows * lax.axis_size("ctx")
    head_count = HEADS
    head_dim = model_width // head_count
    score_scale = head_dim ** (-0.5)
    head_shape = (tok_rows, head_count, head_dim)
    seg_full, pos_full, valid_full = doc_layout(lengths, row_len)
    offset = lax.axis_index("ctx") * tok_rows
    own_seg = lax.dynamic_slice_in_dim(seg_full, offset, tok_rows)
    own_pos = lax.dynamic_slice_in_dim(pos_full, offset, tok_rows)
    own_valid = lax.dynamic_slice_in_dim(valid_full.astype(jnp.float32), offset, tok_rows)
    own_place = offset + jnp.arange(tok_rows, dtype=jnp.int32)
    freq_index = jnp.arange(head_dim // 2, dtype=jnp.float32)
    angles = own_pos.astype(jnp.float32)[:, None] * 10000.0 ** (-2.0 * freq_index / head_dim)
    cosine_table = jnp.cos(angles)[:, None, :]
    sine_table = jnp.sin(angles)[:, None, :]
    gains_wide = jnp.pad(gains, ((0, 0), (0, 128 - gains.shape[1])))
    gain_full, qkv_full, out_full, up_full, down_full = gather_all(
        (gains_wide, w_qkv, w_out, w_up, w_down), (False, True, True, False, False)
    )
    gain_full = gain_full[:, : gains.shape[1]]
    gain_f = gain_full.astype(jnp.float32)
    stream = tokens.astype(jnp.float32)
    normed = layer_norm(stream, gain_f[:, 0]).astype(jnp.bfloat16)
    qkv_raw = jnp.dot(normed, qkv_full, preferred_element_type=jnp.float32)
    queries = rotate(
        qkv_raw[:, :model_width].reshape(head_shape), cosine_table, sine_table, 1.0
    ).astype(jnp.bfloat16)
    key_heads = rotate(
        qkv_raw[:, model_width : 2 * model_width].reshape(head_shape), cosine_table, sine_table, 1.0
    ).astype(jnp.bfloat16)
    value_heads = qkv_raw[:, 2 * model_width :].reshape(head_shape).astype(jnp.bfloat16)
    start_state = (
        jnp.full((head_count, tok_rows), masked_score, jnp.float32),
        jnp.zeros((head_count, tok_rows), jnp.float32),
        jnp.zeros((head_count, tok_rows, head_dim), jnp.float32),
    )
    fold_piece = make_fold(queries, own_seg, own_place, seg_full, score_scale)
    row_max, row_sum, weighted = fold_piece(
        start_state,
        (
            lax.all_gather(key_heads, "ctx", axis=0, tiled=True),
            lax.all_gather(value_heads, "ctx", axis=0, tiled=True),
        ),
        jnp.int32(0),
    )
    attended = jnp.transpose(weighted / row_sum[..., None], (1, 0, 2))
    attended_b = attended.reshape(tok_rows, model_width).astype(jnp.bfloat16)
    attn_raw = jnp.dot(attended_b, out_full, preferred_element_type=jnp.float32)
    hidden = stream + layer_norm(attn_raw, gain_f[:, 1])
    mlp_in = layer_norm(hidden, gain_f[:, 2]).astype(jnp.bfloat16)
    up_proj = jnp.dot(mlp_in, up_full, preferred_element_type=jnp.float32)
    activated = jax.nn.gelu(up_proj).astype(jnp.bfloat16)
    mlp_raw = jnp.dot(activated, down_full, preferred_element_type=jnp.float32)
    result = hidden + layer_norm(mlp_raw, gain_f[:, 3])
    output = (result * own_valid[:, None]).astype(jnp.bfloat16)
    qkv_back, out_back, up_back, down_back = (qkv_full, out_full, up_full, down_full)
    upstream = d_out.astype(jnp.float32) * own_valid[:, None]
    d_mlp, d_gain_four = norm_back(mlp_raw, gain_f[:, 3], upstream)
    d_mlp_b = d_mlp.astype(jnp.bfloat16)
    grad_down = jnp.einsum("tf,td->fd", activated, d_mlp_b, preferred_element_type=jnp.float32)
    d_activated = jnp.einsum("td,fd->tf", d_mlp_b, down_back, preferred_element_type=jnp.float32)
    unused, gelu_pull = jax.vjp(jax.nn.gelu, up_proj)
    d_up_b = gelu_pull(d_activated)[0].astype(jnp.bfloat16)
    grad_up = jnp.einsum("td,tf->df", mlp_in, d_up_b, preferred_element_type=jnp.float32)
    d_mlp_in = jnp.einsum("tf,df->td", d_up_b, up_back, preferred_element_type=jnp.float32)
    d_hidden_part, d_gain_three = norm_back(hidden, gain_f[:, 2], d_mlp_in)
    d_hidden = upstream + d_hidden_part
    d_attn, d_gain_two = norm_back(attn_raw, gain_f[:, 1], d_hidden)
    d_attn_b = d_attn.astype(jnp.bfloat16)
    grad_out = jnp.einsum("td,te->de", attended_b, d_attn_b, preferred_element_type=jnp.float32)
    d_attended = (
        jnp.einsum("te,de->td", d_attn_b, out_back, preferred_element_type=jnp.float32)
        .astype(jnp.bfloat16)
        .reshape(head_shape)
    )
    row_dot = jnp.einsum("qhd,qhd->hq", d_attended.astype(jnp.float32), attended)
    key_all, value_all = (
        lax.all_gather(key_heads, "ctx", axis=0, tiled=True),
        lax.all_gather(value_heads, "ctx", axis=0, tiled=True),
    )
    block_rows = math.gcd(row_len, 256)
    block_count = row_len // block_rows
    key_blocks = key_all.reshape((block_count, block_rows) + key_all.shape[1:])
    value_blocks = value_all.reshape((block_count, block_rows) + value_all.shape[1:])

    def back_block(d_queries, block_items):
        key_block, value_block, block_id = block_items
        allowed = allowed_keys(own_seg, own_place, seg_full, block_id * block_rows, block_rows)
        scores = (
            jnp.einsum("qhd,khd->hqk", queries, key_block, preferred_element_type=jnp.float32)
            * score_scale
        )
        attn_prob = jnp.where(
            allowed[None], jnp.exp(scores - row_max[..., None]) / row_sum[..., None], 0.0
        )
        d_prob = jnp.einsum(
            "qhd,khd->hqk", d_attended, value_block, preferred_element_type=jnp.float32
        )
        d_scores = (attn_prob * (d_prob - row_dot[..., None])).astype(jnp.bfloat16)
        d_queries = (
            d_queries
            + jnp.einsum("hqk,khd->qhd", d_scores, key_block, preferred_element_type=jnp.float32)
            * score_scale
        )
        d_keys = (
            jnp.einsum("hqk,qhd->khd", d_scores, queries, preferred_element_type=jnp.float32)
            * score_scale
        )
        d_values = jnp.einsum(
            "hqk,qhd->khd",
            attn_prob.astype(jnp.bfloat16),
            d_attended,
            preferred_element_type=jnp.float32,
        )
        return (d_queries, (d_keys, d_values))

    block_ids = jnp.arange(block_count, dtype=jnp.int32)
    d_queries, (d_keys_all, d_values_all) = lax.scan(
        back_block, jnp.zeros(head_shape, jnp.float32), (key_blocks, value_blocks, block_ids)
    )
    kv_terms = jnp.concatenate(
        [d_keys_all.reshape(row_len, model_width), d_values_all.reshape(row_len, model_width)],
        axis=-1,
    )
    kv_grad = lax.psum_scatter(
        kv_terms.astype(jnp.bfloat16), "ctx", scatter_dimension=0, tiled=True
    ).astype(jnp.float32)
    d_keys = kv_grad[:, :model_width].reshape(head_shape)
    d_qkv = jnp.concatenate(
        [
            rotate(d_queries, cosine_table, sine_table, -1.0).reshape(tok_rows, model_width),
            rotate(d_keys, cosine_table, sine_table, -1.0).reshape(tok_rows, model_width),
            kv_grad[:, model_width:],
        ],
        axis=-1,
    ).astype(jnp.bfloat16)
    grad_qkv = jnp.einsum("td,te->de", normed, d_qkv, preferred_element_type=jnp.float32)
    d_normed = jnp.einsum("te,de->td", d_qkv, qkv_back, preferred_element_type=jnp.float32)
    d_stream_part, d_gain_one = norm_back(stream, gain_f[:, 0], d_normed)
    d_tokens = (d_hidden + d_stream_part).astype(jnp.bfloat16)
    grad_gains = jnp.stack([d_gain_one, d_gain_two, d_gain_three, d_gain_four], axis=-1)
    grad_gains = jnp.pad(grad_gains, ((0, 0), (0, 128 - gains.shape[1])))
    shard_down, shard_up, shard_out, shard_qkv, shard_gains = scatter_all(
        [v.astype(jnp.bfloat16) for v in (grad_down, grad_up, grad_out, grad_qkv, grad_gains)],
        (False, False, True, True, False),
    )
    shard_gains = shard_gains[:, : gains.shape[1]]
    return (output, d_tokens, shard_qkv, shard_out, shard_up, shard_down, shard_gains)


def solution(mesh):
    return jax.shard_map(
        per_device,
        mesh=mesh,
        in_specs=(
            P(("dp", "ctx"), None),
            P("dp", None),
            P(("dp", "ctx"), None),
            P(("dp", "ctx"), None),
            P(("dp", "ctx"), None),
            P(("dp", "ctx"), None),
            P(("dp", "ctx"), None),
            P(("dp", "ctx"), None),
        ),
        out_specs=(
            P(("dp", "ctx"), None),
            P(("dp", "ctx"), None),
            P(("dp", "ctx"), None),
            P(("dp", "ctx"), None),
            P(("dp", "ctx"), None),
            P(("dp", "ctx"), None),
            P(("dp", "ctx"), None),
        ),
        check_vma=False,
    )
```

```python
import math

import jax
import jax.numpy as jnp
import numpy as np
from jax import lax
from jax.sharding import PartitionSpec as P

import functools
from jax.experimental import pallas as pl
from jax.experimental.pallas import tpu as pltpu

MESH = pl.DeviceIdType.MESH


class Place:
    def __init__(self, dp_size):
        dp = lax.axis_index("dp")
        self.Z = dp_size // 4
        self.z = lax.div(dp, 4)
        self.x = lax.rem(lax.div(dp, 2), 2)
        self.c = lax.rem(dp, 2)
        self.y = lax.axis_index("ctx")
        c, x, y = self.c, self.x, self.y
        self.i2 = y * (1 - c) + x * c
        self.i3 = x * (1 - c) + y * c
        self.sib = self.device(self.z, x, 1 - c, y)
        self.p2 = self.device(self.z, x * (1 - c) + (1 - x) * c, c, (1 - y) * (1 - c) + y * c)
        self.p3 = self.device(self.z, (1 - x) * (1 - c) + x * c, c, y * (1 - c) + (1 - y) * c)

    def device(self, z, x, c, y):
        return ((z * 2 + x) * 2 + c, y)

    def at_z(self, z):
        return self.device(z, self.x, self.c, self.y)

    def block(self, z, a2, a3):
        c = self.c
        return (z * 2 + a3 * (1 - c) + a2 * c) * 2 + a2 * (1 - c) + a3 * c

    def row_block(self, z, a2, a3, core):
        c = self.c
        xx = a3 * (1 - c) + a2 * c
        yy = a2 * (1 - c) + a3 * c
        return ((z * 2 + xx) * 2 + core) * 2 + yy

    def barrier(self):
        bar = pltpu.get_barrier_semaphore()
        for device in (self.sib, self.p2, self.p3):
            pl.semaphore_signal(bar, 1, device_id=device, device_id_type=MESH)
        for k in range(1, self.Z):
            pl.semaphore_signal(
                bar, 1, device_id=self.at_z(lax.rem(self.z + k, self.Z)), device_id_type=MESH
            )
        pl.semaphore_wait(bar, 3 + self.Z - 1)


class Gather:
    def __init__(self, place, shard, full, send, recv, by_z):
        self.g, self.shard, self.full = place, shard, full
        self.send, self.recv = send, recv
        self.rows = shard.shape[0]
        self.by_z = by_z
        Z = place.Z
        self.n_z = 0
        self.n_p2 = 2 * (Z - 1)
        self.n_p3 = self.n_p2 + Z
        self.n_sib = self.n_p3 + 2 * Z
        self.n_own = self.n_sib + 4 * Z
        self.count = self.n_own + 1

    @staticmethod
    def sems(Z):
        return 2 * (Z - 1) + Z + 2 * Z + 4 * Z + 1

    def at(self, index):
        return self.full.at[pl.ds(pl.multiple_of(index * self.rows, self.rows), self.rows)]

    def copy(self, index, number, device, src=None):
        return pltpu.make_async_remote_copy(
            src_ref=self.at(index) if src is None else src,
            dst_ref=self.at(index),
            send_sem=self.send.at[number],
            recv_sem=self.recv.at[number],
            device_id=device,
            device_id_type=MESH,
        )

    def own_copy(self):
        g = self.g
        index = g.row_block(g.z, g.i2, g.i3, g.c)
        return pltpu.make_async_copy(self.shard, self.at(index), self.recv.at[self.n_own])

    def z_copy(self, z, a2_is_other, k, src=None):
        g = self.g
        a2 = (1 - g.i2) if a2_is_other else g.i2
        index = g.row_block(z, a2, g.i3, g.c)
        to = lax.rem(g.z + k, g.Z)
        return self.copy(index, self.n_z + (k - 1) * 2 + int(a2_is_other), g.at_z(to), src)

    def p2_copy(self, z, src=None):
        g = self.g
        return self.copy(g.row_block(z, g.i2, g.i3, g.c), self.n_p2 + z, g.p2, src)

    def p3_copy(self, z, a2, src=None):
        g = self.g
        return self.copy(g.row_block(z, a2, g.i3, g.c), self.n_p3 + z * 2 + a2, g.p3, src)

    def sib_copy(self, z, a2, a3, src=None):
        g = self.g
        number = self.n_sib + g.block(z, a2, a3)
        return self.copy(g.row_block(z, a2, a3, g.c), number, g.sib, src)

    def wait(self, number, index):
        self.copy(index, number, self.g.sib).wait_recv()

    def start(self):
        g, src = self.g, self.shard
        self.own_copy().start()
        self.p2_copy(g.z, src).start()
        self.p3_copy(g.z, g.i2, src).start()
        for k in range(1, g.Z):
            self.z_copy(g.z, False, k, src).start()
        self.sib_copy(g.z, g.i2, g.i3, src).start()

    def arrived_p2(self, z):
        g = self.g
        o2 = 1 - g.i2
        self.wait(self.n_p2 + z, g.row_block(z, o2, g.i3, g.c))
        self.p3_copy(z, o2).start()
        self.sib_copy(z, o2, g.i3).start()

    def first_p2(self):
        g = self.g
        self.arrived_p2(g.z)
        if self.by_z:
            for k in range(1, g.Z):
                self.z_copy(g.z, True, k).start()

    def arrived_z(self, k):
        g = self.g
        z = lax.rem(g.z - k + g.Z, g.Z)
        for other in ((False, True) if self.by_z else (False,)):
            a2 = (1 - g.i2) if other else g.i2
            self.wait(self.n_z + (k - 1) * 2 + int(other), g.row_block(z, a2, g.i3, g.c))
            if not self.by_z:
                self.p2_copy(z).start()
            self.p3_copy(z, a2).start()
            self.sib_copy(z, a2, g.i3).start()

    def later_p2(self, k):
        if not self.by_z:
            self.arrived_p2(lax.rem(self.g.z + k, self.g.Z))

    def arrived_p3(self, k):
        g = self.g
        z = lax.rem(g.z + k, g.Z)
        for a2 in (0, 1):
            self.wait(self.n_p3 + z * 2 + a2, g.row_block(z, a2, 1 - g.i3, g.c))
            self.sib_copy(z, a2, 1 - g.i3).start()

    def arrived_sib(self, z):
        g = self.g
        for xx in (0, 1):
            for yy in (0, 1):
                number = self.n_sib + (z * 2 + xx) * 2 + yy
                self.wait(number, ((z * 2 + xx) * 2 + 1 - g.c) * 2 + yy)

    def own_here(self):
        self.own_copy().wait()

    def sent(self):
        g, src = self.g, self.shard
        self.p2_copy(g.z, src).wait_send()
        self.p3_copy(g.z, g.i2, src).wait_send()
        self.sib_copy(g.z, g.i2, g.i3, src).wait_send()
        for k in range(1, g.Z):
            self.z_copy(g.z, False, k, src).wait_send()
            if self.by_z:
                self.z_copy(g.z, True, k).wait_send()
            z = lax.rem(g.z + k, g.Z)
            if not self.by_z:
                self.p2_copy(z).wait_send()
            self.p3_copy(z, g.i2).wait_send()
            self.sib_copy(z, g.i2, g.i3).wait_send()
        for k in range(g.Z):
            z = lax.rem(g.z + k, g.Z)
            self.p3_copy(z, 1 - g.i2).wait_send()
            self.sib_copy(z, 1 - g.i2, g.i3).wait_send()
            for a2 in (0, 1):
                self.sib_copy(z, a2, 1 - g.i3).wait_send()


def gather_kernel(dp_size, by_z, n, *refs):
    shards, fulls = refs[:n], refs[n : 2 * n]
    sends, recvs = refs[2 * n : 3 * n], refs[3 * n : 4 * n]
    g = Place(dp_size)
    g.barrier()
    ms = [
        Gather(g, shards[i], fulls[i], sends[i], recvs[i], by_z[i]) for i in range(n)
    ]
    for m in ms:
        m.start()
    for m in ms:
        m.first_p2()
        for k in range(1, g.Z):
            m.arrived_z(k)
        for k in range(1, g.Z):
            m.later_p2(k)
        for k in range(g.Z):
            m.arrived_p3(k)
    for m in ms:
        for z in range(g.Z):
            m.arrived_sib(z)
        m.own_here()
    for m in ms:
        m.sent()


def gather_all(shards, by_z):
    dp_size = lax.axis_size("dp")
    devices = dp_size * lax.axis_size("ctx")
    n = len(shards)
    any_spec = pl.BlockSpec(memory_space=pl.ANY)
    return pl.pallas_call(
        functools.partial(gather_kernel, dp_size, by_z, n),
        out_shape=[jax.ShapeDtypeStruct((s.shape[0] * devices, s.shape[1]), s.dtype) for s in shards],
        in_specs=[any_spec] * n,
        out_specs=[any_spec] * n,
        scratch_shapes=[pltpu.SemaphoreType.DMA((Gather.sems(dp_size // 4),))] * (2 * n),
        compiler_params=pltpu.CompilerParams(
            collective_id=0, has_side_effects=True, vmem_limit_bytes=16 * 2**20
        ),
    )(*shards)


class Scatter:
    def __init__(self, place, part, rec3, rec2, recz, out, send, recv, by_z):
        self.g = place
        self.part, self.rec3, self.rec2, self.recz, self.out = part, rec3, rec2, recz, out
        self.send, self.recv, self.by_z = send, recv, by_z
        Z = place.Z
        self.n_p3, self.n_z, self.n_p2 = 0, 2 * Z, 2 * Z + 2 * (Z - 1)

    @staticmethod
    def sems(Z):
        return 2 * Z + 2 * (Z - 1) + Z

    def copy(self, src, dst, number, device):
        return pltpu.make_async_remote_copy(
            src_ref=src,
            dst_ref=dst,
            send_sem=self.send.at[number],
            recv_sem=self.recv.at[number],
            device_id=device,
            device_id_type=MESH,
        )

    def p3_copy(self, z, a2):
        g = self.g
        slot = z * 2 + a2
        return self.copy(
            self.part.at[g.block(z, a2, 1 - g.i3)], self.rec3.at[slot], self.n_p3 + slot, g.p3
        )

    def z_copy(self, k, a2):
        g = self.g
        z = lax.rem(g.z + k, g.Z)
        if self.by_z:
            slot = (k - 1) * 2 + a2
        else:
            slot = k - 1
        return self.copy(
            self.part.at[g.block(z, a2, g.i3)], self.recz.at[slot], self.n_z + slot, g.at_z(z)
        )

    def p2_copy(self, z):
        g = self.g
        slot = 0 if self.by_z else z
        return self.copy(
            self.part.at[g.block(z, 1 - g.i2, g.i3)], self.rec2.at[slot], self.n_p2 + slot, g.p2
        )

    def start(self, z, a2):
        self.p3_copy(z, a2).start()

    def add3(self, k, a2):
        g = self.g
        z = lax.rem(g.z + k, g.Z)
        self.p3_copy(z, a2).wait_recv()
        block = g.block(z, a2, g.i3)
        total = self.part[block].astype(jnp.float32) + self.rec3[z * 2 + a2].astype(jnp.float32)
        self.part[block] = total.astype(jnp.bfloat16)
        if self.by_z and k > 0:
            self.z_copy(k, a2).start()

    def stage3(self, k):
        g = self.g
        if self.by_z:
            for a2 in (0, 1):
                self.add3(k, a2)
        else:
            self.add3(k, 1 - g.i2)
            self.p2_copy(lax.rem(g.z + k, g.Z)).start()
            self.add3(k, g.i2)

    def stage2(self, k):
        g = self.g
        z = lax.rem(g.z + k, g.Z)
        self.p2_copy(z).wait_recv()
        block = g.block(z, g.i2, g.i3)
        total = self.part[block].astype(jnp.float32) + self.rec2[z].astype(jnp.float32)
        if k > 0:
            self.part[block] = total.astype(jnp.bfloat16)
            self.z_copy(k, g.i2).start()
        else:
            self.out[...] = total

    def last_z(self):
        g = self.g
        for k in range(1, g.Z):
            self.z_copy(k, g.i2).wait_recv()
            self.out[...] += self.recz[k - 1].astype(jnp.float32)

    def sum_z(self):
        g = self.g
        block = g.block(g.z, 1 - g.i2, g.i3)
        total = self.part[block].astype(jnp.float32)
        for k in range(1, g.Z):
            self.z_copy(k, 1 - g.i2).wait_recv()
            total += self.recz[(k - 1) * 2 + 1 - g.i2].astype(jnp.float32)
        self.part[block] = total.astype(jnp.bfloat16)
        self.p2_copy(g.z).start()
        total = self.part[g.block(g.z, g.i2, g.i3)].astype(jnp.float32)
        for k in range(1, g.Z):
            self.z_copy(k, g.i2).wait_recv()
            total += self.recz[(k - 1) * 2 + g.i2].astype(jnp.float32)
        self.out[...] = total

    def last_p2(self):
        self.p2_copy(self.g.z).wait_recv()
        self.out[...] += self.rec2[0].astype(jnp.float32)

    def sent(self):
        g = self.g
        for z in range(g.Z):
            for a2 in (0, 1):
                self.p3_copy(z, a2).wait_send()
        for k in range(1, g.Z):
            if self.by_z:
                self.z_copy(k, 0).wait_send()
                self.z_copy(k, 1).wait_send()
            else:
                self.z_copy(k, g.i2).wait_send()
        if self.by_z:
            self.p2_copy(g.z).wait_send()
        else:
            for z in range(g.Z):
                self.p2_copy(z).wait_send()


def scatter_kernel(dp_size, by_z, n, *refs):
    grads, outs = refs[:n], refs[n : 2 * n]
    scr = refs[2 * n :]
    g = Place(dp_size)
    Z = g.Z
    g.barrier()
    ms = []
    sibs = []
    for i in range(n):
        part, rsib, rec3, rec2, recz, send, recv, ssend, srecv, slocal = scr[10 * i : 10 * i + 10]
        ms.append(Scatter(g, part, rec3, rec2, recz, outs[i], send, recv, by_z[i]))
        sibs.append((grads[i], part, rsib, ssend, srecv, slocal))

    def sib_copy(s, q):
        grad, part, rsib, ssend, srecv, slocal = s
        return pltpu.make_async_remote_copy(
            src_ref=grad.at[2 * q + 1 - g.c],
            dst_ref=rsib.at[q],
            send_sem=ssend.at[q],
            recv_sem=srecv.at[q],
            device_id=g.sib,
            device_id_type=MESH,
        )

    def loc_copy(s, q):
        grad, part, rsib, ssend, srecv, slocal = s
        return pltpu.make_async_copy(grad.at[2 * q + g.c], part.at[pl.ds(2 * q, 2)], slocal.at[q])

    for s in sibs:
        for q in range(2 * Z):
            sib_copy(s, q).start()
            loc_copy(s, q).start()
    for s, m in zip(sibs, ms):
        for q in range(2 * Z):
            sib_copy(s, q).wait_recv()
            loc_copy(s, q).wait()
            for j in (0, 1):
                part, rsib = s[1], s[2]
                part[2 * q + j] = (
                    part[2 * q + j].astype(jnp.float32) + rsib[q, j].astype(jnp.float32)
                ).astype(jnp.bfloat16)
        for z in range(Z):
            for a2 in (0, 1):
                m.start(z, a2)
    for m in ms:
        for k in range(1, Z):
            m.stage3(k)
        m.stage3(0)
    for m in ms:
        if not m.by_z:
            for k in range(1, Z):
                m.stage2(k)
            m.stage2(0)
    for m in ms:
        if m.by_z:
            m.sum_z()
    for m in ms:
        if m.by_z:
            m.last_p2()
        else:
            m.last_z()
    for s, m in zip(sibs, ms):
        m.sent()
        for q in range(2 * Z):
            sib_copy(s, q).wait_send()


def scatter_all(grads, by_z):
    dp_size = lax.axis_size("dp")
    Z = dp_size // 4
    n = len(grads)
    scratch, outs, views = [], [], []
    for grad, z_first in zip(grads, by_z):
        rows, cols = grad.shape[0] // (8 * Z), grad.shape[1]
        bf = jnp.bfloat16
        scratch += [
            pltpu.VMEM((4 * Z, rows, cols), bf),
            pltpu.VMEM((2 * Z, 2, rows, cols), bf),
            pltpu.VMEM((2 * Z, rows, cols), bf),
            pltpu.VMEM((1 if z_first else Z, rows, cols), bf),
            pltpu.VMEM(((2 if z_first else 1) * (Z - 1), rows, cols), bf),
            pltpu.SemaphoreType.DMA((Scatter.sems(Z),)),
            pltpu.SemaphoreType.DMA((Scatter.sems(Z),)),
            pltpu.SemaphoreType.DMA((2 * Z,)),
            pltpu.SemaphoreType.DMA((2 * Z,)),
            pltpu.SemaphoreType.DMA((2 * Z,)),
        ]
        outs.append(jax.ShapeDtypeStruct((rows, cols), jnp.float32))
        views.append(grad.reshape(4 * Z, 2, rows, cols))
    return pl.pallas_call(
        functools.partial(scatter_kernel, dp_size, by_z, n),
        out_shape=outs,
        in_specs=[pl.BlockSpec(memory_space=pl.ANY)] * n,
        out_specs=[pl.BlockSpec(memory_space=pltpu.VMEM)] * n,
        scratch_shapes=scratch,
        compiler_params=pltpu.CompilerParams(
            collective_id=1, has_side_effects=True, vmem_limit_bytes=60 * 2**20
        ),
    )(*views)


HEADS = 16
DOCS = 7


epsilon = 1e-05
masked_score = -1e30


def loop(count):
    def run(body):
        def step(i, carry):
            body(i)
            return carry

        lax.fori_loop(0, count, step, 0)

    return run


def dot(a, b):
    return jnp.dot(a, b, preferred_element_type=jnp.float32)


def dot_nt(a, b):
    return lax.dot_general(a, b, (((1,), (1,)), ((), ())), preferred_element_type=jnp.float32)


def normed(v):
    center = v - jnp.mean(v, axis=-1, keepdims=True)
    r = lax.rsqrt(jnp.mean(center * center, axis=-1, keepdims=True) + epsilon)
    return center * r, r


def norm_pull(v, gain, e):
    z, r = normed(v)
    f = e * gain
    dv = r * (
        f
        - jnp.mean(f, axis=-1, keepdims=True)
        - z * jnp.mean(f * z, axis=-1, keepdims=True)
    )
    return dv, e * z


def turn(u, cosine, sine, half):
    lane = lax.broadcasted_iota(jnp.int32, u.shape, 1)
    swapped = jnp.where(
        lax.rem(lane, 2 * half) < half,
        pltpu.roll(u, u.shape[1] - half, 1),
        pltpu.roll(u, half, 1),
    )
    return u * cosine + swapped * sine


def turn_tables(row_len, head_dim):
    half = head_dim // 2
    inverse = 10000.0 ** (-2.0 * np.arange(half) / head_dim)
    angles = np.arange(row_len)[:, None] * inverse[None, :]
    cosine = np.tile(np.cos(angles), (1, 4))
    sine = np.tile(np.concatenate([-np.sin(angles), np.sin(angles)], axis=1), (1, 2))
    return cosine.astype(np.float32), sine.astype(np.float32)


def doc_ends(lens):
    ends = [lens[0, 0]]
    for d in range(1, DOCS):
        ends.append(ends[-1] + lens[0, d])
    return ends


def fill_bias(bias, lens, first, rows):
    ends = doc_ends(lens)
    block = 128

    @loop(bias.shape[0] // block)
    def _(i):
        shape = (block, rows)
        place = first + lax.broadcasted_iota(jnp.int32, shape, 1)
        key = i * block + lax.broadcasted_iota(jnp.int32, shape, 0)
        start = jnp.zeros(shape, jnp.int32)
        for d in range(DOCS):
            start = jnp.where(place >= ends[d], ends[d], start)
        fine = (key >= start) & (key <= place)
        bias[pl.ds(i * block, block), :] = jnp.where(fine, 0.0, masked_score)


def split_heads(v, axis=1):
    spot = lax.broadcasted_iota(jnp.int32, v.shape, axis)
    first = spot < v.shape[axis] // 2
    zero = jnp.zeros_like(v)
    return jnp.where(first, v, zero), jnp.where(first, zero, v)


class Tiles:
    def __init__(self, source, buffer, sems):
        self.source, self.buffer, self.sems = source, buffer, sems

    def copy(self, t):
        slot = lax.rem(t, 2)
        return pltpu.make_async_copy(self.source(t), self.buffer.at[slot], self.sems.at[slot])

    def first(self, t=0):
        self.copy(jnp.int32(t)).start()

    def get(self, t, end):
        @pl.when(t + 1 < end)
        def _():
            self.copy(t + 1).start()

        self.copy(t).wait()
        return self.buffer[lax.rem(t, 2)]


def forward_kernel(dp_size, head_dim, *refs):
    (tok, lens, gs, wq, wo, wu, wd, cosine, sine) = refs[:9]
    (out, wq_f, wo_f, wu_f, wd_f, gain_o, q_o, k_o, v_o, ob_o, lse_o) = refs[9:20]
    (araw_o, h_o, mraw_o, bt_o, gt_o, gp_o, at_o, atx_o) = refs[20:28]
    (g_full, gain, tokx, a, ax, at, atx, q, k, v, vt, bias, ob, lse) = refs[28:42]
    (araw, h, mraw, b, bt, act, actt, gp, wbuf, dbuf) = refs[42:52]
    sems = refs[52:62]
    wsem, dsem, xsem, osem = refs[62:66]
    g = Place(dp_size)
    y = g.y
    rows, width = tok.shape
    half = head_dim // 2
    pairs = width // 128
    scale = head_dim ** (-0.5)
    gg, gq, go, gu, gd = [
        Gather(g, s, f, sems[2 * i], sems[2 * i + 1], False)
        for i, (s, f) in enumerate(
            ((gs, g_full), (wq, wq_f), (wo, wo_f), (wu, wu_f), (wd, wd_f))
        )
    ]
    Z = g.Z
    saves = []

    def save(src, dst):
        copy = pltpu.make_async_copy(src, dst, osem.at[len(saves)])
        copy.start()
        saves.append(copy)

    tok_copy = pltpu.make_async_remote_copy(
        src_ref=tok,
        dst_ref=tokx,
        send_sem=xsem.at[0],
        recv_sem=xsem.at[1],
        device_id=g.device(g.z, g.x, g.c, 1 - y),
        device_id_type=MESH,
    )
    g.barrier()
    gg.start()
    gq.start()

    @pl.when(y == 0)
    def _():
        tok_copy.start()

    go.start()
    fill_bias(bias, lens, y * rows, rows)
    for k_ in range(1, Z):
        gg.arrived_z(k_)
    for k_ in range(Z):
        gg.later_p2(k_)
    for k_ in range(Z):
        gg.arrived_p3(k_)
    for k_ in range(1, Z):
        gq.arrived_z(k_)
    gu.start()
    for z in range(Z):
        gg.arrived_sib(z)
    gg.own_here()
    turned = jnp.transpose(g_full[...].astype(jnp.float32))
    gain[...] = turned[:8]
    save(gain, gain_o)

    def first_norm(src, dst, dst_t):
        @loop(rows // 128)
        def _(i):
            spot = pl.ds(i * 128, 128)
            z, _r = normed(src[spot, :].astype(jnp.float32))
            value = z * gain[0:1, :]
            dst[spot, :] = value.astype(jnp.bfloat16)
            dst_t[:, spot] = jnp.transpose(value).astype(jnp.bfloat16)

    first_norm(tok, a, at)
    save(at, at_o)
    for k_ in range(Z):
        gq.later_p2(k_)

    @pl.when(y == 1)
    def _():
        tok_copy.wait_recv()
        first_norm(tokx, ax, atx)

    save(atx, atx_o)
    for k_ in range(Z):
        gq.arrived_p3(k_)
    for k_ in range(1, Z):
        go.arrived_z(k_)
    for k_ in range(Z):
        go.later_p2(k_)
    for z in range(Z):
        gq.arrived_sib(z)
    gq.own_here()

    tiles = Tiles(lambda t: wq_f.at[:, pl.ds(pl.multiple_of(t * 256, 256), 256)], wbuf, wsem)
    per = width // 256
    first = pl.multiple_of(y * rows, rows)

    def turned_pair(u, start):
        return turn(u, cosine[pl.ds(start, rows), :], sine[pl.ds(start, rows), :], half)

    tiles.first()

    @loop(per)
    def _(t):
        u = dot(a[...], tiles.get(t, 3 * per))
        for j in (0, 1):
            part = turned_pair(u[:, j * 128 : j * 128 + 128], first) * scale
            q[2 * t + j] = part.astype(jnp.bfloat16)

    for k_ in range(Z):
        go.arrived_p3(k_)
    for k_ in range(1, Z):
        gu.arrived_z(k_)
    gd.start()

    def keys(w, t, src, start):
        u = dot(src[...], w)
        for j in (0, 1):
            part = turned_pair(u[:, j * 128 : j * 128 + 128], start)
            k[2 * t + j, pl.ds(start, rows), :] = part.astype(jnp.bfloat16)

    @loop(per)
    def _(t):
        w = tiles.get(t + per, 3 * per)
        keys(w, t, a, first)

        @pl.when(y == 1)
        def _():
            keys(w, t, ax, 0)

    for k_ in range(Z):
        gu.later_p2(k_)

    def values(w, t, src, start):
        u = dot(src[...], w)
        ut = jnp.transpose(u).astype(jnp.bfloat16)
        for j in (0, 1):
            cols = slice(j * 128, j * 128 + 128)
            v[2 * t + j, pl.ds(start, rows), :] = u[:, cols].astype(jnp.bfloat16)
            vt[2 * t + j, :, pl.ds(start, rows)] = ut[cols]

    @loop(per)
    def _(t):
        w = tiles.get(t + 2 * per, 3 * per)
        values(w, t, a, first)

        @pl.when(y == 1)
        def _():
            values(w, t, ax, 0)

    save(q, q_o)
    save(k, k_o)
    save(v, v_o)

    def attend(p, block, count):
        spot = slice(block * 256, block * 256 + 256)
        heads = split_heads(q[p, spot, :])
        kk = k[p, :count, :]
        vv = vt[p, :, :count]
        parts = []
        for i in (0, 1):
            s = dot_nt(kk, heads[i]) + bias[:count, spot]
            m = jnp.max(s, axis=0, keepdims=True)
            e = jnp.exp(s - m)
            total = jnp.sum(e, axis=0, keepdims=True)
            lse[p, i : i + 1, spot] = m + jnp.log(total)
            parts.append(dot(vv, e.astype(jnp.bfloat16)) * (1.0 / total))
        upper = lax.broadcasted_iota(jnp.int32, parts[0].shape, 0) < head_dim
        ob[p, :, spot] = jnp.where(upper, parts[0], parts[1]).astype(jnp.bfloat16)

    events = [lambda: None] * pairs
    events[0] = lambda: [gu.arrived_p3(k_) for k_ in range(Z // 2)]
    events[1] = lambda: [gu.arrived_p3(k_) for k_ in range(Z // 2, Z)]
    events[2] = lambda: [gd.arrived_z(k_) for k_ in range(1, Z)]
    events[4] = lambda: [gd.later_p2(k_) for k_ in range(Z)]
    events[7] = lambda: [gd.arrived_p3(k_) for k_ in range(Z)]

    blocks = rows // 256

    @loop(pairs)
    def _(p):
        for half_row in (0, 1):

            @pl.when(y == half_row)
            def _():
                for block in range(blocks):
                    attend(p, block, (half_row * blocks + block + 1) * 256)

        for i in range(pairs):

            @pl.when(p == i)
            def _():
                events[i]()

    save(ob, ob_o)
    save(lse, lse_o)

    for z in range(Z):
        go.arrived_sib(z)
    go.own_here()
    obf = jnp.transpose(ob[...].reshape(width, rows))
    a[...] = obf
    tiles = Tiles(lambda t: wo_f.at[:, pl.ds(pl.multiple_of(t * 256, 256), 256)], wbuf, wsem)
    tiles.first()

    @loop(per)
    def _(t):
        w = tiles.get(t, per)
        araw[:, pl.ds(pl.multiple_of(t * 256, 256), 256)] = dot(a[...], w)

    save(araw, araw_o)

    @loop(rows // 128)
    def _(i):
        spot = pl.ds(i * 128, 128)
        z, _r = normed(araw[spot, :])
        hidden = tok[spot, :].astype(jnp.float32) + z * gain[1:2, :]
        h[spot, :] = hidden
        z, _r = normed(hidden)
        value = z * gain[2:3, :]
        b[spot, :] = value.astype(jnp.bfloat16)
        bt[:, spot] = jnp.transpose(value).astype(jnp.bfloat16)

    save(h, h_o)
    save(bt, bt_o)

    for z in range(Z):
        gu.arrived_sib(z)
    gu.own_here()
    tiles = Tiles(lambda t: wu_f.at[:, pl.ds(pl.multiple_of(t * 256, 256), 256)], wbuf, wsem)
    ups = act.shape[0]
    tiles.first()
    c0 = math.sqrt(2.0 / math.pi)

    @loop(ups)
    def _(t):
        u = dot(b[...], tiles.get(t, ups))
        square = u * u
        th = jnp.tanh(c0 * (u + 0.044715 * (square * u)))
        value = 0.5 * u * (1.0 + th)
        slope = 0.5 * (1.0 + th) + (0.5 * c0) * u * (1.0 - th * th) * (
            1.0 + (3 * 0.044715) * square
        )
        act[t] = value.astype(jnp.bfloat16)
        actt[t] = jnp.transpose(value).astype(jnp.bfloat16)
        gp[t] = slope.astype(jnp.bfloat16)

    save(actt, gt_o)
    save(gp, gp_o)

    for z in range(Z):
        gd.arrived_sib(z)
    gd.own_here()
    tiles = Tiles(lambda t: wd_f.at[pl.ds(pl.multiple_of(t * 256, 256), 256), :], dbuf, dsem)
    tiles.first()
    mraw[...] = jnp.zeros_like(mraw)

    @loop(ups)
    def _(t):
        mraw[...] += dot(act[t], tiles.get(t, ups))

    save(mraw, mraw_o)
    ends = doc_ends(lens)

    @loop(rows // 128)
    def _(i):
        spot = pl.ds(i * 128, 128)
        z, _r = normed(mraw[spot, :])
        result = h[spot, :] + z * gain[3:4, :]
        place = y * rows + i * 128 + lax.broadcasted_iota(jnp.int32, result.shape, 0)
        result = jnp.where(place < ends[DOCS - 2], result, 0.0)
        out[spot, :] = result.astype(jnp.bfloat16)

    for copy in saves:
        copy.wait()

    @pl.when(y == 0)
    def _():
        tok_copy.wait_send()

    for m in (gg, gq, go, gu, gd):
        m.sent()


def forward(tokens, lengths, gains_wide, w_qkv, w_out, w_up, w_down, tables):
    dp_size = lax.axis_size("dp")
    devices = dp_size * lax.axis_size("ctx")
    rows, width = tokens.shape
    row_len = rows * lax.axis_size("ctx")
    head_dim = width // HEADS
    pairs = width // 128
    ups = w_up.shape[1] // 256
    bf, f32 = jnp.bfloat16, jnp.float32
    any_spec = pl.BlockSpec(memory_space=pl.ANY)
    vm = pl.BlockSpec(memory_space=pltpu.VMEM)
    shape = jax.ShapeDtypeStruct

    def whole(w):
        return shape((w.shape[0] * devices, w.shape[1]), bf)

    outs = [
        shape((rows, width), bf),
        whole(w_qkv),
        whole(w_out),
        whole(w_up),
        whole(w_down),
        shape((8, width), f32),
        shape((pairs, rows, 128), bf),
        shape((pairs, row_len, 128), bf),
        shape((pairs, row_len, 128), bf),
        shape((pairs, 128, rows), bf),
        shape((pairs, 2, rows), f32),
        shape((rows, width), f32),
        shape((rows, width), f32),
        shape((rows, width), f32),
        shape((width, rows), bf),
        shape((ups, 256, rows), bf),
        shape((ups, rows, 256), bf),
        shape((width, rows), bf),
        shape((width, rows), bf),
    ]
    scratch = [
        pltpu.VMEM((width, 128), bf),
        pltpu.VMEM((8, width), f32),
        pltpu.VMEM((rows, width), bf),
        pltpu.VMEM((rows, width), bf),
        pltpu.VMEM((rows, width), bf),
        pltpu.VMEM((width, rows), bf),
        pltpu.VMEM((width, rows), bf),
        pltpu.VMEM((pairs, rows, 128), bf),
        pltpu.VMEM((pairs, row_len, 128), bf),
        pltpu.VMEM((pairs, row_len, 128), bf),
        pltpu.VMEM((pairs, 128, row_len), bf),
        pltpu.VMEM((row_len, rows), f32),
        pltpu.VMEM((pairs, 128, rows), bf),
        pltpu.VMEM((pairs, 2, rows), f32),
        pltpu.VMEM((rows, width), f32),
        pltpu.VMEM((rows, width), f32),
        pltpu.VMEM((rows, width), f32),
        pltpu.VMEM((rows, width), bf),
        pltpu.VMEM((width, rows), bf),
        pltpu.VMEM((ups, rows, 256), bf),
        pltpu.VMEM((ups, 256, rows), bf),
        pltpu.VMEM((ups, rows, 256), bf),
        pltpu.VMEM((2, width, 256), bf),
        pltpu.VMEM((2, 256, width), bf),
    ]
    scratch += [pltpu.SemaphoreType.DMA((Gather.sems(dp_size // 4),))] * 10
    scratch += [pltpu.SemaphoreType.DMA((2,))] * 3 + [pltpu.SemaphoreType.DMA((16,))]
    return pl.pallas_call(
        functools.partial(forward_kernel, dp_size, head_dim),
        out_shape=outs,
        in_specs=[vm, pl.BlockSpec(memory_space=pltpu.SMEM), vm]
        + [any_spec] * 4
        + [vm, vm],
        out_specs=[vm] + [any_spec] * (len(outs) - 1),
        scratch_shapes=scratch,
        compiler_params=pltpu.CompilerParams(
            collective_id=0, has_side_effects=True, vmem_limit_bytes=60 * 2**20
        ),
    )(tokens, lengths, gains_wide, w_qkv, w_out, w_up, w_down, *tables)


def layer_norm(values, gain_vec):
    center = values - jnp.mean(values, axis=-1, keepdims=True)
    spread = jnp.mean(center * center, axis=-1, keepdims=True)
    return center * lax.rsqrt(spread + epsilon) * gain_vec


def norm_back(values, gain_vec, upstream):
    unused, pullback = jax.vjp(layer_norm, values, gain_vec)
    return pullback(upstream)


def rotate(values, cosine_table, sine_table, direction):
    half_dim = values.shape[-1] // 2
    first_half = values[..., :half_dim]
    second_half = values[..., half_dim:]
    return jnp.concatenate(
        [
            first_half * cosine_table - direction * second_half * sine_table,
            second_half * cosine_table + direction * first_half * sine_table,
        ],
        axis=-1,
    )


def doc_layout(lengths, row_len):
    doc_ends = jnp.cumsum(lengths, axis=-1)
    places = jnp.arange(row_len, dtype=jnp.int32)
    passed = places[None, :, None] >= doc_ends[:, None, :]
    segment = jnp.sum(passed.astype(jnp.int32), axis=-1)
    starts = jnp.sum(jnp.where(passed, lengths[:, None, :], 0), axis=-1)
    position = places[None, :] - starts
    is_valid = places[None, :] < doc_ends[:, DOCS - 2][:, None]
    return (segment[0], position[0], is_valid[0])


def allowed_keys(own_seg, own_place, seg_full, first_key, block_rows):
    key_place = first_key + jnp.arange(block_rows, dtype=jnp.int32)
    key_seg = lax.dynamic_slice_in_dim(seg_full, first_key, block_rows)
    return (own_seg[:, None] == key_seg[None, :]) & (key_place[None, :] <= own_place[:, None])


def make_fold(queries, own_seg, own_place, seg_full, score_scale):

    def fold_piece(fold_state, piece, start):
        key_piece, value_piece = piece
        piece_rows = key_piece.shape[0]
        block_rows = math.gcd(piece_rows, 256)
        block_count = piece_rows // block_rows
        key_blocks = key_piece.reshape((block_count, block_rows) + key_piece.shape[1:])
        value_blocks = value_piece.reshape((block_count, block_rows) + value_piece.shape[1:])

        def step_block(carried, block_items):
            row_max, row_sum, weighted = carried
            key_block, value_block, block_id = block_items
            allowed = allowed_keys(own_seg, own_place, seg_full, block_id * block_rows, block_rows)
            scores = (
                jnp.einsum("qhd,khd->hqk", queries, key_block, preferred_element_type=jnp.float32)
                * score_scale
            )
            scores = jnp.where(allowed[None], scores, masked_score)
            new_max = jnp.maximum(row_max, jnp.max(scores, axis=-1))
            factor = jnp.exp(row_max - new_max)
            shifted = jnp.where(allowed[None], jnp.exp(scores - new_max[..., None]), 0.0)
            row_sum = row_sum * factor + jnp.sum(shifted, axis=-1)
            weighted = weighted * factor[..., None] + jnp.einsum(
                "hqk,khd->hqd",
                shifted.astype(jnp.bfloat16),
                value_block,
                preferred_element_type=jnp.float32,
            )
            return ((new_max, row_sum, weighted), None)

        block_ids = jnp.arange(block_count, dtype=jnp.int32)
        fold_state, unused = lax.scan(step_block, fold_state, (key_blocks, value_blocks, block_ids))
        return fold_state

    return fold_piece


def per_device(tokens, lengths, w_qkv, w_out, w_up, w_down, gains, d_out):
    tok_rows, model_width = tokens.shape
    row_len = tok_rows * lax.axis_size("ctx")
    head_count = HEADS
    head_dim = model_width // head_count
    score_scale = head_dim ** (-0.5)
    head_shape = (tok_rows, head_count, head_dim)
    seg_full, pos_full, valid_full = doc_layout(lengths, row_len)
    offset = lax.axis_index("ctx") * tok_rows
    own_seg = lax.dynamic_slice_in_dim(seg_full, offset, tok_rows)
    own_pos = lax.dynamic_slice_in_dim(pos_full, offset, tok_rows)
    own_valid = lax.dynamic_slice_in_dim(valid_full.astype(jnp.float32), offset, tok_rows)
    own_place = offset + jnp.arange(tok_rows, dtype=jnp.int32)
    freq_index = jnp.arange(head_dim // 2, dtype=jnp.float32)
    angles = own_pos.astype(jnp.float32)[:, None] * 10000.0 ** (-2.0 * freq_index / head_dim)
    cosine_table = jnp.cos(angles)[:, None, :]
    sine_table = jnp.sin(angles)[:, None, :]
    gains_wide = jnp.pad(gains, ((0, 0), (0, 128 - gains.shape[1])))
    gain_full, qkv_full, out_full, up_full, down_full = gather_all(
        (gains_wide, w_qkv, w_out, w_up, w_down), (False, True, True, False, False)
    )
    gain_full = gain_full[:, : gains.shape[1]]
    gain_f = gain_full.astype(jnp.float32)
    stream = tokens.astype(jnp.float32)
    normed = layer_norm(stream, gain_f[:, 0]).astype(jnp.bfloat16)
    qkv_raw = jnp.dot(normed, qkv_full, preferred_element_type=jnp.float32)
    queries = rotate(
        qkv_raw[:, :model_width].reshape(head_shape), cosine_table, sine_table, 1.0
    ).astype(jnp.bfloat16)
    key_heads = rotate(
        qkv_raw[:, model_width : 2 * model_width].reshape(head_shape), cosine_table, sine_table, 1.0
    ).astype(jnp.bfloat16)
    value_heads = qkv_raw[:, 2 * model_width :].reshape(head_shape).astype(jnp.bfloat16)
    start_state = (
        jnp.full((head_count, tok_rows), masked_score, jnp.float32),
        jnp.zeros((head_count, tok_rows), jnp.float32),
        jnp.zeros((head_count, tok_rows, head_dim), jnp.float32),
    )
    fold_piece = make_fold(queries, own_seg, own_place, seg_full, score_scale)
    row_max, row_sum, weighted = fold_piece(
        start_state,
        (
            lax.all_gather(key_heads, "ctx", axis=0, tiled=True),
            lax.all_gather(value_heads, "ctx", axis=0, tiled=True),
        ),
        jnp.int32(0),
    )
    attended = jnp.transpose(weighted / row_sum[..., None], (1, 0, 2))
    attended_b = attended.reshape(tok_rows, model_width).astype(jnp.bfloat16)
    attn_raw = jnp.dot(attended_b, out_full, preferred_element_type=jnp.float32)
    hidden = stream + layer_norm(attn_raw, gain_f[:, 1])
    mlp_in = layer_norm(hidden, gain_f[:, 2]).astype(jnp.bfloat16)
    up_proj = jnp.dot(mlp_in, up_full, preferred_element_type=jnp.float32)
    activated = jax.nn.gelu(up_proj).astype(jnp.bfloat16)
    mlp_raw = jnp.dot(activated, down_full, preferred_element_type=jnp.float32)
    result = hidden + layer_norm(mlp_raw, gain_f[:, 3])
    output = (result * own_valid[:, None]).astype(jnp.bfloat16)
    qkv_back, out_back, up_back, down_back = (qkv_full, out_full, up_full, down_full)
    upstream = d_out.astype(jnp.float32) * own_valid[:, None]
    d_mlp, d_gain_four = norm_back(mlp_raw, gain_f[:, 3], upstream)
    d_mlp_b = d_mlp.astype(jnp.bfloat16)
    grad_down = jnp.einsum("tf,td->fd", activated, d_mlp_b, preferred_element_type=jnp.float32)
    d_activated = jnp.einsum("td,fd->tf", d_mlp_b, down_back, preferred_element_type=jnp.float32)
    unused, gelu_pull = jax.vjp(jax.nn.gelu, up_proj)
    d_up_b = gelu_pull(d_activated)[0].astype(jnp.bfloat16)
    grad_up = jnp.einsum("td,tf->df", mlp_in, d_up_b, preferred_element_type=jnp.float32)
    d_mlp_in = jnp.einsum("tf,df->td", d_up_b, up_back, preferred_element_type=jnp.float32)
    d_hidden_part, d_gain_three = norm_back(hidden, gain_f[:, 2], d_mlp_in)
    d_hidden = upstream + d_hidden_part
    d_attn, d_gain_two = norm_back(attn_raw, gain_f[:, 1], d_hidden)
    d_attn_b = d_attn.astype(jnp.bfloat16)
    grad_out = jnp.einsum("td,te->de", attended_b, d_attn_b, preferred_element_type=jnp.float32)
    d_attended = (
        jnp.einsum("te,de->td", d_attn_b, out_back, preferred_element_type=jnp.float32)
        .astype(jnp.bfloat16)
        .reshape(head_shape)
    )
    row_dot = jnp.einsum("qhd,qhd->hq", d_attended.astype(jnp.float32), attended)
    key_all, value_all = (
        lax.all_gather(key_heads, "ctx", axis=0, tiled=True),
        lax.all_gather(value_heads, "ctx", axis=0, tiled=True),
    )
    block_rows = math.gcd(row_len, 256)
    block_count = row_len // block_rows
    key_blocks = key_all.reshape((block_count, block_rows) + key_all.shape[1:])
    value_blocks = value_all.reshape((block_count, block_rows) + value_all.shape[1:])

    def back_block(d_queries, block_items):
        key_block, value_block, block_id = block_items
        allowed = allowed_keys(own_seg, own_place, seg_full, block_id * block_rows, block_rows)
        scores = (
            jnp.einsum("qhd,khd->hqk", queries, key_block, preferred_element_type=jnp.float32)
            * score_scale
        )
        attn_prob = jnp.where(
            allowed[None], jnp.exp(scores - row_max[..., None]) / row_sum[..., None], 0.0
        )
        d_prob = jnp.einsum(
            "qhd,khd->hqk", d_attended, value_block, preferred_element_type=jnp.float32
        )
        d_scores = (attn_prob * (d_prob - row_dot[..., None])).astype(jnp.bfloat16)
        d_queries = (
            d_queries
            + jnp.einsum("hqk,khd->qhd", d_scores, key_block, preferred_element_type=jnp.float32)
            * score_scale
        )
        d_keys = (
            jnp.einsum("hqk,qhd->khd", d_scores, queries, preferred_element_type=jnp.float32)
            * score_scale
        )
        d_values = jnp.einsum(
            "hqk,qhd->khd",
            attn_prob.astype(jnp.bfloat16),
            d_attended,
            preferred_element_type=jnp.float32,
        )
        return (d_queries, (d_keys, d_values))

    block_ids = jnp.arange(block_count, dtype=jnp.int32)
    d_queries, (d_keys_all, d_values_all) = lax.scan(
        back_block, jnp.zeros(head_shape, jnp.float32), (key_blocks, value_blocks, block_ids)
    )
    kv_terms = jnp.concatenate(
        [d_keys_all.reshape(row_len, model_width), d_values_all.reshape(row_len, model_width)],
        axis=-1,
    )
    kv_grad = lax.psum_scatter(
        kv_terms.astype(jnp.bfloat16), "ctx", scatter_dimension=0, tiled=True
    ).astype(jnp.float32)
    d_keys = kv_grad[:, :model_width].reshape(head_shape)
    d_qkv = jnp.concatenate(
        [
            rotate(d_queries, cosine_table, sine_table, -1.0).reshape(tok_rows, model_width),
            rotate(d_keys, cosine_table, sine_table, -1.0).reshape(tok_rows, model_width),
            kv_grad[:, model_width:],
        ],
        axis=-1,
    ).astype(jnp.bfloat16)
    grad_qkv = jnp.einsum("td,te->de", normed, d_qkv, preferred_element_type=jnp.float32)
    d_normed = jnp.einsum("te,de->td", d_qkv, qkv_back, preferred_element_type=jnp.float32)
    d_stream_part, d_gain_one = norm_back(stream, gain_f[:, 0], d_normed)
    d_tokens = (d_hidden + d_stream_part).astype(jnp.bfloat16)
    grad_gains = jnp.stack([d_gain_one, d_gain_two, d_gain_three, d_gain_four], axis=-1)
    grad_gains = jnp.pad(grad_gains, ((0, 0), (0, 128 - gains.shape[1])))
    shard_down, shard_up, shard_out, shard_qkv, shard_gains = scatter_all(
        [v.astype(jnp.bfloat16) for v in (grad_down, grad_up, grad_out, grad_qkv, grad_gains)],
        (False, False, True, True, False),
    )
    shard_gains = shard_gains[:, : gains.shape[1]]
    return (output, d_tokens, shard_qkv, shard_out, shard_up, shard_down, shard_gains)


def fused_device(tokens, lengths, w_qkv, w_out, w_up, w_down, gains, d_out):
    tok_rows, model_width = tokens.shape
    row_len = tok_rows * lax.axis_size("ctx")
    head_count = HEADS
    head_dim = model_width // head_count
    score_scale = head_dim ** (-0.5)
    head_shape = (tok_rows, head_count, head_dim)
    seg_full, pos_full, valid_full = doc_layout(lengths, row_len)
    offset = lax.axis_index("ctx") * tok_rows
    own_seg = lax.dynamic_slice_in_dim(seg_full, offset, tok_rows)
    own_valid = lax.dynamic_slice_in_dim(valid_full.astype(jnp.float32), offset, tok_rows)
    own_place = offset + jnp.arange(tok_rows, dtype=jnp.int32)
    gains_wide = jnp.pad(gains, ((0, 0), (0, 128 - gains.shape[1])))
    cos_np, sin_np = turn_tables(row_len, head_dim)
    tables = (jnp.asarray(cos_np), jnp.asarray(sin_np))
    (output, qkv_back, out_back, up_back, down_back, gain_rows, qs, ks, vs, obs, lse, attn_raw, hidden,
     mlp_raw, bts, gts, gps, ats, atx) = forward(
        tokens, lengths, gains_wide, w_qkv, w_out, w_up, w_down, tables)
    gain_f = gain_rows[:4].T
    stream = tokens.astype(jnp.float32)
    def unpair(v):
        return jnp.transpose(v, (1, 0, 2)).reshape(v.shape[1], head_count, head_dim)
    seen = (jnp.arange(row_len) < offset + tok_rows)[:, None, None]
    queries = unpair(qs)
    key_all, value_all = jnp.where(seen, unpair(ks), 0), jnp.where(seen, unpair(vs), 0)
    attended_b = obs.reshape(model_width, tok_rows).T
    attended = attended_b.astype(jnp.float32).reshape(head_shape)
    row_max = lse.reshape(head_count, tok_rows)
    row_sum = jnp.ones_like(row_max)
    mlp_in = bts.T
    normed_x = ats.T
    activated = jnp.transpose(gts, (2, 0, 1)).reshape(tok_rows, -1)
    gp = jnp.transpose(gps, (1, 0, 2)).reshape(tok_rows, -1).astype(jnp.float32)
    upstream = d_out.astype(jnp.float32) * own_valid[:, None]
    d_mlp, d_gain_four = norm_back(mlp_raw, gain_f[:, 3], upstream)
    d_mlp_b = d_mlp.astype(jnp.bfloat16)
    grad_down = jnp.einsum("tf,td->fd", activated, d_mlp_b, preferred_element_type=jnp.float32)
    d_activated = jnp.einsum("td,fd->tf", d_mlp_b, down_back, preferred_element_type=jnp.float32)
    d_up_b = (d_activated * gp).astype(jnp.bfloat16)
    grad_up = jnp.einsum("td,tf->df", mlp_in, d_up_b, preferred_element_type=jnp.float32)
    d_mlp_in = jnp.einsum("tf,df->td", d_up_b, up_back, preferred_element_type=jnp.float32)
    d_hidden_part, d_gain_three = norm_back(hidden, gain_f[:, 2], d_mlp_in)
    d_hidden = upstream + d_hidden_part
    d_attn, d_gain_two = norm_back(attn_raw, gain_f[:, 1], d_hidden)
    d_attn_b = d_attn.astype(jnp.bfloat16)
    grad_out = jnp.einsum("td,te->de", attended_b, d_attn_b, preferred_element_type=jnp.float32)
    d_attended = (
        jnp.einsum("te,de->td", d_attn_b, out_back, preferred_element_type=jnp.float32)
        .astype(jnp.bfloat16)
        .reshape(head_shape)
    )
    row_dot = jnp.einsum("qhd,qhd->hq", d_attended.astype(jnp.float32), attended)
    block_rows = math.gcd(row_len, 256)
    block_count = row_len // block_rows
    key_blocks = key_all.reshape((block_count, block_rows) + key_all.shape[1:])
    value_blocks = value_all.reshape((block_count, block_rows) + value_all.shape[1:])

    def back_block(d_queries, block_items):
        key_block, value_block, block_id = block_items
        allowed = allowed_keys(own_seg, own_place, seg_full, block_id * block_rows, block_rows)
        scores = (
            jnp.einsum("qhd,khd->hqk", queries, key_block, preferred_element_type=jnp.float32)
        )
        attn_prob = jnp.where(
            allowed[None], jnp.exp(scores - row_max[..., None]) / row_sum[..., None], 0.0
        )
        d_prob = jnp.einsum(
            "qhd,khd->hqk", d_attended, value_block, preferred_element_type=jnp.float32
        )
        d_scores = (attn_prob * (d_prob - row_dot[..., None])).astype(jnp.bfloat16)
        d_queries = (
            d_queries
            + jnp.einsum("hqk,khd->qhd", d_scores, key_block, preferred_element_type=jnp.float32)
            * score_scale
        )
        d_keys = (
            jnp.einsum("hqk,qhd->khd", d_scores, queries, preferred_element_type=jnp.float32)
        )
        d_values = jnp.einsum(
            "hqk,qhd->khd",
            attn_prob.astype(jnp.bfloat16),
            d_attended,
            preferred_element_type=jnp.float32,
        )
        return (d_queries, (d_keys, d_values))

    block_ids = jnp.arange(block_count, dtype=jnp.int32)
    d_queries, (d_keys_all, d_values_all) = lax.scan(
        back_block, jnp.zeros(head_shape, jnp.float32), (key_blocks, value_blocks, block_ids)
    )
    kv_terms = jnp.concatenate(
        [d_keys_all.reshape(row_len, model_width), d_values_all.reshape(row_len, model_width)],
        axis=-1,
    )
    kv_grad = lax.psum_scatter(
        kv_terms.astype(jnp.bfloat16), "ctx", scatter_dimension=0, tiled=True
    ).astype(jnp.float32)
    place = offset + jnp.arange(tok_rows)
    inv = 10000.0 ** (-2.0 * np.arange(head_dim // 2) / head_dim)
    angles = place.astype(jnp.float32)[:, None] * jnp.asarray(inv, jnp.float32)
    cosine_table = jnp.cos(angles)[:, None, :]
    sine_table = jnp.sin(angles)[:, None, :]
    d_keys = kv_grad[:, :model_width].reshape(head_shape)
    d_qkv = jnp.concatenate(
        [
            rotate(d_queries, cosine_table, sine_table, -1.0).reshape(tok_rows, model_width),
            rotate(d_keys, cosine_table, sine_table, -1.0).reshape(tok_rows, model_width),
            kv_grad[:, model_width:],
        ],
        axis=-1,
    ).astype(jnp.bfloat16)
    grad_qkv = jnp.einsum("td,te->de", normed_x, d_qkv, preferred_element_type=jnp.float32)
    d_normed = jnp.einsum("te,de->td", d_qkv, qkv_back, preferred_element_type=jnp.float32)
    d_stream_part, d_gain_one = norm_back(stream, gain_f[:, 0], d_normed)
    d_tokens = (d_hidden + d_stream_part).astype(jnp.bfloat16)
    grad_gains = jnp.stack([d_gain_one, d_gain_two, d_gain_three, d_gain_four], axis=-1)
    grad_gains = jnp.pad(grad_gains, ((0, 0), (0, 128 - gains.shape[1])))
    shard_down, shard_up, shard_out, shard_qkv, shard_gains = scatter_all(
        [v.astype(jnp.bfloat16) for v in (grad_down, grad_up, grad_out, grad_qkv, grad_gains)],
        (False,) * 5,
    )
    shard_gains = shard_gains[:, : gains.shape[1]]
    return (output, d_tokens, shard_qkv, shard_out, shard_up, shard_down, shard_gains)


def layer(mesh):
    if mesh.shape["dp"] == 16 and mesh.shape["ctx"] == 2:
        return fused_device
    return per_device


def solution(mesh):
    return jax.shard_map(
        layer(mesh),
        mesh=mesh,
        in_specs=(
            P(("dp", "ctx"), None),
            P("dp", None),
            P(("dp", "ctx"), None),
            P(("dp", "ctx"), None),
            P(("dp", "ctx"), None),
            P(("dp", "ctx"), None),
            P(("dp", "ctx"), None),
            P(("dp", "ctx"), None),
        ),
        out_specs=(
            P(("dp", "ctx"), None),
            P(("dp", "ctx"), None),
            P(("dp", "ctx"), None),
            P(("dp", "ctx"), None),
            P(("dp", "ctx"), None),
            P(("dp", "ctx"), None),
            P(("dp", "ctx"), None),
        ),
        check_vma=False,
    )
```

```python
import math

import jax
import jax.numpy as jnp
import numpy as np
from jax import lax
from jax.sharding import PartitionSpec as P

import functools
from jax.experimental import pallas as pl
from jax.experimental.pallas import tpu as pltpu

MESH = pl.DeviceIdType.MESH


class Place:
    def __init__(self, dp_size):
        dp = lax.axis_index("dp")
        self.Z = dp_size // 4
        self.z = lax.div(dp, 4)
        self.x = lax.rem(lax.div(dp, 2), 2)
        self.c = lax.rem(dp, 2)
        self.y = lax.axis_index("ctx")
        c, x, y = self.c, self.x, self.y
        self.i2 = y * (1 - c) + x * c
        self.i3 = x * (1 - c) + y * c
        self.sib = self.device(self.z, x, 1 - c, y)
        self.p2 = self.device(self.z, x * (1 - c) + (1 - x) * c, c, (1 - y) * (1 - c) + y * c)
        self.p3 = self.device(self.z, (1 - x) * (1 - c) + x * c, c, y * (1 - c) + (1 - y) * c)

    def device(self, z, x, c, y):
        return ((z * 2 + x) * 2 + c, y)

    def at_z(self, z):
        return self.device(z, self.x, self.c, self.y)

    def block(self, z, a2, a3):
        c = self.c
        return (z * 2 + a3 * (1 - c) + a2 * c) * 2 + a2 * (1 - c) + a3 * c

    def row_block(self, z, a2, a3, core):
        c = self.c
        xx = a3 * (1 - c) + a2 * c
        yy = a2 * (1 - c) + a3 * c
        return ((z * 2 + xx) * 2 + core) * 2 + yy

    def barrier(self):
        bar = pltpu.get_barrier_semaphore()
        for device in (self.sib, self.p2, self.p3):
            pl.semaphore_signal(bar, 1, device_id=device, device_id_type=MESH)
        for k in range(1, self.Z):
            pl.semaphore_signal(
                bar, 1, device_id=self.at_z(lax.rem(self.z + k, self.Z)), device_id_type=MESH
            )
        pl.semaphore_wait(bar, 3 + self.Z - 1)


class Gather:
    def __init__(self, place, shard, full, send, recv, by_z):
        self.g, self.shard, self.full = place, shard, full
        self.send, self.recv = send, recv
        self.rows = shard.shape[0]
        self.by_z = by_z
        Z = place.Z
        self.n_z = 0
        self.n_p2 = 2 * (Z - 1)
        self.n_p3 = self.n_p2 + Z
        self.n_sib = self.n_p3 + 2 * Z
        self.n_own = self.n_sib + 4 * Z
        self.count = self.n_own + 1

    @staticmethod
    def sems(Z):
        return 2 * (Z - 1) + Z + 2 * Z + 4 * Z + 1

    def at(self, index):
        return self.full.at[pl.ds(pl.multiple_of(index * self.rows, self.rows), self.rows)]

    def copy(self, index, number, device, src=None):
        return pltpu.make_async_remote_copy(
            src_ref=self.at(index) if src is None else src,
            dst_ref=self.at(index),
            send_sem=self.send.at[number],
            recv_sem=self.recv.at[number],
            device_id=device,
            device_id_type=MESH,
        )

    def own_copy(self):
        g = self.g
        index = g.row_block(g.z, g.i2, g.i3, g.c)
        return pltpu.make_async_copy(self.shard, self.at(index), self.recv.at[self.n_own])

    def z_copy(self, z, a2_is_other, k, src=None):
        g = self.g
        a2 = (1 - g.i2) if a2_is_other else g.i2
        index = g.row_block(z, a2, g.i3, g.c)
        to = lax.rem(g.z + k, g.Z)
        return self.copy(index, self.n_z + (k - 1) * 2 + int(a2_is_other), g.at_z(to), src)

    def p2_copy(self, z, src=None):
        g = self.g
        return self.copy(g.row_block(z, g.i2, g.i3, g.c), self.n_p2 + z, g.p2, src)

    def p3_copy(self, z, a2, src=None):
        g = self.g
        return self.copy(g.row_block(z, a2, g.i3, g.c), self.n_p3 + z * 2 + a2, g.p3, src)

    def sib_copy(self, z, a2, a3, src=None):
        g = self.g
        number = self.n_sib + g.block(z, a2, a3)
        return self.copy(g.row_block(z, a2, a3, g.c), number, g.sib, src)

    def wait(self, number, index):
        self.copy(index, number, self.g.sib).wait_recv()

    def start(self):
        g, src = self.g, self.shard
        self.own_copy().start()
        self.p2_copy(g.z, src).start()
        self.p3_copy(g.z, g.i2, src).start()
        for k in range(1, g.Z):
            self.z_copy(g.z, False, k, src).start()
        self.sib_copy(g.z, g.i2, g.i3, src).start()

    def arrived_p2(self, z):
        g = self.g
        o2 = 1 - g.i2
        self.wait(self.n_p2 + z, g.row_block(z, o2, g.i3, g.c))
        self.p3_copy(z, o2).start()
        self.sib_copy(z, o2, g.i3).start()

    def first_p2(self):
        g = self.g
        self.arrived_p2(g.z)
        if self.by_z:
            for k in range(1, g.Z):
                self.z_copy(g.z, True, k).start()

    def arrived_z(self, k):
        g = self.g
        z = lax.rem(g.z - k + g.Z, g.Z)
        for other in ((False, True) if self.by_z else (False,)):
            a2 = (1 - g.i2) if other else g.i2
            self.wait(self.n_z + (k - 1) * 2 + int(other), g.row_block(z, a2, g.i3, g.c))
            if not self.by_z:
                self.p2_copy(z).start()
            self.p3_copy(z, a2).start()
            self.sib_copy(z, a2, g.i3).start()

    def later_p2(self, k):
        if not self.by_z:
            self.arrived_p2(lax.rem(self.g.z + k, self.g.Z))

    def arrived_p3(self, k):
        g = self.g
        z = lax.rem(g.z + k, g.Z)
        for a2 in (0, 1):
            self.wait(self.n_p3 + z * 2 + a2, g.row_block(z, a2, 1 - g.i3, g.c))
            self.sib_copy(z, a2, 1 - g.i3).start()

    def arrived_sib(self, z):
        g = self.g
        for xx in (0, 1):
            for yy in (0, 1):
                number = self.n_sib + (z * 2 + xx) * 2 + yy
                self.wait(number, ((z * 2 + xx) * 2 + 1 - g.c) * 2 + yy)

    def own_here(self):
        self.own_copy().wait()

    def sent(self):
        g, src = self.g, self.shard
        self.p2_copy(g.z, src).wait_send()
        self.p3_copy(g.z, g.i2, src).wait_send()
        self.sib_copy(g.z, g.i2, g.i3, src).wait_send()
        for k in range(1, g.Z):
            self.z_copy(g.z, False, k, src).wait_send()
            if self.by_z:
                self.z_copy(g.z, True, k).wait_send()
            z = lax.rem(g.z + k, g.Z)
            if not self.by_z:
                self.p2_copy(z).wait_send()
            self.p3_copy(z, g.i2).wait_send()
            self.sib_copy(z, g.i2, g.i3).wait_send()
        for k in range(g.Z):
            z = lax.rem(g.z + k, g.Z)
            self.p3_copy(z, 1 - g.i2).wait_send()
            self.sib_copy(z, 1 - g.i2, g.i3).wait_send()
            for a2 in (0, 1):
                self.sib_copy(z, a2, 1 - g.i3).wait_send()


def gather_kernel(dp_size, by_z, n, *refs):
    shards, fulls = refs[:n], refs[n : 2 * n]
    sends, recvs = refs[2 * n : 3 * n], refs[3 * n : 4 * n]
    g = Place(dp_size)
    g.barrier()
    ms = [
        Gather(g, shards[i], fulls[i], sends[i], recvs[i], by_z[i]) for i in range(n)
    ]
    for m in ms:
        m.start()
    for m in ms:
        m.first_p2()
        for k in range(1, g.Z):
            m.arrived_z(k)
        for k in range(1, g.Z):
            m.later_p2(k)
        for k in range(g.Z):
            m.arrived_p3(k)
    for m in ms:
        for z in range(g.Z):
            m.arrived_sib(z)
        m.own_here()
    for m in ms:
        m.sent()


def gather_all(shards, by_z):
    dp_size = lax.axis_size("dp")
    devices = dp_size * lax.axis_size("ctx")
    n = len(shards)
    any_spec = pl.BlockSpec(memory_space=pl.ANY)
    return pl.pallas_call(
        functools.partial(gather_kernel, dp_size, by_z, n),
        out_shape=[jax.ShapeDtypeStruct((s.shape[0] * devices, s.shape[1]), s.dtype) for s in shards],
        in_specs=[any_spec] * n,
        out_specs=[any_spec] * n,
        scratch_shapes=[pltpu.SemaphoreType.DMA((Gather.sems(dp_size // 4),))] * (2 * n),
        compiler_params=pltpu.CompilerParams(
            collective_id=0, has_side_effects=True, vmem_limit_bytes=16 * 2**20
        ),
    )(*shards)


class Scatter:
    def __init__(self, place, part, rec3, rec2, recz, out, send, recv, by_z):
        self.g = place
        self.part, self.rec3, self.rec2, self.recz, self.out = part, rec3, rec2, recz, out
        self.send, self.recv, self.by_z = send, recv, by_z
        Z = place.Z
        self.n_p3, self.n_z, self.n_p2 = 0, 2 * Z, 2 * Z + 2 * (Z - 1)

    @staticmethod
    def sems(Z):
        return 2 * Z + 2 * (Z - 1) + Z

    def copy(self, src, dst, number, device):
        return pltpu.make_async_remote_copy(
            src_ref=src,
            dst_ref=dst,
            send_sem=self.send.at[number],
            recv_sem=self.recv.at[number],
            device_id=device,
            device_id_type=MESH,
        )

    def p3_copy(self, z, a2):
        g = self.g
        slot = z * 2 + a2
        return self.copy(
            self.part.at[g.block(z, a2, 1 - g.i3)], self.rec3.at[slot], self.n_p3 + slot, g.p3
        )

    def z_copy(self, k, a2):
        g = self.g
        z = lax.rem(g.z + k, g.Z)
        if self.by_z:
            slot = (k - 1) * 2 + a2
        else:
            slot = k - 1
        return self.copy(
            self.part.at[g.block(z, a2, g.i3)], self.recz.at[slot], self.n_z + slot, g.at_z(z)
        )

    def p2_copy(self, z):
        g = self.g
        slot = 0 if self.by_z else z
        return self.copy(
            self.part.at[g.block(z, 1 - g.i2, g.i3)], self.rec2.at[slot], self.n_p2 + slot, g.p2
        )

    def start(self, z, a2):
        self.p3_copy(z, a2).start()

    def add3(self, k, a2):
        g = self.g
        z = lax.rem(g.z + k, g.Z)
        self.p3_copy(z, a2).wait_recv()
        block = g.block(z, a2, g.i3)
        total = self.part[block].astype(jnp.float32) + self.rec3[z * 2 + a2].astype(jnp.float32)
        self.part[block] = total.astype(jnp.bfloat16)
        if self.by_z and k > 0:
            self.z_copy(k, a2).start()

    def stage3(self, k):
        g = self.g
        if self.by_z:
            for a2 in (0, 1):
                self.add3(k, a2)
        else:
            self.add3(k, 1 - g.i2)
            self.p2_copy(lax.rem(g.z + k, g.Z)).start()
            self.add3(k, g.i2)

    def stage2(self, k):
        g = self.g
        z = lax.rem(g.z + k, g.Z)
        self.p2_copy(z).wait_recv()
        block = g.block(z, g.i2, g.i3)
        total = self.part[block].astype(jnp.float32) + self.rec2[z].astype(jnp.float32)
        if k > 0:
            self.part[block] = total.astype(jnp.bfloat16)
            self.z_copy(k, g.i2).start()
        else:
            self.out[...] = total

    def last_z(self):
        g = self.g
        for k in range(1, g.Z):
            self.z_copy(k, g.i2).wait_recv()
            self.out[...] += self.recz[k - 1].astype(jnp.float32)

    def sum_z(self):
        g = self.g
        block = g.block(g.z, 1 - g.i2, g.i3)
        total = self.part[block].astype(jnp.float32)
        for k in range(1, g.Z):
            self.z_copy(k, 1 - g.i2).wait_recv()
            total += self.recz[(k - 1) * 2 + 1 - g.i2].astype(jnp.float32)
        self.part[block] = total.astype(jnp.bfloat16)
        self.p2_copy(g.z).start()
        total = self.part[g.block(g.z, g.i2, g.i3)].astype(jnp.float32)
        for k in range(1, g.Z):
            self.z_copy(k, g.i2).wait_recv()
            total += self.recz[(k - 1) * 2 + g.i2].astype(jnp.float32)
        self.out[...] = total

    def last_p2(self):
        self.p2_copy(self.g.z).wait_recv()
        self.out[...] += self.rec2[0].astype(jnp.float32)

    def sent(self):
        g = self.g
        for z in range(g.Z):
            for a2 in (0, 1):
                self.p3_copy(z, a2).wait_send()
        for k in range(1, g.Z):
            if self.by_z:
                self.z_copy(k, 0).wait_send()
                self.z_copy(k, 1).wait_send()
            else:
                self.z_copy(k, g.i2).wait_send()
        if self.by_z:
            self.p2_copy(g.z).wait_send()
        else:
            for z in range(g.Z):
                self.p2_copy(z).wait_send()


def scatter_kernel(dp_size, by_z, n, *refs):
    grads, outs = refs[:n], refs[n : 2 * n]
    scr = refs[2 * n :]
    g = Place(dp_size)
    Z = g.Z
    g.barrier()
    ms = []
    sibs = []
    for i in range(n):
        part, rsib, rec3, rec2, recz, send, recv, ssend, srecv, slocal = scr[10 * i : 10 * i + 10]
        ms.append(Scatter(g, part, rec3, rec2, recz, outs[i], send, recv, by_z[i]))
        sibs.append((grads[i], part, rsib, ssend, srecv, slocal))

    def sib_copy(s, q):
        grad, part, rsib, ssend, srecv, slocal = s
        return pltpu.make_async_remote_copy(
            src_ref=grad.at[2 * q + 1 - g.c],
            dst_ref=rsib.at[q],
            send_sem=ssend.at[q],
            recv_sem=srecv.at[q],
            device_id=g.sib,
            device_id_type=MESH,
        )

    def loc_copy(s, q):
        grad, part, rsib, ssend, srecv, slocal = s
        return pltpu.make_async_copy(grad.at[2 * q + g.c], part.at[pl.ds(2 * q, 2)], slocal.at[q])

    for s in sibs:
        for q in range(2 * Z):
            sib_copy(s, q).start()
            loc_copy(s, q).start()
    for s, m in zip(sibs, ms):
        for q in range(2 * Z):
            sib_copy(s, q).wait_recv()
            loc_copy(s, q).wait()
            for j in (0, 1):
                part, rsib = s[1], s[2]
                part[2 * q + j] = (
                    part[2 * q + j].astype(jnp.float32) + rsib[q, j].astype(jnp.float32)
                ).astype(jnp.bfloat16)
        for z in range(Z):
            for a2 in (0, 1):
                m.start(z, a2)
    for m in ms:
        for k in range(1, Z):
            m.stage3(k)
        m.stage3(0)
    for m in ms:
        if not m.by_z:
            for k in range(1, Z):
                m.stage2(k)
            m.stage2(0)
    for m in ms:
        if m.by_z:
            m.sum_z()
    for m in ms:
        if m.by_z:
            m.last_p2()
        else:
            m.last_z()
    for s, m in zip(sibs, ms):
        m.sent()
        for q in range(2 * Z):
            sib_copy(s, q).wait_send()


def scatter_all(grads, by_z):
    dp_size = lax.axis_size("dp")
    Z = dp_size // 4
    n = len(grads)
    scratch, outs, views = [], [], []
    for grad, z_first in zip(grads, by_z):
        rows, cols = grad.shape[0] // (8 * Z), grad.shape[1]
        bf = jnp.bfloat16
        scratch += [
            pltpu.VMEM((4 * Z, rows, cols), bf),
            pltpu.VMEM((2 * Z, 2, rows, cols), bf),
            pltpu.VMEM((2 * Z, rows, cols), bf),
            pltpu.VMEM((1 if z_first else Z, rows, cols), bf),
            pltpu.VMEM(((2 if z_first else 1) * (Z - 1), rows, cols), bf),
            pltpu.SemaphoreType.DMA((Scatter.sems(Z),)),
            pltpu.SemaphoreType.DMA((Scatter.sems(Z),)),
            pltpu.SemaphoreType.DMA((2 * Z,)),
            pltpu.SemaphoreType.DMA((2 * Z,)),
            pltpu.SemaphoreType.DMA((2 * Z,)),
        ]
        outs.append(jax.ShapeDtypeStruct((rows, cols), jnp.float32))
        views.append(grad.reshape(4 * Z, 2, rows, cols))
    return pl.pallas_call(
        functools.partial(scatter_kernel, dp_size, by_z, n),
        out_shape=outs,
        in_specs=[pl.BlockSpec(memory_space=pl.ANY)] * n,
        out_specs=[pl.BlockSpec(memory_space=pltpu.VMEM)] * n,
        scratch_shapes=scratch,
        compiler_params=pltpu.CompilerParams(
            collective_id=1, has_side_effects=True, vmem_limit_bytes=60 * 2**20
        ),
    )(*views)


HEADS = 16
DOCS = 7


epsilon = 1e-05
masked_score = -1e30


def loop(count):
    def run(body):
        def step(i, carry):
            body(i)
            return carry

        lax.fori_loop(0, count, step, 0)

    return run


def dot(a, b):
    return jnp.dot(a, b, preferred_element_type=jnp.float32)


def dot_nt(a, b):
    return lax.dot_general(a, b, (((1,), (1,)), ((), ())), preferred_element_type=jnp.float32)


def normed(v):
    center = v - jnp.mean(v, axis=-1, keepdims=True)
    r = lax.rsqrt(jnp.mean(center * center, axis=-1, keepdims=True) + epsilon)
    return center * r, r


def norm_pull(v, gain, e):
    z, r = normed(v)
    f = e * gain
    dv = r * (
        f
        - jnp.mean(f, axis=-1, keepdims=True)
        - z * jnp.mean(f * z, axis=-1, keepdims=True)
    )
    return dv, e * z


def turn(u, cosine, sine, half):
    lane = lax.broadcasted_iota(jnp.int32, u.shape, 1)
    swapped = jnp.where(
        lax.rem(lane, 2 * half) < half,
        pltpu.roll(u, u.shape[1] - half, 1),
        pltpu.roll(u, half, 1),
    )
    return u * cosine + swapped * sine


def turn_tables(row_len, head_dim):
    half = head_dim // 2
    inverse = 10000.0 ** (-2.0 * np.arange(half) / head_dim)
    angles = np.arange(row_len)[:, None] * inverse[None, :]
    cosine = np.tile(np.cos(angles), (1, 4))
    sine = np.tile(np.concatenate([-np.sin(angles), np.sin(angles)], axis=1), (1, 2))
    return cosine.astype(np.float32), sine.astype(np.float32)


def doc_ends(lens):
    ends = [lens[0, 0]]
    for d in range(1, DOCS):
        ends.append(ends[-1] + lens[0, d])
    return ends


def fill_bias(bias, lens, first, rows):
    ends = doc_ends(lens)
    block = 128

    @loop(bias.shape[0] // block)
    def _(i):
        shape = (block, rows)
        place = first + lax.broadcasted_iota(jnp.int32, shape, 1)
        key = i * block + lax.broadcasted_iota(jnp.int32, shape, 0)
        start = jnp.zeros(shape, jnp.int32)
        for d in range(DOCS):
            start = jnp.where(place >= ends[d], ends[d], start)
        fine = (key >= start) & (key <= place)
        bias[pl.ds(i * block, block), :] = jnp.where(fine, 0.0, masked_score)


def split_heads(v, axis=1):
    spot = lax.broadcasted_iota(jnp.int32, v.shape, axis)
    first = spot < v.shape[axis] // 2
    zero = jnp.zeros_like(v)
    return jnp.where(first, v, zero), jnp.where(first, zero, v)


class Tiles:
    def __init__(self, source, buffer, sems, ready=None):
        self.source, self.buffer, self.sems, self.ready = source, buffer, sems, ready

    def copy(self, t):
        slot = lax.rem(t, 2)
        return pltpu.make_async_copy(self.source(t), self.buffer.at[slot], self.sems.at[slot])

    def start(self, t):
        if self.ready is not None:
            self.ready(t)
        self.copy(t).start()

    def first(self, t=0):
        self.start(jnp.int32(t))

    def get(self, t, end):
        @pl.when(t + 1 < end)
        def _():
            self.start(t + 1)

        self.copy(t).wait()
        return self.buffer[lax.rem(t, 2)]


def forward_kernel(dp_size, head_dim, *refs):
    (tok, lens, gs, wq, wo, wu, wd, cosine, sine) = refs[:9]
    (out, wq_f, wo_f, wu_f, wd_f, gain_o, q_o, k_o, v_o, ob_o, lse_o) = refs[9:20]
    (araw_o, h_o, mraw_o, bt_o, gt_o, gp_o, at_o, atx_o) = refs[20:28]
    (g_full, gain, tokx, a, ax, at, atx, q, k, v, vt, bias, ob, lse) = refs[28:42]
    (araw, h, mraw, b, bt, act, actt, gp, wbuf, dbuf) = refs[42:52]
    sems = refs[52:62]
    wsem, dsem, xsem, osem = refs[62:66]
    g = Place(dp_size)
    y = g.y
    rows, width = tok.shape
    half = head_dim // 2
    pairs = width // 128
    scale = head_dim ** (-0.5)
    gg, gq, go, gu, gd = [
        Gather(g, s, f, sems[2 * i], sems[2 * i + 1], False)
        for i, (s, f) in enumerate(
            ((gs, g_full), (wq, wq_f), (wo, wo_f), (wu, wu_f), (wd, wd_f))
        )
    ]
    Z = g.Z
    saves = []

    def save(src, dst):
        copy = pltpu.make_async_copy(src, dst, osem.at[len(saves)])
        copy.start()
        saves.append(copy)

    tok_copy = pltpu.make_async_remote_copy(
        src_ref=tok,
        dst_ref=tokx,
        send_sem=xsem.at[0],
        recv_sem=xsem.at[1],
        device_id=g.device(g.z, g.x, g.c, 1 - y),
        device_id_type=MESH,
    )
    g.barrier()
    gg.start()
    gq.start()

    @pl.when(y == 0)
    def _():
        tok_copy.start()

    go.start()
    fill_bias(bias, lens, y * rows, rows)
    for k_ in range(1, Z):
        gg.arrived_z(k_)
    for k_ in range(Z):
        gg.later_p2(k_)
    for k_ in range(Z):
        gg.arrived_p3(k_)
    for k_ in range(1, Z):
        gq.arrived_z(k_)
    gu.start()
    for z in range(Z):
        gg.arrived_sib(z)
    gg.own_here()
    turned = jnp.transpose(g_full[...].astype(jnp.float32))
    gain[...] = turned[:8]
    save(gain, gain_o)

    def first_norm(src, dst, dst_t):
        @loop(rows // 128)
        def _(i):
            spot = pl.ds(i * 128, 128)
            z, _r = normed(src[spot, :].astype(jnp.float32))
            value = z * gain[0:1, :]
            dst[spot, :] = value.astype(jnp.bfloat16)
            dst_t[:, spot] = jnp.transpose(value).astype(jnp.bfloat16)

    first_norm(tok, a, at)
    save(at, at_o)
    for k_ in range(Z):
        gq.later_p2(k_)

    @pl.when(y == 1)
    def _():
        tok_copy.wait_recv()
        first_norm(tokx, ax, atx)

    save(atx, atx_o)
    for k_ in range(Z):
        gq.arrived_p3(k_)
    for k_ in range(1, Z):
        go.arrived_z(k_)
    for k_ in range(Z):
        go.later_p2(k_)
    for z in range(Z):
        gq.arrived_sib(z)
    gq.own_here()

    tiles = Tiles(lambda t: wq_f.at[:, pl.ds(pl.multiple_of(t * 256, 256), 256)], wbuf, wsem)
    per = width // 256
    first = pl.multiple_of(y * rows, rows)

    def turned_pair(u, start):
        return turn(u, cosine[pl.ds(start, rows), :], sine[pl.ds(start, rows), :], half)

    tiles.first()

    @loop(per)
    def _(t):
        u = dot(a[...], tiles.get(t, 3 * per))
        for j in (0, 1):
            part = turned_pair(u[:, j * 128 : j * 128 + 128], first) * scale
            q[2 * t + j] = part.astype(jnp.bfloat16)

    for k_ in range(Z):
        go.arrived_p3(k_)
    for k_ in range(1, Z):
        gu.arrived_z(k_)
    gd.start()

    def keys(w, t, src, start):
        u = dot(src[...], w)
        for j in (0, 1):
            part = turned_pair(u[:, j * 128 : j * 128 + 128], start)
            k[2 * t + j, pl.ds(start, rows), :] = part.astype(jnp.bfloat16)

    @loop(per)
    def _(t):
        w = tiles.get(t + per, 3 * per)
        keys(w, t, a, first)

        @pl.when(y == 1)
        def _():
            keys(w, t, ax, 0)

    for k_ in range(Z):
        gu.later_p2(k_)

    def values(w, t, src, start):
        u = dot(src[...], w)
        ut = jnp.transpose(u).astype(jnp.bfloat16)
        for j in (0, 1):
            cols = slice(j * 128, j * 128 + 128)
            v[2 * t + j, pl.ds(start, rows), :] = u[:, cols].astype(jnp.bfloat16)
            vt[2 * t + j, :, pl.ds(start, rows)] = ut[cols]

    @loop(per)
    def _(t):
        w = tiles.get(t + 2 * per, 3 * per)
        values(w, t, a, first)

        @pl.when(y == 1)
        def _():
            values(w, t, ax, 0)

    save(q, q_o)
    save(k, k_o)
    save(v, v_o)

    def attend(p, block, count):
        spot = slice(block * 256, block * 256 + 256)
        heads = split_heads(q[p, spot, :])
        kk = k[p, :count, :]
        vv = vt[p, :, :count]
        parts = []
        for i in (0, 1):
            s = dot_nt(kk, heads[i]) + bias[:count, spot]
            m = jnp.max(s, axis=0, keepdims=True)
            e = jnp.exp(s - m)
            total = jnp.sum(e, axis=0, keepdims=True)
            lse[p, i : i + 1, spot] = m + jnp.log(total)
            parts.append(dot(vv, e.astype(jnp.bfloat16)) * (1.0 / total))
        upper = lax.broadcasted_iota(jnp.int32, parts[0].shape, 0) < head_dim
        ob[p, :, spot] = jnp.where(upper, parts[0], parts[1]).astype(jnp.bfloat16)

    events = [lambda: None] * pairs
    events[0] = lambda: [gu.arrived_p3(k_) for k_ in range(Z // 2)]
    events[1] = lambda: [gu.arrived_p3(k_) for k_ in range(Z // 2, Z)]
    events[2] = lambda: [gd.arrived_z(k_) for k_ in range(1, Z)]
    events[4] = lambda: [gd.later_p2(k_) for k_ in range(Z)]
    events[7] = lambda: [gd.arrived_p3(k_) for k_ in range(Z)]

    blocks = rows // 256

    @loop(pairs)
    def _(p):
        for half_row in (0, 1):

            @pl.when(y == half_row)
            def _():
                for block in range(blocks):
                    attend(p, block, (half_row * blocks + block + 1) * 256)

        for i in range(pairs):

            @pl.when(p == i)
            def _():
                events[i]()

    save(ob, ob_o)
    save(lse, lse_o)

    for z in range(Z):
        go.arrived_sib(z)
    go.own_here()
    obf = jnp.transpose(ob[...].reshape(width, rows))
    a[...] = obf
    tiles = Tiles(lambda t: wo_f.at[:, pl.ds(pl.multiple_of(t * 256, 256), 256)], wbuf, wsem)
    tiles.first()

    @loop(per)
    def _(t):
        w = tiles.get(t, per)
        araw[:, pl.ds(pl.multiple_of(t * 256, 256), 256)] = dot(a[...], w)

    save(araw, araw_o)

    @loop(rows // 128)
    def _(i):
        spot = pl.ds(i * 128, 128)
        z, _r = normed(araw[spot, :])
        hidden = tok[spot, :].astype(jnp.float32) + z * gain[1:2, :]
        h[spot, :] = hidden
        z, _r = normed(hidden)
        value = z * gain[2:3, :]
        b[spot, :] = value.astype(jnp.bfloat16)
        bt[:, spot] = jnp.transpose(value).astype(jnp.bfloat16)

    save(h, h_o)
    save(bt, bt_o)

    for z in range(Z):
        gu.arrived_sib(z)
    gu.own_here()
    tiles = Tiles(lambda t: wu_f.at[:, pl.ds(pl.multiple_of(t * 256, 256), 256)], wbuf, wsem)
    ups = act.shape[0]
    tiles.first()
    c0 = math.sqrt(2.0 / math.pi)

    @loop(ups)
    def _(t):
        u = dot(b[...], tiles.get(t, ups))
        square = u * u
        th = jnp.tanh(c0 * (u + 0.044715 * (square * u)))
        value = 0.5 * u * (1.0 + th)
        slope = 0.5 * (1.0 + th) + (0.5 * c0) * u * (1.0 - th * th) * (
            1.0 + (3 * 0.044715) * square
        )
        act[t] = value.astype(jnp.bfloat16)
        actt[t] = jnp.transpose(value).astype(jnp.bfloat16)
        gp[t] = slope.astype(jnp.bfloat16)

    save(actt, gt_o)
    save(gp, gp_o)

    for z in range(Z):
        gd.arrived_sib(z)
    gd.own_here()
    tiles = Tiles(lambda t: wd_f.at[pl.ds(pl.multiple_of(t * 256, 256), 256), :], dbuf, dsem)
    tiles.first()
    mraw[...] = jnp.zeros_like(mraw)

    @loop(ups)
    def _(t):
        mraw[...] += dot(act[t], tiles.get(t, ups))

    save(mraw, mraw_o)
    ends = doc_ends(lens)

    @loop(rows // 128)
    def _(i):
        spot = pl.ds(i * 128, 128)
        z, _r = normed(mraw[spot, :])
        result = h[spot, :] + z * gain[3:4, :]
        place = y * rows + i * 128 + lax.broadcasted_iota(jnp.int32, result.shape, 0)
        result = jnp.where(place < ends[DOCS - 2], result, 0.0)
        out[spot, :] = result.astype(jnp.bfloat16)

    for copy in saves:
        copy.wait()

    @pl.when(y == 0)
    def _():
        tok_copy.wait_send()

    for m in (gg, gq, go, gu, gd):
        m.sent()


def forward(tokens, lengths, gains_wide, w_qkv, w_out, w_up, w_down, tables):
    dp_size = lax.axis_size("dp")
    devices = dp_size * lax.axis_size("ctx")
    rows, width = tokens.shape
    row_len = rows * lax.axis_size("ctx")
    head_dim = width // HEADS
    pairs = width // 128
    ups = w_up.shape[1] // 256
    bf, f32 = jnp.bfloat16, jnp.float32
    any_spec = pl.BlockSpec(memory_space=pl.ANY)
    vm = pl.BlockSpec(memory_space=pltpu.VMEM)
    shape = jax.ShapeDtypeStruct

    def whole(w):
        return shape((w.shape[0] * devices, w.shape[1]), bf)

    outs = [
        shape((rows, width), bf),
        whole(w_qkv),
        whole(w_out),
        whole(w_up),
        whole(w_down),
        shape((8, width), f32),
        shape((pairs, rows, 128), bf),
        shape((pairs, row_len, 128), bf),
        shape((pairs, row_len, 128), bf),
        shape((pairs, 128, rows), bf),
        shape((pairs, 2, rows), f32),
        shape((rows, width), f32),
        shape((rows, width), f32),
        shape((rows, width), f32),
        shape((width, rows), bf),
        shape((ups, 256, rows), bf),
        shape((ups, rows, 256), bf),
        shape((width, rows), bf),
        shape((width, rows), bf),
    ]
    scratch = [
        pltpu.VMEM((width, 128), bf),
        pltpu.VMEM((8, width), f32),
        pltpu.VMEM((rows, width), bf),
        pltpu.VMEM((rows, width), bf),
        pltpu.VMEM((rows, width), bf),
        pltpu.VMEM((width, rows), bf),
        pltpu.VMEM((width, rows), bf),
        pltpu.VMEM((pairs, rows, 128), bf),
        pltpu.VMEM((pairs, row_len, 128), bf),
        pltpu.VMEM((pairs, row_len, 128), bf),
        pltpu.VMEM((pairs, 128, row_len), bf),
        pltpu.VMEM((row_len, rows), f32),
        pltpu.VMEM((pairs, 128, rows), bf),
        pltpu.VMEM((pairs, 2, rows), f32),
        pltpu.VMEM((rows, width), f32),
        pltpu.VMEM((rows, width), f32),
        pltpu.VMEM((rows, width), f32),
        pltpu.VMEM((rows, width), bf),
        pltpu.VMEM((width, rows), bf),
        pltpu.VMEM((ups, rows, 256), bf),
        pltpu.VMEM((ups, 256, rows), bf),
        pltpu.VMEM((ups, rows, 256), bf),
        pltpu.VMEM((2, width, 256), bf),
        pltpu.VMEM((2, 256, width), bf),
    ]
    scratch += [pltpu.SemaphoreType.DMA((Gather.sems(dp_size // 4),))] * 10
    scratch += [pltpu.SemaphoreType.DMA((2,))] * 3 + [pltpu.SemaphoreType.DMA((16,))]
    return pl.pallas_call(
        functools.partial(forward_kernel, dp_size, head_dim),
        out_shape=outs,
        in_specs=[vm, pl.BlockSpec(memory_space=pltpu.SMEM), vm]
        + [any_spec] * 4
        + [vm, vm],
        out_specs=[vm] + [any_spec] * (len(outs) - 1),
        scratch_shapes=scratch,
        compiler_params=pltpu.CompilerParams(
            collective_id=0, has_side_effects=True, vmem_limit_bytes=60 * 2**20
        ),
    )(tokens, lengths, gains_wide, w_qkv, w_out, w_up, w_down, *tables)


class Share:
    def __init__(self, place, part, first, landing, unit, n, send, recv, write):
        self.g, self.part, self.first = place, part, first
        self.rec3, self.rec2, self.recz = landing
        self.unit, self.n, self.send, self.recv, self.write = unit, n, send, recv, write
        self.kind = part.dtype
        self.n_z, self.n_p2 = 2 * place.Z, 3 * place.Z - 1

    @staticmethod
    def sems(Z):
        return 4 * Z - 1

    def slots(self, block):
        return self.part.at[pl.ds(self.first, self.n), block]

    def copy(self, block, landing, slot, number, device):
        return pltpu.make_async_remote_copy(
            src_ref=self.slots(block),
            dst_ref=landing.at[pl.ds(self.unit, self.n), slot],
            send_sem=self.send.at[number],
            recv_sem=self.recv.at[number],
            device_id=device,
            device_id_type=MESH,
        )

    def p3_copy(self, z, a2):
        g = self.g
        slot = z * 2 + a2
        return self.copy(g.block(z, a2, 1 - g.i3), self.rec3, slot, slot, g.p3)

    def p2_copy(self, z):
        g = self.g
        return self.copy(g.block(z, 1 - g.i2, g.i3), self.rec2, z, self.n_p2 + z, g.p2)

    def z_copy(self, k):
        g = self.g
        z = lax.rem(g.z + k, g.Z)
        return self.copy(
            g.block(z, g.i2, g.i3), self.recz, k - 1, self.n_z + k - 1, g.at_z(z)
        )

    def value(self, ref, *index):
        return ref[(pl.ds(self.unit, self.n),) + index].astype(jnp.float32)

    def own(self, block):
        return self.part[pl.ds(self.first, self.n), block].astype(jnp.float32)

    def start(self, z):
        for a2 in (0, 1):
            self.p3_copy(z, a2).start()

    def start_all(self):
        g = self.g
        for k in range(1, g.Z + 1):
            self.start(lax.rem(g.z + k, g.Z))

    def add3(self, z, a2):
        g = self.g
        self.p3_copy(z, a2).wait_recv()
        block = g.block(z, a2, g.i3)
        total = self.own(block) + self.value(self.rec3, z * 2 + a2)
        self.part[pl.ds(self.first, self.n), block] = total.astype(self.kind)

    def stage3(self, *ks):
        g = self.g
        for k in ks:
            z = lax.rem(g.z + k, g.Z)
            self.add3(z, 1 - g.i2)
            self.p2_copy(z).start()
            self.add3(z, g.i2)

    def stage2(self, *ks):
        g = self.g
        for k in ks:
            z = lax.rem(g.z + k, g.Z)
            self.p2_copy(z).wait_recv()
            block = g.block(z, g.i2, g.i3)
            total = self.own(block) + self.value(self.rec2, z)
            self.part[pl.ds(self.first, self.n), block] = total.astype(self.kind)
            self.z_copy(k).start()

    def last(self):
        g = self.g
        self.p2_copy(g.z).wait_recv()
        total = self.own(g.block(g.z, g.i2, g.i3)) + self.value(self.rec2, g.z)
        for k in range(1, g.Z):
            self.z_copy(k).wait_recv()
            total += self.value(self.recz, k - 1)
        self.write(total)

    def sent(self):
        g = self.g
        for z in range(g.Z):
            for a2 in (0, 1):
                self.p3_copy(z, a2).wait_send()
            self.p2_copy(z).wait_send()
        for k in range(1, g.Z):
            self.z_copy(k).wait_send()


def backward_kernel(dp_size, head_dim, *refs):
    (tok, dout, lens, gain, cosine, sine, wq, wo, wu, wd) = refs[:10]
    (q_i, k_i, v_i, ob_i, lse_i, araw_i, h_i, mraw_i, bt_i, gt_i, gp_i, at_i, atx_i) = refs[10:23]
    (dtok, out_q, out_o, out_u, out_d, out_g) = refs[23:29]
    (gts, dus, dzs) = refs[29:32]
    (part, rec3, rec2, recz, gpart, grec3, grec2, grecz) = refs[32:40]
    (f1, f2, acc, dm, dms, da, das, dz, bt, bts, obts, ats, atx, atxs) = refs[40:54]
    (q, ob, lse, do, bias, dk, dv, dg, dgs, dgt, dnx, dnxs, tile) = refs[54:67]
    (kbuf, vbuf, wbuf, dbuf, gbuf, gsbuf, gpbuf, sbuf) = refs[67:75]
    tsems = refs[75:84]
    usend, urecv, gsend, grecv, zsend, zrecv, osend, orecv, lsem = refs[84:93]
    dnsem = refs[93]
    gsems, rsems = refs[94:100], refs[100:106]
    at, xbuf = bt, gpbuf
    g = Place(dp_size)
    Z, y, c = g.Z, g.y, g.c
    rows, width = tok.shape
    half = head_dim // 2
    pairs = width // 128
    scale = head_dim ** (-0.5)
    ups = gp_i.shape[0]
    per = width // 256
    bf, f32 = jnp.bfloat16, jnp.float32
    first = pl.multiple_of(y * rows, rows)

    def to_sib(src, dst, send, recv):
        return pltpu.make_async_remote_copy(
            src_ref=src,
            dst_ref=dst,
            send_sem=send,
            recv_sem=recv,
            device_id=g.sib,
            device_id_type=MESH,
        )

    def load(src, dst, i):
        return pltpu.make_async_copy(src, dst, lsem.at[i])

    loads = [
        load(mraw_i, f1, 0),
        load(h_i, f2, 1),
        load(bt_i.at[:, c], bt, 2),
        load(atx_i.at[:, c], atx, 5),
        load(q_i, q, 6),
        load(ob_i, ob, 7),
        load(lse_i, lse, 8),
    ]
    araw_load = load(araw_i, f1, 9)
    at_load = load(at_i.at[:, c], at, 4)
    gt_sends = [
        to_sib(gt_i.at[i, 1 - c], gts.at[i], gsend.at[i], grecv.at[i]) for i in range(2 * Z)
    ]
    bt_send = to_sib(bt_i.at[:, 1 - c], bts, osend.at[0], orecv.at[0])
    ob_send = to_sib(ob_i.at[:, 1 - c], obts, osend.at[1], orecv.at[1])
    at_send = to_sib(at_i.at[:, 1 - c], ats, osend.at[2], orecv.at[2])
    atx_send = to_sib(atx_i.at[:, 1 - c], atxs, osend.at[3], orecv.at[3])
    dm_send = to_sib(dm, dms, osend.at[4], orecv.at[4])
    da_send = to_sib(da, das, osend.at[5], orecv.at[5])
    dg_send = to_sib(dg, dgs, osend.at[6], orecv.at[6])
    dnx_send = pltpu.make_async_remote_copy(
        src_ref=dnx,
        dst_ref=dnxs,
        send_sem=dnsem.at[0],
        recv_sem=dnsem.at[1],
        device_id=g.device(g.z, g.x, c, 1 - y),
        device_id_type=MESH,
    )

    def du_send(t):
        return to_sib(dz.at[t], dus.at[t], usend.at[t], urecv.at[t])

    def dz_send(t):
        return to_sib(dz.at[t], dzs.at[t], zsend.at[t], zrecv.at[t])

    landing = (rec3, rec2, recz)

    def write_d(total):
        out_d[...] = total.reshape(out_d.shape)

    def write_into(out, column):
        def write(total):
            for i in range(total.shape[0]):
                out[:, column + i * width : column + (i + 1) * width] = total[i]

        return write

    def write_g(total):
        out_g[...] = total[0]

    s_d = Share(g, part, 0, landing, 0, 4, gsems[0], rsems[0], write_d)
    s_u = [
        Share(g, part, 4 + 2 * i, landing, 4 + 2 * i, 2, gsems[1 + i], rsems[1 + i],
              write_into(out_u, 2 * i * width))
        for i in (0, 1)
    ]
    s_o = Share(g, part, 8, landing, 8, 1, gsems[3], rsems[3], write_into(out_o, 0))
    s_q = Share(g, part, 0, landing, 9, 3, gsems[4], rsems[4], write_into(out_q, 0))
    s_g = Share(g, gpart, 0, (grec3, grec2, grecz), 0, 1, gsems[5], rsems[5], write_g)

    for copy in loads[:2]:
        copy.start()
    g.barrier()
    for copy in gt_sends:
        copy.start()
    bt_send.start()
    ob_send.start()
    at_send.start()

    @pl.when(y == 1)
    def _():
        atx_send.start()

    for copy in loads[2:]:
        copy.start()
    dg[...] = jnp.zeros_like(dg)
    ends = doc_ends(lens)

    def upstream(i):
        e = dout[pl.ds(i * 128, 128), :].astype(f32)
        place = y * rows + i * 128 + lax.broadcasted_iota(jnp.int32, e.shape, 0)
        return jnp.where(place < ends[DOCS - 2], e, 0.0)

    def gain_sum(index, term):
        dg[index : index + 1, :] += jnp.sum(term, axis=0, keepdims=True)

    loads[0].wait()

    @loop(rows // 128)
    def _(i):
        spot = pl.ds(i * 128, 128)
        dv_, term = norm_pull(f1[spot, :], gain[3:4, :], upstream(i))
        dm[spot, :] = dv_.astype(bf)
        gain_sum(3, term)

    dm_send.start()
    araw_load.start()

    def tile_of(j):
        return lax.rem(g.z + 1 + lax.div(j, 2), Z) * 2 + lax.rem(j, 2)

    def gt_ready(j):
        i = tile_of(j)
        to_sib(gt_i.at[i, 1 - c], gts.at[i], gsend.at[i], grecv.at[i]).wait_recv()

    own_g = Tiles(lambda j: gt_i.at[tile_of(j), c], gbuf, tsems[0])
    sib_g = Tiles(lambda j: gts.at[tile_of(j)], gsbuf, tsems[1], gt_ready)
    own_g.first()
    sib_g.first()
    dm_send.wait_recv()

    @loop(2 * Z)
    def _(j):
        i = tile_of(j)
        total = dot(own_g.get(j, 2 * Z), dm[...]) + dot(sib_g.get(j, 2 * Z), dms[...])
        total = total.astype(bf).reshape(2, 4, total.shape[0] // 8, width)
        for a in (0, 1):
            for e in range(4):
                part[e, 2 * i + a] = total[a, e]

        @pl.when(lax.rem(j, 2) == 1)
        def _():
            s_d.start(lax.div(i, 2))

    downs = Tiles(lambda t: wd.at[pl.ds(pl.multiple_of(t * 256, 256), 256), :], dbuf, tsems[2])
    upw = Tiles(lambda t: wu.at[:, pl.ds(pl.multiple_of(t * 256, 256), 256)], wbuf, tsems[3])
    slopes = Tiles(lambda t: gp_i.at[t], gpbuf, tsems[4])
    for tiles in (downs, upw, slopes):
        tiles.first()
    acc[...] = jnp.zeros_like(acc)

    def run_at(t, events):
        for i, event in events.items():

            @pl.when(t == i)
            def _():
                event()

    @loop(ups)
    def _(t):
        du = dot_nt(dm[...], downs.get(t, ups)) * slopes.get(t, ups).astype(f32)
        du = du.astype(bf)
        dz[t] = du
        du_send(t).start()
        acc[...] += dot_nt(du, upw.get(t, ups))
        run_at(t, {7: lambda: s_d.stage3(1), 14: lambda: s_d.stage3(2)})

    def du_ready(t):
        du_send(t).wait_recv()

    loads[2].wait()
    bt_send.wait_recv()
    sib_du = Tiles(lambda t: dus.at[t], sbuf, tsems[5], du_ready)
    sib_du.first()
    for i in (0, 1):

        @loop(ups // 2)
        def _(t2):
            t = t2 + i * (ups // 2)
            total = dot(bt[...].reshape(-1, rows), dz[t])
            total += dot(bts[...].reshape(-1, rows), sib_du.get(t, ups))
            total = total.astype(bf).reshape(4 * Z, -1, 256)
            column = pl.ds(pl.multiple_of(lax.rem(t, per) * 256, 256), 256)
            part[4 + lax.div(t, per), :, :, column] = total

        s_u[i].start_all()
        s_d.stage3(3 if i == 0 else 0)

    at_load.start()

    loads[1].wait()
    araw_load.wait()

    @loop(rows // 128)
    def _(i):
        spot = pl.ds(i * 128, 128)
        dv_, term = norm_pull(f2[spot, :], gain[2:3, :], acc[spot, :])
        gain_sum(2, term)
        dh = upstream(i) + dv_
        f2[spot, :] = dh
        dv_, term = norm_pull(f1[spot, :], gain[1:2, :], dh)
        gain_sum(1, term)
        da[spot, :] = dv_.astype(bf)

    da_send.start()
    s_d.stage2(1)
    outs = Tiles(lambda t: wo.at[pl.ds(pl.multiple_of(t * 256, 256), 256), :], dbuf, tsems[2])
    outs.first()

    @loop(per)
    def _(t):
        u = dot_nt(da[...], outs.get(t, per)).astype(bf)
        do[2 * t] = u[:, :128]
        do[2 * t + 1] = u[:, 128:]

    loads[5].wait()
    ob_send.wait_recv()
    da_send.wait_recv()

    @loop(per)
    def _(t):
        column = pl.ds(pl.multiple_of(t * 256, 256), 256)
        total = dot(ob[:, c].reshape(-1, rows), da[:, column])
        total += dot(obts[...].reshape(-1, rows), das[:, column])
        part[8, :, :, column] = total.astype(bf).reshape(4 * Z, -1, 256)

    s_o.start_all()
    s_d.stage2(2, 3)
    for t in range(ups):
        du_send(t).wait_send()

    fill_bias(bias, lens, y * rows, rows)
    loads[4].wait()
    loads[6].wait()
    keys = Tiles(lambda p: k_i.at[p], kbuf, tsems[6])
    values = Tiles(lambda p: v_i.at[p], vbuf, tsems[7])
    keys.first()
    values.first()
    blocks = rows // 256

    def attend(p, block, count, fresh, kk, vv, kt):
        spot = slice(block * 256, block * 256 + 256)
        qs = split_heads(q[p, spot, :])
        dos = split_heads(do[p, spot, :])
        dot_o = jnp.transpose(do[p, spot, :].astype(f32)) * ob_pair(p, spot)
        parts = []
        dk_, dv_ = [], []
        for i in (0, 1):
            delta = jnp.sum(
                dot_o[i * head_dim : (i + 1) * head_dim], axis=0, keepdims=True
            )
            s = dot_nt(kk, qs[i]) + bias[:count, spot]
            prob = jnp.exp(s - lse[p, i : i + 1, spot])
            ds = (prob * (dot_nt(vv, dos[i]) - delta)).astype(bf)
            dv_.append(dot(prob.astype(bf), dos[i]))
            dk_.append(dot(ds, qs[i]))
            parts.append(dot(kt, ds))
        if fresh:
            dk[:count, :] = dk_[0] + dk_[1]
            dv[:count, :] = dv_[0] + dv_[1]
        else:
            dk[:count, :] += dk_[0] + dk_[1]
            dv[:count, :] += dv_[0] + dv_[1]
        upper = lax.broadcasted_iota(jnp.int32, parts[0].shape, 0) < head_dim
        dq = jnp.transpose(jnp.where(upper, parts[0], parts[1]) * scale)
        start = pl.multiple_of(first + block * 256, 256)
        dq = turn(dq, cosine[pl.ds(start, 256), :], -sine[pl.ds(start, 256), :], half)
        dz[lax.div(p, 2), spot, lanes(p)] = dq.astype(bf)

    def ob_pair(p, spot):
        return ob[p, :, :, spot].astype(f32).reshape(128, -1)

    def lanes(p):
        return pl.ds(pl.multiple_of(lax.rem(p, 2) * 128, 128), 128)

    def keep(p, start, base):
        spot = pl.ds(start, rows)
        u = turn(dk[spot, :], cosine[spot, :], -sine[spot, :], half)
        dz[base + lax.div(p, 2), :, lanes(p)] = u.astype(bf)
        dz[base + per + lax.div(p, 2), :, lanes(p)] = dv[spot, :].astype(bf)

    events = {
        0: lambda: s_u[0].stage3(1, 2),
        1: lambda: (s_u[0].stage3(3, 0), s_d.last()),
        2: lambda: s_u[1].stage3(1, 2),
        3: lambda: s_u[0].stage2(1, 2, 3),
        4: lambda: s_u[1].stage3(3, 0),
        5: lambda: (s_o.stage3(1, 2, 3, 0), s_u[1].stage2(1, 2, 3)),
        6: lambda: (s_o.stage2(1, 2, 3), s_u[0].last()),
        7: lambda: s_u[1].last(),
    }

    @loop(pairs)
    def _(p):
        kk = keys.get(p, pairs)
        vv = values.get(p, pairs)
        kt = jnp.transpose(kk.astype(f32)).astype(bf)
        for half_row in (0, 1):

            @pl.when(y == half_row)
            def _():
                for block in reversed(range(blocks)):
                    count = (half_row * blocks + block + 1) * 256
                    attend(p, block, count, block == blocks - 1, kk[:count], vv[:count], kt[:, :count])

        keep(p, first, per)

        @pl.when(y == 1)
        def _():
            keep(p, 0, 3 * per)

        @pl.when(lax.rem(p, 2) == 1)
        def _():
            for e in range(3):
                dz_send(e * per + lax.div(p, 2)).start()

            @pl.when(y == 1)
            def _():
                for e in (3, 4):
                    dz_send(e * per + lax.div(p, 2)).start()

        run_at(p, events)

    s_o.last()

    qkv_w = Tiles(lambda t: wq.at[:, pl.ds(pl.multiple_of(t * 256, 256), 256)], wbuf, tsems[3])

    @pl.when(y == 1)
    def _():
        acc[...] = jnp.zeros_like(acc)
        qkv_w.first(per)

        @loop(2 * per)
        def _(t):
            acc[...] += dot_nt(dz[t + 3 * per], qkv_w.get(t + per, 3 * per))

        dnx[...] = acc[...].astype(bf)
        dnx_send.start()

    s_d.sent()
    loads[3].wait()
    at_load.wait()
    at_send.wait_recv()

    @pl.when(y == 1)
    def _():
        atx_send.wait_recv()

    def dz_ready(t):
        dz_send(t).wait_recv()

    sib_dz = Tiles(lambda t: dzs.at[t], sbuf, tsems[5], dz_ready)
    sib_dx = Tiles(lambda t: dzs.at[t], xbuf, tsems[8], dz_ready)
    sib_dz.first()

    @pl.when(y == 1)
    def _():
        sib_dx.first(3 * per)

    @loop(3 * per)
    def _(t):
        tile[...] = dot(at[...].reshape(-1, rows), dz[t])
        tile[...] += dot(ats[...].reshape(-1, rows), sib_dz.get(t, 3 * per))

        @pl.when((y == 1) & (t >= per))
        def _():
            tx = t + 2 * per
            tile[...] += dot(atx[...].reshape(-1, rows), dz[tx])
            tile[...] += dot(atxs[...].reshape(-1, rows), sib_dx.get(tx, 5 * per))

        column = pl.ds(pl.multiple_of(lax.rem(t, per) * 256, 256), 256)
        part[lax.div(t, per), :, :, column] = tile[...].astype(bf).reshape(4 * Z, -1, 256)

    s_q.start_all()

    acc[...] = jnp.zeros_like(acc)
    qkv_w.first()

    @loop(3 * per)
    def _(t):
        acc[...] += dot_nt(dz[t], qkv_w.get(t, 3 * per))

    @pl.when(y == 0)
    def _():
        dnx_send.wait_recv()
        acc[...] += dnxs[...].astype(f32)

    @loop(rows // 128)
    def _(i):
        spot = pl.ds(i * 128, 128)
        dv_, term = norm_pull(tok[spot, :].astype(f32), gain[0:1, :], acc[spot, :])
        gain_sum(0, term)
        dtok[spot, :] = (f2[spot, :] + dv_).astype(bf)

    dg_send.start()
    s_q.stage3(1)
    dg_send.wait_recv()
    wide = jnp.concatenate([dg[...] + dgs[...], jnp.zeros((120, width), f32)], axis=0)
    dgt[...] = jnp.transpose(wide).reshape(dgt.shape)
    gpart[0] = dgt[:, c].reshape(gpart.shape[1:])
    s_g.start_all()
    s_q.stage3(2, 3, 0)
    s_g.stage3(1, 2, 3, 0)
    s_q.stage2(1, 2, 3)
    s_g.stage2(1, 2, 3)
    s_q.last()
    s_g.last()

    for copy in gt_sends + [bt_send, ob_send, at_send, dm_send, da_send, dg_send]:
        copy.wait_send()
    for t in range(3 * per):
        dz_send(t).wait_send()

    @pl.when(y == 1)
    def _():
        atx_send.wait_send()
        dnx_send.wait_send()
        for t in range(3 * per, 5 * per):
            dz_send(t).wait_send()

    for s in (s_u[0], s_u[1], s_o, s_q, s_g):
        s.sent()


def backward(tokens, d_out, lengths, gain_rows, tables, weights, saved, shards):
    dp_size = lax.axis_size("dp")
    Z = dp_size // 4
    rows, width = tokens.shape
    row_len = rows * lax.axis_size("ctx")
    head_dim = width // HEADS
    pairs = width // 128
    per = width // 256
    bf, f32 = jnp.bfloat16, jnp.float32
    ups = saved[10].shape[0]
    any_spec = pl.BlockSpec(memory_space=pl.ANY)
    vm = pl.BlockSpec(memory_space=pltpu.VMEM)
    smem = pl.BlockSpec(memory_space=pltpu.SMEM)
    shape = jax.ShapeDtypeStruct
    block = 32
    saved = list(saved)
    for i in (3, 8, 11, 12):
        saved[i] = saved[i].reshape(2 * Z, 2, width // (4 * Z), rows)
    saved[9] = saved[9].reshape(2 * Z, 2, 256, rows)
    outs = [
        shape((rows, width), bf),
        shape((shards[0].shape[0], shards[0].shape[1]), f32),
        shape(shards[1].shape, f32),
        shape(shards[2].shape, f32),
        shape(shards[3].shape, f32),
        shape((block, 128), f32),
        shape((2 * Z, 256, rows), bf),
        shape((ups, rows, 256), bf),
        shape((5 * per, rows, 256), bf),
    ]
    core_rows = (2 * Z, width // (4 * Z), rows)
    scratch = [
        pltpu.VMEM((9, 4 * Z, block, width), bf),
        pltpu.VMEM((12, 2 * Z, block, width), bf),
        pltpu.VMEM((12, Z, block, width), bf),
        pltpu.VMEM((12, Z - 1, block, width), bf),
        pltpu.VMEM((1, 4 * Z, block, 128), f32),
        pltpu.VMEM((1, 2 * Z, block, 128), f32),
        pltpu.VMEM((1, Z, block, 128), f32),
        pltpu.VMEM((1, Z - 1, block, 128), f32),
        pltpu.VMEM((rows, width), f32),
        pltpu.VMEM((rows, width), f32),
        pltpu.VMEM((rows, width), f32),
        pltpu.VMEM((rows, width), bf),
        pltpu.VMEM((rows, width), bf),
        pltpu.VMEM((rows, width), bf),
        pltpu.VMEM((rows, width), bf),
        pltpu.VMEM((max(ups, 5 * per), rows, 256), bf),
    ]
    scratch += [pltpu.VMEM(core_rows, bf)] * 6
    scratch += [
        pltpu.VMEM((pairs, rows, 128), bf),
        pltpu.VMEM((2 * Z, 2, width // (4 * Z), rows), bf),
        pltpu.VMEM((pairs, 2, rows), f32),
        pltpu.VMEM((pairs, rows, 128), bf),
        pltpu.VMEM((row_len, rows), f32),
        pltpu.VMEM((row_len, 128), f32),
        pltpu.VMEM((row_len, 128), f32),
        pltpu.VMEM((8, width), f32),
        pltpu.VMEM((8, width), f32),
        pltpu.VMEM((2 * Z, 2, width // (4 * Z), 128), f32),
        pltpu.VMEM((rows, width), bf),
        pltpu.VMEM((rows, width), bf),
        pltpu.VMEM((rows, 256), f32),
        pltpu.VMEM((2, row_len, 128), bf),
        pltpu.VMEM((2, row_len, 128), bf),
        pltpu.VMEM((2, width, 256), bf),
        pltpu.VMEM((2, 256, width), bf),
        pltpu.VMEM((2, 256, rows), bf),
        pltpu.VMEM((2, 256, rows), bf),
        pltpu.VMEM((2, rows, 256), bf),
        pltpu.VMEM((2, rows, 256), bf),
    ]
    dma = pltpu.SemaphoreType.DMA
    scratch += [dma((2,))] * 9
    scratch += [dma((ups,))] * 2 + [dma((2 * Z,))] * 2 + [dma((5 * per,))] * 2
    scratch += [dma((7,))] * 2 + [dma((10,)), dma((2,))]
    scratch += [dma((Share.sems(Z),))] * 12
    return pl.pallas_call(
        functools.partial(backward_kernel, dp_size, head_dim),
        out_shape=outs,
        in_specs=[vm, vm, smem, vm, vm, vm] + [any_spec] * 17,
        out_specs=[vm] * 6 + [any_spec] * 3,
        scratch_shapes=scratch,
        compiler_params=pltpu.CompilerParams(
            collective_id=1, has_side_effects=True, vmem_limit_bytes=63 * 2**20
        ),
    )(tokens, d_out, lengths, gain_rows, *tables, *weights, *saved)


def layer_norm(values, gain_vec):
    center = values - jnp.mean(values, axis=-1, keepdims=True)
    spread = jnp.mean(center * center, axis=-1, keepdims=True)
    return center * lax.rsqrt(spread + epsilon) * gain_vec


def norm_back(values, gain_vec, upstream):
    unused, pullback = jax.vjp(layer_norm, values, gain_vec)
    return pullback(upstream)


def rotate(values, cosine_table, sine_table, direction):
    half_dim = values.shape[-1] // 2
    first_half = values[..., :half_dim]
    second_half = values[..., half_dim:]
    return jnp.concatenate(
        [
            first_half * cosine_table - direction * second_half * sine_table,
            second_half * cosine_table + direction * first_half * sine_table,
        ],
        axis=-1,
    )


def doc_layout(lengths, row_len):
    doc_ends = jnp.cumsum(lengths, axis=-1)
    places = jnp.arange(row_len, dtype=jnp.int32)
    passed = places[None, :, None] >= doc_ends[:, None, :]
    segment = jnp.sum(passed.astype(jnp.int32), axis=-1)
    starts = jnp.sum(jnp.where(passed, lengths[:, None, :], 0), axis=-1)
    position = places[None, :] - starts
    is_valid = places[None, :] < doc_ends[:, DOCS - 2][:, None]
    return (segment[0], position[0], is_valid[0])


def allowed_keys(own_seg, own_place, seg_full, first_key, block_rows):
    key_place = first_key + jnp.arange(block_rows, dtype=jnp.int32)
    key_seg = lax.dynamic_slice_in_dim(seg_full, first_key, block_rows)
    return (own_seg[:, None] == key_seg[None, :]) & (key_place[None, :] <= own_place[:, None])


def make_fold(queries, own_seg, own_place, seg_full, score_scale):

    def fold_piece(fold_state, piece, start):
        key_piece, value_piece = piece
        piece_rows = key_piece.shape[0]
        block_rows = math.gcd(piece_rows, 256)
        block_count = piece_rows // block_rows
        key_blocks = key_piece.reshape((block_count, block_rows) + key_piece.shape[1:])
        value_blocks = value_piece.reshape((block_count, block_rows) + value_piece.shape[1:])

        def step_block(carried, block_items):
            row_max, row_sum, weighted = carried
            key_block, value_block, block_id = block_items
            allowed = allowed_keys(own_seg, own_place, seg_full, block_id * block_rows, block_rows)
            scores = (
                jnp.einsum("qhd,khd->hqk", queries, key_block, preferred_element_type=jnp.float32)
                * score_scale
            )
            scores = jnp.where(allowed[None], scores, masked_score)
            new_max = jnp.maximum(row_max, jnp.max(scores, axis=-1))
            factor = jnp.exp(row_max - new_max)
            shifted = jnp.where(allowed[None], jnp.exp(scores - new_max[..., None]), 0.0)
            row_sum = row_sum * factor + jnp.sum(shifted, axis=-1)
            weighted = weighted * factor[..., None] + jnp.einsum(
                "hqk,khd->hqd",
                shifted.astype(jnp.bfloat16),
                value_block,
                preferred_element_type=jnp.float32,
            )
            return ((new_max, row_sum, weighted), None)

        block_ids = jnp.arange(block_count, dtype=jnp.int32)
        fold_state, unused = lax.scan(step_block, fold_state, (key_blocks, value_blocks, block_ids))
        return fold_state

    return fold_piece


def per_device(tokens, lengths, w_qkv, w_out, w_up, w_down, gains, d_out):
    tok_rows, model_width = tokens.shape
    row_len = tok_rows * lax.axis_size("ctx")
    head_count = HEADS
    head_dim = model_width // head_count
    score_scale = head_dim ** (-0.5)
    head_shape = (tok_rows, head_count, head_dim)
    seg_full, pos_full, valid_full = doc_layout(lengths, row_len)
    offset = lax.axis_index("ctx") * tok_rows
    own_seg = lax.dynamic_slice_in_dim(seg_full, offset, tok_rows)
    own_pos = lax.dynamic_slice_in_dim(pos_full, offset, tok_rows)
    own_valid = lax.dynamic_slice_in_dim(valid_full.astype(jnp.float32), offset, tok_rows)
    own_place = offset + jnp.arange(tok_rows, dtype=jnp.int32)
    freq_index = jnp.arange(head_dim // 2, dtype=jnp.float32)
    angles = own_pos.astype(jnp.float32)[:, None] * 10000.0 ** (-2.0 * freq_index / head_dim)
    cosine_table = jnp.cos(angles)[:, None, :]
    sine_table = jnp.sin(angles)[:, None, :]
    gains_wide = jnp.pad(gains, ((0, 0), (0, 128 - gains.shape[1])))
    gain_full, qkv_full, out_full, up_full, down_full = gather_all(
        (gains_wide, w_qkv, w_out, w_up, w_down), (False, True, True, False, False)
    )
    gain_full = gain_full[:, : gains.shape[1]]
    gain_f = gain_full.astype(jnp.float32)
    stream = tokens.astype(jnp.float32)
    normed = layer_norm(stream, gain_f[:, 0]).astype(jnp.bfloat16)
    qkv_raw = jnp.dot(normed, qkv_full, preferred_element_type=jnp.float32)
    queries = rotate(
        qkv_raw[:, :model_width].reshape(head_shape), cosine_table, sine_table, 1.0
    ).astype(jnp.bfloat16)
    key_heads = rotate(
        qkv_raw[:, model_width : 2 * model_width].reshape(head_shape), cosine_table, sine_table, 1.0
    ).astype(jnp.bfloat16)
    value_heads = qkv_raw[:, 2 * model_width :].reshape(head_shape).astype(jnp.bfloat16)
    start_state = (
        jnp.full((head_count, tok_rows), masked_score, jnp.float32),
        jnp.zeros((head_count, tok_rows), jnp.float32),
        jnp.zeros((head_count, tok_rows, head_dim), jnp.float32),
    )
    fold_piece = make_fold(queries, own_seg, own_place, seg_full, score_scale)
    row_max, row_sum, weighted = fold_piece(
        start_state,
        (
            lax.all_gather(key_heads, "ctx", axis=0, tiled=True),
            lax.all_gather(value_heads, "ctx", axis=0, tiled=True),
        ),
        jnp.int32(0),
    )
    attended = jnp.transpose(weighted / row_sum[..., None], (1, 0, 2))
    attended_b = attended.reshape(tok_rows, model_width).astype(jnp.bfloat16)
    attn_raw = jnp.dot(attended_b, out_full, preferred_element_type=jnp.float32)
    hidden = stream + layer_norm(attn_raw, gain_f[:, 1])
    mlp_in = layer_norm(hidden, gain_f[:, 2]).astype(jnp.bfloat16)
    up_proj = jnp.dot(mlp_in, up_full, preferred_element_type=jnp.float32)
    activated = jax.nn.gelu(up_proj).astype(jnp.bfloat16)
    mlp_raw = jnp.dot(activated, down_full, preferred_element_type=jnp.float32)
    result = hidden + layer_norm(mlp_raw, gain_f[:, 3])
    output = (result * own_valid[:, None]).astype(jnp.bfloat16)
    qkv_back, out_back, up_back, down_back = (qkv_full, out_full, up_full, down_full)
    upstream = d_out.astype(jnp.float32) * own_valid[:, None]
    d_mlp, d_gain_four = norm_back(mlp_raw, gain_f[:, 3], upstream)
    d_mlp_b = d_mlp.astype(jnp.bfloat16)
    grad_down = jnp.einsum("tf,td->fd", activated, d_mlp_b, preferred_element_type=jnp.float32)
    d_activated = jnp.einsum("td,fd->tf", d_mlp_b, down_back, preferred_element_type=jnp.float32)
    unused, gelu_pull = jax.vjp(jax.nn.gelu, up_proj)
    d_up_b = gelu_pull(d_activated)[0].astype(jnp.bfloat16)
    grad_up = jnp.einsum("td,tf->df", mlp_in, d_up_b, preferred_element_type=jnp.float32)
    d_mlp_in = jnp.einsum("tf,df->td", d_up_b, up_back, preferred_element_type=jnp.float32)
    d_hidden_part, d_gain_three = norm_back(hidden, gain_f[:, 2], d_mlp_in)
    d_hidden = upstream + d_hidden_part
    d_attn, d_gain_two = norm_back(attn_raw, gain_f[:, 1], d_hidden)
    d_attn_b = d_attn.astype(jnp.bfloat16)
    grad_out = jnp.einsum("td,te->de", attended_b, d_attn_b, preferred_element_type=jnp.float32)
    d_attended = (
        jnp.einsum("te,de->td", d_attn_b, out_back, preferred_element_type=jnp.float32)
        .astype(jnp.bfloat16)
        .reshape(head_shape)
    )
    row_dot = jnp.einsum("qhd,qhd->hq", d_attended.astype(jnp.float32), attended)
    key_all, value_all = (
        lax.all_gather(key_heads, "ctx", axis=0, tiled=True),
        lax.all_gather(value_heads, "ctx", axis=0, tiled=True),
    )
    block_rows = math.gcd(row_len, 256)
    block_count = row_len // block_rows
    key_blocks = key_all.reshape((block_count, block_rows) + key_all.shape[1:])
    value_blocks = value_all.reshape((block_count, block_rows) + value_all.shape[1:])

    def back_block(d_queries, block_items):
        key_block, value_block, block_id = block_items
        allowed = allowed_keys(own_seg, own_place, seg_full, block_id * block_rows, block_rows)
        scores = (
            jnp.einsum("qhd,khd->hqk", queries, key_block, preferred_element_type=jnp.float32)
            * score_scale
        )
        attn_prob = jnp.where(
            allowed[None], jnp.exp(scores - row_max[..., None]) / row_sum[..., None], 0.0
        )
        d_prob = jnp.einsum(
            "qhd,khd->hqk", d_attended, value_block, preferred_element_type=jnp.float32
        )
        d_scores = (attn_prob * (d_prob - row_dot[..., None])).astype(jnp.bfloat16)
        d_queries = (
            d_queries
            + jnp.einsum("hqk,khd->qhd", d_scores, key_block, preferred_element_type=jnp.float32)
            * score_scale
        )
        d_keys = (
            jnp.einsum("hqk,qhd->khd", d_scores, queries, preferred_element_type=jnp.float32)
            * score_scale
        )
        d_values = jnp.einsum(
            "hqk,qhd->khd",
            attn_prob.astype(jnp.bfloat16),
            d_attended,
            preferred_element_type=jnp.float32,
        )
        return (d_queries, (d_keys, d_values))

    block_ids = jnp.arange(block_count, dtype=jnp.int32)
    d_queries, (d_keys_all, d_values_all) = lax.scan(
        back_block, jnp.zeros(head_shape, jnp.float32), (key_blocks, value_blocks, block_ids)
    )
    kv_terms = jnp.concatenate(
        [d_keys_all.reshape(row_len, model_width), d_values_all.reshape(row_len, model_width)],
        axis=-1,
    )
    kv_grad = lax.psum_scatter(
        kv_terms.astype(jnp.bfloat16), "ctx", scatter_dimension=0, tiled=True
    ).astype(jnp.float32)
    d_keys = kv_grad[:, :model_width].reshape(head_shape)
    d_qkv = jnp.concatenate(
        [
            rotate(d_queries, cosine_table, sine_table, -1.0).reshape(tok_rows, model_width),
            rotate(d_keys, cosine_table, sine_table, -1.0).reshape(tok_rows, model_width),
            kv_grad[:, model_width:],
        ],
        axis=-1,
    ).astype(jnp.bfloat16)
    grad_qkv = jnp.einsum("td,te->de", normed, d_qkv, preferred_element_type=jnp.float32)
    d_normed = jnp.einsum("te,de->td", d_qkv, qkv_back, preferred_element_type=jnp.float32)
    d_stream_part, d_gain_one = norm_back(stream, gain_f[:, 0], d_normed)
    d_tokens = (d_hidden + d_stream_part).astype(jnp.bfloat16)
    grad_gains = jnp.stack([d_gain_one, d_gain_two, d_gain_three, d_gain_four], axis=-1)
    grad_gains = jnp.pad(grad_gains, ((0, 0), (0, 128 - gains.shape[1])))
    shard_down, shard_up, shard_out, shard_qkv, shard_gains = scatter_all(
        [v.astype(jnp.bfloat16) for v in (grad_down, grad_up, grad_out, grad_qkv, grad_gains)],
        (False, False, True, True, False),
    )
    shard_gains = shard_gains[:, : gains.shape[1]]
    return (output, d_tokens, shard_qkv, shard_out, shard_up, shard_down, shard_gains)


def fused_device(tokens, lengths, w_qkv, w_out, w_up, w_down, gains, d_out):
    rows, width = tokens.shape
    row_len = rows * lax.axis_size("ctx")
    gains_wide = jnp.pad(gains, ((0, 0), (0, 128 - gains.shape[1])))
    tables = tuple(jnp.asarray(v) for v in turn_tables(row_len, width // HEADS))
    output, wq, wo, wu, wd, gain_rows, *saved = forward(
        tokens, lengths, gains_wide, w_qkv, w_out, w_up, w_down, tables
    )
    d_tokens, grad_qkv, grad_out, grad_up, grad_down, grad_gains = backward(
        tokens,
        d_out,
        lengths,
        gain_rows,
        tables,
        (wq, wo, wu, wd),
        saved,
        (w_qkv, w_out, w_up, w_down),
    )[:6]
    return (
        output,
        d_tokens,
        grad_qkv,
        grad_out,
        grad_up,
        grad_down,
        grad_gains[:, : gains.shape[1]],
    )


def layer(mesh):
    if mesh.shape["dp"] == 16 and mesh.shape["ctx"] == 2:
        return fused_device
    return per_device


def solution(mesh):
    return jax.shard_map(
        layer(mesh),
        mesh=mesh,
        in_specs=(
            P(("dp", "ctx"), None),
            P("dp", None),
            P(("dp", "ctx"), None),
            P(("dp", "ctx"), None),
            P(("dp", "ctx"), None),
            P(("dp", "ctx"), None),
            P(("dp", "ctx"), None),
            P(("dp", "ctx"), None),
        ),
        out_specs=(
            P(("dp", "ctx"), None),
            P(("dp", "ctx"), None),
            P(("dp", "ctx"), None),
            P(("dp", "ctx"), None),
            P(("dp", "ctx"), None),
            P(("dp", "ctx"), None),
            P(("dp", "ctx"), None),
        ),
        check_vma=False,
    )
```

```python
import functools
import math

import jax
import jax.numpy as jnp
import numpy as np
from jax import lax
from jax.experimental import pallas as pl
from jax.experimental.pallas import tpu as pltpu
from jax.sharding import PartitionSpec as P

HEADS = 16
DOCS = 7
MODES = (False, False, False, False)

epsilon = 1e-05
masked_score = -1e30


MESH = pl.DeviceIdType.MESH


def when(condition, body):
    if isinstance(condition, bool):
        if condition:
            body()
    else:
        pl.when(condition)(body)


def unless(condition, body):
    if isinstance(condition, bool):
        if not condition:
            body()
    else:
        pl.when(jnp.logical_not(condition))(body)


def pick(condition, one, other):
    if isinstance(condition, bool):
        return one if condition else other
    return jnp.where(condition, one, other)


class Place:
    def __init__(self, dp_size):
        dp = lax.axis_index("dp")
        self.Z = dp_size // 4
        self.z = lax.div(dp, 4)
        self.x = lax.rem(lax.div(dp, 2), 2)
        self.c = lax.rem(dp, 2)
        self.y = lax.axis_index("ctx")
        c, x, y = self.c, self.x, self.y
        self.i2 = y * (1 - c) + x * c
        self.i3 = x * (1 - c) + y * c
        self.sib = self.device(self.z, x, 1 - c, y)
        self.p2 = self.device(self.z, x * (1 - c) + (1 - x) * c, c, (1 - y) * (1 - c) + y * c)
        self.p3 = self.device(self.z, (1 - x) * (1 - c) + x * c, c, y * (1 - c) + (1 - y) * c)

    def device(self, z, x, c, y):
        return ((z * 2 + x) * 2 + c, y)

    def above(self, k):
        return lax.rem(self.z + k, self.Z)

    def below(self, k):
        return lax.rem(self.z - k + self.Z, self.Z)

    def at_z(self, z):
        return self.device(z, self.x, self.c, self.y)

    def block(self, z, a2, a3):
        c = self.c
        return (z * 2 + a3 * (1 - c) + a2 * c) * 2 + a2 * (1 - c) + a3 * c

    def row_block(self, z, a2, a3, core):
        c = self.c
        xx = a3 * (1 - c) + a2 * c
        yy = a2 * (1 - c) + a3 * c
        return ((z * 2 + xx) * 2 + core) * 2 + yy

    def barrier(self):
        bar = pltpu.get_barrier_semaphore()
        for device in (self.sib, self.p2, self.p3):
            pl.semaphore_signal(bar, 1, device_id=device, device_id_type=MESH)
        for k in range(1, self.Z):
            pl.semaphore_signal(
                bar, 1, device_id=self.at_z(self.above(k)), device_id_type=MESH
            )
        pl.semaphore_wait(bar, 3 + self.Z - 1)


class Gather:
    def __init__(self, place, shard, full, send, recv, by_z):
        self.g, self.shard, self.full = place, shard, full
        self.send, self.recv = send, recv
        self.rows = shard.shape[0]
        self.by_z = by_z
        Z = place.Z
        self.n_z = 0
        self.n_p2 = 2 * (Z - 1)
        self.n_p3 = self.n_p2 + Z
        self.n_sib = self.n_p3 + 2 * Z
        self.n_own = self.n_sib + 4 * Z

    @staticmethod
    def sems(Z):
        return 2 * (Z - 1) + Z + 2 * Z + 4 * Z + 1

    def at(self, index):
        return self.full.at[pl.ds(pl.multiple_of(index * self.rows, self.rows), self.rows)]

    def copy(self, index, number, device, src=None):
        return pltpu.make_async_remote_copy(
            src_ref=self.at(index) if src is None else src,
            dst_ref=self.at(index),
            send_sem=self.send.at[number],
            recv_sem=self.recv.at[number],
            device_id=device,
            device_id_type=MESH,
        )

    def own_copy(self):
        g = self.g
        index = g.row_block(g.z, g.i2, g.i3, g.c)
        return pltpu.make_async_copy(self.shard, self.at(index), self.recv.at[self.n_own])

    def z_copy(self, other, k, src=None):
        g = self.g
        a2 = (1 - g.i2) if other else g.i2
        number = self.n_z + (k - 1) * 2 + int(other)
        return self.copy(g.row_block(g.z, a2, g.i3, g.c), number, g.at_z(g.above(k)), src)

    def p2_copy(self, z, src=None):
        g = self.g
        return self.copy(g.row_block(z, g.i2, g.i3, g.c), self.n_p2 + z, g.p2, src)

    def p3_copy(self, z, a2, src=None):
        g = self.g
        return self.copy(g.row_block(z, a2, g.i3, g.c), self.n_p3 + z * 2 + a2, g.p3, src)

    def sib_copy(self, z, a2, a3, src=None):
        g = self.g
        number = self.n_sib + g.block(z, a2, a3)
        return self.copy(g.row_block(z, a2, a3, g.c), number, g.sib, src)

    def wait(self, number, index):
        self.copy(index, number, self.g.sib).wait_recv()

    def start(self):
        g, src = self.g, self.shard
        self.p2_copy(g.z, src).start()
        self.p3_copy(g.z, g.i2, src).start()
        for k in range(1, g.Z):
            self.z_copy(False, k, src).start()
        self.sib_copy(g.z, g.i2, g.i3, src).start()
        self.own_copy().start()

    def first_p2(self):
        g = self.g
        o2 = 1 - g.i2
        self.wait(self.n_p2 + g.z, g.row_block(g.z, o2, g.i3, g.c))

        def along_z():
            for k in range(1, g.Z):
                self.z_copy(True, k).start()

        when(self.by_z, along_z)
        self.p3_copy(g.z, o2).start()
        self.sib_copy(g.z, o2, g.i3).start()

    def arrived_z(self, k):
        g = self.g
        z = g.below(k)
        self.wait(self.n_z + (k - 1) * 2, g.row_block(z, g.i2, g.i3, g.c))
        unless(self.by_z, lambda: self.p2_copy(z).start())
        self.p3_copy(z, g.i2).start()
        self.sib_copy(z, g.i2, g.i3).start()

    def later_p2(self, k):
        g = self.g
        z = g.below(k)
        o2 = 1 - g.i2
        number = pick(self.by_z, self.n_z + (k - 1) * 2 + 1, self.n_p2 + z)
        self.wait(number, g.row_block(z, o2, g.i3, g.c))
        self.p3_copy(z, o2).start()
        self.sib_copy(z, o2, g.i3).start()

    def all_z(self):
        for k in range(1, self.g.Z):
            self.arrived_z(k)

    def all_p2(self):
        for k in range(1, self.g.Z):
            self.later_p2(k)

    def arrived_p3(self, z):
        g = self.g
        for a2 in (0, 1):
            self.wait(self.n_p3 + z * 2 + a2, g.row_block(z, a2, 1 - g.i3, g.c))
            self.sib_copy(z, a2, 1 - g.i3).start()

    def all_p3(self):
        g = self.g
        for k in range(g.Z):
            self.arrived_p3(g.below(k))

    def arrived_sib(self, z):
        g = self.g
        for xx in (0, 1):
            for yy in (0, 1):
                number = self.n_sib + (z * 2 + xx) * 2 + yy
                self.wait(number, ((z * 2 + xx) * 2 + 1 - g.c) * 2 + yy)

    def complete(self):
        for z in range(self.g.Z):
            self.arrived_sib(z)
        self.own_copy().wait()

    def sent(self):
        g, src = self.g, self.shard
        self.p2_copy(g.z, src).wait_send()
        self.p3_copy(g.z, g.i2, src).wait_send()
        self.sib_copy(g.z, g.i2, g.i3, src).wait_send()
        for k in range(1, g.Z):
            self.z_copy(False, k, src).wait_send()
            z = g.above(k)
            when(self.by_z, lambda: self.z_copy(True, k).wait_send())
            unless(self.by_z, lambda: self.p2_copy(z).wait_send())
            self.p3_copy(z, g.i2).wait_send()
            self.sib_copy(z, g.i2, g.i3).wait_send()
        for z in range(g.Z):
            self.p3_copy(z, 1 - g.i2).wait_send()
            self.sib_copy(z, 1 - g.i2, g.i3).wait_send()
            for a2 in (0, 1):
                self.sib_copy(z, a2, 1 - g.i3).wait_send()


class Share:
    def __init__(self, place, part, first, landing, unit, n, send, recv, write, by_z):
        self.g, self.part, self.first = place, part, first
        self.rec3, self.rec = landing
        self.unit, self.n, self.send, self.recv, self.write = unit, n, send, recv, write
        self.kind, self.by_z = part.dtype, by_z

    @staticmethod
    def sems(Z):
        return 4 * Z - 1

    def copy(self, block, landing, slot, number, device):
        return pltpu.make_async_remote_copy(
            src_ref=self.part.at[pl.ds(self.first, self.n), block],
            dst_ref=landing.at[pl.ds(self.unit, self.n), slot],
            send_sem=self.send.at[number],
            recv_sem=self.recv.at[number],
            device_id=device,
            device_id_type=MESH,
        )

    def p3_copy(self, z, a2):
        g = self.g
        slot = z * 2 + a2
        return self.copy(g.block(z, a2, 1 - g.i3), self.rec3, slot, slot, g.p3)

    def p2_copy(self, z):
        g = self.g
        slot = pick(self.by_z, 0, z)
        block = g.block(z, 1 - g.i2, g.i3)
        return self.copy(block, self.rec, slot, 2 * g.Z + slot, g.p2)

    def z_copy(self, k, a2, by_z):
        g = self.g
        z = g.above(k)
        slot = 1 + (k - 1) * 2 + a2 if by_z else g.Z + k - 1
        return self.copy(g.block(z, a2, g.i3), self.rec, slot, 2 * g.Z + slot, g.at_z(z))

    def landed(self, ref, slot):
        return ref[pl.ds(self.unit, self.n), slot].astype(jnp.float32)

    def own(self, block):
        return self.part[pl.ds(self.first, self.n), block].astype(jnp.float32)

    def put(self, block, total):
        self.part[pl.ds(self.first, self.n), block] = total.astype(self.kind)

    def start(self, z):
        for a2 in (0, 1):
            self.p3_copy(z, a2).start()

    def start_all(self):
        g = self.g
        for k in range(1, g.Z + 1):
            self.start(g.above(k))

    def add3(self, z, a2):
        g = self.g
        self.p3_copy(z, a2).wait_recv()
        block = g.block(z, a2, g.i3)
        self.put(block, self.own(block) + self.landed(self.rec3, z * 2 + a2))

    def stage3(self, *ks):
        g = self.g
        for k in ks:
            z = g.above(k)
            o2 = 1 - g.i2
            self.add3(z, o2)
            if k > 0:
                when(self.by_z, lambda: self.z_copy(k, o2, True).start())
            unless(self.by_z, lambda: self.p2_copy(z).start())
            self.add3(z, g.i2)
            if k > 0:
                when(self.by_z, lambda: self.z_copy(k, g.i2, True).start())

    def stage2(self):
        g = self.g

        def with_p2():
            for k in range(1, g.Z):
                z = g.above(k)
                self.p2_copy(z).wait_recv()
                block = g.block(z, g.i2, g.i3)
                self.put(block, self.own(block) + self.landed(self.rec, z))
                self.z_copy(k, g.i2, False).start()

        def along_z():
            o2 = 1 - g.i2
            block = g.block(g.z, o2, g.i3)
            total = self.own(block)
            for k in range(1, g.Z):
                self.z_copy(k, o2, True).wait_recv()
                total += self.landed(self.rec, 1 + (k - 1) * 2 + o2)
            self.put(block, total)
            self.p2_copy(g.z).start()

        when(self.by_z, along_z)
        unless(self.by_z, with_p2)

    def last(self):
        g = self.g

        def finish(by_z):
            total = self.own(g.block(g.z, g.i2, g.i3))
            for k in range(1, g.Z):
                self.z_copy(k, g.i2, by_z).wait_recv()
                slot = 1 + (k - 1) * 2 + g.i2 if by_z else g.Z + k - 1
                total += self.landed(self.rec, slot)
            self.p2_copy(g.z).wait_recv()
            total += self.landed(self.rec, 0 if by_z else g.z)
            self.write(total)

        when(self.by_z, lambda: finish(True))
        unless(self.by_z, lambda: finish(False))

    def sent(self):
        g = self.g
        for z in range(g.Z):
            for a2 in (0, 1):
                self.p3_copy(z, a2).wait_send()

        def by_z():
            self.p2_copy(g.z).wait_send()
            for k in range(1, g.Z):
                for a2 in (0, 1):
                    self.z_copy(k, a2, True).wait_send()

        def by_p2():
            for z in range(g.Z):
                self.p2_copy(z).wait_send()
            for k in range(1, g.Z):
                self.z_copy(k, g.i2, False).wait_send()

        when(self.by_z, by_z)
        unless(self.by_z, by_p2)


def loop(count):
    def run(body):
        def step(i, carry):
            body(i)
            return carry

        lax.fori_loop(0, count, step, 0)

    return run


def run_at(t, events):
    for i, event in events.items():
        pl.when(t == i)(event)


def dot(a, b):
    return jnp.dot(a, b, preferred_element_type=jnp.float32)


def dot_nt(a, b):
    return lax.dot_general(a, b, (((1,), (1,)), ((), ())), preferred_element_type=jnp.float32)


def normed(v):
    center = v - jnp.mean(v, axis=-1, keepdims=True)
    r = lax.rsqrt(jnp.mean(center * center, axis=-1, keepdims=True) + epsilon)
    return center * r, r


def norm_pull(v, gain, e):
    z, r = normed(v)
    f = e * gain
    dv = r * (
        f
        - jnp.mean(f, axis=-1, keepdims=True)
        - z * jnp.mean(f * z, axis=-1, keepdims=True)
    )
    return dv, e * z


def turn(u, cosine, sine, half):
    lane = lax.broadcasted_iota(jnp.int32, u.shape, 1)
    swapped = jnp.where(
        lax.rem(lane, 2 * half) < half,
        pltpu.roll(u, u.shape[1] - half, 1),
        pltpu.roll(u, half, 1),
    )
    return u * cosine + swapped * sine


def turn_tables(row_len, head_dim):
    half = head_dim // 2
    inverse = 10000.0 ** (-2.0 * np.arange(half) / head_dim)
    angles = np.arange(row_len)[:, None] * inverse[None, :]
    cosine = np.tile(np.cos(angles), (1, 4))
    sine = np.tile(np.concatenate([-np.sin(angles), np.sin(angles)], axis=1), (1, 2))
    return cosine.astype(np.float32), sine.astype(np.float32)


def doc_ends(lens):
    ends = [lens[0, 0]]
    for d in range(1, DOCS):
        ends.append(ends[-1] + lens[0, d])
    return ends


def fill_bias(bias, lens, first, rows):
    ends = doc_ends(lens)
    block = 128
    blocks = bias.shape[1] // block

    @loop(bias.shape[0] * blocks)
    def _(i):
        shape = (block, rows)
        place = first + lax.broadcasted_iota(jnp.int32, shape, 1)
        key = i * block + lax.broadcasted_iota(jnp.int32, shape, 0)
        start = jnp.zeros(shape, jnp.int32)
        for d in range(DOCS):
            start = jnp.where(place >= ends[d], ends[d], start)
        fine = (key >= start) & (key <= place)
        spot = pl.ds(lax.rem(i, blocks) * block, block)
        bias[lax.div(i, blocks), spot, :] = jnp.where(fine, 0.0, masked_score)


def split_heads(v, axis=1):
    spot = lax.broadcasted_iota(jnp.int32, v.shape, axis)
    first = spot < v.shape[axis] // 2
    zero = jnp.zeros_like(v)
    return jnp.where(first, v, zero), jnp.where(first, zero, v)


class Tiles:
    def __init__(self, source, buffer, sems, ready=None):
        self.source, self.buffer, self.sems, self.ready = source, buffer, sems, ready
        self.depth = buffer.shape[0]

    def copy(self, t):
        slot = lax.rem(t, self.depth)
        return pltpu.make_async_copy(self.source(t), self.buffer.at[slot], self.sems.at[slot])

    def start(self, t):
        if self.ready is not None:
            self.ready(t)
        self.copy(t).start()

    def first(self, end, begin=0):
        for t in range(begin, min(begin + self.depth - 1, end)):
            self.start(jnp.int32(t))

    def get(self, t, end):
        later = t + self.depth - 1

        @pl.when(later < end)
        def _():
            self.start(later)

        self.copy(t).wait()
        return self.buffer[lax.rem(t, self.depth)]


def columns(t, size):
    return pl.ds(pl.multiple_of(t * size, size), size)


def forward_kernel(dp_size, head_dim, *refs):
    (tok, lens, gs, wq, wo, wu, wd, cosine, sine) = refs[:9]
    (out, wq_f, wo_f, wu_f, wd_f, gain_o, q_o, k_o, v_o, ob_o, lse_o) = refs[9:20]
    (araw_o, h_o, mraw_o, bt_o, gt_o, gp_o, at_o, atx_o) = refs[20:28]
    (g_full, gain, tokx, a, ax, at, atx, q, k, v, vt, bias, ob, lse) = refs[28:42]
    (araw, h, mraw, b, bt, act, actt, gp, wbuf, dbuf) = refs[42:52]
    sems = refs[52:62]
    wsem, dsem, xsem, osem = refs[62:66]
    g = Place(dp_size)
    y = g.y
    rows, width = tok.shape
    half = head_dim // 2
    pairs = width // 128
    scale = head_dim ** (-0.5)
    on_core = g.c == 0
    gg, gq, go, gu, gd = [
        Gather(g, s, f, sems[2 * i], sems[2 * i + 1], mode)
        for i, (s, f, mode) in enumerate(
            (
                (gs, g_full, False),
                (wq, wq_f, MODES[0] and on_core),
                (wo, wo_f, MODES[1] and on_core),
                (wu, wu_f, MODES[2] and on_core),
                (wd, wd_f, MODES[3] and on_core),
            )
        )
    ]
    Z = g.Z
    saves = []

    def save(src, dst):
        copy = pltpu.make_async_copy(src, dst, osem.at[len(saves)])
        copy.start()
        saves.append(copy)

    tok_copy = pltpu.make_async_remote_copy(
        src_ref=tok,
        dst_ref=tokx,
        send_sem=xsem.at[0],
        recv_sem=xsem.at[1],
        device_id=g.device(g.z, g.x, g.c, 1 - y),
        device_id_type=MESH,
    )
    g.barrier()
    gg.start()
    gq.start()
    go.start()
    gu.start()
    fill_bias(bias, lens, y * rows, rows)
    gg.first_p2()
    gg.all_z()
    gg.all_p2()
    gg.all_p3()
    gq.first_p2()
    gq.all_z()
    gg.complete()
    turned = jnp.transpose(g_full[...].astype(jnp.float32))
    gain[...] = turned[:8]
    save(gain, gain_o)

    def first_norm(src, dst, dst_t):
        @loop(rows // 128)
        def _(i):
            spot = pl.ds(i * 128, 128)
            z, _r = normed(src[spot, :].astype(jnp.float32))
            value = z * gain[0:1, :]
            dst[spot, :] = value.astype(jnp.bfloat16)
            dst_t[:, spot] = jnp.transpose(value).astype(jnp.bfloat16)

    gq.all_p2()

    @pl.when(y == 0)
    def _():
        tok_copy.start()

    gd.start()
    first_norm(tok, a, at)
    save(at, at_o)
    go.first_p2()
    go.all_z()
    gq.all_p3()
    go.all_p2()
    gq.complete()

    tiles = Tiles(lambda t: wq_f.at[:, columns(t, 512)], wbuf, wsem)
    per = width // 512
    first = pl.multiple_of(y * rows, rows)

    def turned_pair(u, start):
        return turn(u, cosine[pl.ds(start, rows), :], sine[pl.ds(start, rows), :], half)

    tiles.first(3 * per)

    @loop(per)
    def _(t):
        u = dot(a[...], tiles.get(t, 3 * per))
        for j in range(4):
            part = turned_pair(u[:, j * 128 : j * 128 + 128], first) * scale
            q[4 * t + j] = part.astype(jnp.bfloat16)

    gu.first_p2()
    go.all_p3()

    def keys(w, t, src, start):
        u = dot(src[...], w)
        for j in range(4):
            part = turned_pair(u[:, j * 128 : j * 128 + 128], start)
            k[4 * t + j, pl.ds(start, rows), :] = part.astype(jnp.bfloat16)

    def values(w, t, src, start):
        u = dot(src[...], w)
        ut = jnp.transpose(u).astype(jnp.bfloat16)
        for j in range(4):
            cols = slice(j * 128, j * 128 + 128)
            v[4 * t + j, pl.ds(start, rows), :] = u[:, cols].astype(jnp.bfloat16)
            vt[4 * t + j, :, pl.ds(start, rows)] = ut[cols]

    @loop(per)
    def _(t):
        keys(tiles.get(t + per, 3 * per), t, a, first)

    @loop(per)
    def _(t):
        values(tiles.get(t + 2 * per, 3 * per), t, a, first)

    gu.all_z()
    gd.first_p2()

    @pl.when(y == 1)
    def _():
        tok_copy.wait_recv()
        first_norm(tokx, ax, atx)
        tiles.first(3 * per, per)

        @loop(per)
        def _(t):
            keys(tiles.get(t + per, 3 * per), t, ax, 0)

        @loop(per)
        def _(t):
            values(tiles.get(t + 2 * per, 3 * per), t, ax, 0)

    save(atx, atx_o)
    save(q, q_o)
    save(k, k_o)
    save(v, v_o)

    def attend(p, block, count):
        spot = slice(block * 256, block * 256 + 256)
        heads = split_heads(q[p, spot, :])
        kk = k[p, :count, :]
        vv = vt[p, :, :count]
        parts = []
        for i in (0, 1):
            s = dot_nt(kk, heads[i]) + bias[0, :count, spot]
            m = jnp.max(s, axis=0, keepdims=True)
            e = jnp.exp(s - m)
            total = jnp.sum(e, axis=0, keepdims=True)
            lse[p, i : i + 1, spot] = m + jnp.log(total)
            parts.append(dot(vv, e.astype(jnp.bfloat16)) * (1.0 / total))
        upper = lax.broadcasted_iota(jnp.int32, parts[0].shape, 0) < head_dim
        ob[p, :, spot] = jnp.where(upper, parts[0], parts[1]).astype(jnp.bfloat16)

    events = {
        0: lambda: gu.all_p2(),
        2: lambda: gd.all_z(),
        4: lambda: gu.all_p3(),
        6: lambda: gd.all_p2(),
    }
    blocks = rows // 256

    @loop(pairs)
    def _(p):
        for half_row in (0, 1):

            @pl.when(y == half_row)
            def _():
                for block in range(blocks):
                    attend(p, block, (half_row * blocks + block + 1) * 256)

        run_at(p, events)

    save(ob, ob_o)
    save(lse, lse_o)

    go.complete()
    tiles = Tiles(lambda t: wo_f.at[:, columns(t, 512)], wbuf, wsem)
    tiles.first(per)
    a[...] = jnp.transpose(ob[...].reshape(width, rows))

    @loop(per)
    def _(t):
        w = tiles.get(t, per)
        araw[:, columns(t, 512)] = dot(a[...], w)

    save(araw, araw_o)

    @loop(rows // 128)
    def _(i):
        spot = pl.ds(i * 128, 128)
        z, _r = normed(araw[spot, :])
        hidden = tok[spot, :].astype(jnp.float32) + z * gain[1:2, :]
        h[spot, :] = hidden
        z, _r = normed(hidden)
        value = z * gain[2:3, :]
        b[spot, :] = value.astype(jnp.bfloat16)
        bt[:, spot] = jnp.transpose(value).astype(jnp.bfloat16)

    save(h, h_o)
    save(bt, bt_o)

    gu.complete()
    tiles = Tiles(lambda t: wu_f.at[:, columns(t, 512)], wbuf, wsem)
    ups = act.shape[0]
    tiles.first(ups)
    c0 = math.sqrt(2.0 / math.pi)

    @loop(ups)
    def _(t):
        u = dot(b[...], tiles.get(t, ups))
        square = u * u
        th = jnp.tanh(c0 * (u + 0.044715 * (square * u)))
        value = 0.5 * u * (1.0 + th)
        slope = 0.5 * (1.0 + th) + (0.5 * c0) * u * (1.0 - th * th) * (
            1.0 + (3 * 0.044715) * square
        )
        act[t] = value.astype(jnp.bfloat16)
        actt[t] = jnp.transpose(value).astype(jnp.bfloat16).reshape(2, 256, rows)
        gp[t] = slope.astype(jnp.bfloat16)

    save(actt, gt_o)
    save(gp, gp_o)

    gd.all_p3()
    gd.complete()
    tiles = Tiles(lambda t: wd_f.at[columns(t, 512), :], dbuf, dsem)
    tiles.first(ups)
    mraw[...] = jnp.zeros_like(mraw)

    @loop(ups)
    def _(t):
        mraw[...] += dot(act[t], tiles.get(t, ups))

    save(mraw, mraw_o)
    ends = doc_ends(lens)

    @loop(rows // 128)
    def _(i):
        spot = pl.ds(i * 128, 128)
        z, _r = normed(mraw[spot, :])
        result = h[spot, :] + z * gain[3:4, :]
        place = y * rows + i * 128 + lax.broadcasted_iota(jnp.int32, result.shape, 0)
        result = jnp.where(place < ends[DOCS - 2], result, 0.0)
        out[spot, :] = result.astype(jnp.bfloat16)

    for copy in saves:
        copy.wait()

    @pl.when(y == 0)
    def _():
        tok_copy.wait_send()

    for m in (gg, gq, go, gu, gd):
        m.sent()


def forward(tokens, lengths, gains_wide, w_qkv, w_out, w_up, w_down, tables):
    dp_size = lax.axis_size("dp")
    devices = dp_size * lax.axis_size("ctx")
    rows, width = tokens.shape
    row_len = rows * lax.axis_size("ctx")
    head_dim = width // HEADS
    pairs = width // 128
    ups = w_up.shape[1] // 512
    bf, f32 = jnp.bfloat16, jnp.float32
    any_spec = pl.BlockSpec(memory_space=pl.ANY)
    vm = pl.BlockSpec(memory_space=pltpu.VMEM)
    shape = jax.ShapeDtypeStruct

    def whole(w):
        return shape((w.shape[0] * devices, w.shape[1]), bf)

    outs = [
        shape((rows, width), bf),
        whole(w_qkv),
        whole(w_out),
        whole(w_up),
        whole(w_down),
        shape((8, width), f32),
        shape((pairs, rows, 128), bf),
        shape((pairs, row_len, 128), bf),
        shape((pairs, row_len, 128), bf),
        shape((pairs, 128, rows), bf),
        shape((pairs, 2, rows), f32),
        shape((rows, width), f32),
        shape((rows, width), f32),
        shape((rows, width), f32),
        shape((width, rows), bf),
        shape((ups, 2, 256, rows), bf),
        shape((ups, rows, 512), bf),
        shape((width, rows), bf),
        shape((width, rows), bf),
    ]
    scratch = [
        pltpu.VMEM((width, 128), bf),
        pltpu.VMEM((8, width), f32),
        pltpu.VMEM((rows, width), bf),
        pltpu.VMEM((rows, width), bf),
        pltpu.VMEM((rows, width), bf),
        pltpu.VMEM((width, rows), bf),
        pltpu.VMEM((width, rows), bf),
        pltpu.VMEM((pairs, rows, 128), bf),
        pltpu.VMEM((pairs, row_len, 128), bf),
        pltpu.VMEM((pairs, row_len, 128), bf),
        pltpu.VMEM((pairs, 128, row_len), bf),
        pltpu.VMEM((1, row_len, rows), f32),
        pltpu.VMEM((pairs, 128, rows), bf),
        pltpu.VMEM((pairs, 2, rows), f32),
        pltpu.VMEM((rows, width), f32),
        pltpu.VMEM((rows, width), f32),
        pltpu.VMEM((rows, width), f32),
        pltpu.VMEM((rows, width), bf),
        pltpu.VMEM((width, rows), bf),
        pltpu.VMEM((ups, rows, 512), bf),
        pltpu.VMEM((ups, 2, 256, rows), bf),
        pltpu.VMEM((ups, rows, 512), bf),
        pltpu.VMEM((3, width, 512), bf),
        pltpu.VMEM((3, 512, width), bf),
    ]
    scratch += [pltpu.SemaphoreType.DMA((Gather.sems(dp_size // 4),))] * 10
    scratch += [pltpu.SemaphoreType.DMA((3,))] * 3 + [pltpu.SemaphoreType.DMA((16,))]
    return pl.pallas_call(
        functools.partial(forward_kernel, dp_size, head_dim),
        out_shape=outs,
        in_specs=[vm, pl.BlockSpec(memory_space=pltpu.SMEM), vm]
        + [any_spec] * 4
        + [vm, vm],
        out_specs=[vm] + [any_spec] * (len(outs) - 1),
        scratch_shapes=scratch,
        compiler_params=pltpu.CompilerParams(
            collective_id=0, has_side_effects=True, vmem_limit_bytes=60 * 2**20
        ),
    )(tokens, lengths, gains_wide, w_qkv, w_out, w_up, w_down, *tables)


def backward_kernel(dp_size, head_dim, *refs):
    (tok, dout, lens, gain, cosine, sine, wq, wo, wu, wd) = refs[:10]
    (q_i, k_i, v_i, ob_i, lse_i, araw_i, h_i, mraw_i, bt_i, gt_i, gp_i, at_i, atx_i) = refs[10:23]
    (dtok, out_q, out_o, out_u, out_d, out_g) = refs[23:29]
    (gts, dus, dzs) = refs[29:32]
    (part, rec3, rec, gpart, grec3, grec) = refs[32:38]
    (f1, f2, acc, dm, dms, da, das, dz, bt, bts, obts, ats, atx, atxs) = refs[38:52]
    (q, ob, lse, dk, dv, dg, dgs, dgt, dnxs) = refs[52:61]
    (kbuf, vbuf, wbuf, dbuf, gbuf, gsbuf, gpbuf, sbuf) = refs[61:69]
    tsems = refs[69:79]
    usend, urecv, gsend, grecv, zsend, zrecv, osend, orecv, lsem = refs[79:88]
    dnsem = refs[88]
    gsems, rsems = refs[89:95], refs[95:101]
    at, xbuf, do, dnx = bt, gpbuf, dm, da
    g = Place(dp_size)
    Z, y, c = g.Z, g.y, g.c
    rows, width = tok.shape
    half = head_dim // 2
    pairs = width // 128
    scale = head_dim ** (-0.5)
    ups = gp_i.shape[0]
    per = width // 512
    bf, f32 = jnp.bfloat16, jnp.float32
    first = pl.multiple_of(y * rows, rows)

    def to_sib(src, dst, send, recv):
        return pltpu.make_async_remote_copy(
            src_ref=src,
            dst_ref=dst,
            send_sem=send,
            recv_sem=recv,
            device_id=g.sib,
            device_id_type=MESH,
        )

    def load(src, dst, i):
        return pltpu.make_async_copy(src, dst, lsem.at[i])

    h_load = load(h_i, f2, 0)
    bt_load = load(bt_i.at[:, c], bt, 1)
    atx_load = load(atx_i.at[:, c], atx, 2)
    q_load = load(q_i, q, 3)
    ob_load = load(ob_i, ob, 4)
    lse_load = load(lse_i, lse, 5)
    at_load = load(at_i.at[:, c], at, 6)

    def gt_send(i):
        return to_sib(gt_i.at[i, 1 - c], gts.at[i], gsend.at[i], grecv.at[i])

    bt_send = to_sib(bt_i.at[:, 1 - c], bts, osend.at[0], orecv.at[0])
    ob_send = to_sib(ob_i.at[:, 1 - c], obts, osend.at[1], orecv.at[1])
    at_send = to_sib(at_i.at[:, 1 - c], ats, osend.at[2], orecv.at[2])
    atx_send = to_sib(atx_i.at[:, 1 - c], atxs, osend.at[3], orecv.at[3])
    dm_send = to_sib(dm, dms, osend.at[4], orecv.at[4])
    da_send = to_sib(da, das, osend.at[5], orecv.at[5])
    dg_send = to_sib(dg, dgs, osend.at[6], orecv.at[6])
    dnx_send = pltpu.make_async_remote_copy(
        src_ref=dnx,
        dst_ref=dnxs,
        send_sem=dnsem.at[0],
        recv_sem=dnsem.at[1],
        device_id=g.device(g.z, g.x, c, 1 - y),
        device_id_type=MESH,
    )

    def du_send(t):
        return to_sib(dz.at[t], dus.at[t], usend.at[t], urecv.at[t])

    def dz_send(t):
        return to_sib(dz.at[t], dzs.at[t], zsend.at[t], zrecv.at[t])

    landing = (rec3, rec)

    def write_d(total):
        out_d[...] = total.reshape(out_d.shape)

    def write_into(out, column):
        def write(total):
            for i in range(total.shape[0]):
                out[:, column + i * width : column + (i + 1) * width] = total[i]

        return write

    def write_g(total):
        out_g[...] = total[0]

    on_core = c == 0
    s_d = Share(
        g, part, 0, landing, 0, 4, gsems[0], rsems[0], write_d, MODES[3] and on_core
    )
    s_u = [
        Share(
            g, part, 4 + 2 * i, landing, 4 + 2 * i, 2, gsems[1 + i], rsems[1 + i],
            write_into(out_u, 2 * i * width), MODES[2] and on_core,
        )
        for i in (0, 1)
    ]
    s_o = Share(
        g, part, 8, landing, 8, 1, gsems[3], rsems[3], write_into(out_o, 0),
        MODES[1] and on_core,
    )
    s_q = Share(
        g, part, 0, landing, 9, 3, gsems[4], rsems[4], write_into(out_q, 0),
        MODES[0] and on_core,
    )
    s_g = Share(g, gpart, 0, (grec3, grec), 0, 1, gsems[5], rsems[5], write_g, False)

    mraws = Tiles(lambda i: mraw_i.at[columns(i, 128), :], f1, tsems[9])
    araws = Tiles(lambda i: araw_i.at[columns(i, 128), :], f1, tsems[9])
    mraws.first(rows // 128)
    g.barrier()
    for k in range(1, Z + 1):
        for i in (0, 1):
            gt_send(g.above(k) * 2 + i).start()
    for copy in (bt_send, ob_send, at_send):
        copy.start()

    @pl.when(y == 1)
    def _():
        atx_send.start()

    def gt_ready(j):
        for i in (0, 1):
            gt_send(g.above(j + 1) * 2 + i).wait_recv()

    own_g = Tiles(lambda j: gt_i.at[pl.ds(g.above(j + 1) * 2, 2), c], gbuf, tsems[0])
    sib_g = Tiles(lambda j: gts.at[pl.ds(g.above(j + 1) * 2, 2)], gsbuf, tsems[1], gt_ready)
    own_g.first(Z)
    for copy in (h_load, bt_load, atx_load, q_load, ob_load, lse_load):
        copy.start()
    dg[...] = jnp.zeros_like(dg)
    ends = doc_ends(lens)

    def upstream(i):
        e = dout[pl.ds(i * 128, 128), :].astype(f32)
        place = y * rows + i * 128 + lax.broadcasted_iota(jnp.int32, e.shape, 0)
        return jnp.where(place < ends[DOCS - 2], e, 0.0)

    def gain_sum(index, term):
        dg[index : index + 1, :] += jnp.sum(term, axis=0, keepdims=True)

    @loop(rows // 128)
    def _(i):
        value, term = norm_pull(mraws.get(i, rows // 128), gain[3:4, :], upstream(i))
        dm[pl.ds(i * 128, 128), :] = value.astype(bf)
        gain_sum(3, term)

    dm_send.start()
    downs = Tiles(lambda t: wd.at[columns(t, 512), :], dbuf, tsems[2])
    upw = Tiles(lambda t: wu.at[:, columns(t, 512)], wbuf, tsems[3])
    slopes = Tiles(lambda t: gp_i.at[t], gpbuf, tsems[4])
    for tiles in (downs, upw, slopes):
        tiles.first(ups)
    sib_g.first(Z)
    dm_send.wait_recv()

    @loop(Z)
    def _(j):
        z = g.above(j + 1)
        total = dot(own_g.get(j, Z).reshape(512, rows), dm[...])
        total += dot(sib_g.get(j, Z).reshape(512, rows), dms[...])
        total = total.astype(bf).reshape(4, 4, 32, width)
        for a in range(4):
            for e in range(4):
                part[e, 4 * z + a] = total[a, e]
        s_d.start(z)

    def add_to(halves, value, weights):
        for j in (0, 1):
            halves[j] += dot_nt(value, weights[j * 512 : (j + 1) * 512])

    acc[...] = jnp.zeros_like(acc)

    @loop(ups)
    def _(t):
        du = dot_nt(dm[...], downs.get(t, ups)) * slopes.get(t, ups).astype(f32)
        du = du.astype(bf)
        dz[t] = du
        du_send(t).start()
        add_to(acc, du, upw.get(t, ups))
        run_at(t, {3: lambda: s_d.stage3(1), 7: lambda: s_d.stage3(2)})

    outs = Tiles(lambda t: wo.at[columns(t, 512), :], dbuf, tsems[2])
    outs.first(per)
    bt_load.wait()
    bt_send.wait_recv()
    sib_du = Tiles(lambda t: dus.at[t], sbuf, tsems[5], lambda t: du_send(t).wait_recv())
    sib_du.first(ups)
    for i in (0, 1):

        @loop(ups // 2)
        def _(t2):
            t = t2 + i * (ups // 2)
            total = dot(bt[...].reshape(-1, rows), dz[t])
            total += dot(bts[...].reshape(-1, rows), sib_du.get(t, ups))
            part[4 + lax.div(t, per), :, :, columns(lax.rem(t, per), 512)] = (
                total.astype(bf).reshape(4 * Z, 32, 512)
            )

        s_u[i].start_all()
        s_d.stage3(3 if i == 0 else 0)

    at_load.start()

    araws.first(rows // 128)
    h_load.wait()

    @loop(rows // 128)
    def _(i):
        spot = pl.ds(i * 128, 128)
        e = jnp.concatenate([acc[0, spot, :], acc[1, spot, :]], axis=1)
        value, term = norm_pull(f2[spot, :], gain[2:3, :], e)
        gain_sum(2, term)
        dh = upstream(i) + value
        f2[spot, :] = dh
        value, term = norm_pull(araws.get(i, rows // 128), gain[1:2, :], dh)
        gain_sum(1, term)
        da[spot, :] = value.astype(bf)

    da_send.start()
    dm_send.wait_send()
    s_d.stage2()

    @loop(per)
    def _(t):
        do[:, columns(t, 512)] = dot_nt(da[...], outs.get(t, per)).astype(bf)

    ob_load.wait()
    ob_send.wait_recv()
    da_send.wait_recv()

    @loop(per)
    def _(t):
        total = dot(ob[:, c].reshape(-1, rows), da[:, columns(t, 512)])
        total += dot(obts[...].reshape(-1, rows), das[:, columns(t, 512)])
        part[8, :, :, columns(t, 512)] = total.astype(bf).reshape(4 * Z, 32, 512)

    s_o.start_all()
    for t in range(ups):
        du_send(t).wait_send()

    keys = Tiles(lambda p: k_i.at[p], kbuf, tsems[6])
    values = Tiles(lambda p: v_i.at[p], vbuf, tsems[7])
    keys.first(pairs)
    values.first(pairs)
    fill_bias(acc, lens, y * rows, rows)
    q_load.wait()
    lse_load.wait()
    blocks = rows // 256

    def bias(count, spot):
        if count <= 512:
            return acc[0, :count, spot]
        return jnp.concatenate([acc[0, :, spot], acc[1, : count - 512, spot]], axis=0)

    def attend(p, block, count, fresh, kk, vv, kt):
        spot = slice(block * 256, block * 256 + 256)
        qs = split_heads(q[p, spot, :])
        do_pair = do[spot, columns(p, 128)]
        dos = split_heads(do_pair)
        ob_pair = ob[p, :, :, spot].astype(f32).reshape(128, -1)
        dot_o = jnp.transpose(do_pair.astype(f32)) * ob_pair
        mask = bias(count, spot)
        parts, dk_, dv_ = [], [], []
        for i in (0, 1):
            delta = jnp.sum(
                dot_o[i * head_dim : (i + 1) * head_dim], axis=0, keepdims=True
            )
            s = dot_nt(kk, qs[i]) + mask
            prob = jnp.exp(s - lse[p, i : i + 1, spot])
            ds = (prob * (dot_nt(vv, dos[i]) - delta)).astype(bf)
            dv_.append(dot(prob.astype(bf), dos[i]))
            dk_.append(dot(ds, qs[i]))
            parts.append(dot(kt, ds))
        if fresh:
            dk[:count, :] = dk_[0] + dk_[1]
            dv[:count, :] = dv_[0] + dv_[1]
        else:
            dk[:count, :] += dk_[0] + dk_[1]
            dv[:count, :] += dv_[0] + dv_[1]
        upper = lax.broadcasted_iota(jnp.int32, parts[0].shape, 0) < head_dim
        dq = jnp.transpose(jnp.where(upper, parts[0], parts[1]) * scale)
        start = pl.multiple_of(first + block * 256, 256)
        dq = turn(dq, cosine[pl.ds(start, 256), :], -sine[pl.ds(start, 256), :], half)
        dz[lax.div(p, 4), spot, lanes(p)] = dq.astype(bf)

    def lanes(p):
        return columns(lax.rem(p, 4), 128)

    def keep(p, start, base):
        spot = pl.ds(start, rows)
        u = turn(dk[spot, :], cosine[spot, :], -sine[spot, :], half)
        dz[base + lax.div(p, 4), :, lanes(p)] = u.astype(bf)
        dz[base + per + lax.div(p, 4), :, lanes(p)] = dv[spot, :].astype(bf)

    events = {
        0: lambda: s_u[0].stage3(1, 2),
        1: lambda: s_u[0].stage3(3, 0),
        2: lambda: s_d.last(),
        3: lambda: s_u[0].stage2(),
        4: lambda: s_u[1].stage3(1, 2, 3, 0),
        5: lambda: s_o.stage3(1, 2, 3, 0),
        6: lambda: (s_u[1].stage2(), s_u[0].last())[1],
        7: lambda: s_o.stage2(),
    }

    @loop(pairs)
    def _(p):
        kk = keys.get(p, pairs)
        vv = values.get(p, pairs)
        kt = jnp.transpose(kk.astype(f32)).astype(bf)
        for half_row in (0, 1):

            @pl.when(y == half_row)
            def _():
                for block in reversed(range(blocks)):
                    count = (half_row * blocks + block + 1) * 256
                    attend(p, block, count, block == blocks - 1, kk[:count], vv[:count], kt[:, :count])

        keep(p, first, per)

        @pl.when(y == 1)
        def _():
            keep(p, 0, 3 * per)

        @pl.when(lax.rem(p, 4) == 3)
        def _():
            for e in range(3):
                dz_send(e * per + lax.div(p, 4)).start()

            @pl.when(y == 1)
            def _():
                for e in (3, 4):
                    dz_send(e * per + lax.div(p, 4)).start()

        run_at(p, events)

    qkv_w = Tiles(lambda t: wq.at[:, columns(t, 512)], wbuf, tsems[3])

    @pl.when(y == 1)
    def _():
        qkv_w.first(3 * per, per)
        acc[...] = jnp.zeros_like(acc)
        da_send.wait_send()

        @loop(2 * per)
        def _(t):
            add_to(acc, dz[t + 3 * per], qkv_w.get(t + per, 3 * per))

        dnx[:, :512] = acc[0].astype(bf)
        dnx[:, 512:] = acc[1].astype(bf)
        dnx_send.start()

    qkv_w.first(3 * per)
    s_d.sent()
    atx_load.wait()
    at_load.wait()
    at_send.wait_recv()

    @pl.when(y == 1)
    def _():
        atx_send.wait_recv()

    def dz_ready(t):
        dz_send(t).wait_recv()

    sib_dz = Tiles(lambda t: dzs.at[t], sbuf, tsems[5], dz_ready)
    sib_dx = Tiles(lambda t: dzs.at[t], xbuf, tsems[8], dz_ready)
    sib_dz.first(3 * per)

    @pl.when(y == 1)
    def _():
        sib_dx.first(5 * per, 3 * per)

    @loop(3 * per)
    def _(t):
        acc[0] = dot(at[...].reshape(-1, rows), dz[t]) + dot(
            ats[...].reshape(-1, rows), sib_dz.get(t, 3 * per)
        )

        @pl.when((y == 1) & (t >= per))
        def _():
            tx = t + 2 * per
            acc[0] += dot(atx[...].reshape(-1, rows), dz[tx]) + dot(
                atxs[...].reshape(-1, rows), sib_dx.get(tx, 5 * per)
            )

        part[lax.div(t, per), :, :, columns(lax.rem(t, per), 512)] = (
            acc[0].astype(bf).reshape(4 * Z, 32, 512)
        )

    s_q.start_all()
    s_u[1].last()
    s_o.last()

    acc[...] = jnp.zeros_like(acc)

    @loop(3 * per)
    def _(t):
        add_to(acc, dz[t], qkv_w.get(t, 3 * per))

    @pl.when(y == 0)
    def _():
        dnx_send.wait_recv()
        acc[0] += dnxs[:, :512].astype(f32)
        acc[1] += dnxs[:, 512:].astype(f32)

    @loop(rows // 128)
    def _(i):
        spot = pl.ds(i * 128, 128)
        e = jnp.concatenate([acc[0, spot, :], acc[1, spot, :]], axis=1)
        value, term = norm_pull(tok[spot, :].astype(f32), gain[0:1, :], e)
        gain_sum(0, term)
        dtok[spot, :] = (f2[spot, :] + value).astype(bf)

    dg_send.start()
    s_q.stage3(1)
    dg_send.wait_recv()
    wide = jnp.concatenate([dg[...] + dgs[...], jnp.zeros((120, width), f32)], axis=0)
    dgt[...] = jnp.transpose(wide).reshape(dgt.shape)
    gpart[0] = dgt[:, c].reshape(gpart.shape[1:])
    s_g.start_all()
    s_q.stage3(2, 3, 0)
    s_g.stage3(1, 2, 3, 0)
    s_q.stage2()
    s_g.stage2()
    s_q.last()
    s_g.last()

    for i in range(2 * Z):
        gt_send(i).wait_send()
    for copy in (bt_send, ob_send, at_send, dg_send):
        copy.wait_send()
    for t in range(3 * per):
        dz_send(t).wait_send()

    @pl.when(y == 0)
    def _():
        da_send.wait_send()

    @pl.when(y == 1)
    def _():
        atx_send.wait_send()
        dnx_send.wait_send()
        for t in range(3 * per, 5 * per):
            dz_send(t).wait_send()

    for s in (s_u[0], s_u[1], s_o, s_q, s_g):
        s.sent()


def backward(tokens, d_out, lengths, gain_rows, tables, weights, saved, shards):
    dp_size = lax.axis_size("dp")
    Z = dp_size // 4
    rows, width = tokens.shape
    row_len = rows * lax.axis_size("ctx")
    head_dim = width // HEADS
    pairs = width // 128
    per = width // 512
    bf, f32 = jnp.bfloat16, jnp.float32
    ups = saved[10].shape[0]
    any_spec = pl.BlockSpec(memory_space=pl.ANY)
    vm = pl.BlockSpec(memory_space=pltpu.VMEM)
    smem = pl.BlockSpec(memory_space=pltpu.SMEM)
    shape = jax.ShapeDtypeStruct
    block = 32
    saved = list(saved)
    for i in (3, 8, 11, 12):
        saved[i] = saved[i].reshape(2 * Z, 2, width // (4 * Z), rows)
    outs = [
        shape((rows, width), bf),
        shape(shards[0].shape, f32),
        shape(shards[1].shape, f32),
        shape(shards[2].shape, f32),
        shape(shards[3].shape, f32),
        shape((block, 128), f32),
        shape((2 * Z, 256, rows), bf),
        shape((ups, rows, 512), bf),
        shape((5 * per, rows, 512), bf),
    ]
    core_rows = (2 * Z, width // (4 * Z), rows)
    scratch = [
        pltpu.VMEM((9, 4 * Z, block, width), bf),
        pltpu.VMEM((12, 2 * Z, block, width), bf),
        pltpu.VMEM((12, 2 * Z - 1, block, width), bf),
        pltpu.VMEM((1, 4 * Z, block, 128), f32),
        pltpu.VMEM((1, 2 * Z, block, 128), f32),
        pltpu.VMEM((1, 2 * Z - 1, block, 128), f32),
        pltpu.VMEM((2, 128, width), f32),
        pltpu.VMEM((rows, width), f32),
        pltpu.VMEM((2, rows, 512), f32),
        pltpu.VMEM((rows, width), bf),
        pltpu.VMEM((rows, width), bf),
        pltpu.VMEM((rows, width), bf),
        pltpu.VMEM((rows, width), bf),
        pltpu.VMEM((max(ups, 5 * per), rows, 512), bf),
    ]
    scratch += [pltpu.VMEM(core_rows, bf)] * 6
    scratch += [
        pltpu.VMEM((pairs, rows, 128), bf),
        pltpu.VMEM((2 * Z, 2, width // (4 * Z), rows), bf),
        pltpu.VMEM((pairs, 2, rows), f32),
        pltpu.VMEM((row_len, 128), f32),
        pltpu.VMEM((row_len, 128), f32),
        pltpu.VMEM((8, width), f32),
        pltpu.VMEM((8, width), f32),
        pltpu.VMEM((2 * Z, 2, width // (4 * Z), 128), f32),
        pltpu.VMEM((rows, width), bf),
        pltpu.VMEM((2, row_len, 128), bf),
        pltpu.VMEM((2, row_len, 128), bf),
        pltpu.VMEM((2, width, 512), bf),
        pltpu.VMEM((2, 512, width), bf),
        pltpu.VMEM((2, 2, 256, rows), bf),
        pltpu.VMEM((2, 2, 256, rows), bf),
        pltpu.VMEM((2, rows, 512), bf),
        pltpu.VMEM((2, rows, 512), bf),
    ]
    dma = pltpu.SemaphoreType.DMA
    scratch += [dma((3,))] * 10
    scratch += [dma((ups,))] * 2 + [dma((2 * Z,))] * 2 + [dma((5 * per,))] * 2
    scratch += [dma((7,))] * 2 + [dma((7,)), dma((2,))]
    scratch += [dma((Share.sems(Z),))] * 12
    return pl.pallas_call(
        functools.partial(backward_kernel, dp_size, head_dim),
        out_shape=outs,
        in_specs=[vm, vm, smem, vm, vm, vm] + [any_spec] * 17,
        out_specs=[vm] * 6 + [any_spec] * 3,
        scratch_shapes=scratch,
        compiler_params=pltpu.CompilerParams(
            collective_id=1, has_side_effects=True, vmem_limit_bytes=63 * 2**20
        ),
    )(tokens, d_out, lengths, gain_rows, *tables, *weights, *saved)


def layer_norm(values, gain_vec):
    center = values - jnp.mean(values, axis=-1, keepdims=True)
    spread = jnp.mean(center * center, axis=-1, keepdims=True)
    return center * lax.rsqrt(spread + epsilon) * gain_vec


def norm_back(values, gain_vec, upstream):
    unused, pullback = jax.vjp(layer_norm, values, gain_vec)
    return pullback(upstream)


def rotate(values, cosine_table, sine_table, direction):
    half_dim = values.shape[-1] // 2
    first_half = values[..., :half_dim]
    second_half = values[..., half_dim:]
    return jnp.concatenate(
        [
            first_half * cosine_table - direction * second_half * sine_table,
            second_half * cosine_table + direction * first_half * sine_table,
        ],
        axis=-1,
    )


def doc_layout(lengths, row_len):
    doc_ends = jnp.cumsum(lengths, axis=-1)
    places = jnp.arange(row_len, dtype=jnp.int32)
    passed = places[None, :, None] >= doc_ends[:, None, :]
    segment = jnp.sum(passed.astype(jnp.int32), axis=-1)
    starts = jnp.sum(jnp.where(passed, lengths[:, None, :], 0), axis=-1)
    position = places[None, :] - starts
    is_valid = places[None, :] < doc_ends[:, DOCS - 2][:, None]
    return (segment[0], position[0], is_valid[0])


def allowed_keys(own_seg, own_place, seg_full, first_key, block_rows):
    key_place = first_key + jnp.arange(block_rows, dtype=jnp.int32)
    key_seg = lax.dynamic_slice_in_dim(seg_full, first_key, block_rows)
    return (own_seg[:, None] == key_seg[None, :]) & (key_place[None, :] <= own_place[:, None])


def make_fold(queries, own_seg, own_place, seg_full, score_scale):

    def fold_piece(fold_state, piece, start):
        key_piece, value_piece = piece
        piece_rows = key_piece.shape[0]
        block_rows = math.gcd(piece_rows, 256)
        block_count = piece_rows // block_rows
        key_blocks = key_piece.reshape((block_count, block_rows) + key_piece.shape[1:])
        value_blocks = value_piece.reshape((block_count, block_rows) + value_piece.shape[1:])

        def step_block(carried, block_items):
            row_max, row_sum, weighted = carried
            key_block, value_block, block_id = block_items
            allowed = allowed_keys(own_seg, own_place, seg_full, block_id * block_rows, block_rows)
            scores = (
                jnp.einsum("qhd,khd->hqk", queries, key_block, preferred_element_type=jnp.float32)
                * score_scale
            )
            scores = jnp.where(allowed[None], scores, masked_score)
            new_max = jnp.maximum(row_max, jnp.max(scores, axis=-1))
            factor = jnp.exp(row_max - new_max)
            shifted = jnp.where(allowed[None], jnp.exp(scores - new_max[..., None]), 0.0)
            row_sum = row_sum * factor + jnp.sum(shifted, axis=-1)
            weighted = weighted * factor[..., None] + jnp.einsum(
                "hqk,khd->hqd",
                shifted.astype(jnp.bfloat16),
                value_block,
                preferred_element_type=jnp.float32,
            )
            return ((new_max, row_sum, weighted), None)

        block_ids = jnp.arange(block_count, dtype=jnp.int32)
        fold_state, unused = lax.scan(step_block, fold_state, (key_blocks, value_blocks, block_ids))
        return fold_state

    return fold_piece


def per_device(tokens, lengths, w_qkv, w_out, w_up, w_down, gains, d_out):
    tok_rows, model_width = tokens.shape
    row_len = tok_rows * lax.axis_size("ctx")
    head_count = HEADS
    head_dim = model_width // head_count
    score_scale = head_dim ** (-0.5)
    head_shape = (tok_rows, head_count, head_dim)
    seg_full, pos_full, valid_full = doc_layout(lengths, row_len)
    offset = lax.axis_index("ctx") * tok_rows
    own_seg = lax.dynamic_slice_in_dim(seg_full, offset, tok_rows)
    own_pos = lax.dynamic_slice_in_dim(pos_full, offset, tok_rows)
    own_valid = lax.dynamic_slice_in_dim(valid_full.astype(jnp.float32), offset, tok_rows)
    own_place = offset + jnp.arange(tok_rows, dtype=jnp.int32)
    freq_index = jnp.arange(head_dim // 2, dtype=jnp.float32)
    angles = own_pos.astype(jnp.float32)[:, None] * 10000.0 ** (-2.0 * freq_index / head_dim)
    cosine_table = jnp.cos(angles)[:, None, :]
    sine_table = jnp.sin(angles)[:, None, :]
    qkv_full, out_full, up_full, down_full, gain_full = (
        lax.all_gather(w_qkv, ("dp", "ctx"), axis=0, tiled=True),
        lax.all_gather(w_out, ("dp", "ctx"), axis=0, tiled=True),
        lax.all_gather(w_up, ("dp", "ctx"), axis=0, tiled=True),
        lax.all_gather(w_down, ("dp", "ctx"), axis=0, tiled=True),
        lax.all_gather(gains, ("dp", "ctx"), axis=0, tiled=True),
    )
    gain_f = gain_full.astype(jnp.float32)
    stream = tokens.astype(jnp.float32)
    normed = layer_norm(stream, gain_f[:, 0]).astype(jnp.bfloat16)
    qkv_raw = jnp.dot(normed, qkv_full, preferred_element_type=jnp.float32)
    queries = rotate(
        qkv_raw[:, :model_width].reshape(head_shape), cosine_table, sine_table, 1.0
    ).astype(jnp.bfloat16)
    key_heads = rotate(
        qkv_raw[:, model_width : 2 * model_width].reshape(head_shape), cosine_table, sine_table, 1.0
    ).astype(jnp.bfloat16)
    value_heads = qkv_raw[:, 2 * model_width :].reshape(head_shape).astype(jnp.bfloat16)
    start_state = (
        jnp.full((head_count, tok_rows), masked_score, jnp.float32),
        jnp.zeros((head_count, tok_rows), jnp.float32),
        jnp.zeros((head_count, tok_rows, head_dim), jnp.float32),
    )
    fold_piece = make_fold(queries, own_seg, own_place, seg_full, score_scale)
    row_max, row_sum, weighted = fold_piece(
        start_state,
        (
            lax.all_gather(key_heads, "ctx", axis=0, tiled=True),
            lax.all_gather(value_heads, "ctx", axis=0, tiled=True),
        ),
        jnp.int32(0),
    )
    attended = jnp.transpose(weighted / row_sum[..., None], (1, 0, 2))
    attended_b = attended.reshape(tok_rows, model_width).astype(jnp.bfloat16)
    attn_raw = jnp.dot(attended_b, out_full, preferred_element_type=jnp.float32)
    hidden = stream + layer_norm(attn_raw, gain_f[:, 1])
    mlp_in = layer_norm(hidden, gain_f[:, 2]).astype(jnp.bfloat16)
    up_proj = jnp.dot(mlp_in, up_full, preferred_element_type=jnp.float32)
    activated = jax.nn.gelu(up_proj).astype(jnp.bfloat16)
    mlp_raw = jnp.dot(activated, down_full, preferred_element_type=jnp.float32)
    result = hidden + layer_norm(mlp_raw, gain_f[:, 3])
    output = (result * own_valid[:, None]).astype(jnp.bfloat16)
    qkv_back, out_back, up_back, down_back = (
        lax.all_gather(w_qkv, ("dp", "ctx"), axis=0, tiled=True),
        lax.all_gather(w_out, ("dp", "ctx"), axis=0, tiled=True),
        lax.all_gather(w_up, ("dp", "ctx"), axis=0, tiled=True),
        lax.all_gather(w_down, ("dp", "ctx"), axis=0, tiled=True),
    )
    upstream = d_out.astype(jnp.float32) * own_valid[:, None]
    d_mlp, d_gain_four = norm_back(mlp_raw, gain_f[:, 3], upstream)
    d_mlp_b = d_mlp.astype(jnp.bfloat16)
    grad_down = jnp.einsum("tf,td->fd", activated, d_mlp_b, preferred_element_type=jnp.float32)
    d_activated = jnp.einsum("td,fd->tf", d_mlp_b, down_back, preferred_element_type=jnp.float32)
    unused, gelu_pull = jax.vjp(jax.nn.gelu, up_proj)
    d_up_b = gelu_pull(d_activated)[0].astype(jnp.bfloat16)
    grad_up = jnp.einsum("td,tf->df", mlp_in, d_up_b, preferred_element_type=jnp.float32)
    d_mlp_in = jnp.einsum("tf,df->td", d_up_b, up_back, preferred_element_type=jnp.float32)
    d_hidden_part, d_gain_three = norm_back(hidden, gain_f[:, 2], d_mlp_in)
    d_hidden = upstream + d_hidden_part
    d_attn, d_gain_two = norm_back(attn_raw, gain_f[:, 1], d_hidden)
    d_attn_b = d_attn.astype(jnp.bfloat16)
    grad_out = jnp.einsum("td,te->de", attended_b, d_attn_b, preferred_element_type=jnp.float32)
    d_attended = (
        jnp.einsum("te,de->td", d_attn_b, out_back, preferred_element_type=jnp.float32)
        .astype(jnp.bfloat16)
        .reshape(head_shape)
    )
    row_dot = jnp.einsum("qhd,qhd->hq", d_attended.astype(jnp.float32), attended)
    key_all, value_all = (
        lax.all_gather(key_heads, "ctx", axis=0, tiled=True),
        lax.all_gather(value_heads, "ctx", axis=0, tiled=True),
    )
    block_rows = math.gcd(row_len, 256)
    block_count = row_len // block_rows
    key_blocks = key_all.reshape((block_count, block_rows) + key_all.shape[1:])
    value_blocks = value_all.reshape((block_count, block_rows) + value_all.shape[1:])

    def back_block(d_queries, block_items):
        key_block, value_block, block_id = block_items
        allowed = allowed_keys(own_seg, own_place, seg_full, block_id * block_rows, block_rows)
        scores = (
            jnp.einsum("qhd,khd->hqk", queries, key_block, preferred_element_type=jnp.float32)
            * score_scale
        )
        attn_prob = jnp.where(
            allowed[None], jnp.exp(scores - row_max[..., None]) / row_sum[..., None], 0.0
        )
        d_prob = jnp.einsum(
            "qhd,khd->hqk", d_attended, value_block, preferred_element_type=jnp.float32
        )
        d_scores = (attn_prob * (d_prob - row_dot[..., None])).astype(jnp.bfloat16)
        d_queries = (
            d_queries
            + jnp.einsum("hqk,khd->qhd", d_scores, key_block, preferred_element_type=jnp.float32)
            * score_scale
        )
        d_keys = (
            jnp.einsum("hqk,qhd->khd", d_scores, queries, preferred_element_type=jnp.float32)
            * score_scale
        )
        d_values = jnp.einsum(
            "hqk,qhd->khd",
            attn_prob.astype(jnp.bfloat16),
            d_attended,
            preferred_element_type=jnp.float32,
        )
        return (d_queries, (d_keys, d_values))

    block_ids = jnp.arange(block_count, dtype=jnp.int32)
    d_queries, (d_keys_all, d_values_all) = lax.scan(
        back_block, jnp.zeros(head_shape, jnp.float32), (key_blocks, value_blocks, block_ids)
    )
    kv_terms = jnp.concatenate(
        [d_keys_all.reshape(row_len, model_width), d_values_all.reshape(row_len, model_width)],
        axis=-1,
    )
    kv_grad = lax.psum_scatter(
        kv_terms.astype(jnp.bfloat16), "ctx", scatter_dimension=0, tiled=True
    ).astype(jnp.float32)
    d_keys = kv_grad[:, :model_width].reshape(head_shape)
    d_qkv = jnp.concatenate(
        [
            rotate(d_queries, cosine_table, sine_table, -1.0).reshape(tok_rows, model_width),
            rotate(d_keys, cosine_table, sine_table, -1.0).reshape(tok_rows, model_width),
            kv_grad[:, model_width:],
        ],
        axis=-1,
    ).astype(jnp.bfloat16)
    grad_qkv = jnp.einsum("td,te->de", normed, d_qkv, preferred_element_type=jnp.float32)
    d_normed = jnp.einsum("te,de->td", d_qkv, qkv_back, preferred_element_type=jnp.float32)
    d_stream_part, d_gain_one = norm_back(stream, gain_f[:, 0], d_normed)
    d_tokens = (d_hidden + d_stream_part).astype(jnp.bfloat16)
    grad_gains = jnp.stack([d_gain_one, d_gain_two, d_gain_three, d_gain_four], axis=-1)
    shard_qkv, shard_out, shard_up, shard_down, shard_gains = (
        lax.psum_scatter(grad_qkv, ("dp", "ctx"), scatter_dimension=0, tiled=True),
        lax.psum_scatter(grad_out, ("dp", "ctx"), scatter_dimension=0, tiled=True),
        lax.psum_scatter(grad_up, ("dp", "ctx"), scatter_dimension=0, tiled=True),
        lax.psum_scatter(grad_down, ("dp", "ctx"), scatter_dimension=0, tiled=True),
        lax.psum_scatter(grad_gains, ("dp", "ctx"), scatter_dimension=0, tiled=True),
    )
    return (output, d_tokens, shard_qkv, shard_out, shard_up, shard_down, shard_gains)


def fused_device(tokens, lengths, w_qkv, w_out, w_up, w_down, gains, d_out):
    rows, width = tokens.shape
    row_len = rows * lax.axis_size("ctx")
    gains_wide = jnp.pad(gains, ((0, 0), (0, 128 - gains.shape[1])))
    tables = tuple(jnp.asarray(v) for v in turn_tables(row_len, width // HEADS))
    output, wq, wo, wu, wd, gain_rows, *saved = forward(
        tokens, lengths, gains_wide, w_qkv, w_out, w_up, w_down, tables
    )
    d_tokens, grad_qkv, grad_out, grad_up, grad_down, grad_gains = backward(
        tokens,
        d_out,
        lengths,
        gain_rows,
        tables,
        (wq, wo, wu, wd),
        saved,
        (w_qkv, w_out, w_up, w_down),
    )[:6]
    return (
        output,
        d_tokens,
        grad_qkv,
        grad_out,
        grad_up,
        grad_down,
        grad_gains[:, : gains.shape[1]],
    )


def layer(mesh):
    if mesh.shape["dp"] == 16 and mesh.shape["ctx"] == 2:
        return fused_device
    return per_device


def solution(mesh):
    return jax.shard_map(
        layer(mesh),
        mesh=mesh,
        in_specs=(
            P(("dp", "ctx"), None),
            P("dp", None),
            P(("dp", "ctx"), None),
            P(("dp", "ctx"), None),
            P(("dp", "ctx"), None),
            P(("dp", "ctx"), None),
            P(("dp", "ctx"), None),
            P(("dp", "ctx"), None),
        ),
        out_specs=(
            P(("dp", "ctx"), None),
            P(("dp", "ctx"), None),
            P(("dp", "ctx"), None),
            P(("dp", "ctx"), None),
            P(("dp", "ctx"), None),
            P(("dp", "ctx"), None),
            P(("dp", "ctx"), None),
        ),
        check_vma=False,
    )
```

```python
import functools
import math

import jax
import jax.numpy as jnp
import numpy as np
from jax import lax
from jax.experimental import pallas as pl
from jax.experimental.pallas import tpu as pltpu
from jax.sharding import PartitionSpec as P

HEADS = 16
DOCS = 7

GATHER_BY_Z = (False, None, None, True)
SHARE_BY_Z = (None, True, False, None)

GATHER_PLAN = {
    "start": ("gsz", "gsp2", "gsp3", "gssib", "qsz", "qsp3",),
    "norm": ("gF", "gZ0", "ussib", "dsp2", "qsp2", "gZ1", "usp2", "osp3", "qF", "osz", "osp2", "qZ0", "qZ1", "gZ2", "usp3", "gP0", "oF", "dssib", "qZ2", "gT0", "usz", "qP0", "qP2", "uF", "qT0", "qT1", "gP2", "qP1", "gP1", "qT3", "oZ2", "gT1", "oZ0", "qssib", "ossib", "uT0", "oP0", "gT3", "token", "gT2", "oZ1", "qT2",),
    "qkv": ("uZ2", "uZ0",),
    ("k", 1): ("oP2", "oP1",),
    ("v", 0): ("dF",),
    ("v", 1): ("oT1",),
    ("pair", 5): ("dsz",),
    ("pair", 6): ("uP0",),
    "other": ("oT0",),
    ("more", 0): ("uZ1", "uP2", "oT3",),
    ("more", 1): ("uP1", "oT2",),
    ("more", 3): ("dsp3",),
    ("more", 4): ("uT1",),
    ("more", 5): ("dP1",),
    ("more", 6): ("dZ0",),
    "out": ("uT2", "dP0", "dZ2",),
    "up": ("uT3",),
    ("up", 0): ("dZ1",),
    ("up", 1): ("dP2",),
    ("up", 2): ("dT1",),
    ("up", 4): ("dT0",),
    ("up", 6): ("dT2",),
    ("up", 7): ("dT3",),
}

NEAR = ((1, 2, 3), (0, 2, 3), (1, 3, 0), (2, 1, 0))
FAR = ((3, 2, 1), (3, 0, 2), (0, 1, 3), (0, 1, 2))

SHARE_PLAN = {
    ("du", 6): ("d31",),
    ("up", 4): ("d30",),
    ("up", 6): ("d21",),
    "out": ("d32",),
    ("more", 1): ("d20",),
    ("more", 2): ("v30",),
    ("more", 6): ("u31", "v20", "v31", "u32", "v32", "u30", "u21",),
    ("more", 7): ("d22",),
    "other": ("o30",),
    ("pair", 1): ("o32",),
    ("pair", 2): ("v22",),
    ("pair", 3): ("v21", "u22",),
    "half": ("u20",),
    ("pair", 6): ("o31",),
    "input": ("a30",),
    "gains": ("a32", "a31", "a20", "o21", "a33", "b31",),
    "end": ("a22", "a21", "b32", "b22", "b30", "d33", "o33", "b21", "b20", "o22", "dE", "g31", "u33", "o20", "oE", "aE", "b33", "g30", "g32", "g33", "g21", "dL", "uE", "v33", "oL", "aL", "bE", "g20", "g22", "uL", "vE", "bL", "gE", "vL", "gL",),
}

epsilon = 1e-05
masked_score = -1e30


MESH = pl.DeviceIdType.MESH


def when(condition, body):
    if isinstance(condition, bool):
        if condition:
            body()
    else:
        pl.when(condition)(body)


def unless(condition, body):
    if isinstance(condition, bool):
        if not condition:
            body()
    else:
        pl.when(jnp.logical_not(condition))(body)


def pick(condition, one, other):
    if isinstance(condition, bool):
        return one if condition else other
    return jnp.where(condition, one, other)


class Place:
    def __init__(self, dp_size):
        dp = lax.axis_index("dp")
        self.Z = dp_size // 4
        self.z = lax.div(dp, 4)
        self.x = lax.rem(lax.div(dp, 2), 2)
        self.c = lax.rem(dp, 2)
        self.y = lax.axis_index("ctx")
        c, x, y = self.c, self.x, self.y
        self.i2 = y * (1 - c) + x * c
        self.i3 = x * (1 - c) + y * c
        self.sib = self.device(self.z, x, 1 - c, y)
        self.p2 = self.device(self.z, x * (1 - c) + (1 - x) * c, c, (1 - y) * (1 - c) + y * c)
        self.p3 = self.device(self.z, (1 - x) * (1 - c) + x * c, c, y * (1 - c) + (1 - y) * c)

    def device(self, z, x, c, y):
        return ((z * 2 + x) * 2 + c, y)

    def above(self, k):
        return lax.rem(self.z + k, self.Z)

    def below(self, k):
        return lax.rem(self.z - k + self.Z, self.Z)

    def at_z(self, z):
        return self.device(z, self.x, self.c, self.y)

    def near(self, j):
        if self.Z != 4:
            return self.below(j + 1)
        return sum(jnp.where(self.z == z, row[j], 0) for z, row in enumerate(NEAR))

    def order(self, j):
        if j == self.Z - 1:
            return self.z
        if self.Z != 4:
            return self.above(j + 1)
        return sum(jnp.where(self.z == z, row[j], 0) for z, row in enumerate(FAR))

    def far(self, z):
        return jnp.abs(z - self.z) == self.Z - 1

    def between(self, z):
        last = self.Z - 1
        return ((z == 0) & (self.z == last - 1)) | ((z == last) & (self.z == 1))

    def block(self, z, a2, a3):
        c = self.c
        return (z * 2 + a3 * (1 - c) + a2 * c) * 2 + a2 * (1 - c) + a3 * c

    def row_block(self, z, a2, a3, core):
        c = self.c
        xx = a3 * (1 - c) + a2 * c
        yy = a2 * (1 - c) + a3 * c
        return ((z * 2 + xx) * 2 + core) * 2 + yy

    def barrier(self):
        bar = pltpu.get_barrier_semaphore()
        for device in (self.sib, self.p2, self.p3):
            pl.semaphore_signal(bar, 1, device_id=device, device_id_type=MESH)
        for k in range(1, self.Z):
            pl.semaphore_signal(
                bar, 1, device_id=self.at_z(self.above(k)), device_id_type=MESH
            )
        pl.semaphore_wait(bar, 3 + self.Z - 1)


class Gather:
    def __init__(self, place, shard, full, send, recv, by_z):
        self.g, self.shard, self.full = place, shard, full
        self.send, self.recv = send, recv
        self.rows = shard.shape[0]
        self.by_z = by_z
        Z = place.Z
        self.n_z = 0
        self.n_pass = 2 * Z
        self.n_p2 = 2 * Z + 2
        self.n_p3 = self.n_p2 + Z
        self.n_sib = self.n_p3 + 2 * Z
        self.n_own = self.n_sib + 4 * Z

    @staticmethod
    def sems(Z):
        return 9 * Z + 3

    def at(self, index):
        return self.full.at[pl.ds(pl.multiple_of(index * self.rows, self.rows), self.rows)]

    def copy(self, index, send, recv, device, src=None):
        return pltpu.make_async_remote_copy(
            src_ref=self.at(index) if src is None else src,
            dst_ref=self.at(index),
            send_sem=self.send.at[send],
            recv_sem=self.recv.at[recv],
            device_id=device,
            device_id_type=MESH,
        )

    def own_copy(self):
        g = self.g
        index = g.row_block(g.z, g.i2, g.i3, g.c)
        return pltpu.make_async_copy(self.shard, self.at(index), self.recv.at[self.n_own])

    def z_copy(self, other, z, src=None):
        g = self.g
        a2 = (1 - g.i2) if other else g.i2
        return self.copy(
            g.row_block(g.z, a2, g.i3, g.c),
            self.n_z + z * 2 + int(other),
            self.n_z + g.z * 2 + int(other),
            g.at_z(z),
            src,
        )

    def pass_copy(self, other, z):
        g = self.g
        a2 = (1 - g.i2) if other else g.i2
        return self.copy(
            g.row_block(z, a2, g.i3, g.c),
            self.n_pass + int(other),
            self.n_z + z * 2 + int(other),
            g.at_z(g.Z - 1 - z),
        )

    def p2_copy(self, z, src=None):
        g = self.g
        number = self.n_p2 + z
        return self.copy(g.row_block(z, g.i2, g.i3, g.c), number, number, g.p2, src)

    def p3_copy(self, z, a2, src=None):
        g = self.g
        number = self.n_p3 + z * 2 + a2
        return self.copy(g.row_block(z, a2, g.i3, g.c), number, number, g.p3, src)

    def sib_copy(self, z, a2, a3, src=None):
        g = self.g
        number = self.n_sib + g.block(z, a2, a3)
        return self.copy(g.row_block(z, a2, a3, g.c), number, number, g.sib, src)

    def wait(self, number, index):
        self.copy(index, number, number, self.g.sib).wait_recv()

    def each_z(self, act):
        g = self.g
        for k in range(1, g.Z):
            z = g.above(k)
            unless(g.far(z), lambda: act(z))

    def start_z(self):
        self.each_z(lambda z: self.z_copy(False, z, self.shard).start())

    def start_p2(self):
        self.p2_copy(self.g.z, self.shard).start()

    def start_p3(self):
        self.p3_copy(self.g.z, self.g.i2, self.shard).start()

    def start_sib(self):
        self.sib_copy(self.g.z, self.g.i2, self.g.i3, self.shard).start()
        self.own_copy().start()

    def first(self):
        g = self.g
        o2 = 1 - g.i2
        self.wait(self.n_p2 + g.z, g.row_block(g.z, o2, g.i3, g.c))
        when(self.by_z, lambda: self.each_z(lambda z: self.z_copy(True, z).start()))
        self.p3_copy(g.z, o2).start()
        self.sib_copy(g.z, o2, g.i3).start()

    def relay(self, j, z, other):
        if j == self.g.Z - 2:
            pl.when(self.g.between(z))(lambda: self.pass_copy(other, z).start())

    def from_z(self, j):
        g = self.g
        z = g.near(j)
        self.wait(self.n_z + z * 2, g.row_block(z, g.i2, g.i3, g.c))
        self.relay(j, z, False)
        unless(self.by_z, lambda: self.p2_copy(z).start())
        self.p3_copy(z, g.i2).start()
        self.sib_copy(z, g.i2, g.i3).start()

    def from_p2(self, j):
        g = self.g
        z = g.near(j)
        o2 = 1 - g.i2
        number = pick(self.by_z, self.n_z + z * 2 + 1, self.n_p2 + z)
        self.wait(number, g.row_block(z, o2, g.i3, g.c))
        when(self.by_z, lambda: self.relay(j, z, True))
        self.p3_copy(z, o2).start()
        self.sib_copy(z, o2, g.i3).start()

    def from_p3(self, j):
        g = self.g
        z = g.near(j - 1) if j else g.z
        for a2 in (0, 1):
            self.wait(self.n_p3 + z * 2 + a2, g.row_block(z, a2, 1 - g.i3, g.c))
            self.sib_copy(z, a2, 1 - g.i3).start()

    def complete(self):
        g = self.g
        for z in range(g.Z):
            for xx in (0, 1):
                for yy in (0, 1):
                    number = self.n_sib + (z * 2 + xx) * 2 + yy
                    self.wait(number, ((z * 2 + xx) * 2 + 1 - g.c) * 2 + yy)
        self.own_copy().wait()

    def sent(self):
        g, src = self.g, self.shard
        self.p2_copy(g.z, src).wait_send()
        self.p3_copy(g.z, g.i2, src).wait_send()
        self.sib_copy(g.z, g.i2, g.i3, src).wait_send()
        self.each_z(lambda z: self.z_copy(False, z, src).wait_send())
        when(self.by_z, lambda: self.each_z(lambda z: self.z_copy(True, z).wait_send()))
        end = g.near(g.Z - 2)

        def passed():
            self.pass_copy(False, end).wait_send()
            when(self.by_z, lambda: self.pass_copy(True, end).wait_send())

        pl.when(g.between(end))(passed)
        for k in range(1, g.Z):
            z = g.above(k)
            unless(self.by_z, lambda: self.p2_copy(z).wait_send())
            self.p3_copy(z, g.i2).wait_send()
            self.sib_copy(z, g.i2, g.i3).wait_send()
        for z in range(g.Z):
            self.p3_copy(z, 1 - g.i2).wait_send()
            self.sib_copy(z, 1 - g.i2, g.i3).wait_send()
            for a2 in (0, 1):
                self.sib_copy(z, a2, 1 - g.i3).wait_send()


class Share:
    def __init__(self, place, part, first, landing, unit, n, send, recv, write, by_z, cols=None):
        self.g, self.part, self.first = place, part, first
        self.rec3, self.rec = landing
        self.unit, self.n, self.send, self.recv, self.write = unit, n, send, recv, write
        self.kind, self.by_z = part.dtype, by_z
        self.cols = pl.ds(0, part.shape[-1]) if cols is None else cols

    @staticmethod
    def sems(Z):
        return 4 * Z - 1

    def copy(self, block, landing, slot, number, device):
        rows = slice(None)
        return pltpu.make_async_remote_copy(
            src_ref=self.part.at[pl.ds(self.first, self.n), block, rows, self.cols],
            dst_ref=landing.at[pl.ds(self.unit, self.n), slot, rows, self.cols],
            send_sem=self.send.at[number],
            recv_sem=self.recv.at[number],
            device_id=device,
            device_id_type=MESH,
        )

    def p3_copy(self, z, a2):
        g = self.g
        slot = z * 2 + a2
        return self.copy(g.block(z, a2, 1 - g.i3), self.rec3, slot, slot, g.p3)

    def p2_copy(self, z):
        g = self.g
        slot = pick(self.by_z, 0, z)
        block = g.block(z, 1 - g.i2, g.i3)
        return self.copy(block, self.rec, slot, 2 * g.Z + slot, g.p2)

    def z_slot(self, k, a2, by_z):
        return 1 + (k - 1) * 2 + a2 if by_z else self.g.Z + k - 1

    def z_copy(self, z, a2, by_z):
        g = self.g
        slot = self.z_slot(lax.rem(z - g.z + g.Z, g.Z), a2, by_z)
        return self.copy(g.block(z, a2, g.i3), self.rec, slot, 2 * g.Z + slot, g.at_z(z))

    def z_wait(self, k, a2, by_z):
        g = self.g
        slot = self.z_slot(k, a2, by_z)
        block = g.block(g.z, a2, g.i3)
        self.copy(block, self.rec, slot, 2 * g.Z + slot, g.sib).wait_recv()
        return self.landed(self.rec, slot)

    def landed(self, ref, slot):
        return ref[pl.ds(self.unit, self.n), slot, :, self.cols].astype(jnp.float32)

    def own(self, block):
        return self.part[pl.ds(self.first, self.n), block, :, self.cols].astype(jnp.float32)

    def add_to(self, block, ref, slot):
        spot = (pl.ds(self.first, self.n), block, slice(None), self.cols)
        self.part[spot] += ref[pl.ds(self.unit, self.n), slot, :, self.cols]

    def put(self, block, total):
        self.part[pl.ds(self.first, self.n), block, :, self.cols] = total.astype(self.kind)

    def start(self, z):
        for a2 in (0, 1):
            self.p3_copy(z, a2).start()

    def start_all(self):
        for j in range(self.g.Z):
            self.start(self.g.order(j))

    def add3(self, z, a2):
        g = self.g
        self.p3_copy(z, a2).wait_recv()
        self.add_to(g.block(z, a2, g.i3), self.rec3, z * 2 + a2)

    def stage3(self, j):
        g = self.g
        z = g.order(j)
        o2 = 1 - g.i2
        own = j == g.Z - 1
        self.add3(z, o2)
        if not own:
            when(self.by_z, lambda: self.z_copy(z, o2, True).start())
        unless(self.by_z, lambda: self.p2_copy(z).start())
        self.add3(z, g.i2)
        if not own:
            when(self.by_z, lambda: self.z_copy(z, g.i2, True).start())

    def stage2(self, j):
        g = self.g

        def with_p2():
            z = g.order(j)
            self.p2_copy(z).wait_recv()
            self.add_to(g.block(z, g.i2, g.i3), self.rec, z)
            self.z_copy(z, g.i2, False).start()

        unless(self.by_z, with_p2)

    def sum_z(self):
        g = self.g

        def along_z():
            o2 = 1 - g.i2
            block = g.block(g.z, o2, g.i3)
            total = self.own(block)
            for k in range(1, g.Z):
                total += self.z_wait(k, o2, True)
            self.put(block, total)
            self.p2_copy(g.z).start()

        when(self.by_z, along_z)

    def last(self):
        g = self.g

        def finish(by_z):
            total = self.own(g.block(g.z, g.i2, g.i3))
            for k in range(1, g.Z):
                total += self.z_wait(k, g.i2, by_z)
            self.p2_copy(g.z).wait_recv()
            total += self.landed(self.rec, 0 if by_z else g.z)
            self.write(total)

        when(self.by_z, lambda: finish(True))
        unless(self.by_z, lambda: finish(False))

    def sent(self):
        g = self.g
        for z in range(g.Z):
            for a2 in (0, 1):
                self.p3_copy(z, a2).wait_send()

        def by_z():
            self.p2_copy(g.z).wait_send()
            for k in range(1, g.Z):
                for a2 in (0, 1):
                    self.z_copy(g.above(k), a2, True).wait_send()

        def by_p2():
            for z in range(g.Z):
                self.p2_copy(z).wait_send()
            for k in range(1, g.Z):
                self.z_copy(g.above(k), g.i2, False).wait_send()

        when(self.by_z, by_z)
        unless(self.by_z, by_p2)


def loop(count):
    def run(body):
        def step(i, carry):
            body(i)
            return carry

        lax.fori_loop(0, count, step, 0)

    return run


def run_at(t, events):
    for i, event in events.items():
        pl.when(t == i)(event)


def dot(a, b):
    return jnp.dot(a, b, preferred_element_type=jnp.float32)


def dot_nt(a, b):
    return lax.dot_general(a, b, (((1,), (1,)), ((), ())), preferred_element_type=jnp.float32)


def normed(v):
    center = v - jnp.mean(v, axis=-1, keepdims=True)
    r = lax.rsqrt(jnp.mean(center * center, axis=-1, keepdims=True) + epsilon)
    return center * r, r


def norm_pull(v, gain, e):
    z, r = normed(v)
    f = e * gain
    dv = r * (
        f
        - jnp.mean(f, axis=-1, keepdims=True)
        - z * jnp.mean(f * z, axis=-1, keepdims=True)
    )
    return dv, e * z


def turn(u, cosine, sine, half):
    lane = lax.broadcasted_iota(jnp.int32, u.shape, 1)
    swapped = jnp.where(
        lax.rem(lane, 2 * half) < half,
        pltpu.roll(u, u.shape[1] - half, 1),
        pltpu.roll(u, half, 1),
    )
    return u * cosine + swapped * sine


def turn_tables(row_len, head_dim):
    half = head_dim // 2
    inverse = 10000.0 ** (-2.0 * np.arange(half) / head_dim)
    angles = np.arange(row_len)[:, None] * inverse[None, :]
    cosine = np.tile(np.cos(angles), (1, 4))
    sine = np.tile(np.concatenate([-np.sin(angles), np.sin(angles)], axis=1), (1, 2))
    return cosine.astype(np.float32), sine.astype(np.float32)


def doc_ends(lens):
    ends = [lens[0, 0]]
    for d in range(1, DOCS):
        ends.append(ends[-1] + lens[0, d])
    return ends


def fill_bias(bias, lens, first, rows):
    ends = doc_ends(lens)
    block = 128
    blocks = bias.shape[1] // block

    @loop(bias.shape[0] * blocks)
    def _(i):
        place = first + lax.broadcasted_iota(jnp.int32, (1, rows), 1)
        key = i * block + lax.broadcasted_iota(jnp.int32, (block, rows), 0)
        start = jnp.zeros((1, rows), jnp.int32)
        for d in range(DOCS):
            start = jnp.where(place >= ends[d], ends[d], start)
        fine = (key >= start) & (key <= place)
        spot = pl.ds(lax.rem(i, blocks) * block, block)
        bias[lax.div(i, blocks), spot, :] = jnp.where(fine, 0.0, masked_score)


def split_heads(v, axis=1):
    spot = lax.broadcasted_iota(jnp.int32, v.shape, axis)
    first = spot < v.shape[axis] // 2
    zero = jnp.zeros_like(v)
    return jnp.where(first, v, zero), jnp.where(first, zero, v)


class Tiles:
    def __init__(self, source, buffer, sems, ready=None):
        self.source, self.buffer, self.sems, self.ready = source, buffer, sems, ready
        self.depth = buffer.shape[0]

    def copy(self, t):
        slot = lax.rem(t, self.depth)
        return pltpu.make_async_copy(self.source(t), self.buffer.at[slot], self.sems.at[slot])

    def start(self, t):
        if self.ready is not None:
            self.ready(t)
        self.copy(t).start()

    def first(self, end, begin=0):
        for t in range(begin, min(begin + self.depth - 1, end)):
            self.start(jnp.int32(t))

    def get(self, t, end):
        later = t + self.depth - 1

        @pl.when(later < end)
        def _():
            self.start(later)

        self.copy(t).wait()
        return self.buffer[lax.rem(t, self.depth)]


def columns(t, size):
    return pl.ds(pl.multiple_of(t * size, size), size)


def forward_kernel(dp_size, head_dim, *refs):
    (tok, lens, gs, wq, wo, wu, wd, cosine, sine) = refs[:9]
    (out, wq_f, wo_f, wu_f, wd_f, gain_o, q_o, k_o, v_o, ob_o, lse_o) = refs[9:20]
    (araw_o, h_o, mraw_o, bt_o, gt_o, gp_o, at_o, atx_o, tokx_o) = refs[20:29]
    (g_full, gain, tokx, a, ax, at, atx, q, k, v, vt, bias, ob, lse) = refs[29:43]
    (araw, h, mraw, b, bt, act, actt, gp, wbuf, dbuf) = refs[43:53]
    sems = refs[53:63]
    wsem, dsem, xsem, osem = refs[63:67]
    o_own = refs[67]
    g = Place(dp_size)
    y = g.y
    rows, width = tok.shape
    half = head_dim // 2
    pairs = width // 128
    scale = head_dim ** (-0.5)
    modes = [g.c == 0 if m is None else m for m in GATHER_BY_Z]
    gg, gq, go, gu, gd = [
        Gather(g, s, f, sems[2 * i], sems[2 * i + 1], mode)
        for i, (s, f, mode) in enumerate(
            (
                (gs, g_full, False),
                (wq, wq_f, modes[0]),
                (wo, wo_f, modes[1]),
                (wu, wu_f, modes[2]),
                (wd, wd_f, modes[3]),
            )
        )
    ]
    Z = g.Z
    saves = []

    def save(src, dst):
        copy = pltpu.make_async_copy(src, dst, osem.at[len(saves)])
        copy.start()
        saves.append(copy)

    tok_copy = pltpu.make_async_remote_copy(
        src_ref=tok,
        dst_ref=tokx,
        send_sem=xsem.at[0],
        recv_sem=xsem.at[1],
        device_id=g.device(g.z, g.x, g.c, 1 - y),
        device_id_type=MESH,
    )
    named = {"g": gg, "q": gq, "o": go, "u": gu, "d": gd}

    def serve(slot):
        for step in GATHER_PLAN.get(slot, ()):
            m, kind = named.get(step[0]), step[1]
            if step == "token":
                pl.when(y == 0)(lambda: tok_copy.start())
            elif kind == "s":
                getattr(m, "start_" + step[2:])()
            elif kind == "F":
                m.first()
            else:
                act = {"Z": m.from_z, "P": m.from_p2, "T": m.from_p3}[kind]
                act(int(step[2:]))

    def serve_at(name, t, count):
        for i in range(count):
            if (name, i) in GATHER_PLAN:
                pl.when(t == i)(functools.partial(serve, (name, i)))

    g.barrier()
    serve("start")
    fill_bias(bias, lens, y * rows, rows)
    serve("norm")
    gg.complete()
    turned = jnp.transpose(g_full[...].astype(jnp.float32))
    gain[...] = turned[:8]
    save(gain, gain_o)

    def first_norm(src, dst, dst_t):
        @loop(rows // 128)
        def _(i):
            spot = pl.ds(i * 128, 128)
            z, _r = normed(src[spot, :].astype(jnp.float32))
            value = z * gain[0:1, :]
            dst[spot, :] = value.astype(jnp.bfloat16)
            dst_t[:, spot] = jnp.transpose(value).astype(jnp.bfloat16)

    first_norm(tok, a, at)
    save(at, at_o)
    serve("qkv")
    gq.complete()

    tiles = Tiles(lambda t: wq_f.at[:, columns(t, 512)], wbuf, wsem)
    per = width // 512
    first = pl.multiple_of(y * rows, rows)

    def turned_pair(u, start):
        return turn(u, cosine[pl.ds(start, rows), :], sine[pl.ds(start, rows), :], half)

    tiles.first(3 * per)

    @loop(per)
    def _(t):
        serve_at("q", t, per)
        u = dot(a[...], tiles.get(t, 3 * per))
        for j in range(4):
            part = turned_pair(u[:, j * 128 : j * 128 + 128], first) * scale
            q[4 * t + j] = part.astype(jnp.bfloat16)

    def keys(w, t, src, start):
        u = dot(src[...], w)
        for j in range(4):
            part = turned_pair(u[:, j * 128 : j * 128 + 128], start)
            k[4 * t + j, pl.ds(start, rows), :] = part.astype(jnp.bfloat16)

    def values(w, t, src, start):
        u = dot(src[...], w)
        ut = jnp.transpose(u).astype(jnp.bfloat16)
        for j in range(4):
            cols = slice(j * 128, j * 128 + 128)
            v[4 * t + j, pl.ds(start, rows), :] = u[:, cols].astype(jnp.bfloat16)
            vt[4 * t + j, :, pl.ds(start, rows)] = ut[cols]

    @loop(per)
    def _(t):
        serve_at("k", t, per)
        keys(tiles.get(t + per, 3 * per), t, a, first)

    @loop(per)
    def _(t):
        serve_at("v", t, per)
        values(tiles.get(t + 2 * per, 3 * per), t, a, first)

    def attend(p, block, keys_at):
        spot = slice(block * 256, block * 256 + 256)
        heads = split_heads(q[p, spot, :])
        kk = k[p, keys_at, :]
        vv = vt[p, :, keys_at]
        mask = bias[0, keys_at, spot]
        parts, logs = [], []
        for i in (0, 1):
            s = dot_nt(kk, heads[i]) + mask
            m = jnp.max(s, axis=0, keepdims=True)
            e = jnp.exp(s - m)
            total = jnp.sum(e, axis=0, keepdims=True)
            logs.append(m + jnp.log(total))
            parts.append(dot(vv, e.astype(jnp.bfloat16)) * (1.0 / total))
        return spot, parts, logs

    upper = lax.broadcasted_iota(jnp.int32, (128, 256), 0) < head_dim
    blocks = rows // 256

    @loop(pairs)
    def _(p):
        serve_at("pair", p, pairs)
        for block in range(blocks):
            spot, parts, logs = attend(p, block, pl.ds(first, (block + 1) * 256))
            for i in (0, 1):
                lse[p, i : i + 1, spot] = logs[i]
            o_own[p, :, spot] = jnp.where(upper, parts[0], parts[1])

    serve("other")

    @pl.when(y == 1)
    def _():
        tok_copy.wait_recv()
        first_norm(tokx, ax, atx)
        tiles.first(3 * per, per)

        @loop(per)
        def _(t):
            keys(tiles.get(t + per, 3 * per), t, ax, 0)

        @loop(per)
        def _(t):
            values(tiles.get(t + 2 * per, 3 * per), t, ax, 0)

    save(atx, atx_o)
    save(tokx, tokx_o)
    save(q, q_o)
    save(k, k_o)
    save(v, v_o)

    @pl.when(y == 0)
    def _():
        @loop(pairs)
        def _(p):
            serve_at("more", p, pairs)
            ob[p] = o_own[p].astype(jnp.bfloat16)

    @pl.when(y == 1)
    def _():
        @loop(pairs)
        def _(p):
            serve_at("more", p, pairs)
            for block in range(blocks):
                spot, parts, logs = attend(p, block, pl.ds(0, rows))
                shares = []
                for i in (0, 1):
                    old = lse[p, i : i + 1, spot]
                    top = jnp.maximum(old, logs[i])
                    both = top + jnp.log(jnp.exp(old - top) + jnp.exp(logs[i] - top))
                    lse[p, i : i + 1, spot] = both
                    shares.append((jnp.exp(old - both), jnp.exp(logs[i] - both)))
                own = o_own[p, :, spot]
                first_head = own * shares[0][0] + parts[0] * shares[0][1]
                second_head = own * shares[1][0] + parts[1] * shares[1][1]
                ob[p, :, spot] = jnp.where(upper, first_head, second_head).astype(jnp.bfloat16)

    save(ob, ob_o)
    save(lse, lse_o)

    serve("out")
    go.complete()
    tiles = Tiles(lambda t: wo_f.at[:, columns(t, 512)], wbuf, wsem)
    tiles.first(per)
    a[...] = jnp.transpose(ob[...].reshape(width, rows))

    @loop(per)
    def _(t):
        w = tiles.get(t, per)
        araw[:, columns(t, 512)] = dot(a[...], w)

    save(araw, araw_o)

    @loop(rows // 128)
    def _(i):
        spot = pl.ds(i * 128, 128)
        z, _r = normed(araw[spot, :])
        hidden = tok[spot, :].astype(jnp.float32) + z * gain[1:2, :]
        h[spot, :] = hidden
        z, _r = normed(hidden)
        value = z * gain[2:3, :]
        b[spot, :] = value.astype(jnp.bfloat16)
        bt[:, spot] = jnp.transpose(value).astype(jnp.bfloat16)

    save(h, h_o)
    save(bt, bt_o)

    serve("up")
    gu.complete()
    tiles = Tiles(lambda t: wu_f.at[:, columns(t, 512)], wbuf, wsem)
    ups = act.shape[0]
    tiles.first(ups)
    c0 = math.sqrt(2.0 / math.pi)

    @loop(ups)
    def _(t):
        serve_at("up", t, ups)
        u = dot(b[...], tiles.get(t, ups))
        square = u * u
        th = jnp.tanh(c0 * (u + 0.044715 * (square * u)))
        value = 0.5 * u * (1.0 + th)
        slope = 0.5 * (1.0 + th) + (0.5 * c0) * u * (1.0 - th * th) * (
            1.0 + (3 * 0.044715) * square
        )
        act[t] = value.astype(jnp.bfloat16)
        actt[t] = jnp.transpose(value).astype(jnp.bfloat16).reshape(2, 256, rows)
        gp[t] = slope.astype(jnp.bfloat16)

    save(actt, gt_o)
    save(gp, gp_o)

    serve("down")
    gd.complete()
    tiles = Tiles(lambda t: wd_f.at[columns(t, 512), :], dbuf, dsem)
    tiles.first(ups)
    mraw[...] = jnp.zeros_like(mraw)

    @loop(ups)
    def _(t):
        mraw[...] += dot(act[t], tiles.get(t, ups))

    save(mraw, mraw_o)
    ends = doc_ends(lens)

    @loop(rows // 128)
    def _(i):
        spot = pl.ds(i * 128, 128)
        z, _r = normed(mraw[spot, :])
        result = h[spot, :] + z * gain[3:4, :]
        place = y * rows + i * 128 + lax.broadcasted_iota(jnp.int32, result.shape, 0)
        result = jnp.where(place < ends[DOCS - 2], result, 0.0)
        out[spot, :] = result.astype(jnp.bfloat16)

    for copy in saves:
        copy.wait()

    @pl.when(y == 0)
    def _():
        tok_copy.wait_send()

    for m in (gg, gq, go, gu, gd):
        m.sent()


def forward(tokens, lengths, gains_wide, w_qkv, w_out, w_up, w_down, tables):
    dp_size = lax.axis_size("dp")
    devices = dp_size * lax.axis_size("ctx")
    rows, width = tokens.shape
    row_len = rows * lax.axis_size("ctx")
    head_dim = width // HEADS
    pairs = width // 128
    ups = w_up.shape[1] // 512
    bf, f32 = jnp.bfloat16, jnp.float32
    any_spec = pl.BlockSpec(memory_space=pl.ANY)
    vm = pl.BlockSpec(memory_space=pltpu.VMEM)
    shape = jax.ShapeDtypeStruct

    def whole(w):
        return shape((w.shape[0] * devices, w.shape[1]), bf)

    outs = [
        shape((rows, width), bf),
        whole(w_qkv),
        whole(w_out),
        whole(w_up),
        whole(w_down),
        shape((8, width), f32),
        shape((pairs, rows, 128), bf),
        shape((pairs, row_len, 128), bf),
        shape((pairs, row_len, 128), bf),
        shape((pairs, 128, rows), bf),
        shape((pairs, 2, rows), f32),
        shape((rows, width), f32),
        shape((rows, width), f32),
        shape((rows, width), f32),
        shape((width, rows), bf),
        shape((ups, 2, 256, rows), bf),
        shape((ups, rows, 512), bf),
        shape((width, rows), bf),
        shape((width, rows), bf),
        shape((rows, width), bf),
    ]
    scratch = [
        pltpu.VMEM((width, 128), bf),
        pltpu.VMEM((8, width), f32),
        pltpu.VMEM((rows, width), bf),
        pltpu.VMEM((rows, width), bf),
        pltpu.VMEM((rows, width), bf),
        pltpu.VMEM((width, rows), bf),
        pltpu.VMEM((width, rows), bf),
        pltpu.VMEM((pairs, rows, 128), bf),
        pltpu.VMEM((pairs, row_len, 128), bf),
        pltpu.VMEM((pairs, row_len, 128), bf),
        pltpu.VMEM((pairs, 128, row_len), bf),
        pltpu.VMEM((1, row_len, rows), f32),
        pltpu.VMEM((pairs, 128, rows), bf),
        pltpu.VMEM((pairs, 2, rows), f32),
        pltpu.VMEM((rows, width), f32),
        pltpu.VMEM((rows, width), f32),
        pltpu.VMEM((rows, width), f32),
        pltpu.VMEM((rows, width), bf),
        pltpu.VMEM((width, rows), bf),
        pltpu.VMEM((ups, rows, 512), bf),
        pltpu.VMEM((ups, 2, 256, rows), bf),
        pltpu.VMEM((ups, rows, 512), bf),
        pltpu.VMEM((3, width, 512), bf),
        pltpu.VMEM((3, 512, width), bf),
    ]
    scratch += [pltpu.SemaphoreType.DMA((Gather.sems(dp_size // 4),))] * 10
    scratch += [pltpu.SemaphoreType.DMA((3,))] * 3 + [pltpu.SemaphoreType.DMA((16,))]
    scratch += [pltpu.VMEM((pairs, 128, rows), f32)]
    return pl.pallas_call(
        functools.partial(forward_kernel, dp_size, head_dim),
        out_shape=outs,
        in_specs=[vm, pl.BlockSpec(memory_space=pltpu.SMEM), vm]
        + [any_spec] * 4
        + [vm, vm],
        out_specs=[vm] + [any_spec] * (len(outs) - 1),
        scratch_shapes=scratch,
        compiler_params=pltpu.CompilerParams(
            collective_id=0, has_side_effects=True, vmem_limit_bytes=60 * 2**20
        ),
    )(tokens, lengths, gains_wide, w_qkv, w_out, w_up, w_down, *tables)


def backward_kernel(dp_size, head_dim, *refs):
    (tok_i, dout, lens, gain, cosine_i, sine_i, wq, wo, wu, wd) = refs[:10]
    (q_i, k_i, v_i, ob_i, lse_i, araw_i, h_i, mraw_i, bt_i, gt_i, gp_i, at_i, atx_i, tokx_i) = refs[10:24]
    (dtok, out_q, out_o, out_u, out_d, out_g) = refs[24:30]
    (gts, dus, dzs) = refs[30:33]
    (part, rec3, rec, gpart, grec3, grec) = refs[33:39]
    (f1, f2, acc, dm, dms, da, das, dz, bt, bts, obts, ats, atx, atxs) = refs[39:53]
    (q, ob, lse, dk, dv, dg, dgs, dgt, dnxs) = refs[53:62]
    (kbuf, vbuf, wbuf, dbuf, gbuf, gpbuf, sbuf) = refs[62:69]
    tsems = refs[69:79]
    usend, urecv, gsend, grecv, zsend, zrecv, osend, orecv, lsem = refs[79:88]
    dnsem = refs[88]
    gsems, rsems = refs[89:96], refs[96:103]
    tok, cosine, sine = refs[103:106]
    at, xbuf, do, dnx, tokx = bt, gpbuf, dm, da, das
    g = Place(dp_size)
    Z, y, c = g.Z, g.y, g.c
    rows, width = dout.shape
    half = head_dim // 2
    pairs = width // 128
    scale = head_dim ** (-0.5)
    ups = gp_i.shape[0]
    per = width // 512
    bf, f32 = jnp.bfloat16, jnp.float32
    first = pl.multiple_of(y * rows, rows)

    def to_sib(src, dst, send, recv):
        return pltpu.make_async_remote_copy(
            src_ref=src,
            dst_ref=dst,
            send_sem=send,
            recv_sem=recv,
            device_id=g.sib,
            device_id_type=MESH,
        )

    def load(src, dst, i):
        return pltpu.make_async_copy(src, dst, lsem.at[i])

    h_load = load(h_i, f2, 0)
    bt_load = load(bt_i.at[:, c], bt, 1)
    atx_load = load(atx_i.at[:, c], atx, 2)
    q_load = load(q_i, q, 3)
    ob_load = load(ob_i, ob, 4)
    lse_load = load(lse_i, lse, 5)
    at_load = load(at_i.at[:, c], at, 6)
    tokx_load = load(tokx_i, tokx, 7)
    tok_load = load(tok_i, tok, 8)
    cosine_load = load(cosine_i, cosine, 9)
    sine_load = load(sine_i, sine, 10)

    def gt_send(i):
        half_z = pl.ds(pl.multiple_of(lax.rem(i, 2) * 256, 256), 256)
        return to_sib(
            gt_i.at[i, 1 - c], gts.at[lax.div(i, 2), half_z], gsend.at[i], grecv.at[i]
        )

    bt_send = to_sib(bt_i.at[:, 1 - c], bts, osend.at[0], orecv.at[0])
    ob_send = to_sib(ob_i.at[:, 1 - c], obts, osend.at[1], orecv.at[1])
    at_send = to_sib(at_i.at[:, 1 - c], ats, osend.at[2], orecv.at[2])
    atx_send = to_sib(atx_i.at[:, 1 - c], atxs, osend.at[3], orecv.at[3])

    def dm_send(i):
        spot = columns(i, 128)
        return to_sib(dm.at[spot, :], dms.at[spot, :], osend.at[7 + i], orecv.at[7 + i])

    da_send = to_sib(da, das, osend.at[5], orecv.at[5])
    dg_send = to_sib(dg, dgs, osend.at[6], orecv.at[6])
    dnx_send = pltpu.make_async_remote_copy(
        src_ref=dnx,
        dst_ref=dnxs,
        send_sem=dnsem.at[0],
        recv_sem=dnsem.at[1],
        device_id=g.device(g.z, g.x, c, 1 - y),
        device_id_type=MESH,
    )

    def du_send(t):
        return to_sib(dz.at[t], dus.at[t], usend.at[t], urecv.at[t])

    def dz_send(e, p):
        t = e * per + lax.div(p, 4)
        spot = columns(lax.rem(p, 4), 128)
        n = e * pairs + p
        return to_sib(dz.at[t, :, spot], dzs.at[t, :, spot], zsend.at[n], zrecv.at[n])

    landing = (rec3, rec)

    def write_d(total):
        out_d[...] = total.reshape(out_d.shape)

    def write_into(out, column):
        def write(total):
            for i in range(total.shape[0]):
                begin = column + i * width
                out[:, begin : begin + total.shape[2]] = total[i]

        return write

    def write_g(total):
        out_g[...] = total[0]

    modes = [c == 0 if m is None else m for m in SHARE_BY_Z]
    s_d = Share(
        g, part, 0, landing, 0, 4, gsems[0], rsems[0], write_d, modes[3]
    )
    s_u = [
        Share(
            g, part, 4 + 2 * i, landing, 4 + 2 * i, 2, gsems[1 + i], rsems[1 + i],
            write_into(out_u, 2 * i * width), modes[2],
        )
        for i in (0, 1)
    ]
    s_o = Share(
        g, part, 8, landing, 8, 1, gsems[3], rsems[3], write_into(out_o, 0),
        modes[1],
    )
    s_q = [
        Share(
            g, part, 9, landing, 9, 3, gsems[4 + i], rsems[4 + i],
            write_into(out_q, i * 512), modes[0], pl.ds(i * 512, 512),
        )
        for i in (0, 1)
    ]
    s_g = Share(g, gpart, 0, (grec3, grec), 0, 1, gsems[6], rsems[6], write_g, False)
    named = {"d": s_d, "u": s_u[0], "v": s_u[1], "o": s_o, "a": s_q[0], "b": s_q[1], "g": s_g}

    def serve(slot):
        for step in SHARE_PLAN.get(slot, ()):
            s = named[step[0]]
            if step[1] == "L":
                s.last()
            elif step[1] == "E":
                s.sum_z()
            else:
                (s.stage3 if step[1] == "3" else s.stage2)(int(step[2]))

    def serve_at(name, t, count):
        for i in range(count):
            if (name, i) in SHARE_PLAN:
                pl.when(t == i)(functools.partial(serve, (name, i)))

    mraws = Tiles(lambda i: mraw_i.at[columns(i, 128), :], f1, tsems[9])
    araws = Tiles(lambda i: araw_i.at[columns(i, 128), :], f1, tsems[9])
    mraws.first(rows // 128)
    g.barrier()
    for j in range(Z):
        for i in (0, 1):
            gt_send(g.order(j) * 2 + i).start()
    for copy in (bt_send, ob_send, at_send):
        copy.start()

    @pl.when(y == 1)
    def _():
        atx_send.start()

    def z_of(j):
        return sum(jnp.where(j == i, g.order(i), 0) for i in range(Z))

    def gt_ready(j):
        for i in (0, 1):
            gt_send(z_of(j) * 2 + i).wait_recv()

    own_g = Tiles(lambda j: gt_i.at[pl.ds(z_of(j) * 2, 2), c], gbuf, tsems[0])
    sib_g = Tiles(lambda j: gts.at[z_of(j)], sbuf, tsems[1], gt_ready)
    own_g.first(Z)
    for copy in (
        h_load, bt_load, atx_load, q_load, ob_load, lse_load, cosine_load, sine_load, tok_load
    ):
        copy.start()
    dg[...] = jnp.zeros_like(dg)
    ends = doc_ends(lens)

    def upstream(i):
        e = dout[pl.ds(i * 128, 128), :].astype(f32)
        place = y * rows + i * 128 + lax.broadcasted_iota(jnp.int32, e.shape, 0)
        return jnp.where(place < ends[DOCS - 2], e, 0.0)

    def gain_sum(index, term):
        dg[index : index + 1, :] += jnp.sum(term, axis=0, keepdims=True)

    @loop(rows // 128)
    def _(i):
        value, term = norm_pull(mraws.get(i, rows // 128), gain[3:4, :], upstream(i))
        dm[pl.ds(i * 128, 128), :] = value.astype(bf)
        gain_sum(3, term)
        dm_send(i).start()

    downs = Tiles(lambda t: wd.at[columns(t, 512), :], dbuf, tsems[2])
    upw = Tiles(lambda t: wu.at[:, columns(t, 512)], wbuf, tsems[3])
    slopes = Tiles(lambda t: gp_i.at[t], gpbuf, tsems[4])
    for tiles in (downs, upw, slopes):
        tiles.first(ups)
    araws.first(rows // 128)
    keys = Tiles(lambda p: k_i.at[p], kbuf, tsems[6])
    values = Tiles(lambda p: v_i.at[p], vbuf, tsems[7])
    keys.first(pairs)
    values.first(pairs)
    sib_g.first(Z)
    for i in range(rows // 128):
        dm_send(i).wait_recv()

    @loop(Z)
    def _(j):
        z = z_of(j)
        total = dot(own_g.get(j, Z).reshape(512, rows), dm[...])
        total += dot(sib_g.get(j, Z), dms[...])
        total = total.astype(bf).reshape(4, 4, 32, width)
        for a in range(4):
            for e in range(4):
                part[e, 4 * z + a] = total[a, e]
        s_d.start(z)

    def add_to(halves, value, weights):
        for j in (0, 1):
            halves[j] += dot_nt(value, weights[j * 512 : (j + 1) * 512])

    sib_du = Tiles(lambda t: dus.at[t], sbuf, tsems[5], lambda t: du_send(t).wait_recv())
    acc[...] = jnp.zeros_like(acc)

    @loop(ups)
    def _(t):
        serve_at("du", t, ups)
        du = dot_nt(dm[...], downs.get(t, ups)) * slopes.get(t, ups).astype(f32)
        du = du.astype(bf)
        dz[t] = du
        du_send(t).start()
        add_to(acc, du, upw.get(t, ups))
        pl.when(t == 3)(lambda: sib_du.first(ups))

    outs = Tiles(lambda t: wo.at[columns(t, 512), :], dbuf, tsems[2])
    outs.first(per)
    bt_load.wait()
    bt_send.wait_recv()
    for i in (0, 1):

        @loop(ups // 2)
        def _(t2):
            t = t2 + i * (ups // 2)
            serve_at("up", t, ups)
            total = dot(bt[...].reshape(-1, rows), dz[t])
            total += dot(bts[...].reshape(-1, rows), sib_du.get(t, ups))
            part[4 + lax.div(t, per), :, :, columns(lax.rem(t, per), 512)] = (
                total.astype(bf).reshape(4 * Z, 32, 512)
            )

        s_u[i].start_all()

    at_load.start()

    serve("norm")
    h_load.wait()

    @loop(rows // 128)
    def _(i):
        spot = pl.ds(i * 128, 128)
        e = jnp.concatenate([acc[0, spot, :], acc[1, spot, :]], axis=1)
        value, term = norm_pull(f2[spot, :], gain[2:3, :], e)
        gain_sum(2, term)
        dh = upstream(i) + value
        f2[spot, :] = dh
        value, term = norm_pull(araws.get(i, rows // 128), gain[1:2, :], dh)
        gain_sum(1, term)
        da[spot, :] = value.astype(bf)

    da_send.start()
    for i in range(rows // 128):
        dm_send(i).wait_send()
    serve("do")

    @loop(per)
    def _(t):
        do[:, columns(t, 512)] = dot_nt(da[...], outs.get(t, per)).astype(bf)

    serve("out")
    ob_load.wait()
    ob_send.wait_recv()
    da_send.wait_recv()

    @loop(per)
    def _(t):
        total = dot(ob[:, c].reshape(-1, rows), da[:, columns(t, 512)])
        total += dot(obts[...].reshape(-1, rows), das[:, columns(t, 512)])
        part[8, :, :, columns(t, 512)] = total.astype(bf).reshape(4 * Z, 32, 512)

    s_o.start_all()
    for t in range(ups):
        du_send(t).wait_send()

    qkv_w = Tiles(lambda t: wq.at[:, columns(t, 512)], wbuf, tsems[3])
    pl.when(y == 1)(lambda: qkv_w.first(3 * per, per))
    serve("mask")
    fill_bias(acc, lens, y * rows, rows)
    pl.when(y == 1)(lambda: tokx_load.start())
    for copy in (q_load, lse_load, cosine_load, sine_load, tok_load):
        copy.wait()
    blocks = rows // 256

    def attend(p, block, base, count, fresh):
        spot = slice(block * 256, block * 256 + 256)
        slot = lax.rem(p, 2)
        kk = kbuf[slot, pl.ds(base, count), :]
        vv = vbuf[slot, pl.ds(base, count), :]
        kt = jnp.transpose(kk.astype(f32)).astype(bf)
        qs = split_heads(q[p, spot, :])
        do_pair = do[spot, columns(p, 128)]
        dos = split_heads(do_pair)
        ob_pair = ob[p, :, :, spot].astype(f32).reshape(128, -1)
        dot_o = jnp.transpose(do_pair.astype(f32)) * ob_pair
        mask = acc[lax.div(base, 512), :count, spot]
        parts, dk_, dv_ = [], [], []
        for i in (0, 1):
            delta = jnp.sum(
                dot_o[i * head_dim : (i + 1) * head_dim], axis=0, keepdims=True
            )
            s = dot_nt(kk, qs[i]) + mask
            prob = jnp.exp(s - lse[p, i : i + 1, spot])
            ds = (prob * (dot_nt(vv, dos[i]) - delta)).astype(bf)
            dv_.append(dot(prob.astype(bf), dos[i]))
            dk_.append(dot(ds, qs[i]))
            parts.append(dot(kt, ds))
        if fresh:
            dk[:count, :] = dk_[0] + dk_[1]
            dv[:count, :] = dv_[0] + dv_[1]
        else:
            dk[:count, :] += dk_[0] + dk_[1]
            dv[:count, :] += dv_[0] + dv_[1]
        upper = lax.broadcasted_iota(jnp.int32, parts[0].shape, 0) < head_dim
        dq = jnp.transpose(jnp.where(upper, parts[0], parts[1]) * scale)
        start = pl.multiple_of(first + block * 256, 256)
        return spot, turn(dq, cosine[pl.ds(start, 256), :], -sine[pl.ds(start, 256), :], half)

    def lanes(p):
        return columns(lax.rem(p, 4), 128)

    def keep(p, start, base):
        spot = pl.ds(start, rows)
        u = turn(dk[...], cosine[spot, :], -sine[spot, :], half)
        dz[base + lax.div(p, 4), :, lanes(p)] = u.astype(bf)
        dz[base + per + lax.div(p, 4), :, lanes(p)] = dv[...].astype(bf)

    def other_half():
        acc[...] = jnp.zeros_like(acc)
        da_send.wait_send()
        tokx_load.wait()

        @loop(2 * per)
        def _(t):
            add_to(acc, dz[t + 3 * per], qkv_w.get(t + per, 3 * per))

        @loop(rows // 128)
        def _(i):
            spot = pl.ds(i * 128, 128)
            e = jnp.concatenate([acc[0, spot, :], acc[1, spot, :]], axis=1)
            value, term = norm_pull(tokx[spot, :].astype(f32), gain[0:1, :], e)
            gain_sum(0, term)
            dnx[spot, :] = value.astype(bf)

        dnx_send.start()

    def qkv_gradient(h):
        at_both = (at[...].reshape(-1, rows), ats[...].reshape(-1, rows))

        def ready(i):
            for j in range(4):
                dz_send(i, h * 4 + j).wait_recv()

        sib_dz = Tiles(lambda i: dzs.at[i * per + h], sbuf, tsems[5], ready)
        sib_dx = Tiles(lambda i: dzs.at[i * per + h], xbuf, tsems[8], ready)
        sib_dz.first(3)
        pl.when(y == 1)(lambda: sib_dx.first(5, 3))

        @loop(3)
        def _(e):
            def total():
                return dot(at_both[0], dz[e * per + h]) + dot(at_both[1], sib_dz.get(e, 3))

            def keep_total(value):
                part[9 + e, :, :, columns(h, 512)] = value.astype(bf).reshape(4 * Z, 32, 512)

            both = (y == 1) & (e > 0)

            @pl.when(jnp.logical_not(both))
            def _():
                keep_total(total())

            @pl.when(both)
            def _():
                value = total() + dot(atx[...].reshape(-1, rows), dz[(e + 2) * per + h])
                keep_total(value + dot(atxs[...].reshape(-1, rows), sib_dx.get(e + 2, 5)))

        for i in (0, 1):
            pl.when(h == i)(lambda: s_q[i].start_all())

    @pl.when(y == 0)
    def _():
        for p in range(pairs):
            serve(("more", p))
        serve("other")

    @pl.when(y == 1)
    def _():
        @loop(pairs)
        def _(p):
            serve_at("more", p, pairs)
            keys.get(p, pairs)
            values.get(p, pairs)
            for block in range(blocks):
                spot, dq = attend(p, block, 0, rows, block == 0)
                dz[lax.div(p, 4), spot, lanes(p)] = dq.astype(bf)
            keep(p, 0, 3 * per)
            for e in (3, 4):
                dz_send(e, p).start()

        serve("other")
        keys.first(pairs)
        values.first(pairs)
        other_half()
        fill_bias(acc, lens, y * rows, rows)

    @loop(pairs)
    def _(p):
        serve_at("pair", p, pairs)
        keys.get(p, pairs)
        values.get(p, pairs)
        for block in reversed(range(blocks)):
            spot, dq = attend(p, block, first, (block + 1) * 256, block == blocks - 1)
            before = dz[lax.div(p, 4), spot, lanes(p)].astype(f32)
            dq += jnp.where(y == 1, before, 0.0)
            dz[lax.div(p, 4), spot, lanes(p)] = dq.astype(bf)
        keep(p, first, per)
        for e in range(3):
            dz_send(e, p).start()

        @pl.when(p == pairs // 2 - 1)
        def _():
            serve("half")
            at_load.wait()
            at_send.wait_recv()
            atx_load.wait()
            pl.when(y == 1)(lambda: atx_send.wait_recv())

        @pl.when(p == pairs - 1)
        def _():
            serve("rest")

        @pl.when(lax.rem(p, 4) == 3)
        def _():
            qkv_gradient(lax.div(p, 4))

    serve("input")
    qkv_w.first(3 * per)

    acc[...] = jnp.zeros_like(acc)

    @loop(3 * per)
    def _(t):
        add_to(acc, dz[t], qkv_w.get(t, 3 * per))

    @loop(rows // 128)
    def _(i):
        spot = pl.ds(i * 128, 128)
        e = jnp.concatenate([acc[0, spot, :], acc[1, spot, :]], axis=1)
        value, term = norm_pull(tok[spot, :].astype(f32), gain[0:1, :], e)
        gain_sum(0, term)
        f2[spot, :] += value

    dg_send.start()
    serve("gains")
    dg_send.wait_recv()
    wide = jnp.concatenate([dg[...] + dgs[...], jnp.zeros((120, width), f32)], axis=0)
    dgt[...] = jnp.transpose(wide).reshape(dgt.shape)
    gpart[0] = dgt[:, c].reshape(gpart.shape[1:])
    s_g.start_all()
    serve("end")

    @pl.when(y == 0)
    def _():
        dnx_send.wait_recv()
        dtok[...] = (f2[...] + dnxs[...].astype(f32)).astype(bf)

    @pl.when(y == 1)
    def _():
        dtok[...] = f2[...].astype(bf)

    for i in range(2 * Z):
        gt_send(jnp.int32(i)).wait_send()
    for copy in (bt_send, ob_send, at_send, dg_send):
        copy.wait_send()
    @loop(pairs)
    def _(p):
        for e in range(3):
            dz_send(e, p).wait_send()

    @pl.when(y == 0)
    def _():
        da_send.wait_send()

    @pl.when(y == 1)
    def _():
        atx_send.wait_send()
        dnx_send.wait_send()

        @loop(pairs)
        def _(p):
            for e in (3, 4):
                dz_send(e, p).wait_send()

    for s in (s_d, s_u[0], s_u[1], s_o, s_q[0], s_q[1], s_g):
        s.sent()


def backward(tokens, d_out, lengths, gain_rows, tables, weights, saved, shards):
    dp_size = lax.axis_size("dp")
    Z = dp_size // 4
    rows, width = tokens.shape
    row_len = rows * lax.axis_size("ctx")
    head_dim = width // HEADS
    pairs = width // 128
    per = width // 512
    bf, f32 = jnp.bfloat16, jnp.float32
    ups = saved[10].shape[0]
    any_spec = pl.BlockSpec(memory_space=pl.ANY)
    vm = pl.BlockSpec(memory_space=pltpu.VMEM)
    smem = pl.BlockSpec(memory_space=pltpu.SMEM)
    shape = jax.ShapeDtypeStruct
    block = 32
    saved = list(saved)
    for i in (3, 8, 11, 12):
        saved[i] = saved[i].reshape(2 * Z, 2, width // (4 * Z), rows)
    outs = [
        shape((rows, width), bf),
        shape(shards[0].shape, f32),
        shape(shards[1].shape, f32),
        shape(shards[2].shape, f32),
        shape(shards[3].shape, f32),
        shape((block, 128), f32),
        shape((Z, 512, rows), bf),
        shape((ups, rows, 512), bf),
        shape((5 * per, rows, 512), bf),
    ]
    core_rows = (2 * Z, width // (4 * Z), rows)
    scratch = [
        pltpu.VMEM((12, 4 * Z, block, width), bf),
        pltpu.VMEM((12, 2 * Z, block, width), bf),
        pltpu.VMEM((12, 2 * Z - 1, block, width), bf),
        pltpu.VMEM((1, 4 * Z, block, 128), f32),
        pltpu.VMEM((1, 2 * Z, block, 128), f32),
        pltpu.VMEM((1, 2 * Z - 1, block, 128), f32),
        pltpu.VMEM((2, 128, width), f32),
        pltpu.VMEM((rows, width), f32),
        pltpu.VMEM((2, rows, 512), f32),
        pltpu.VMEM((rows, width), bf),
        pltpu.VMEM((rows, width), bf),
        pltpu.VMEM((rows, width), bf),
        pltpu.VMEM((rows, width), bf),
        pltpu.VMEM((max(ups, 5 * per), rows, 512), bf),
    ]
    scratch += [pltpu.VMEM(core_rows, bf)] * 6
    scratch += [
        pltpu.VMEM((pairs, rows, 128), bf),
        pltpu.VMEM((2 * Z, 2, width // (4 * Z), rows), bf),
        pltpu.VMEM((pairs, 2, rows), f32),
        pltpu.VMEM((rows, 128), f32),
        pltpu.VMEM((rows, 128), f32),
        pltpu.VMEM((8, width), f32),
        pltpu.VMEM((8, width), f32),
        pltpu.VMEM((2 * Z, 2, width // (4 * Z), 128), f32),
        pltpu.VMEM((rows, width), bf),
        pltpu.VMEM((2, row_len, 128), bf),
        pltpu.VMEM((2, row_len, 128), bf),
        pltpu.VMEM((2, width, 512), bf),
        pltpu.VMEM((2, 512, width), bf),
        pltpu.VMEM((2, 2, 256, rows), bf),
        pltpu.VMEM((2, rows, 512), bf),
        pltpu.VMEM((2, rows, 512), bf),
    ]
    dma = pltpu.SemaphoreType.DMA
    scratch += [dma((3,))] * 10
    scratch += [dma((ups,))] * 2 + [dma((2 * Z,))] * 2 + [dma((5 * pairs,))] * 2
    scratch += [dma((11,))] * 2 + [dma((11,)), dma((2,))]
    scratch += [dma((Share.sems(Z),))] * 14
    scratch += [pltpu.VMEM((rows, width), bf)] + [pltpu.VMEM((row_len, 128), f32)] * 2
    return pl.pallas_call(
        functools.partial(backward_kernel, dp_size, head_dim),
        out_shape=outs,
        in_specs=[any_spec, vm, smem, vm] + [any_spec] * 20,
        out_specs=[vm] * 6 + [any_spec] * 3,
        scratch_shapes=scratch,
        compiler_params=pltpu.CompilerParams(
            collective_id=1, has_side_effects=True, vmem_limit_bytes=63 * 2**20
        ),
    )(tokens, d_out, lengths, gain_rows, *tables, *weights, *saved)


def hand_on(*arrays):
    n = len(arrays) - 1

    def kernel(*refs):
        sources, targets, sems = refs[: n + 1], refs[n + 1 : 2 * n + 2], refs[-1]
        copies = [
            pltpu.make_async_copy(sources[i], targets[i], sems.at[i]) for i in range(n)
        ]
        for copy in copies:
            copy.start()
        targets[n][...] = sources[n][:, : targets[n].shape[1]]
        for copy in copies:
            copy.wait()

    any_spec = pl.BlockSpec(memory_space=pl.ANY)
    vm = pl.BlockSpec(memory_space=pltpu.VMEM)
    shapes = [jax.ShapeDtypeStruct(a.shape, a.dtype) for a in arrays[:n]]
    shapes.append(jax.ShapeDtypeStruct((arrays[n].shape[0], 4), arrays[n].dtype))
    return pl.pallas_call(
        kernel,
        out_shape=shapes,
        in_specs=[vm] * (n + 1),
        out_specs=[any_spec] * n + [vm],
        scratch_shapes=[pltpu.SemaphoreType.DMA((n,))],
    )(*arrays)


def layer_norm(values, gain_vec):
    center = values - jnp.mean(values, axis=-1, keepdims=True)
    spread = jnp.mean(center * center, axis=-1, keepdims=True)
    return center * lax.rsqrt(spread + epsilon) * gain_vec


def norm_back(values, gain_vec, upstream):
    unused, pullback = jax.vjp(layer_norm, values, gain_vec)
    return pullback(upstream)


def rotate(values, cosine_table, sine_table, direction):
    half_dim = values.shape[-1] // 2
    first_half = values[..., :half_dim]
    second_half = values[..., half_dim:]
    return jnp.concatenate(
        [
            first_half * cosine_table - direction * second_half * sine_table,
            second_half * cosine_table + direction * first_half * sine_table,
        ],
        axis=-1,
    )


def doc_layout(lengths, row_len):
    doc_ends = jnp.cumsum(lengths, axis=-1)
    places = jnp.arange(row_len, dtype=jnp.int32)
    passed = places[None, :, None] >= doc_ends[:, None, :]
    segment = jnp.sum(passed.astype(jnp.int32), axis=-1)
    starts = jnp.sum(jnp.where(passed, lengths[:, None, :], 0), axis=-1)
    position = places[None, :] - starts
    is_valid = places[None, :] < doc_ends[:, DOCS - 2][:, None]
    return (segment[0], position[0], is_valid[0])


def allowed_keys(own_seg, own_place, seg_full, first_key, block_rows):
    key_place = first_key + jnp.arange(block_rows, dtype=jnp.int32)
    key_seg = lax.dynamic_slice_in_dim(seg_full, first_key, block_rows)
    return (own_seg[:, None] == key_seg[None, :]) & (key_place[None, :] <= own_place[:, None])


def make_fold(queries, own_seg, own_place, seg_full, score_scale):

    def fold_piece(fold_state, piece, start):
        key_piece, value_piece = piece
        piece_rows = key_piece.shape[0]
        block_rows = math.gcd(piece_rows, 256)
        block_count = piece_rows // block_rows
        key_blocks = key_piece.reshape((block_count, block_rows) + key_piece.shape[1:])
        value_blocks = value_piece.reshape((block_count, block_rows) + value_piece.shape[1:])

        def step_block(carried, block_items):
            row_max, row_sum, weighted = carried
            key_block, value_block, block_id = block_items
            allowed = allowed_keys(own_seg, own_place, seg_full, block_id * block_rows, block_rows)
            scores = (
                jnp.einsum("qhd,khd->hqk", queries, key_block, preferred_element_type=jnp.float32)
                * score_scale
            )
            scores = jnp.where(allowed[None], scores, masked_score)
            new_max = jnp.maximum(row_max, jnp.max(scores, axis=-1))
            factor = jnp.exp(row_max - new_max)
            shifted = jnp.where(allowed[None], jnp.exp(scores - new_max[..., None]), 0.0)
            row_sum = row_sum * factor + jnp.sum(shifted, axis=-1)
            weighted = weighted * factor[..., None] + jnp.einsum(
                "hqk,khd->hqd",
                shifted.astype(jnp.bfloat16),
                value_block,
                preferred_element_type=jnp.float32,
            )
            return ((new_max, row_sum, weighted), None)

        block_ids = jnp.arange(block_count, dtype=jnp.int32)
        fold_state, unused = lax.scan(step_block, fold_state, (key_blocks, value_blocks, block_ids))
        return fold_state

    return fold_piece


def per_device(tokens, lengths, w_qkv, w_out, w_up, w_down, gains, d_out):
    tok_rows, model_width = tokens.shape
    row_len = tok_rows * lax.axis_size("ctx")
    head_count = HEADS
    head_dim = model_width // head_count
    score_scale = head_dim ** (-0.5)
    head_shape = (tok_rows, head_count, head_dim)
    seg_full, pos_full, valid_full = doc_layout(lengths, row_len)
    offset = lax.axis_index("ctx") * tok_rows
    own_seg = lax.dynamic_slice_in_dim(seg_full, offset, tok_rows)
    own_pos = lax.dynamic_slice_in_dim(pos_full, offset, tok_rows)
    own_valid = lax.dynamic_slice_in_dim(valid_full.astype(jnp.float32), offset, tok_rows)
    own_place = offset + jnp.arange(tok_rows, dtype=jnp.int32)
    freq_index = jnp.arange(head_dim // 2, dtype=jnp.float32)
    angles = own_pos.astype(jnp.float32)[:, None] * 10000.0 ** (-2.0 * freq_index / head_dim)
    cosine_table = jnp.cos(angles)[:, None, :]
    sine_table = jnp.sin(angles)[:, None, :]
    qkv_full, out_full, up_full, down_full, gain_full = (
        lax.all_gather(w_qkv, ("dp", "ctx"), axis=0, tiled=True),
        lax.all_gather(w_out, ("dp", "ctx"), axis=0, tiled=True),
        lax.all_gather(w_up, ("dp", "ctx"), axis=0, tiled=True),
        lax.all_gather(w_down, ("dp", "ctx"), axis=0, tiled=True),
        lax.all_gather(gains, ("dp", "ctx"), axis=0, tiled=True),
    )
    gain_f = gain_full.astype(jnp.float32)
    stream = tokens.astype(jnp.float32)
    normed = layer_norm(stream, gain_f[:, 0]).astype(jnp.bfloat16)
    qkv_raw = jnp.dot(normed, qkv_full, preferred_element_type=jnp.float32)
    queries = rotate(
        qkv_raw[:, :model_width].reshape(head_shape), cosine_table, sine_table, 1.0
    ).astype(jnp.bfloat16)
    key_heads = rotate(
        qkv_raw[:, model_width : 2 * model_width].reshape(head_shape), cosine_table, sine_table, 1.0
    ).astype(jnp.bfloat16)
    value_heads = qkv_raw[:, 2 * model_width :].reshape(head_shape).astype(jnp.bfloat16)
    start_state = (
        jnp.full((head_count, tok_rows), masked_score, jnp.float32),
        jnp.zeros((head_count, tok_rows), jnp.float32),
        jnp.zeros((head_count, tok_rows, head_dim), jnp.float32),
    )
    fold_piece = make_fold(queries, own_seg, own_place, seg_full, score_scale)
    row_max, row_sum, weighted = fold_piece(
        start_state,
        (
            lax.all_gather(key_heads, "ctx", axis=0, tiled=True),
            lax.all_gather(value_heads, "ctx", axis=0, tiled=True),
        ),
        jnp.int32(0),
    )
    attended = jnp.transpose(weighted / row_sum[..., None], (1, 0, 2))
    attended_b = attended.reshape(tok_rows, model_width).astype(jnp.bfloat16)
    attn_raw = jnp.dot(attended_b, out_full, preferred_element_type=jnp.float32)
    hidden = stream + layer_norm(attn_raw, gain_f[:, 1])
    mlp_in = layer_norm(hidden, gain_f[:, 2]).astype(jnp.bfloat16)
    up_proj = jnp.dot(mlp_in, up_full, preferred_element_type=jnp.float32)
    activated = jax.nn.gelu(up_proj).astype(jnp.bfloat16)
    mlp_raw = jnp.dot(activated, down_full, preferred_element_type=jnp.float32)
    result = hidden + layer_norm(mlp_raw, gain_f[:, 3])
    output = (result * own_valid[:, None]).astype(jnp.bfloat16)
    qkv_back, out_back, up_back, down_back = (
        lax.all_gather(w_qkv, ("dp", "ctx"), axis=0, tiled=True),
        lax.all_gather(w_out, ("dp", "ctx"), axis=0, tiled=True),
        lax.all_gather(w_up, ("dp", "ctx"), axis=0, tiled=True),
        lax.all_gather(w_down, ("dp", "ctx"), axis=0, tiled=True),
    )
    upstream = d_out.astype(jnp.float32) * own_valid[:, None]
    d_mlp, d_gain_four = norm_back(mlp_raw, gain_f[:, 3], upstream)
    d_mlp_b = d_mlp.astype(jnp.bfloat16)
    grad_down = jnp.einsum("tf,td->fd", activated, d_mlp_b, preferred_element_type=jnp.float32)
    d_activated = jnp.einsum("td,fd->tf", d_mlp_b, down_back, preferred_element_type=jnp.float32)
    unused, gelu_pull = jax.vjp(jax.nn.gelu, up_proj)
    d_up_b = gelu_pull(d_activated)[0].astype(jnp.bfloat16)
    grad_up = jnp.einsum("td,tf->df", mlp_in, d_up_b, preferred_element_type=jnp.float32)
    d_mlp_in = jnp.einsum("tf,df->td", d_up_b, up_back, preferred_element_type=jnp.float32)
    d_hidden_part, d_gain_three = norm_back(hidden, gain_f[:, 2], d_mlp_in)
    d_hidden = upstream + d_hidden_part
    d_attn, d_gain_two = norm_back(attn_raw, gain_f[:, 1], d_hidden)
    d_attn_b = d_attn.astype(jnp.bfloat16)
    grad_out = jnp.einsum("td,te->de", attended_b, d_attn_b, preferred_element_type=jnp.float32)
    d_attended = (
        jnp.einsum("te,de->td", d_attn_b, out_back, preferred_element_type=jnp.float32)
        .astype(jnp.bfloat16)
        .reshape(head_shape)
    )
    row_dot = jnp.einsum("qhd,qhd->hq", d_attended.astype(jnp.float32), attended)
    key_all, value_all = (
        lax.all_gather(key_heads, "ctx", axis=0, tiled=True),
        lax.all_gather(value_heads, "ctx", axis=0, tiled=True),
    )
    block_rows = math.gcd(row_len, 256)
    block_count = row_len // block_rows
    key_blocks = key_all.reshape((block_count, block_rows) + key_all.shape[1:])
    value_blocks = value_all.reshape((block_count, block_rows) + value_all.shape[1:])

    def back_block(d_queries, block_items):
        key_block, value_block, block_id = block_items
        allowed = allowed_keys(own_seg, own_place, seg_full, block_id * block_rows, block_rows)
        scores = (
            jnp.einsum("qhd,khd->hqk", queries, key_block, preferred_element_type=jnp.float32)
            * score_scale
        )
        attn_prob = jnp.where(
            allowed[None], jnp.exp(scores - row_max[..., None]) / row_sum[..., None], 0.0
        )
        d_prob = jnp.einsum(
            "qhd,khd->hqk", d_attended, value_block, preferred_element_type=jnp.float32
        )
        d_scores = (attn_prob * (d_prob - row_dot[..., None])).astype(jnp.bfloat16)
        d_queries = (
            d_queries
            + jnp.einsum("hqk,khd->qhd", d_scores, key_block, preferred_element_type=jnp.float32)
            * score_scale
        )
        d_keys = (
            jnp.einsum("hqk,qhd->khd", d_scores, queries, preferred_element_type=jnp.float32)
            * score_scale
        )
        d_values = jnp.einsum(
            "hqk,qhd->khd",
            attn_prob.astype(jnp.bfloat16),
            d_attended,
            preferred_element_type=jnp.float32,
        )
        return (d_queries, (d_keys, d_values))

    block_ids = jnp.arange(block_count, dtype=jnp.int32)
    d_queries, (d_keys_all, d_values_all) = lax.scan(
        back_block, jnp.zeros(head_shape, jnp.float32), (key_blocks, value_blocks, block_ids)
    )
    kv_terms = jnp.concatenate(
        [d_keys_all.reshape(row_len, model_width), d_values_all.reshape(row_len, model_width)],
        axis=-1,
    )
    kv_grad = lax.psum_scatter(
        kv_terms.astype(jnp.bfloat16), "ctx", scatter_dimension=0, tiled=True
    ).astype(jnp.float32)
    d_keys = kv_grad[:, :model_width].reshape(head_shape)
    d_qkv = jnp.concatenate(
        [
            rotate(d_queries, cosine_table, sine_table, -1.0).reshape(tok_rows, model_width),
            rotate(d_keys, cosine_table, sine_table, -1.0).reshape(tok_rows, model_width),
            kv_grad[:, model_width:],
        ],
        axis=-1,
    ).astype(jnp.bfloat16)
    grad_qkv = jnp.einsum("td,te->de", normed, d_qkv, preferred_element_type=jnp.float32)
    d_normed = jnp.einsum("te,de->td", d_qkv, qkv_back, preferred_element_type=jnp.float32)
    d_stream_part, d_gain_one = norm_back(stream, gain_f[:, 0], d_normed)
    d_tokens = (d_hidden + d_stream_part).astype(jnp.bfloat16)
    grad_gains = jnp.stack([d_gain_one, d_gain_two, d_gain_three, d_gain_four], axis=-1)
    shard_qkv, shard_out, shard_up, shard_down, shard_gains = (
        lax.psum_scatter(grad_qkv, ("dp", "ctx"), scatter_dimension=0, tiled=True),
        lax.psum_scatter(grad_out, ("dp", "ctx"), scatter_dimension=0, tiled=True),
        lax.psum_scatter(grad_up, ("dp", "ctx"), scatter_dimension=0, tiled=True),
        lax.psum_scatter(grad_down, ("dp", "ctx"), scatter_dimension=0, tiled=True),
        lax.psum_scatter(grad_gains, ("dp", "ctx"), scatter_dimension=0, tiled=True),
    )
    return (output, d_tokens, shard_qkv, shard_out, shard_up, shard_down, shard_gains)


def fused_device(tokens, lengths, w_qkv, w_out, w_up, w_down, gains, d_out):
    rows, width = tokens.shape
    row_len = rows * lax.axis_size("ctx")
    gains_wide = jnp.pad(gains, ((0, 0), (0, 128 - gains.shape[1])))
    tables = tuple(jnp.asarray(v) for v in turn_tables(row_len, width // HEADS))
    output, wq, wo, wu, wd, gain_rows, *saved = forward(
        tokens, lengths, gains_wide, w_qkv, w_out, w_up, w_down, tables
    )
    d_tokens, grad_qkv, grad_out, grad_up, grad_down, grad_gains = backward(
        tokens,
        d_out,
        lengths,
        gain_rows,
        tables,
        (wq, wo, wu, wd),
        saved,
        (w_qkv, w_out, w_up, w_down),
    )[:6]
    return tuple(
        hand_on(output, d_tokens, grad_qkv, grad_out, grad_up, grad_down, grad_gains)
    )


def layer(mesh):
    if mesh.shape["dp"] == 16 and mesh.shape["ctx"] == 2:
        return fused_device
    return per_device


def solution(mesh):
    return jax.shard_map(
        layer(mesh),
        mesh=mesh,
        in_specs=(
            P(("dp", "ctx"), None),
            P("dp", None),
            P(("dp", "ctx"), None),
            P(("dp", "ctx"), None),
            P(("dp", "ctx"), None),
            P(("dp", "ctx"), None),
            P(("dp", "ctx"), None),
            P(("dp", "ctx"), None),
        ),
        out_specs=(
            P(("dp", "ctx"), None),
            P(("dp", "ctx"), None),
            P(("dp", "ctx"), None),
            P(("dp", "ctx"), None),
            P(("dp", "ctx"), None),
            P(("dp", "ctx"), None),
            P(("dp", "ctx"), None),
        ),
        check_vma=False,
    )
```

```python
import functools
import math

import jax
import jax.numpy as jnp
import numpy as np
from jax import lax
from jax.experimental import pallas as pl
from jax.experimental.pallas import tpu as pltpu
from jax.sharding import PartitionSpec as P

HEADS = 16
DOCS = 7

GATHER_BY_Z = (False, None, None, True)
SHARE_BY_Z = (None, None, None, None)

TOKENS = 999
GATHER_PLAN = {
    "norm": {
        0: (41, 110, 230, 100, 320, 140, 330, 0, 400, 51, 141, 10, 130, 150, 40, 42, 142, 62, 52, 50, 30, 151, 160, 60, 152, 999, 410, 63, 61, 430, 162, 161, 340,),
    },
    "qkv": {
        0: (241, 163, 420, 240,),
    },
    "k": {
        0: (210,),
    },
    "v": {
        1: (350,),
    },
    "pair": {
        2: (250, 342,),
        6: (242, 251, 341,),
        7: (352,),
    },
    "other": {
        0: (252,),
    },
    "more": {
        0: (351, 450,),
        1: (360, 452, 260,),
        2: (460,),
        3: (261,),
        4: (361, 262, 442,),
        5: (440,),
        6: (451, 263, 441,),
    },
    "out": {
        0: (362,),
    },
    "to up": {
        0: (363, 463,),
    },
    "up": {
        0: (461,),
        5: (462,),
    },
    "start": {
        0: (300, 20, 120, 200, 310, 220,),
    },
}

NEAR = ((1, 2, 3), (0, 2, 3), (1, 3, 0), (2, 1, 0))
FAR = ((3, 2, 1), (3, 0, 2), (0, 1, 3), (0, 1, 2))

SHARE_PLAN = {
    "du": {
        4: (0,),
    },
    "up": {
        0: (10,),
    },
    "norm": {
        0: (1,),
    },
    "do": {
        0: (2,),
    },
    "out": {
        0: (100,),
    },
    "more": {
        1: (101,),
        5: (12,),
        6: (111, 11,),
    },
    "pair": {
        0: (110, 200,),
        1: (202,),
        3: (102,),
        4: (212,),
        5: (201, 211,),
        6: (112,),
    },
    "half": {
        0: (210,),
    },
    "input": {
        0: (300, 302, 301, 3,),
    },
    "gains": {
        0: (401, 103, 120, 312, 311, 402,),
    },
    "end": {
        0: (310, 400, 500, 501, 502, 503, 411, 403, 303, 320, 412, 512, 410, 510, 203, 511, 20, 130, 220, 330, 420, 520, 30, 230, 430, 530,),
    },
}

epsilon = 1e-05
masked_score = -1e30


MESH = pl.DeviceIdType.MESH


def when(condition, body):
    if isinstance(condition, bool):
        if condition:
            body()
    else:
        pl.when(condition)(body)


def unless(condition, body):
    if isinstance(condition, bool):
        if not condition:
            body()
    else:
        pl.when(jnp.logical_not(condition))(body)


def pick(condition, one, other):
    if isinstance(condition, bool):
        return one if condition else other
    return jnp.where(condition, one, other)


class Place:
    def __init__(self, dp_size):
        dp = lax.axis_index("dp")
        self.Z = dp_size // 4
        self.z = lax.div(dp, 4)
        self.x = lax.rem(lax.div(dp, 2), 2)
        self.c = lax.rem(dp, 2)
        self.y = lax.axis_index("ctx")
        c, x, y = self.c, self.x, self.y
        self.i2 = y * (1 - c) + x * c
        self.i3 = x * (1 - c) + y * c
        self.sib = self.device(self.z, x, 1 - c, y)
        self.p2 = self.device(self.z, x * (1 - c) + (1 - x) * c, c, (1 - y) * (1 - c) + y * c)
        self.p3 = self.device(self.z, (1 - x) * (1 - c) + x * c, c, y * (1 - c) + (1 - y) * c)

    def device(self, z, x, c, y):
        return ((z * 2 + x) * 2 + c, y)

    def above(self, k):
        return lax.rem(self.z + k, self.Z)

    def below(self, k):
        return lax.rem(self.z - k + self.Z, self.Z)

    def at_z(self, z):
        return self.device(z, self.x, self.c, self.y)

    def near(self, j):
        if self.Z != 4:
            return self.below(j + 1)
        return sum(jnp.where(self.z == z, row[j], 0) for z, row in enumerate(NEAR))

    def order(self, j):
        if j == self.Z - 1:
            return self.z
        if self.Z != 4:
            return self.above(j + 1)
        return sum(jnp.where(self.z == z, row[j], 0) for z, row in enumerate(FAR))

    def far(self, z):
        return jnp.abs(z - self.z) == self.Z - 1

    def between(self, z):
        last = self.Z - 1
        return ((z == 0) & (self.z == last - 1)) | ((z == last) & (self.z == 1))

    def block(self, z, a2, a3):
        c = self.c
        return (z * 2 + a3 * (1 - c) + a2 * c) * 2 + a2 * (1 - c) + a3 * c

    def row_block(self, z, a2, a3, core):
        c = self.c
        xx = a3 * (1 - c) + a2 * c
        yy = a2 * (1 - c) + a3 * c
        return ((z * 2 + xx) * 2 + core) * 2 + yy

    def barrier(self):
        bar = pltpu.get_barrier_semaphore()
        for device in (self.sib, self.p2, self.p3):
            pl.semaphore_signal(bar, 1, device_id=device, device_id_type=MESH)
        for k in range(1, self.Z):
            pl.semaphore_signal(
                bar, 1, device_id=self.at_z(self.above(k)), device_id_type=MESH
            )
        pl.semaphore_wait(bar, 3 + self.Z - 1)


class Gather:
    def __init__(self, place, shard, full, send, recv, by_z):
        self.g, self.shard, self.full = place, shard, full
        self.send, self.recv = send, recv
        self.rows = shard.shape[0]
        self.by_z = by_z
        Z = place.Z
        self.n_z = 0
        self.n_pass = 2 * Z
        self.n_p2 = 2 * Z + 2
        self.n_p3 = self.n_p2 + Z
        self.n_sib = self.n_p3 + 2 * Z
        self.n_own = self.n_sib + 2 * Z

    @staticmethod
    def sems(Z):
        return 7 * Z + 3

    def at(self, index):
        return self.full.at[pl.ds(pl.multiple_of(index * self.rows, self.rows), self.rows)]

    def copy(self, index, send, recv, device, src=None):
        return pltpu.make_async_remote_copy(
            src_ref=self.at(index) if src is None else src,
            dst_ref=self.at(index),
            send_sem=self.send.at[send],
            recv_sem=self.recv.at[recv],
            device_id=device,
            device_id_type=MESH,
        )

    def own_copy(self):
        g = self.g
        index = g.row_block(g.z, g.i2, g.i3, g.c)
        return pltpu.make_async_copy(self.shard, self.at(index), self.recv.at[self.n_own])

    def z_copy(self, other, z, src=None):
        g = self.g
        a2 = (1 - g.i2) if other else g.i2
        return self.copy(
            g.row_block(g.z, a2, g.i3, g.c),
            self.n_z + z * 2 + int(other),
            self.n_z + g.z * 2 + int(other),
            g.at_z(z),
            src,
        )

    def pass_copy(self, other, z):
        g = self.g
        a2 = (1 - g.i2) if other else g.i2
        return self.copy(
            g.row_block(z, a2, g.i3, g.c),
            self.n_pass + int(other),
            self.n_z + z * 2 + int(other),
            g.at_z(g.Z - 1 - z),
        )

    def p2_copy(self, z, src=None):
        g = self.g
        number = self.n_p2 + z
        return self.copy(g.row_block(z, g.i2, g.i3, g.c), number, number, g.p2, src)

    def p3_copy(self, z, a2, src=None):
        g = self.g
        number = self.n_p3 + z * 2 + a2
        return self.copy(g.row_block(z, a2, g.i3, g.c), number, number, g.p3, src)

    def sib_copy(self, z, xx, core):
        rows = 2 * self.rows
        spot = pl.ds(pl.multiple_of(((z * 2 + xx) * 2 + core) * rows, rows), rows)
        number = self.n_sib + z * 2 + xx
        return pltpu.make_async_remote_copy(
            src_ref=self.full.at[spot],
            dst_ref=self.full.at[spot],
            send_sem=self.send.at[number],
            recv_sem=self.recv.at[number],
            device_id=self.g.sib,
            device_id_type=MESH,
        )

    def wait(self, number, index):
        self.copy(index, number, number, self.g.sib).wait_recv()

    def each_z(self, act):
        g = self.g
        for k in range(1, g.Z):
            z = g.above(k)
            unless(g.far(z), lambda: act(z))

    def start_z(self):
        self.each_z(lambda z: self.z_copy(False, z, self.shard).start())

    def start_p2(self):
        self.p2_copy(self.g.z, self.shard).start()

    def start_p3(self):
        self.p3_copy(self.g.z, self.g.i2, self.shard).start()
        self.own_copy().start()

    def first(self):
        g = self.g
        o2 = 1 - g.i2
        self.wait(self.n_p2 + g.z, g.row_block(g.z, o2, g.i3, g.c))
        when(self.by_z, lambda: self.each_z(lambda z: self.z_copy(True, z).start()))
        self.p3_copy(g.z, o2).start()

    def relay(self, j, z, other):
        if j == self.g.Z - 2:
            pl.when(self.g.between(z))(lambda: self.pass_copy(other, z).start())

    def from_z(self, j):
        g = self.g
        z = g.near(j)
        self.wait(self.n_z + z * 2, g.row_block(z, g.i2, g.i3, g.c))
        self.relay(j, z, False)
        unless(self.by_z, lambda: self.p2_copy(z).start())
        self.p3_copy(z, g.i2).start()

    def from_p2(self, j):
        g = self.g
        z = g.near(j)
        o2 = 1 - g.i2
        number = pick(self.by_z, self.n_z + z * 2 + 1, self.n_p2 + z)
        self.wait(number, g.row_block(z, o2, g.i3, g.c))
        when(self.by_z, lambda: self.relay(j, z, True))
        self.p3_copy(z, o2).start()

    def from_p3(self, j):
        g = self.g
        z = g.near(j - 1) if j else g.z
        for a2 in (0, 1):
            self.wait(self.n_p3 + z * 2 + a2, g.row_block(z, a2, 1 - g.i3, g.c))
        if j == 0:
            self.own_copy().wait()
        for xx in (0, 1):
            self.sib_copy(z, xx, g.c).start()

    def complete(self):
        g = self.g
        for z in range(g.Z):
            for xx in (0, 1):
                self.sib_copy(z, xx, 1 - g.c).wait_recv()

    def sent(self):
        g, src = self.g, self.shard
        self.p2_copy(g.z, src).wait_send()
        self.p3_copy(g.z, g.i2, src).wait_send()
        self.each_z(lambda z: self.z_copy(False, z, src).wait_send())
        when(self.by_z, lambda: self.each_z(lambda z: self.z_copy(True, z).wait_send()))
        end = g.near(g.Z - 2)

        def passed():
            self.pass_copy(False, end).wait_send()
            when(self.by_z, lambda: self.pass_copy(True, end).wait_send())

        pl.when(g.between(end))(passed)
        for k in range(1, g.Z):
            z = g.above(k)
            unless(self.by_z, lambda: self.p2_copy(z).wait_send())
            self.p3_copy(z, g.i2).wait_send()
        for z in range(g.Z):
            self.p3_copy(z, 1 - g.i2).wait_send()
            for xx in (0, 1):
                self.sib_copy(z, xx, g.c).wait_send()


class Share:
    def __init__(self, place, part, first, landing, unit, n, send, recv, write, by_z, cols=None):
        self.g, self.part, self.first = place, part, first
        self.rec3, self.rec = landing
        self.unit, self.n, self.send, self.recv, self.write = unit, n, send, recv, write
        self.kind, self.by_z = part.dtype, by_z
        self.cols = pl.ds(0, part.shape[-1]) if cols is None else cols

    @staticmethod
    def sems(Z):
        return 4 * Z - 1

    def copy(self, block, landing, slot, number, device):
        rows = slice(None)
        return pltpu.make_async_remote_copy(
            src_ref=self.part.at[pl.ds(self.first, self.n), block, rows, self.cols],
            dst_ref=landing.at[pl.ds(self.unit, self.n), slot, rows, self.cols],
            send_sem=self.send.at[number],
            recv_sem=self.recv.at[number],
            device_id=device,
            device_id_type=MESH,
        )

    def p3_copy(self, z, a2):
        g = self.g
        slot = z * 2 + a2
        return self.copy(g.block(z, a2, 1 - g.i3), self.rec3, slot, slot, g.p3)

    def p2_copy(self, z):
        g = self.g
        slot = pick(self.by_z, 0, z)
        block = g.block(z, 1 - g.i2, g.i3)
        return self.copy(block, self.rec, slot, 2 * g.Z + slot, g.p2)

    def z_slot(self, k, a2, by_z):
        return 1 + (k - 1) * 2 + a2 if by_z else self.g.Z + k - 1

    def z_copy(self, z, a2, by_z):
        g = self.g
        slot = self.z_slot(lax.rem(z - g.z + g.Z, g.Z), a2, by_z)
        return self.copy(g.block(z, a2, g.i3), self.rec, slot, 2 * g.Z + slot, g.at_z(z))

    def z_wait(self, k, a2, by_z):
        g = self.g
        slot = self.z_slot(k, a2, by_z)
        block = g.block(g.z, a2, g.i3)
        self.copy(block, self.rec, slot, 2 * g.Z + slot, g.sib).wait_recv()
        return self.landed(self.rec, slot)

    def landed(self, ref, slot):
        return ref[pl.ds(self.unit, self.n), slot, :, self.cols].astype(jnp.float32)

    def own(self, block):
        return self.part[pl.ds(self.first, self.n), block, :, self.cols].astype(jnp.float32)

    def add_to(self, block, ref, slot):
        spot = (pl.ds(self.first, self.n), block, slice(None), self.cols)
        self.part[spot] += ref[pl.ds(self.unit, self.n), slot, :, self.cols]

    def put(self, block, total):
        self.part[pl.ds(self.first, self.n), block, :, self.cols] = total.astype(self.kind)

    def start(self, z):
        for a2 in (0, 1):
            self.p3_copy(z, a2).start()

    def start_all(self):
        for j in range(self.g.Z):
            self.start(self.g.order(j))

    def add3(self, z, a2):
        g = self.g
        self.p3_copy(z, a2).wait_recv()
        self.add_to(g.block(z, a2, g.i3), self.rec3, z * 2 + a2)

    def stage3(self, j):
        g = self.g
        z = g.order(j)
        o2 = 1 - g.i2
        own = j == g.Z - 1
        self.add3(z, o2)
        if not own:
            when(self.by_z, lambda: self.z_copy(z, o2, True).start())
        unless(self.by_z, lambda: self.p2_copy(z).start())
        self.add3(z, g.i2)
        if not own:
            when(self.by_z, lambda: self.z_copy(z, g.i2, True).start())

    def stage2(self, j):
        g = self.g

        def with_p2():
            z = g.order(j)
            self.p2_copy(z).wait_recv()
            self.add_to(g.block(z, g.i2, g.i3), self.rec, z)
            self.z_copy(z, g.i2, False).start()

        unless(self.by_z, with_p2)

    def sum_z(self):
        g = self.g

        def along_z():
            o2 = 1 - g.i2
            block = g.block(g.z, o2, g.i3)
            total = self.own(block)
            for k in range(1, g.Z):
                total += self.z_wait(k, o2, True)
            self.put(block, total)
            self.p2_copy(g.z).start()

        when(self.by_z, along_z)

    def last(self):
        g = self.g

        def finish(by_z):
            total = self.own(g.block(g.z, g.i2, g.i3))
            for k in range(1, g.Z):
                total += self.z_wait(k, g.i2, by_z)
            self.p2_copy(g.z).wait_recv()
            total += self.landed(self.rec, 0 if by_z else g.z)
            self.write(total)

        when(self.by_z, lambda: finish(True))
        unless(self.by_z, lambda: finish(False))

    def sent(self):
        g = self.g
        for z in range(g.Z):
            for a2 in (0, 1):
                self.p3_copy(z, a2).wait_send()

        def by_z():
            self.p2_copy(g.z).wait_send()
            for k in range(1, g.Z):
                for a2 in (0, 1):
                    self.z_copy(g.above(k), a2, True).wait_send()

        def by_p2():
            for z in range(g.Z):
                self.p2_copy(z).wait_send()
            for k in range(1, g.Z):
                self.z_copy(g.above(k), g.i2, False).wait_send()

        when(self.by_z, by_z)
        unless(self.by_z, by_p2)


def loop(count):
    def run(body):
        def step(i, carry):
            body(i)
            return carry

        lax.fori_loop(0, count, step, 0)

    return run


def run_at(t, events):
    for i, event in events.items():
        pl.when(t == i)(event)


def dot(a, b):
    return jnp.dot(a, b, preferred_element_type=jnp.float32)


def dot_nt(a, b):
    return lax.dot_general(a, b, (((1,), (1,)), ((), ())), preferred_element_type=jnp.float32)


def normed(v):
    center = v - jnp.mean(v, axis=-1, keepdims=True)
    r = lax.rsqrt(jnp.mean(center * center, axis=-1, keepdims=True) + epsilon)
    return center * r, r


def norm_pull(v, gain, e):
    z, r = normed(v)
    f = e * gain
    dv = r * (
        f
        - jnp.mean(f, axis=-1, keepdims=True)
        - z * jnp.mean(f * z, axis=-1, keepdims=True)
    )
    return dv, e * z


def turn(u, cosine, sine, half):
    lane = lax.broadcasted_iota(jnp.int32, u.shape, 1)
    swapped = jnp.where(
        lax.rem(lane, 2 * half) < half,
        pltpu.roll(u, u.shape[1] - half, 1),
        pltpu.roll(u, half, 1),
    )
    return u * cosine + swapped * sine


def turn_tables(row_len, head_dim):
    half = head_dim // 2
    inverse = 10000.0 ** (-2.0 * np.arange(half) / head_dim)
    angles = np.arange(row_len)[:, None] * inverse[None, :]
    cosine = np.tile(np.cos(angles), (1, 4))
    sine = np.tile(np.concatenate([-np.sin(angles), np.sin(angles)], axis=1), (1, 2))
    return cosine.astype(np.float32), sine.astype(np.float32)


def doc_ends(lens):
    ends = [lens[0, 0]]
    for d in range(1, DOCS):
        ends.append(ends[-1] + lens[0, d])
    return ends


def fill_bias(bias, lens, first, rows):
    ends = doc_ends(lens)
    block = 128
    blocks = bias.shape[1] // block

    @loop(bias.shape[0] * blocks)
    def _(i):
        place = first + lax.broadcasted_iota(jnp.int32, (1, rows), 1)
        key = i * block + lax.broadcasted_iota(jnp.int32, (block, rows), 0)
        start = jnp.zeros((1, rows), jnp.int32)
        for d in range(DOCS):
            start = jnp.where(place >= ends[d], ends[d], start)
        fine = (key >= start) & (key <= place)
        spot = pl.ds(lax.rem(i, blocks) * block, block)
        bias[lax.div(i, blocks), spot, :] = jnp.where(fine, 0.0, masked_score)


def split_heads(v, axis=1):
    spot = lax.broadcasted_iota(jnp.int32, v.shape, axis)
    first = spot < v.shape[axis] // 2
    zero = jnp.zeros_like(v)
    return jnp.where(first, v, zero), jnp.where(first, zero, v)


class Tiles:
    def __init__(self, source, buffer, sems, ready=None):
        self.source, self.buffer, self.sems, self.ready = source, buffer, sems, ready
        self.depth = buffer.shape[0]

    def copy(self, t):
        slot = lax.rem(t, self.depth)
        return pltpu.make_async_copy(self.source(t), self.buffer.at[slot], self.sems.at[slot])

    def start(self, t):
        if self.ready is not None:
            self.ready(t)
        self.copy(t).start()

    def first(self, end, begin=0):
        for t in range(begin, min(begin + self.depth - 1, end)):
            self.start(jnp.int32(t))

    def get(self, t, end):
        later = t + self.depth - 1

        @pl.when(later < end)
        def _():
            self.start(later)

        self.copy(t).wait()
        return self.buffer[lax.rem(t, self.depth)]


def columns(t, size):
    return pl.ds(pl.multiple_of(t * size, size), size)


def forward_kernel(dp_size, head_dim, *refs):
    (tok, lens, gs, wq, wo, wu, wd, cosine, sine) = refs[:9]
    (out, wq_f, wo_f, wu_f, wd_f, gain_o, q_o, k_o, v_o, ob_o, lse_o) = refs[9:20]
    (araw_o, h_o, mraw_o, bt_o, gt_o, gp_o, at_o, atx_o, tokx_o) = refs[20:29]
    (g_full, gain, tokx, a, ax, at, atx, q, k, v, vt, bias, ob, lse) = refs[29:43]
    (araw, h, mraw, b, bt, act, actt, gp, wbuf, dbuf) = refs[43:53]
    sems = refs[53:63]
    wsem, dsem, xsem, osem = refs[63:67]
    o_own = refs[67]
    g = Place(dp_size)
    y = g.y
    rows, width = tok.shape
    half = head_dim // 2
    pairs = width // 128
    scale = head_dim ** (-0.5)
    modes = [g.c == 0 if m is None else m for m in GATHER_BY_Z]
    gg, gq, go, gu, gd = [
        Gather(g, s, f, sems[2 * i], sems[2 * i + 1], mode)
        for i, (s, f, mode) in enumerate(
            (
                (gs, g_full, False),
                (wq, wq_f, modes[0]),
                (wo, wo_f, modes[1]),
                (wu, wu_f, modes[2]),
                (wd, wd_f, modes[3]),
            )
        )
    ]
    Z = g.Z
    saves = []

    def save(src, dst):
        copy = pltpu.make_async_copy(src, dst, osem.at[len(saves)])
        copy.start()
        saves.append(copy)

    tok_copy = pltpu.make_async_remote_copy(
        src_ref=tok,
        dst_ref=tokx,
        send_sem=xsem.at[0],
        recv_sem=xsem.at[1],
        device_id=g.device(g.z, g.x, g.c, 1 - y),
        device_id_type=MESH,
    )
    matrices = (gg, gq, go, gu, gd)

    def serve(name, i=0):
        for step in GATHER_PLAN.get(name, {}).get(i, ()):
            if step == TOKENS:
                pl.when(y == 0)(lambda: tok_copy.start())
                continue
            m, kind, j = matrices[step // 100], step // 10 % 10, step % 10
            if kind < 4:
                (m.start_p2, m.start_p3, m.start_z, m.first)[kind]()
            else:
                (m.from_z, m.from_p2, m.from_p3)[kind - 4](j)

    def serve_at(name, t, count):
        for i in range(count):
            if i in GATHER_PLAN.get(name, {}):
                pl.when(t == i)(functools.partial(serve, name, i))

    g.barrier()
    serve("start")
    fill_bias(bias, lens, y * rows, rows)
    serve("norm")
    gg.complete()
    turned = jnp.transpose(g_full[...].astype(jnp.float32))
    gain[...] = turned[:8]
    save(gain, gain_o)

    def first_norm(src, dst, dst_t):
        @loop(rows // 128)
        def _(i):
            spot = pl.ds(i * 128, 128)
            z, _r = normed(src[spot, :].astype(jnp.float32))
            value = z * gain[0:1, :]
            dst[spot, :] = value.astype(jnp.bfloat16)
            dst_t[:, spot] = jnp.transpose(value).astype(jnp.bfloat16)

    first_norm(tok, a, at)
    save(at, at_o)
    serve("qkv")
    gq.complete()

    tiles = Tiles(lambda t: wq_f.at[:, columns(t, 512)], wbuf, wsem)
    per = width // 512
    first = pl.multiple_of(y * rows, rows)

    def turned_pair(u, start):
        return turn(u, cosine[pl.ds(start, rows), :], sine[pl.ds(start, rows), :], half)

    tiles.first(3 * per)

    @loop(per)
    def _(t):
        serve_at("q", t, per)
        u = dot(a[...], tiles.get(t, 3 * per))
        for j in range(4):
            part = turned_pair(u[:, j * 128 : j * 128 + 128], first) * scale
            q[4 * t + j] = part.astype(jnp.bfloat16)

    def keys(w, t, src, start):
        u = dot(src[...], w)
        for j in range(4):
            part = turned_pair(u[:, j * 128 : j * 128 + 128], start)
            k[4 * t + j, pl.ds(start, rows), :] = part.astype(jnp.bfloat16)

    def values(w, t, src, start):
        u = dot(src[...], w)
        ut = jnp.transpose(u).astype(jnp.bfloat16)
        for j in range(4):
            cols = slice(j * 128, j * 128 + 128)
            v[4 * t + j, pl.ds(start, rows), :] = u[:, cols].astype(jnp.bfloat16)
            vt[4 * t + j, :, pl.ds(start, rows)] = ut[cols]

    @loop(per)
    def _(t):
        serve_at("k", t, per)
        keys(tiles.get(t + per, 3 * per), t, a, first)

    @loop(per)
    def _(t):
        serve_at("v", t, per)
        values(tiles.get(t + 2 * per, 3 * per), t, a, first)

    def attend(p, block, keys_at):
        spot = slice(block * 256, block * 256 + 256)
        heads = split_heads(q[p, spot, :])
        kk = k[p, keys_at, :]
        vv = vt[p, :, keys_at]
        mask = bias[0, keys_at, spot]
        parts, logs = [], []
        for i in (0, 1):
            s = dot_nt(kk, heads[i]) + mask
            m = jnp.max(s, axis=0, keepdims=True)
            e = jnp.exp(s - m)
            total = jnp.sum(e, axis=0, keepdims=True)
            logs.append(m + jnp.log(total))
            parts.append(dot(vv, e.astype(jnp.bfloat16)) * (1.0 / total))
        return spot, parts, logs

    upper = lax.broadcasted_iota(jnp.int32, (128, 256), 0) < head_dim
    blocks = rows // 256

    @loop(pairs)
    def _(p):
        serve_at("pair", p, pairs)
        for block in range(blocks):
            spot, parts, logs = attend(p, block, pl.ds(first, (block + 1) * 256))
            for i in (0, 1):
                lse[p, i : i + 1, spot] = logs[i]
            o_own[p, :, spot] = jnp.where(upper, parts[0], parts[1])

    serve("other")

    @pl.when(y == 1)
    def _():
        tok_copy.wait_recv()
        first_norm(tokx, ax, atx)
        tiles.first(3 * per, per)

        @loop(per)
        def _(t):
            keys(tiles.get(t + per, 3 * per), t, ax, 0)

        @loop(per)
        def _(t):
            values(tiles.get(t + 2 * per, 3 * per), t, ax, 0)

    save(atx, atx_o)
    save(tokx, tokx_o)
    save(q, q_o)
    save(k, k_o)
    save(v, v_o)

    @pl.when(y == 0)
    def _():
        @loop(pairs)
        def _(p):
            serve_at("more", p, pairs)
            ob[p] = o_own[p].astype(jnp.bfloat16)

    @pl.when(y == 1)
    def _():
        @loop(pairs)
        def _(p):
            serve_at("more", p, pairs)
            for block in range(blocks):
                spot, parts, logs = attend(p, block, pl.ds(0, rows))
                shares = []
                for i in (0, 1):
                    old = lse[p, i : i + 1, spot]
                    top = jnp.maximum(old, logs[i])
                    both = top + jnp.log(jnp.exp(old - top) + jnp.exp(logs[i] - top))
                    lse[p, i : i + 1, spot] = both
                    shares.append((jnp.exp(old - both), jnp.exp(logs[i] - both)))
                own = o_own[p, :, spot]
                first_head = own * shares[0][0] + parts[0] * shares[0][1]
                second_head = own * shares[1][0] + parts[1] * shares[1][1]
                ob[p, :, spot] = jnp.where(upper, first_head, second_head).astype(jnp.bfloat16)

    save(ob, ob_o)
    save(lse, lse_o)

    serve("out")
    go.complete()
    tiles = Tiles(lambda t: wo_f.at[:, columns(t, 512)], wbuf, wsem)
    tiles.first(per)
    a[...] = jnp.transpose(ob[...].reshape(width, rows))

    @loop(per)
    def _(t):
        w = tiles.get(t, per)
        araw[:, columns(t, 512)] = dot(a[...], w)

    save(araw, araw_o)

    @loop(rows // 128)
    def _(i):
        spot = pl.ds(i * 128, 128)
        z, _r = normed(araw[spot, :])
        hidden = tok[spot, :].astype(jnp.float32) + z * gain[1:2, :]
        h[spot, :] = hidden
        z, _r = normed(hidden)
        value = z * gain[2:3, :]
        b[spot, :] = value.astype(jnp.bfloat16)
        bt[:, spot] = jnp.transpose(value).astype(jnp.bfloat16)

    save(h, h_o)
    save(bt, bt_o)

    serve("to up")
    gu.complete()
    tiles = Tiles(lambda t: wu_f.at[:, columns(t, 512)], wbuf, wsem)
    ups = act.shape[0]
    tiles.first(ups)
    c0 = math.sqrt(2.0 / math.pi)

    @loop(ups)
    def _(t):
        serve_at("up", t, ups)
        u = dot(b[...], tiles.get(t, ups))
        square = u * u
        th = jnp.tanh(c0 * (u + 0.044715 * (square * u)))
        value = 0.5 * u * (1.0 + th)
        slope = 0.5 * (1.0 + th) + (0.5 * c0) * u * (1.0 - th * th) * (
            1.0 + (3 * 0.044715) * square
        )
        act[t] = value.astype(jnp.bfloat16)
        actt[t] = jnp.transpose(value).astype(jnp.bfloat16).reshape(2, 256, rows)
        gp[t] = slope.astype(jnp.bfloat16)

    save(actt, gt_o)
    save(gp, gp_o)

    serve("down")
    gd.complete()
    tiles = Tiles(lambda t: wd_f.at[columns(t, 512), :], dbuf, dsem)
    tiles.first(ups)
    mraw[...] = jnp.zeros_like(mraw)

    @loop(ups)
    def _(t):
        mraw[...] += dot(act[t], tiles.get(t, ups))

    save(mraw, mraw_o)
    ends = doc_ends(lens)

    @loop(rows // 128)
    def _(i):
        spot = pl.ds(i * 128, 128)
        z, _r = normed(mraw[spot, :])
        result = h[spot, :] + z * gain[3:4, :]
        place = y * rows + i * 128 + lax.broadcasted_iota(jnp.int32, result.shape, 0)
        result = jnp.where(place < ends[DOCS - 2], result, 0.0)
        out[spot, :] = result.astype(jnp.bfloat16)

    for copy in saves:
        copy.wait()

    @pl.when(y == 0)
    def _():
        tok_copy.wait_send()

    for m in (gg, gq, go, gu, gd):
        m.sent()


def forward(tokens, lengths, gains_wide, w_qkv, w_out, w_up, w_down, tables):
    dp_size = lax.axis_size("dp")
    devices = dp_size * lax.axis_size("ctx")
    rows, width = tokens.shape
    row_len = rows * lax.axis_size("ctx")
    head_dim = width // HEADS
    pairs = width // 128
    ups = w_up.shape[1] // 512
    bf, f32 = jnp.bfloat16, jnp.float32
    any_spec = pl.BlockSpec(memory_space=pl.ANY)
    vm = pl.BlockSpec(memory_space=pltpu.VMEM)
    shape = jax.ShapeDtypeStruct

    def whole(w):
        return shape((w.shape[0] * devices, w.shape[1]), bf)

    outs = [
        shape((rows, width), bf),
        whole(w_qkv),
        whole(w_out),
        whole(w_up),
        whole(w_down),
        shape((8, width), f32),
        shape((pairs, rows, 128), bf),
        shape((pairs, row_len, 128), bf),
        shape((pairs, row_len, 128), bf),
        shape((pairs, 128, rows), bf),
        shape((pairs, 2, rows), f32),
        shape((rows, width), f32),
        shape((rows, width), f32),
        shape((rows, width), f32),
        shape((width, rows), bf),
        shape((ups, 2, 256, rows), bf),
        shape((ups, rows, 512), bf),
        shape((width, rows), bf),
        shape((width, rows), bf),
        shape((rows, width), bf),
    ]
    scratch = [
        pltpu.VMEM((width, 128), bf),
        pltpu.VMEM((8, width), f32),
        pltpu.VMEM((rows, width), bf),
        pltpu.VMEM((rows, width), bf),
        pltpu.VMEM((rows, width), bf),
        pltpu.VMEM((width, rows), bf),
        pltpu.VMEM((width, rows), bf),
        pltpu.VMEM((pairs, rows, 128), bf),
        pltpu.VMEM((pairs, row_len, 128), bf),
        pltpu.VMEM((pairs, row_len, 128), bf),
        pltpu.VMEM((pairs, 128, row_len), bf),
        pltpu.VMEM((1, row_len, rows), f32),
        pltpu.VMEM((pairs, 128, rows), bf),
        pltpu.VMEM((pairs, 2, rows), f32),
        pltpu.VMEM((rows, width), f32),
        pltpu.VMEM((rows, width), f32),
        pltpu.VMEM((rows, width), f32),
        pltpu.VMEM((rows, width), bf),
        pltpu.VMEM((width, rows), bf),
        pltpu.VMEM((ups, rows, 512), bf),
        pltpu.VMEM((ups, 2, 256, rows), bf),
        pltpu.VMEM((ups, rows, 512), bf),
        pltpu.VMEM((3, width, 512), bf),
        pltpu.VMEM((3, 512, width), bf),
    ]
    scratch += [pltpu.SemaphoreType.DMA((Gather.sems(dp_size // 4),))] * 10
    scratch += [pltpu.SemaphoreType.DMA((3,))] * 3 + [pltpu.SemaphoreType.DMA((16,))]
    scratch += [pltpu.VMEM((pairs, 128, rows), f32)]
    return pl.pallas_call(
        functools.partial(forward_kernel, dp_size, head_dim),
        out_shape=outs,
        in_specs=[vm, pl.BlockSpec(memory_space=pltpu.SMEM), vm]
        + [any_spec] * 4
        + [vm, vm],
        out_specs=[vm] + [any_spec] * (len(outs) - 1),
        scratch_shapes=scratch,
        compiler_params=pltpu.CompilerParams(
            collective_id=0, has_side_effects=True, vmem_limit_bytes=60 * 2**20
        ),
    )(tokens, lengths, gains_wide, w_qkv, w_out, w_up, w_down, *tables)


def backward_kernel(dp_size, head_dim, *refs):
    (tok_i, dout, lens, gain, cosine_i, sine_i, wq, wo, wu, wd) = refs[:10]
    (q_i, k_i, v_i, ob_i, lse_i, araw_i, h_i, mraw_i, bt_i, gt_i, gp_i, at_i, atx_i, tokx_i) = refs[10:24]
    (dtok, out_q, out_o, out_u, out_d, out_g) = refs[24:30]
    (gts, dus, dzs) = refs[30:33]
    (part, rec3, rec, gpart, grec3, grec) = refs[33:39]
    (f1, f2, acc, dm, dms, da, das, dz, bt, bts, obts, ats, atx, atxs) = refs[39:53]
    (q, ob, lse, dk, dv, dg, dgs, dgt, dnxs) = refs[53:62]
    (kbuf, vbuf, wbuf, dbuf, gbuf, gpbuf, sbuf) = refs[62:69]
    tsems = refs[69:79]
    usend, urecv, gsend, grecv, zsend, zrecv, osend, orecv, lsem = refs[79:88]
    dnsem = refs[88]
    gsems, rsems = refs[89:96], refs[96:103]
    tok, cosine, sine = refs[103:106]
    at, xbuf, do, dnx, tokx = bt, gpbuf, dm, da, das
    g = Place(dp_size)
    Z, y, c = g.Z, g.y, g.c
    rows, width = dout.shape
    half = head_dim // 2
    pairs = width // 128
    scale = head_dim ** (-0.5)
    ups = gp_i.shape[0]
    per = width // 512
    bf, f32 = jnp.bfloat16, jnp.float32
    first = pl.multiple_of(y * rows, rows)

    def to_sib(src, dst, send, recv):
        return pltpu.make_async_remote_copy(
            src_ref=src,
            dst_ref=dst,
            send_sem=send,
            recv_sem=recv,
            device_id=g.sib,
            device_id_type=MESH,
        )

    def load(src, dst, i):
        return pltpu.make_async_copy(src, dst, lsem.at[i])

    h_load = load(h_i, f2, 0)
    bt_load = load(bt_i.at[:, c], bt, 1)
    atx_load = load(atx_i.at[:, c], atx, 2)
    q_load = load(q_i, q, 3)
    ob_load = load(ob_i, ob, 4)
    lse_load = load(lse_i, lse, 5)
    at_load = load(at_i.at[:, c], at, 6)
    tokx_load = load(tokx_i, tokx, 7)
    tok_load = load(tok_i, tok, 8)
    cosine_load = load(cosine_i, cosine, 9)
    sine_load = load(sine_i, sine, 10)

    def gt_send(i):
        half_z = pl.ds(pl.multiple_of(lax.rem(i, 2) * 256, 256), 256)
        return to_sib(
            gt_i.at[i, 1 - c], gts.at[lax.div(i, 2), half_z], gsend.at[i], grecv.at[i]
        )

    bt_send = to_sib(bt_i.at[:, 1 - c], bts, osend.at[0], orecv.at[0])
    ob_send = to_sib(ob_i.at[:, 1 - c], obts, osend.at[1], orecv.at[1])
    at_send = to_sib(at_i.at[:, 1 - c], ats, osend.at[2], orecv.at[2])
    atx_send = to_sib(atx_i.at[:, 1 - c], atxs, osend.at[3], orecv.at[3])

    def dm_send(i):
        spot = columns(i, 128)
        return to_sib(dm.at[spot, :], dms.at[spot, :], osend.at[7 + i], orecv.at[7 + i])

    da_send = to_sib(da, das, osend.at[5], orecv.at[5])
    dg_send = to_sib(dg, dgs, osend.at[6], orecv.at[6])
    dnx_send = pltpu.make_async_remote_copy(
        src_ref=dnx,
        dst_ref=dnxs,
        send_sem=dnsem.at[0],
        recv_sem=dnsem.at[1],
        device_id=g.device(g.z, g.x, c, 1 - y),
        device_id_type=MESH,
    )

    def du_send(t):
        return to_sib(dz.at[t], dus.at[t], usend.at[t], urecv.at[t])

    def dz_send(e, p):
        t = e * per + lax.div(p, 4)
        spot = columns(lax.div(lax.rem(p, 4), 2), 256)
        n = e * (pairs // 2) + lax.div(p, 2)
        return to_sib(dz.at[t, :, spot], dzs.at[t, :, spot], zsend.at[n], zrecv.at[n])

    landing = (rec3, rec)

    def write_d(total):
        out_d[...] = total.reshape(out_d.shape)

    def write_into(out, column):
        def write(total):
            for i in range(total.shape[0]):
                begin = column + i * width
                out[:, begin : begin + total.shape[2]] = total[i]

        return write

    def write_g(total):
        out_g[...] = total[0]

    modes = [c == 0 if m is None else m for m in SHARE_BY_Z]
    s_d = Share(
        g, part, 0, landing, 0, 4, gsems[0], rsems[0], write_d, modes[3]
    )
    s_u = Share(
        g, part, 4, landing, 4, 4, gsems[1], rsems[1], write_into(out_u, 0), modes[2]
    )
    s_o = Share(
        g, part, 8, landing, 8, 1, gsems[3], rsems[3], write_into(out_o, 0),
        modes[1],
    )
    s_q = [
        Share(
            g, part, 9, landing, 9, 3, gsems[4 + i], rsems[4 + i],
            write_into(out_q, i * 512), modes[0], pl.ds(i * 512, 512),
        )
        for i in (0, 1)
    ]
    s_g = Share(g, gpart, 0, (grec3, grec), 0, 1, gsems[6], rsems[6], write_g, False)
    groups = (s_d, s_u, s_o, s_q[0], s_q[1], s_g)

    def serve(name, i=0):
        for step in SHARE_PLAN.get(name, {}).get(i, ()):
            s, kind, j = groups[step // 100], step // 10 % 10, step % 10
            if kind < 2:
                (s.stage3, s.stage2)[kind](j)
            else:
                (s.sum_z, s.last)[kind - 2]()

    def serve_at(name, t, count):
        for i in range(count):
            if i in SHARE_PLAN.get(name, {}):
                pl.when(t == i)(functools.partial(serve, name, i))

    mraws = Tiles(lambda i: mraw_i.at[columns(i, 128), :], f1, tsems[9])
    araws = Tiles(lambda i: araw_i.at[columns(i, 128), :], f1, tsems[9])
    mraws.first(rows // 128)
    g.barrier()
    for j in range(Z):
        for i in (0, 1):
            gt_send(g.order(j) * 2 + i).start()
    for copy in (bt_send, ob_send, at_send):
        copy.start()

    @pl.when(y == 1)
    def _():
        atx_send.start()

    def z_of(j):
        return sum(jnp.where(j == i, g.order(i), 0) for i in range(Z))

    def gt_ready(j):
        for i in (0, 1):
            gt_send(z_of(j) * 2 + i).wait_recv()

    own_g = Tiles(lambda j: gt_i.at[pl.ds(z_of(j) * 2, 2), c], gbuf, tsems[0])
    sib_g = Tiles(lambda j: gts.at[z_of(j)], sbuf, tsems[1], gt_ready)
    own_g.first(Z)
    for copy in (
        h_load, bt_load, atx_load, q_load, ob_load, lse_load, cosine_load, sine_load, tok_load
    ):
        copy.start()
    dg[...] = jnp.zeros_like(dg)
    ends = doc_ends(lens)

    def upstream(i):
        e = dout[pl.ds(i * 128, 128), :].astype(f32)
        place = y * rows + i * 128 + lax.broadcasted_iota(jnp.int32, e.shape, 0)
        return jnp.where(place < ends[DOCS - 2], e, 0.0)

    def gain_sum(index, term):
        dg[index : index + 1, :] += jnp.sum(term, axis=0, keepdims=True)

    @loop(rows // 128)
    def _(i):
        value, term = norm_pull(mraws.get(i, rows // 128), gain[3:4, :], upstream(i))
        dm[pl.ds(i * 128, 128), :] = value.astype(bf)
        gain_sum(3, term)
        dm_send(i).start()

    downs = Tiles(lambda t: wd.at[columns(t, 512), :], dbuf, tsems[2])
    upw = Tiles(lambda t: wu.at[:, columns(t, 512)], wbuf, tsems[3])
    slopes = Tiles(lambda t: gp_i.at[t], gpbuf, tsems[4])
    for tiles in (downs, upw, slopes):
        tiles.first(ups)
    araws.first(rows // 128)
    keys = Tiles(lambda p: k_i.at[p], kbuf, tsems[6])
    values = Tiles(lambda p: v_i.at[p], vbuf, tsems[7])
    keys.first(pairs)
    values.first(pairs)
    sib_g.first(Z)
    for i in range(rows // 128):
        dm_send(i).wait_recv()

    @loop(Z)
    def _(j):
        z = z_of(j)
        total = dot(own_g.get(j, Z).reshape(512, rows), dm[...])
        total += dot(sib_g.get(j, Z), dms[...])
        total = total.astype(bf).reshape(4, 4, 32, width)
        for a in range(4):
            for e in range(4):
                part[e, 4 * z + a] = total[a, e]
        s_d.start(z)

    def add_to(halves, value, weights):
        for j in (0, 1):
            halves[j] += dot_nt(value, weights[j * 512 : (j + 1) * 512])

    sib_du = Tiles(lambda t: dus.at[t], sbuf, tsems[5], lambda t: du_send(t).wait_recv())
    acc[...] = jnp.zeros_like(acc)

    @loop(ups)
    def _(t):
        serve_at("du", t, ups)
        du = dot_nt(dm[...], downs.get(t, ups)) * slopes.get(t, ups).astype(f32)
        du = du.astype(bf)
        dz[t] = du
        du_send(t).start()
        add_to(acc, du, upw.get(t, ups))
        pl.when(t == 3)(lambda: sib_du.first(ups))

    outs = Tiles(lambda t: wo.at[columns(t, 512), :], dbuf, tsems[2])
    outs.first(per)
    bt_load.wait()
    bt_send.wait_recv()
    @loop(ups)
    def _(t):
        serve_at("up", t, ups)
        total = dot(bt[...].reshape(-1, rows), dz[t])
        total += dot(bts[...].reshape(-1, rows), sib_du.get(t, ups))
        part[4 + lax.div(t, per), :, :, columns(lax.rem(t, per), 512)] = (
            total.astype(bf).reshape(4 * Z, 32, 512)
        )

    s_u.start_all()
    at_load.start()

    serve("norm")
    h_load.wait()

    @loop(rows // 128)
    def _(i):
        spot = pl.ds(i * 128, 128)
        e = jnp.concatenate([acc[0, spot, :], acc[1, spot, :]], axis=1)
        value, term = norm_pull(f2[spot, :], gain[2:3, :], e)
        gain_sum(2, term)
        dh = upstream(i) + value
        f2[spot, :] = dh
        value, term = norm_pull(araws.get(i, rows // 128), gain[1:2, :], dh)
        gain_sum(1, term)
        da[spot, :] = value.astype(bf)

    da_send.start()
    for i in range(rows // 128):
        dm_send(i).wait_send()
    serve("do")

    @loop(per)
    def _(t):
        do[:, columns(t, 512)] = dot_nt(da[...], outs.get(t, per)).astype(bf)

    serve("out")
    ob_load.wait()
    ob_send.wait_recv()
    da_send.wait_recv()

    @loop(per)
    def _(t):
        total = dot(ob[:, c].reshape(-1, rows), da[:, columns(t, 512)])
        total += dot(obts[...].reshape(-1, rows), das[:, columns(t, 512)])
        part[8, :, :, columns(t, 512)] = total.astype(bf).reshape(4 * Z, 32, 512)

    s_o.start_all()
    for t in range(ups):
        du_send(t).wait_send()

    qkv_w = Tiles(lambda t: wq.at[:, columns(t, 512)], wbuf, tsems[3])
    pl.when(y == 1)(lambda: qkv_w.first(3 * per, per))
    serve("mask")
    fill_bias(acc, lens, y * rows, rows)
    pl.when(y == 1)(lambda: tokx_load.start())
    for copy in (q_load, lse_load, cosine_load, sine_load, tok_load):
        copy.wait()
    blocks = rows // 256

    def attend(p, block, base, count, fresh):
        spot = slice(block * 256, block * 256 + 256)
        slot = lax.rem(p, 2)
        kk = kbuf[slot, pl.ds(base, count), :]
        vv = vbuf[slot, pl.ds(base, count), :]
        kt = jnp.transpose(kk.astype(f32)).astype(bf)
        qs = split_heads(q[p, spot, :])
        do_pair = do[spot, columns(p, 128)]
        dos = split_heads(do_pair)
        ob_pair = ob[p, :, :, spot].astype(f32).reshape(128, -1)
        dot_o = jnp.transpose(do_pair.astype(f32)) * ob_pair
        mask = acc[lax.div(base, 512), :count, spot]
        parts, dk_, dv_ = [], [], []
        for i in (0, 1):
            delta = jnp.sum(
                dot_o[i * head_dim : (i + 1) * head_dim], axis=0, keepdims=True
            )
            s = dot_nt(kk, qs[i]) + mask
            prob = jnp.exp(s - lse[p, i : i + 1, spot])
            ds = (prob * (dot_nt(vv, dos[i]) - delta)).astype(bf)
            dv_.append(dot(prob.astype(bf), dos[i]))
            dk_.append(dot(ds, qs[i]))
            parts.append(dot(kt, ds))
        if fresh:
            dk[:count, :] = dk_[0] + dk_[1]
            dv[:count, :] = dv_[0] + dv_[1]
        else:
            dk[:count, :] += dk_[0] + dk_[1]
            dv[:count, :] += dv_[0] + dv_[1]
        upper = lax.broadcasted_iota(jnp.int32, parts[0].shape, 0) < head_dim
        dq = jnp.transpose(jnp.where(upper, parts[0], parts[1]) * scale)
        start = pl.multiple_of(first + block * 256, 256)
        return spot, turn(dq, cosine[pl.ds(start, 256), :], -sine[pl.ds(start, 256), :], half)

    def lanes(p):
        return columns(lax.rem(p, 4), 128)

    def keep(p, start, base):
        spot = pl.ds(start, rows)
        u = turn(dk[...], cosine[spot, :], -sine[spot, :], half)
        dz[base + lax.div(p, 4), :, lanes(p)] = u.astype(bf)
        dz[base + per + lax.div(p, 4), :, lanes(p)] = dv[...].astype(bf)

    def other_half():
        acc[...] = jnp.zeros_like(acc)
        da_send.wait_send()
        tokx_load.wait()

        @loop(2 * per)
        def _(t):
            add_to(acc, dz[t + 3 * per], qkv_w.get(t + per, 3 * per))

        @loop(rows // 128)
        def _(i):
            spot = pl.ds(i * 128, 128)
            e = jnp.concatenate([acc[0, spot, :], acc[1, spot, :]], axis=1)
            value, term = norm_pull(tokx[spot, :].astype(f32), gain[0:1, :], e)
            gain_sum(0, term)
            dnx[spot, :] = value.astype(bf)

        dnx_send.start()

    def qkv_gradient(h):
        at_both = (at[...].reshape(-1, rows), ats[...].reshape(-1, rows))

        def ready(i):
            for j in (1, 3):
                dz_send(i, h * 4 + j).wait_recv()

        sib_dz = Tiles(lambda i: dzs.at[i * per + h], sbuf, tsems[5], ready)
        sib_dx = Tiles(lambda i: dzs.at[i * per + h], xbuf, tsems[8], ready)
        sib_dz.first(3)
        pl.when(y == 1)(lambda: sib_dx.first(5, 3))

        @loop(3)
        def _(e):
            def total():
                return dot(at_both[0], dz[e * per + h]) + dot(at_both[1], sib_dz.get(e, 3))

            def keep_total(value):
                part[9 + e, :, :, columns(h, 512)] = value.astype(bf).reshape(4 * Z, 32, 512)

            both = (y == 1) & (e > 0)

            @pl.when(jnp.logical_not(both))
            def _():
                keep_total(total())

            @pl.when(both)
            def _():
                value = total() + dot(atx[...].reshape(-1, rows), dz[(e + 2) * per + h])
                keep_total(value + dot(atxs[...].reshape(-1, rows), sib_dx.get(e + 2, 5)))

        for i in (0, 1):
            pl.when(h == i)(lambda: s_q[i].start_all())

    @pl.when(y == 0)
    def _():
        for p in range(pairs):
            serve("more", p)
        serve("other")

    @pl.when(y == 1)
    def _():
        @loop(pairs)
        def _(p):
            serve_at("more", p, pairs)
            keys.get(p, pairs)
            values.get(p, pairs)
            for block in range(blocks):
                spot, dq = attend(p, block, 0, rows, block == 0)
                dz[lax.div(p, 4), spot, lanes(p)] = dq.astype(bf)
            keep(p, 0, 3 * per)

            @pl.when(lax.rem(p, 2) == 1)
            def _():
                for e in (3, 4):
                    dz_send(e, p).start()

        serve("other")
        keys.first(pairs)
        values.first(pairs)
        other_half()
        fill_bias(acc, lens, y * rows, rows)

    @loop(pairs)
    def _(p):
        serve_at("pair", p, pairs)
        keys.get(p, pairs)
        values.get(p, pairs)
        for block in reversed(range(blocks)):
            spot, dq = attend(p, block, first, (block + 1) * 256, block == blocks - 1)
            before = dz[lax.div(p, 4), spot, lanes(p)].astype(f32)
            dq += jnp.where(y == 1, before, 0.0)
            dz[lax.div(p, 4), spot, lanes(p)] = dq.astype(bf)
        keep(p, first, per)

        @pl.when(lax.rem(p, 2) == 1)
        def _():
            for e in range(3):
                dz_send(e, p).start()

        @pl.when(p == pairs // 2 - 1)
        def _():
            serve("half")
            at_load.wait()
            at_send.wait_recv()
            atx_load.wait()
            pl.when(y == 1)(lambda: atx_send.wait_recv())

        @pl.when(p == pairs - 1)
        def _():
            serve("rest")

        @pl.when(lax.rem(p, 4) == 3)
        def _():
            qkv_gradient(lax.div(p, 4))

    serve("input")
    qkv_w.first(3 * per)

    acc[...] = jnp.zeros_like(acc)

    @loop(3 * per)
    def _(t):
        add_to(acc, dz[t], qkv_w.get(t, 3 * per))

    @loop(rows // 128)
    def _(i):
        spot = pl.ds(i * 128, 128)
        e = jnp.concatenate([acc[0, spot, :], acc[1, spot, :]], axis=1)
        value, term = norm_pull(tok[spot, :].astype(f32), gain[0:1, :], e)
        gain_sum(0, term)
        f2[spot, :] += value

    dg_send.start()
    serve("gains")
    dg_send.wait_recv()
    wide = jnp.concatenate([dg[...] + dgs[...], jnp.zeros((120, width), f32)], axis=0)
    dgt[...] = jnp.transpose(wide).reshape(dgt.shape)
    gpart[0] = dgt[:, c].reshape(gpart.shape[1:])
    s_g.start_all()
    serve("end")

    @pl.when(y == 0)
    def _():
        dnx_send.wait_recv()
        dtok[...] = (f2[...] + dnxs[...].astype(f32)).astype(bf)

    @pl.when(y == 1)
    def _():
        dtok[...] = f2[...].astype(bf)

    for i in range(2 * Z):
        gt_send(jnp.int32(i)).wait_send()
    for copy in (bt_send, ob_send, at_send, dg_send):
        copy.wait_send()
    @loop(pairs // 2)
    def _(i):
        for e in range(3):
            dz_send(e, 2 * i + 1).wait_send()

    @pl.when(y == 0)
    def _():
        da_send.wait_send()

    @pl.when(y == 1)
    def _():
        atx_send.wait_send()
        dnx_send.wait_send()

        @loop(pairs // 2)
        def _(i):
            for e in (3, 4):
                dz_send(e, 2 * i + 1).wait_send()

    for s in (s_d, s_u, s_o, s_q[0], s_q[1], s_g):
        s.sent()


def backward(tokens, d_out, lengths, gain_rows, tables, weights, saved, shards):
    dp_size = lax.axis_size("dp")
    Z = dp_size // 4
    rows, width = tokens.shape
    row_len = rows * lax.axis_size("ctx")
    head_dim = width // HEADS
    pairs = width // 128
    per = width // 512
    bf, f32 = jnp.bfloat16, jnp.float32
    ups = saved[10].shape[0]
    any_spec = pl.BlockSpec(memory_space=pl.ANY)
    vm = pl.BlockSpec(memory_space=pltpu.VMEM)
    smem = pl.BlockSpec(memory_space=pltpu.SMEM)
    shape = jax.ShapeDtypeStruct
    block = 32
    saved = list(saved)
    for i in (3, 8, 11, 12):
        saved[i] = saved[i].reshape(2 * Z, 2, width // (4 * Z), rows)
    outs = [
        shape((rows, width), bf),
        shape(shards[0].shape, f32),
        shape(shards[1].shape, f32),
        shape(shards[2].shape, f32),
        shape(shards[3].shape, f32),
        shape((block, 128), f32),
        shape((Z, 512, rows), bf),
        shape((ups, rows, 512), bf),
        shape((5 * per, rows, 512), bf),
    ]
    core_rows = (2 * Z, width // (4 * Z), rows)
    scratch = [
        pltpu.VMEM((12, 4 * Z, block, width), bf),
        pltpu.VMEM((12, 2 * Z, block, width), bf),
        pltpu.VMEM((12, 2 * Z - 1, block, width), bf),
        pltpu.VMEM((1, 4 * Z, block, 128), f32),
        pltpu.VMEM((1, 2 * Z, block, 128), f32),
        pltpu.VMEM((1, 2 * Z - 1, block, 128), f32),
        pltpu.VMEM((2, 128, width), f32),
        pltpu.VMEM((rows, width), f32),
        pltpu.VMEM((2, rows, 512), f32),
        pltpu.VMEM((rows, width), bf),
        pltpu.VMEM((rows, width), bf),
        pltpu.VMEM((rows, width), bf),
        pltpu.VMEM((rows, width), bf),
        pltpu.VMEM((max(ups, 5 * per), rows, 512), bf),
    ]
    scratch += [pltpu.VMEM(core_rows, bf)] * 6
    scratch += [
        pltpu.VMEM((pairs, rows, 128), bf),
        pltpu.VMEM((2 * Z, 2, width // (4 * Z), rows), bf),
        pltpu.VMEM((pairs, 2, rows), f32),
        pltpu.VMEM((rows, 128), f32),
        pltpu.VMEM((rows, 128), f32),
        pltpu.VMEM((8, width), f32),
        pltpu.VMEM((8, width), f32),
        pltpu.VMEM((2 * Z, 2, width // (4 * Z), 128), f32),
        pltpu.VMEM((rows, width), bf),
        pltpu.VMEM((2, row_len, 128), bf),
        pltpu.VMEM((2, row_len, 128), bf),
        pltpu.VMEM((2, width, 512), bf),
        pltpu.VMEM((2, 512, width), bf),
        pltpu.VMEM((2, 2, 256, rows), bf),
        pltpu.VMEM((2, rows, 512), bf),
        pltpu.VMEM((2, rows, 512), bf),
    ]
    dma = pltpu.SemaphoreType.DMA
    scratch += [dma((3,))] * 10
    scratch += [dma((ups,))] * 2 + [dma((2 * Z,))] * 2 + [dma((5 * pairs,))] * 2
    scratch += [dma((11,))] * 2 + [dma((11,)), dma((2,))]
    scratch += [dma((Share.sems(Z),))] * 14
    scratch += [pltpu.VMEM((rows, width), bf)] + [pltpu.VMEM((row_len, 128), f32)] * 2
    return pl.pallas_call(
        functools.partial(backward_kernel, dp_size, head_dim),
        out_shape=outs,
        in_specs=[any_spec, vm, smem, vm] + [any_spec] * 20,
        out_specs=[vm] * 6 + [any_spec] * 3,
        scratch_shapes=scratch,
        compiler_params=pltpu.CompilerParams(
            collective_id=1, has_side_effects=True, vmem_limit_bytes=63 * 2**20
        ),
    )(tokens, d_out, lengths, gain_rows, *tables, *weights, *saved)


def hand_on(*arrays):
    n = len(arrays) - 1

    def kernel(*refs):
        sources, targets, sems = refs[: n + 1], refs[n + 1 : 2 * n + 2], refs[-1]
        copies = [
            pltpu.make_async_copy(sources[i], targets[i], sems.at[i]) for i in range(n)
        ]
        for copy in copies:
            copy.start()
        targets[n][...] = sources[n][:, : targets[n].shape[1]]
        for copy in copies:
            copy.wait()

    any_spec = pl.BlockSpec(memory_space=pl.ANY)
    vm = pl.BlockSpec(memory_space=pltpu.VMEM)
    shapes = [jax.ShapeDtypeStruct(a.shape, a.dtype) for a in arrays[:n]]
    shapes.append(jax.ShapeDtypeStruct((arrays[n].shape[0], 4), arrays[n].dtype))
    return pl.pallas_call(
        kernel,
        out_shape=shapes,
        in_specs=[vm] * (n + 1),
        out_specs=[any_spec] * n + [vm],
        scratch_shapes=[pltpu.SemaphoreType.DMA((n,))],
    )(*arrays)


def layer_norm(values, gain_vec):
    center = values - jnp.mean(values, axis=-1, keepdims=True)
    spread = jnp.mean(center * center, axis=-1, keepdims=True)
    return center * lax.rsqrt(spread + epsilon) * gain_vec


def norm_back(values, gain_vec, upstream):
    unused, pullback = jax.vjp(layer_norm, values, gain_vec)
    return pullback(upstream)


def rotate(values, cosine_table, sine_table, direction):
    half_dim = values.shape[-1] // 2
    first_half = values[..., :half_dim]
    second_half = values[..., half_dim:]
    return jnp.concatenate(
        [
            first_half * cosine_table - direction * second_half * sine_table,
            second_half * cosine_table + direction * first_half * sine_table,
        ],
        axis=-1,
    )


def doc_layout(lengths, row_len):
    doc_ends = jnp.cumsum(lengths, axis=-1)
    places = jnp.arange(row_len, dtype=jnp.int32)
    passed = places[None, :, None] >= doc_ends[:, None, :]
    segment = jnp.sum(passed.astype(jnp.int32), axis=-1)
    starts = jnp.sum(jnp.where(passed, lengths[:, None, :], 0), axis=-1)
    position = places[None, :] - starts
    is_valid = places[None, :] < doc_ends[:, DOCS - 2][:, None]
    return (segment[0], position[0], is_valid[0])


def allowed_keys(own_seg, own_place, seg_full, first_key, block_rows):
    key_place = first_key + jnp.arange(block_rows, dtype=jnp.int32)
    key_seg = lax.dynamic_slice_in_dim(seg_full, first_key, block_rows)
    return (own_seg[:, None] == key_seg[None, :]) & (key_place[None, :] <= own_place[:, None])


def make_fold(queries, own_seg, own_place, seg_full, score_scale):

    def fold_piece(fold_state, piece, start):
        key_piece, value_piece = piece
        piece_rows = key_piece.shape[0]
        block_rows = math.gcd(piece_rows, 256)
        block_count = piece_rows // block_rows
        key_blocks = key_piece.reshape((block_count, block_rows) + key_piece.shape[1:])
        value_blocks = value_piece.reshape((block_count, block_rows) + value_piece.shape[1:])

        def step_block(carried, block_items):
            row_max, row_sum, weighted = carried
            key_block, value_block, block_id = block_items
            allowed = allowed_keys(own_seg, own_place, seg_full, block_id * block_rows, block_rows)
            scores = (
                jnp.einsum("qhd,khd->hqk", queries, key_block, preferred_element_type=jnp.float32)
                * score_scale
            )
            scores = jnp.where(allowed[None], scores, masked_score)
            new_max = jnp.maximum(row_max, jnp.max(scores, axis=-1))
            factor = jnp.exp(row_max - new_max)
            shifted = jnp.where(allowed[None], jnp.exp(scores - new_max[..., None]), 0.0)
            row_sum = row_sum * factor + jnp.sum(shifted, axis=-1)
            weighted = weighted * factor[..., None] + jnp.einsum(
                "hqk,khd->hqd",
                shifted.astype(jnp.bfloat16),
                value_block,
                preferred_element_type=jnp.float32,
            )
            return ((new_max, row_sum, weighted), None)

        block_ids = jnp.arange(block_count, dtype=jnp.int32)
        fold_state, unused = lax.scan(step_block, fold_state, (key_blocks, value_blocks, block_ids))
        return fold_state

    return fold_piece


def per_device(tokens, lengths, w_qkv, w_out, w_up, w_down, gains, d_out):
    tok_rows, model_width = tokens.shape
    row_len = tok_rows * lax.axis_size("ctx")
    head_count = HEADS
    head_dim = model_width // head_count
    score_scale = head_dim ** (-0.5)
    head_shape = (tok_rows, head_count, head_dim)
    seg_full, pos_full, valid_full = doc_layout(lengths, row_len)
    offset = lax.axis_index("ctx") * tok_rows
    own_seg = lax.dynamic_slice_in_dim(seg_full, offset, tok_rows)
    own_pos = lax.dynamic_slice_in_dim(pos_full, offset, tok_rows)
    own_valid = lax.dynamic_slice_in_dim(valid_full.astype(jnp.float32), offset, tok_rows)
    own_place = offset + jnp.arange(tok_rows, dtype=jnp.int32)
    freq_index = jnp.arange(head_dim // 2, dtype=jnp.float32)
    angles = own_pos.astype(jnp.float32)[:, None] * 10000.0 ** (-2.0 * freq_index / head_dim)
    cosine_table = jnp.cos(angles)[:, None, :]
    sine_table = jnp.sin(angles)[:, None, :]
    qkv_full, out_full, up_full, down_full, gain_full = (
        lax.all_gather(w_qkv, ("dp", "ctx"), axis=0, tiled=True),
        lax.all_gather(w_out, ("dp", "ctx"), axis=0, tiled=True),
        lax.all_gather(w_up, ("dp", "ctx"), axis=0, tiled=True),
        lax.all_gather(w_down, ("dp", "ctx"), axis=0, tiled=True),
        lax.all_gather(gains, ("dp", "ctx"), axis=0, tiled=True),
    )
    gain_f = gain_full.astype(jnp.float32)
    stream = tokens.astype(jnp.float32)
    normed = layer_norm(stream, gain_f[:, 0]).astype(jnp.bfloat16)
    qkv_raw = jnp.dot(normed, qkv_full, preferred_element_type=jnp.float32)
    queries = rotate(
        qkv_raw[:, :model_width].reshape(head_shape), cosine_table, sine_table, 1.0
    ).astype(jnp.bfloat16)
    key_heads = rotate(
        qkv_raw[:, model_width : 2 * model_width].reshape(head_shape), cosine_table, sine_table, 1.0
    ).astype(jnp.bfloat16)
    value_heads = qkv_raw[:, 2 * model_width :].reshape(head_shape).astype(jnp.bfloat16)
    start_state = (
        jnp.full((head_count, tok_rows), masked_score, jnp.float32),
        jnp.zeros((head_count, tok_rows), jnp.float32),
        jnp.zeros((head_count, tok_rows, head_dim), jnp.float32),
    )
    fold_piece = make_fold(queries, own_seg, own_place, seg_full, score_scale)
    row_max, row_sum, weighted = fold_piece(
        start_state,
        (
            lax.all_gather(key_heads, "ctx", axis=0, tiled=True),
            lax.all_gather(value_heads, "ctx", axis=0, tiled=True),
        ),
        jnp.int32(0),
    )
    attended = jnp.transpose(weighted / row_sum[..., None], (1, 0, 2))
    attended_b = attended.reshape(tok_rows, model_width).astype(jnp.bfloat16)
    attn_raw = jnp.dot(attended_b, out_full, preferred_element_type=jnp.float32)
    hidden = stream + layer_norm(attn_raw, gain_f[:, 1])
    mlp_in = layer_norm(hidden, gain_f[:, 2]).astype(jnp.bfloat16)
    up_proj = jnp.dot(mlp_in, up_full, preferred_element_type=jnp.float32)
    activated = jax.nn.gelu(up_proj).astype(jnp.bfloat16)
    mlp_raw = jnp.dot(activated, down_full, preferred_element_type=jnp.float32)
    result = hidden + layer_norm(mlp_raw, gain_f[:, 3])
    output = (result * own_valid[:, None]).astype(jnp.bfloat16)
    qkv_back, out_back, up_back, down_back = (
        lax.all_gather(w_qkv, ("dp", "ctx"), axis=0, tiled=True),
        lax.all_gather(w_out, ("dp", "ctx"), axis=0, tiled=True),
        lax.all_gather(w_up, ("dp", "ctx"), axis=0, tiled=True),
        lax.all_gather(w_down, ("dp", "ctx"), axis=0, tiled=True),
    )
    upstream = d_out.astype(jnp.float32) * own_valid[:, None]
    d_mlp, d_gain_four = norm_back(mlp_raw, gain_f[:, 3], upstream)
    d_mlp_b = d_mlp.astype(jnp.bfloat16)
    grad_down = jnp.einsum("tf,td->fd", activated, d_mlp_b, preferred_element_type=jnp.float32)
    d_activated = jnp.einsum("td,fd->tf", d_mlp_b, down_back, preferred_element_type=jnp.float32)
    unused, gelu_pull = jax.vjp(jax.nn.gelu, up_proj)
    d_up_b = gelu_pull(d_activated)[0].astype(jnp.bfloat16)
    grad_up = jnp.einsum("td,tf->df", mlp_in, d_up_b, preferred_element_type=jnp.float32)
    d_mlp_in = jnp.einsum("tf,df->td", d_up_b, up_back, preferred_element_type=jnp.float32)
    d_hidden_part, d_gain_three = norm_back(hidden, gain_f[:, 2], d_mlp_in)
    d_hidden = upstream + d_hidden_part
    d_attn, d_gain_two = norm_back(attn_raw, gain_f[:, 1], d_hidden)
    d_attn_b = d_attn.astype(jnp.bfloat16)
    grad_out = jnp.einsum("td,te->de", attended_b, d_attn_b, preferred_element_type=jnp.float32)
    d_attended = (
        jnp.einsum("te,de->td", d_attn_b, out_back, preferred_element_type=jnp.float32)
        .astype(jnp.bfloat16)
        .reshape(head_shape)
    )
    row_dot = jnp.einsum("qhd,qhd->hq", d_attended.astype(jnp.float32), attended)
    key_all, value_all = (
        lax.all_gather(key_heads, "ctx", axis=0, tiled=True),
        lax.all_gather(value_heads, "ctx", axis=0, tiled=True),
    )
    block_rows = math.gcd(row_len, 256)
    block_count = row_len // block_rows
    key_blocks = key_all.reshape((block_count, block_rows) + key_all.shape[1:])
    value_blocks = value_all.reshape((block_count, block_rows) + value_all.shape[1:])

    def back_block(d_queries, block_items):
        key_block, value_block, block_id = block_items
        allowed = allowed_keys(own_seg, own_place, seg_full, block_id * block_rows, block_rows)
        scores = (
            jnp.einsum("qhd,khd->hqk", queries, key_block, preferred_element_type=jnp.float32)
            * score_scale
        )
        attn_prob = jnp.where(
            allowed[None], jnp.exp(scores - row_max[..., None]) / row_sum[..., None], 0.0
        )
        d_prob = jnp.einsum(
            "qhd,khd->hqk", d_attended, value_block, preferred_element_type=jnp.float32
        )
        d_scores = (attn_prob * (d_prob - row_dot[..., None])).astype(jnp.bfloat16)
        d_queries = (
            d_queries
            + jnp.einsum("hqk,khd->qhd", d_scores, key_block, preferred_element_type=jnp.float32)
            * score_scale
        )
        d_keys = (
            jnp.einsum("hqk,qhd->khd", d_scores, queries, preferred_element_type=jnp.float32)
            * score_scale
        )
        d_values = jnp.einsum(
            "hqk,qhd->khd",
            attn_prob.astype(jnp.bfloat16),
            d_attended,
            preferred_element_type=jnp.float32,
        )
        return (d_queries, (d_keys, d_values))

    block_ids = jnp.arange(block_count, dtype=jnp.int32)
    d_queries, (d_keys_all, d_values_all) = lax.scan(
        back_block, jnp.zeros(head_shape, jnp.float32), (key_blocks, value_blocks, block_ids)
    )
    kv_terms = jnp.concatenate(
        [d_keys_all.reshape(row_len, model_width), d_values_all.reshape(row_len, model_width)],
        axis=-1,
    )
    kv_grad = lax.psum_scatter(
        kv_terms.astype(jnp.bfloat16), "ctx", scatter_dimension=0, tiled=True
    ).astype(jnp.float32)
    d_keys = kv_grad[:, :model_width].reshape(head_shape)
    d_qkv = jnp.concatenate(
        [
            rotate(d_queries, cosine_table, sine_table, -1.0).reshape(tok_rows, model_width),
            rotate(d_keys, cosine_table, sine_table, -1.0).reshape(tok_rows, model_width),
            kv_grad[:, model_width:],
        ],
        axis=-1,
    ).astype(jnp.bfloat16)
    grad_qkv = jnp.einsum("td,te->de", normed, d_qkv, preferred_element_type=jnp.float32)
    d_normed = jnp.einsum("te,de->td", d_qkv, qkv_back, preferred_element_type=jnp.float32)
    d_stream_part, d_gain_one = norm_back(stream, gain_f[:, 0], d_normed)
    d_tokens = (d_hidden + d_stream_part).astype(jnp.bfloat16)
    grad_gains = jnp.stack([d_gain_one, d_gain_two, d_gain_three, d_gain_four], axis=-1)
    shard_qkv, shard_out, shard_up, shard_down, shard_gains = (
        lax.psum_scatter(grad_qkv, ("dp", "ctx"), scatter_dimension=0, tiled=True),
        lax.psum_scatter(grad_out, ("dp", "ctx"), scatter_dimension=0, tiled=True),
        lax.psum_scatter(grad_up, ("dp", "ctx"), scatter_dimension=0, tiled=True),
        lax.psum_scatter(grad_down, ("dp", "ctx"), scatter_dimension=0, tiled=True),
        lax.psum_scatter(grad_gains, ("dp", "ctx"), scatter_dimension=0, tiled=True),
    )
    return (output, d_tokens, shard_qkv, shard_out, shard_up, shard_down, shard_gains)


def fused_device(tokens, lengths, w_qkv, w_out, w_up, w_down, gains, d_out):
    rows, width = tokens.shape
    row_len = rows * lax.axis_size("ctx")
    gains_wide = jnp.pad(gains, ((0, 0), (0, 128 - gains.shape[1])))
    tables = tuple(jnp.asarray(v) for v in turn_tables(row_len, width // HEADS))
    output, wq, wo, wu, wd, gain_rows, *saved = forward(
        tokens, lengths, gains_wide, w_qkv, w_out, w_up, w_down, tables
    )
    d_tokens, grad_qkv, grad_out, grad_up, grad_down, grad_gains = backward(
        tokens,
        d_out,
        lengths,
        gain_rows,
        tables,
        (wq, wo, wu, wd),
        saved,
        (w_qkv, w_out, w_up, w_down),
    )[:6]
    return tuple(
        hand_on(output, d_tokens, grad_qkv, grad_out, grad_up, grad_down, grad_gains)
    )


def layer(mesh):
    if mesh.shape["dp"] == 16 and mesh.shape["ctx"] == 2:
        return fused_device
    return per_device


def solution(mesh):
    return jax.shard_map(
        layer(mesh),
        mesh=mesh,
        in_specs=(
            P(("dp", "ctx"), None),
            P("dp", None),
            P(("dp", "ctx"), None),
            P(("dp", "ctx"), None),
            P(("dp", "ctx"), None),
            P(("dp", "ctx"), None),
            P(("dp", "ctx"), None),
            P(("dp", "ctx"), None),
        ),
        out_specs=(
            P(("dp", "ctx"), None),
            P(("dp", "ctx"), None),
            P(("dp", "ctx"), None),
            P(("dp", "ctx"), None),
            P(("dp", "ctx"), None),
            P(("dp", "ctx"), None),
            P(("dp", "ctx"), None),
        ),
        check_vma=False,
    )
```

```python
import functools
import math

import jax
import jax.numpy as jnp
import numpy as np
from jax import lax
from jax.experimental import pallas as pl
from jax.experimental.pallas import tpu as pltpu
from jax.sharding import PartitionSpec as P

HEADS = 16
DOCS = 7

GATHER_BY_Z = (False, None, None, True)
SHARE_BY_Z = (None, None, None, None)

TOKENS = 999
GATHER_PLAN = {
    "norm": {
        0: (230, 210, 320, 10, 330, 110, 30, 130, 140, 141, 41, 150, 40, 142, 151, 152, 42, 52, 242, 50, 51, 420, 161, 310, 252, 240, 162, 60, 163, 999, 160, 61, 250, 63, 62, 340, 241, 342,),
    },
    "qkv": {
        0: (430, 410,),
    },
    "q": {
        1: (263,),
    },
    "v": {
        0: (251,),
        1: (350,),
    },
    "pair": {
        3: (360,),
        4: (260,),
        5: (352, 341,),
    },
    "other": {
        0: (440,),
    },
    "more": {
        0: (351,),
        2: (450, 261,),
        3: (441, 460,),
        4: (452,),
        5: (262,),
        7: (363, 442,),
    },
    "to up": {
        0: (361, 451, 362,),
    },
    "up": {
        1: (461,),
        3: (463,),
        5: (462,),
    },
    "start": {
        0: (300, 400, 120, 20, 220, 200, 100, 0,),
    },
}

NEAR = ((1, 2, 3), (0, 2, 3), (1, 3, 0), (2, 1, 0))
FAR = ((3, 2, 1), (3, 0, 2), (0, 1, 3), (0, 1, 2))

SHARE_PLAN = {
    "du": {
        3: (0,),
    },
    "up": {
        3: (10,),
        4: (1, 2,),
    },
    "out": {
        0: (100,),
    },
    "mask": {
        0: (12,),
    },
    "more": {
        1: (101,),
    },
    "other": {
        0: (110,),
    },
    "pair": {
        0: (200, 11,),
        1: (102,),
        2: (201,),
        3: (210, 112, 202, 212,),
        4: (111,),
        6: (3,),
    },
    "half": {
        0: (211,),
    },
    "input": {
        0: (301, 300,),
    },
    "gains": {
        0: (302, 400, 312, 311, 401, 310,),
    },
    "end": {
        0: (402, 303, 203, 412, 410, 500, 501, 502, 103, 220, 320, 403, 411, 510, 511, 512, 20, 120, 230, 330, 420, 503, 30, 130, 430, 520, 530,),
    },
}

epsilon = 1e-05
masked_score = -1e30


MESH = pl.DeviceIdType.MESH


def when(condition, body):
    if isinstance(condition, bool):
        if condition:
            body()
    else:
        pl.when(condition)(body)


def unless(condition, body):
    if isinstance(condition, bool):
        if not condition:
            body()
    else:
        pl.when(jnp.logical_not(condition))(body)


def pick(condition, one, other):
    if isinstance(condition, bool):
        return one if condition else other
    return jnp.where(condition, one, other)


class Place:
    def __init__(self, dp_size):
        dp = lax.axis_index("dp")
        self.Z = dp_size // 4
        self.z = lax.div(dp, 4)
        self.x = lax.rem(lax.div(dp, 2), 2)
        self.c = lax.rem(dp, 2)
        self.y = lax.axis_index("ctx")
        c, x, y = self.c, self.x, self.y
        self.i2 = y * (1 - c) + x * c
        self.i3 = x * (1 - c) + y * c
        self.sib = self.device(self.z, x, 1 - c, y)
        self.p2 = self.device(self.z, x * (1 - c) + (1 - x) * c, c, (1 - y) * (1 - c) + y * c)
        self.p3 = self.device(self.z, (1 - x) * (1 - c) + x * c, c, y * (1 - c) + (1 - y) * c)

    def device(self, z, x, c, y):
        return ((z * 2 + x) * 2 + c, y)

    def above(self, k):
        return lax.rem(self.z + k, self.Z)

    def below(self, k):
        return lax.rem(self.z - k + self.Z, self.Z)

    def at_z(self, z):
        return self.device(z, self.x, self.c, self.y)

    def near(self, j):
        if self.Z != 4:
            return self.below(j + 1)
        return sum(jnp.where(self.z == z, row[j], 0) for z, row in enumerate(NEAR))

    def order(self, j):
        if j == self.Z - 1:
            return self.z
        if self.Z != 4:
            return self.above(j + 1)
        return sum(jnp.where(self.z == z, row[j], 0) for z, row in enumerate(FAR))

    def far(self, z):
        return jnp.abs(z - self.z) == self.Z - 1

    def between(self, z):
        last = self.Z - 1
        return ((z == 0) & (self.z == last - 1)) | ((z == last) & (self.z == 1))

    def block(self, z, a2, a3):
        c = self.c
        return (z * 2 + a3 * (1 - c) + a2 * c) * 2 + a2 * (1 - c) + a3 * c

    def row_block(self, z, a2, a3, core):
        c = self.c
        xx = a3 * (1 - c) + a2 * c
        yy = a2 * (1 - c) + a3 * c
        return ((z * 2 + xx) * 2 + core) * 2 + yy

    def barrier(self):
        bar = pltpu.get_barrier_semaphore()
        for device in (self.sib, self.p2, self.p3):
            pl.semaphore_signal(bar, 1, device_id=device, device_id_type=MESH)
        for k in range(1, self.Z):
            pl.semaphore_signal(
                bar, 1, device_id=self.at_z(self.above(k)), device_id_type=MESH
            )
        pl.semaphore_wait(bar, 3 + self.Z - 1)


class Gather:
    def __init__(self, place, shard, full, send, recv, by_z):
        self.g, self.shard, self.full = place, shard, full
        self.send, self.recv = send, recv
        self.rows = shard.shape[0]
        self.by_z = by_z
        Z = place.Z
        self.n_z = 0
        self.n_pass = 2 * Z
        self.n_p2 = 2 * Z + 2
        self.n_p3 = self.n_p2 + Z
        self.n_sib = self.n_p3 + 2 * Z
        self.n_own = self.n_sib + 2 * Z

    @staticmethod
    def sems(Z):
        return 7 * Z + 3

    def at(self, index):
        return self.full.at[pl.ds(pl.multiple_of(index * self.rows, self.rows), self.rows)]

    def copy(self, index, send, recv, device, src=None):
        return pltpu.make_async_remote_copy(
            src_ref=self.at(index) if src is None else src,
            dst_ref=self.at(index),
            send_sem=self.send.at[send],
            recv_sem=self.recv.at[recv],
            device_id=device,
            device_id_type=MESH,
        )

    def own_copy(self):
        g = self.g
        index = g.row_block(g.z, g.i2, g.i3, g.c)
        return pltpu.make_async_copy(self.shard, self.at(index), self.recv.at[self.n_own])

    def z_copy(self, other, z, src=None):
        g = self.g
        a2 = (1 - g.i2) if other else g.i2
        return self.copy(
            g.row_block(g.z, a2, g.i3, g.c),
            self.n_z + z * 2 + int(other),
            self.n_z + g.z * 2 + int(other),
            g.at_z(z),
            src,
        )

    def pass_copy(self, other, z):
        g = self.g
        a2 = (1 - g.i2) if other else g.i2
        return self.copy(
            g.row_block(z, a2, g.i3, g.c),
            self.n_pass + int(other),
            self.n_z + z * 2 + int(other),
            g.at_z(g.Z - 1 - z),
        )

    def p2_copy(self, z, src=None):
        g = self.g
        number = self.n_p2 + z
        return self.copy(g.row_block(z, g.i2, g.i3, g.c), number, number, g.p2, src)

    def p3_copy(self, z, a2, src=None):
        g = self.g
        number = self.n_p3 + z * 2 + a2
        return self.copy(g.row_block(z, a2, g.i3, g.c), number, number, g.p3, src)

    def sib_copy(self, z, xx, core):
        rows = 2 * self.rows
        spot = pl.ds(pl.multiple_of(((z * 2 + xx) * 2 + core) * rows, rows), rows)
        number = self.n_sib + z * 2 + xx
        return pltpu.make_async_remote_copy(
            src_ref=self.full.at[spot],
            dst_ref=self.full.at[spot],
            send_sem=self.send.at[number],
            recv_sem=self.recv.at[number],
            device_id=self.g.sib,
            device_id_type=MESH,
        )

    def wait(self, number, index):
        self.copy(index, number, number, self.g.sib).wait_recv()

    def each_z(self, act):
        g = self.g
        for k in range(1, g.Z):
            z = g.above(k)
            unless(g.far(z), lambda: act(z))

    def start_z(self):
        self.each_z(lambda z: self.z_copy(False, z, self.shard).start())

    def start_p2(self):
        self.p2_copy(self.g.z, self.shard).start()

    def start_p3(self):
        self.p3_copy(self.g.z, self.g.i2, self.shard).start()
        self.own_copy().start()

    def first(self):
        g = self.g
        o2 = 1 - g.i2
        self.wait(self.n_p2 + g.z, g.row_block(g.z, o2, g.i3, g.c))
        when(self.by_z, lambda: self.each_z(lambda z: self.z_copy(True, z).start()))
        self.p3_copy(g.z, o2).start()

    def relay(self, j, z, other):
        if j == self.g.Z - 2:
            pl.when(self.g.between(z))(lambda: self.pass_copy(other, z).start())

    def from_z(self, j):
        g = self.g
        z = g.near(j)
        self.wait(self.n_z + z * 2, g.row_block(z, g.i2, g.i3, g.c))
        self.relay(j, z, False)
        unless(self.by_z, lambda: self.p2_copy(z).start())
        self.p3_copy(z, g.i2).start()

    def from_p2(self, j):
        g = self.g
        z = g.near(j)
        o2 = 1 - g.i2
        number = pick(self.by_z, self.n_z + z * 2 + 1, self.n_p2 + z)
        self.wait(number, g.row_block(z, o2, g.i3, g.c))
        when(self.by_z, lambda: self.relay(j, z, True))
        self.p3_copy(z, o2).start()

    def from_p3(self, j):
        g = self.g
        z = g.near(j - 1) if j else g.z
        for a2 in (0, 1):
            self.wait(self.n_p3 + z * 2 + a2, g.row_block(z, a2, 1 - g.i3, g.c))
        if j == 0:
            self.own_copy().wait()
        for xx in (0, 1):
            self.sib_copy(z, xx, g.c).start()

    def complete(self):
        g = self.g
        for z in range(g.Z):
            for xx in (0, 1):
                self.sib_copy(z, xx, 1 - g.c).wait_recv()

    def sent(self):
        g, src = self.g, self.shard
        self.p2_copy(g.z, src).wait_send()
        self.p3_copy(g.z, g.i2, src).wait_send()
        self.each_z(lambda z: self.z_copy(False, z, src).wait_send())
        when(self.by_z, lambda: self.each_z(lambda z: self.z_copy(True, z).wait_send()))
        end = g.near(g.Z - 2)

        def passed():
            self.pass_copy(False, end).wait_send()
            when(self.by_z, lambda: self.pass_copy(True, end).wait_send())

        pl.when(g.between(end))(passed)
        for k in range(1, g.Z):
            z = g.above(k)
            unless(self.by_z, lambda: self.p2_copy(z).wait_send())
            self.p3_copy(z, g.i2).wait_send()
        for z in range(g.Z):
            self.p3_copy(z, 1 - g.i2).wait_send()
            for xx in (0, 1):
                self.sib_copy(z, xx, g.c).wait_send()


class Share:
    def __init__(self, place, part, first, landing, unit, n, send, recv, write, by_z, cols=None):
        self.g, self.part, self.first = place, part, first
        self.rec3, self.rec = landing
        self.unit, self.n, self.send, self.recv, self.write = unit, n, send, recv, write
        self.kind, self.by_z = part.dtype, by_z
        self.cols = pl.ds(0, part.shape[-1]) if cols is None else cols

    @staticmethod
    def sems(Z):
        return 4 * Z - 1

    def copy(self, block, landing, slot, number, device):
        rows = slice(None)
        return pltpu.make_async_remote_copy(
            src_ref=self.part.at[pl.ds(self.first, self.n), block, rows, self.cols],
            dst_ref=landing.at[pl.ds(self.unit, self.n), slot, rows, self.cols],
            send_sem=self.send.at[number],
            recv_sem=self.recv.at[number],
            device_id=device,
            device_id_type=MESH,
        )

    def p3_copy(self, z, a2):
        g = self.g
        slot = z * 2 + a2
        return self.copy(g.block(z, a2, 1 - g.i3), self.rec3, slot, slot, g.p3)

    def p2_copy(self, z):
        g = self.g
        slot = pick(self.by_z, 0, z)
        block = g.block(z, 1 - g.i2, g.i3)
        return self.copy(block, self.rec, slot, 2 * g.Z + slot, g.p2)

    def z_slot(self, k, a2, by_z):
        return 1 + (k - 1) * 2 + a2 if by_z else self.g.Z + k - 1

    def z_copy(self, z, a2, by_z):
        g = self.g
        slot = self.z_slot(lax.rem(z - g.z + g.Z, g.Z), a2, by_z)
        return self.copy(g.block(z, a2, g.i3), self.rec, slot, 2 * g.Z + slot, g.at_z(z))

    def z_wait(self, k, a2, by_z):
        g = self.g
        slot = self.z_slot(k, a2, by_z)
        block = g.block(g.z, a2, g.i3)
        self.copy(block, self.rec, slot, 2 * g.Z + slot, g.sib).wait_recv()
        return self.landed(self.rec, slot)

    def landed(self, ref, slot):
        return ref[pl.ds(self.unit, self.n), slot, :, self.cols].astype(jnp.float32)

    def own(self, block):
        return self.part[pl.ds(self.first, self.n), block, :, self.cols].astype(jnp.float32)

    def add_to(self, block, ref, slot):
        spot = (pl.ds(self.first, self.n), block, slice(None), self.cols)
        self.part[spot] += ref[pl.ds(self.unit, self.n), slot, :, self.cols]

    def put(self, block, total):
        self.part[pl.ds(self.first, self.n), block, :, self.cols] = total.astype(self.kind)

    def start(self, z):
        for a2 in (0, 1):
            self.p3_copy(z, a2).start()

    def start_all(self):
        for j in range(self.g.Z):
            self.start(self.g.order(j))

    def add3(self, z, a2):
        g = self.g
        self.p3_copy(z, a2).wait_recv()
        self.add_to(g.block(z, a2, g.i3), self.rec3, z * 2 + a2)

    def stage3(self, j):
        g = self.g
        z = g.order(j)
        o2 = 1 - g.i2
        own = j == g.Z - 1
        self.add3(z, o2)
        if not own:
            when(self.by_z, lambda: self.z_copy(z, o2, True).start())
        unless(self.by_z, lambda: self.p2_copy(z).start())
        self.add3(z, g.i2)
        if not own:
            when(self.by_z, lambda: self.z_copy(z, g.i2, True).start())

    def stage2(self, j):
        g = self.g

        def with_p2():
            z = g.order(j)
            self.p2_copy(z).wait_recv()
            self.add_to(g.block(z, g.i2, g.i3), self.rec, z)
            self.z_copy(z, g.i2, False).start()

        unless(self.by_z, with_p2)

    def sum_z(self):
        g = self.g

        def along_z():
            o2 = 1 - g.i2
            block = g.block(g.z, o2, g.i3)
            total = self.own(block)
            for k in range(1, g.Z):
                total += self.z_wait(k, o2, True)
            self.put(block, total)
            self.p2_copy(g.z).start()

        when(self.by_z, along_z)

    def last(self):
        g = self.g

        def finish(by_z):
            total = self.own(g.block(g.z, g.i2, g.i3))
            for k in range(1, g.Z):
                total += self.z_wait(k, g.i2, by_z)
            self.p2_copy(g.z).wait_recv()
            total += self.landed(self.rec, 0 if by_z else g.z)
            self.write(total)

        when(self.by_z, lambda: finish(True))
        unless(self.by_z, lambda: finish(False))

    def sent(self):
        g = self.g
        for z in range(g.Z):
            for a2 in (0, 1):
                self.p3_copy(z, a2).wait_send()

        def by_z():
            self.p2_copy(g.z).wait_send()
            for k in range(1, g.Z):
                for a2 in (0, 1):
                    self.z_copy(g.above(k), a2, True).wait_send()

        def by_p2():
            for z in range(g.Z):
                self.p2_copy(z).wait_send()
            for k in range(1, g.Z):
                self.z_copy(g.above(k), g.i2, False).wait_send()

        when(self.by_z, by_z)
        unless(self.by_z, by_p2)


def loop(count):
    def run(body):
        def step(i, carry):
            body(i)
            return carry

        lax.fori_loop(0, count, step, 0)

    return run


def run_at(t, events):
    for i, event in events.items():
        pl.when(t == i)(event)


def dot(a, b):
    return jnp.dot(a, b, preferred_element_type=jnp.float32)


def dot_nt(a, b):
    return lax.dot_general(a, b, (((1,), (1,)), ((), ())), preferred_element_type=jnp.float32)


def normed(v):
    center = v - jnp.mean(v, axis=-1, keepdims=True)
    r = lax.rsqrt(jnp.mean(center * center, axis=-1, keepdims=True) + epsilon)
    return center * r, r


def norm_pull(v, gain, e):
    z, r = normed(v)
    f = e * gain
    dv = r * (
        f
        - jnp.mean(f, axis=-1, keepdims=True)
        - z * jnp.mean(f * z, axis=-1, keepdims=True)
    )
    return dv, e * z


def turn(u, cosine, sine, half):
    lane = lax.broadcasted_iota(jnp.int32, u.shape, 1)
    swapped = jnp.where(
        lax.rem(lane, 2 * half) < half,
        pltpu.roll(u, u.shape[1] - half, 1),
        pltpu.roll(u, half, 1),
    )
    return u * cosine + swapped * sine


def turn_tables(row_len, head_dim):
    half = head_dim // 2
    inverse = 10000.0 ** (-2.0 * np.arange(half) / head_dim)
    angles = np.arange(row_len)[:, None] * inverse[None, :]
    cosine = np.tile(np.cos(angles), (1, 4))
    sine = np.tile(np.concatenate([-np.sin(angles), np.sin(angles)], axis=1), (1, 2))
    return cosine.astype(np.float32), sine.astype(np.float32)


def doc_ends(lens):
    ends = [lens[0, 0]]
    for d in range(1, DOCS):
        ends.append(ends[-1] + lens[0, d])
    return ends


def fill_bias(bias, lens, first, rows):
    ends = doc_ends(lens)
    block = 128
    blocks = bias.shape[1] // block

    @loop(bias.shape[0] * blocks)
    def _(i):
        place = first + lax.broadcasted_iota(jnp.int32, (1, rows), 1)
        key = i * block + lax.broadcasted_iota(jnp.int32, (block, rows), 0)
        start = jnp.zeros((1, rows), jnp.int32)
        for d in range(DOCS):
            start = jnp.where(place >= ends[d], ends[d], start)
        fine = (key >= start) & (key <= place)
        spot = pl.ds(lax.rem(i, blocks) * block, block)
        bias[lax.div(i, blocks), spot, :] = jnp.where(fine, 0.0, masked_score)


def split_heads(v, axis=1):
    spot = lax.broadcasted_iota(jnp.int32, v.shape, axis)
    first = spot < v.shape[axis] // 2
    zero = jnp.zeros_like(v)
    return jnp.where(first, v, zero), jnp.where(first, zero, v)


class Tiles:
    def __init__(self, source, buffer, sems, ready=None):
        self.source, self.buffer, self.sems, self.ready = source, buffer, sems, ready
        self.depth = buffer.shape[0]

    def copy(self, t):
        slot = lax.rem(t, self.depth)
        return pltpu.make_async_copy(self.source(t), self.buffer.at[slot], self.sems.at[slot])

    def start(self, t):
        if self.ready is not None:
            self.ready(t)
        self.copy(t).start()

    def first(self, end, begin=0):
        for t in range(begin, min(begin + self.depth - 1, end)):
            self.start(jnp.int32(t))

    def get(self, t, end):
        later = t + self.depth - 1

        @pl.when(later < end)
        def _():
            self.start(later)

        self.copy(t).wait()
        return self.buffer[lax.rem(t, self.depth)]


def columns(t, size):
    return pl.ds(pl.multiple_of(t * size, size), size)


def forward_kernel(dp_size, head_dim, *refs):
    (tok_i, lens, gs, wq, wo, wu, wd, cosine_i, sine_i) = refs[:9]
    (out, wq_f, wo_f, wu_f, wd_f, gain_o, q_o, k_o, v_o, ob_o, lse_o) = refs[9:20]
    (araw_o, h_o, mraw_o, bt_o, gt_o, gp_o, at_o, atx_o, tokx_o) = refs[20:29]
    (g_full, gain, tokx, a, ax, at, atx, q, k, v, vt, bias, ob, lse) = refs[29:43]
    (araw, h, mraw, b, bt, act, actt, gp, wbuf, dbuf) = refs[43:53]
    sems = refs[53:63]
    wsem, dsem, xsem, osem = refs[63:67]
    o_own, tok, cosine, sine = refs[67:71]
    g = Place(dp_size)
    y = g.y
    rows, width = tok.shape
    half = head_dim // 2
    pairs = width // 128
    scale = head_dim ** (-0.5)
    modes = [g.c == 0 if m is None else m for m in GATHER_BY_Z]
    gg, gq, go, gu, gd = [
        Gather(g, s, f, sems[2 * i], sems[2 * i + 1], mode)
        for i, (s, f, mode) in enumerate(
            (
                (gs, g_full, False),
                (wq, wq_f, modes[0]),
                (wo, wo_f, modes[1]),
                (wu, wu_f, modes[2]),
                (wd, wd_f, modes[3]),
            )
        )
    ]
    Z = g.Z
    saves = []

    def save(src, dst):
        copy = pltpu.make_async_copy(src, dst, osem.at[len(saves)])
        copy.start()
        saves.append(copy)

    tok_copy = pltpu.make_async_remote_copy(
        src_ref=tok_i,
        dst_ref=tokx,
        send_sem=xsem.at[0],
        recv_sem=xsem.at[1],
        device_id=g.device(g.z, g.x, g.c, 1 - y),
        device_id_type=MESH,
    )
    matrices = (gg, gq, go, gu, gd)

    def serve(name, i=0):
        for step in GATHER_PLAN.get(name, {}).get(i, ()):
            if step == TOKENS:
                pl.when(y == 0)(lambda: tok_copy.start())
                continue
            m, kind, j = matrices[step // 100], step // 10 % 10, step % 10
            if kind < 4:
                (m.start_p2, m.start_p3, m.start_z, m.first)[kind]()
            else:
                (m.from_z, m.from_p2, m.from_p3)[kind - 4](j)

    def serve_at(name, t, count):
        for i in range(count):
            if i in GATHER_PLAN.get(name, {}):
                pl.when(t == i)(functools.partial(serve, name, i))

    loads = [
        pltpu.make_async_copy(src, dst, osem.at[16 + i])
        for i, (src, dst) in enumerate(((tok_i, tok), (cosine_i, cosine), (sine_i, sine)))
    ]
    g.barrier()
    serve("start")
    for copy in loads:
        copy.start()
    fill_bias(bias, lens, y * rows, rows)
    serve("norm")
    gg.complete()
    turned = jnp.transpose(g_full[...].astype(jnp.float32))
    gain[...] = turned[:8]
    save(gain, gain_o)

    def first_norm(src, dst, dst_t):
        @loop(rows // 128)
        def _(i):
            spot = pl.ds(i * 128, 128)
            z, _r = normed(src[spot, :].astype(jnp.float32))
            value = z * gain[0:1, :]
            dst[spot, :] = value.astype(jnp.bfloat16)
            dst_t[:, spot] = jnp.transpose(value).astype(jnp.bfloat16)

    loads[0].wait()
    first_norm(tok, a, at)
    save(at, at_o)
    serve("qkv")
    gq.complete()

    loads[1].wait()
    loads[2].wait()
    tiles = Tiles(lambda t: wq_f.at[:, columns(t, 512)], wbuf, wsem)
    per = width // 512
    first = pl.multiple_of(y * rows, rows)

    def turned_pair(u, start):
        return turn(u, cosine[pl.ds(start, rows), :], sine[pl.ds(start, rows), :], half)

    tiles.first(3 * per)

    @loop(per)
    def _(t):
        serve_at("q", t, per)
        u = dot(a[...], tiles.get(t, 3 * per))
        for j in range(4):
            part = turned_pair(u[:, j * 128 : j * 128 + 128], first) * scale
            q[4 * t + j] = part.astype(jnp.bfloat16)

    def keys(w, t, src, start):
        u = dot(src[...], w)
        for j in range(4):
            part = turned_pair(u[:, j * 128 : j * 128 + 128], start)
            k[4 * t + j, pl.ds(start, rows), :] = part.astype(jnp.bfloat16)

    def values(w, t, src, start):
        u = dot(src[...], w)
        ut = jnp.transpose(u).astype(jnp.bfloat16)
        for j in range(4):
            cols = slice(j * 128, j * 128 + 128)
            v[4 * t + j, pl.ds(start, rows), :] = u[:, cols].astype(jnp.bfloat16)
            vt[4 * t + j, :, pl.ds(start, rows)] = ut[cols]

    @loop(per)
    def _(t):
        serve_at("k", t, per)
        keys(tiles.get(t + per, 3 * per), t, a, first)

    @loop(per)
    def _(t):
        serve_at("v", t, per)
        values(tiles.get(t + 2 * per, 3 * per), t, a, first)

    def attend(p, block, keys_at):
        spot = slice(block * 256, block * 256 + 256)
        heads = split_heads(q[p, spot, :])
        kk = k[p, keys_at, :]
        vv = vt[p, :, keys_at]
        mask = bias[0, keys_at, spot]
        parts, logs = [], []
        for i in (0, 1):
            s = dot_nt(kk, heads[i]) + mask
            m = jnp.max(s, axis=0, keepdims=True)
            e = jnp.exp(s - m)
            total = jnp.sum(e, axis=0, keepdims=True)
            logs.append(m + jnp.log(total))
            parts.append(dot(vv, e.astype(jnp.bfloat16)) * (1.0 / total))
        return spot, parts, logs

    upper = lax.broadcasted_iota(jnp.int32, (128, 256), 0) < head_dim
    blocks = rows // 256

    @loop(pairs)
    def _(p):
        serve_at("pair", p, pairs)
        for block in range(blocks):
            spot, parts, logs = attend(p, block, pl.ds(first, (block + 1) * 256))
            for i in (0, 1):
                lse[p, i : i + 1, spot] = logs[i]
            o_own[p, :, spot] = jnp.where(upper, parts[0], parts[1])

    serve("other")

    @pl.when(y == 1)
    def _():
        tok_copy.wait_recv()
        first_norm(tokx, ax, atx)
        tiles.first(3 * per, per)

        @loop(per)
        def _(t):
            keys(tiles.get(t + per, 3 * per), t, ax, 0)

        @loop(per)
        def _(t):
            values(tiles.get(t + 2 * per, 3 * per), t, ax, 0)

    save(atx, atx_o)
    save(tokx, tokx_o)
    save(q, q_o)
    save(k, k_o)
    save(v, v_o)

    @pl.when(y == 0)
    def _():
        @loop(pairs)
        def _(p):
            serve_at("more", p, pairs)
            ob[p] = o_own[p].astype(jnp.bfloat16)

    @pl.when(y == 1)
    def _():
        @loop(pairs)
        def _(p):
            serve_at("more", p, pairs)
            for block in range(blocks):
                spot, parts, logs = attend(p, block, pl.ds(0, rows))
                shares = []
                for i in (0, 1):
                    old = lse[p, i : i + 1, spot]
                    top = jnp.maximum(old, logs[i])
                    both = top + jnp.log(jnp.exp(old - top) + jnp.exp(logs[i] - top))
                    lse[p, i : i + 1, spot] = both
                    shares.append((jnp.exp(old - both), jnp.exp(logs[i] - both)))
                own = o_own[p, :, spot]
                first_head = own * shares[0][0] + parts[0] * shares[0][1]
                second_head = own * shares[1][0] + parts[1] * shares[1][1]
                ob[p, :, spot] = jnp.where(upper, first_head, second_head).astype(jnp.bfloat16)

    save(ob, ob_o)
    save(lse, lse_o)

    serve("out")
    go.complete()
    tiles = Tiles(lambda t: wo_f.at[:, columns(t, 512)], wbuf, wsem)
    tiles.first(per)
    a[...] = jnp.transpose(ob[...].reshape(width, rows))

    @loop(per)
    def _(t):
        w = tiles.get(t, per)
        araw[:, columns(t, 512)] = dot(a[...], w)

    save(araw, araw_o)

    @loop(rows // 128)
    def _(i):
        spot = pl.ds(i * 128, 128)
        z, _r = normed(araw[spot, :])
        hidden = tok[spot, :].astype(jnp.float32) + z * gain[1:2, :]
        h[spot, :] = hidden
        z, _r = normed(hidden)
        value = z * gain[2:3, :]
        b[spot, :] = value.astype(jnp.bfloat16)
        bt[:, spot] = jnp.transpose(value).astype(jnp.bfloat16)

    save(h, h_o)
    save(bt, bt_o)

    serve("to up")
    gu.complete()
    tiles = Tiles(lambda t: wu_f.at[:, columns(t, 512)], wbuf, wsem)
    ups = act.shape[0]
    tiles.first(ups)
    c0 = math.sqrt(2.0 / math.pi)

    @loop(ups)
    def _(t):
        serve_at("up", t, ups)
        u = dot(b[...], tiles.get(t, ups))
        square = u * u
        th = jnp.tanh(c0 * (u + 0.044715 * (square * u)))
        value = 0.5 * u * (1.0 + th)
        slope = 0.5 * (1.0 + th) + (0.5 * c0) * u * (1.0 - th * th) * (
            1.0 + (3 * 0.044715) * square
        )
        act[t] = value.astype(jnp.bfloat16)
        actt[t] = jnp.transpose(value).astype(jnp.bfloat16).reshape(2, 256, rows)
        gp[t] = slope.astype(jnp.bfloat16)

    save(actt, gt_o)
    save(gp, gp_o)

    serve("down")
    gd.complete()
    tiles = Tiles(lambda t: wd_f.at[columns(t, 512), :], dbuf, dsem)
    tiles.first(ups)
    mraw[...] = jnp.zeros_like(mraw)

    @loop(ups)
    def _(t):
        mraw[...] += dot(act[t], tiles.get(t, ups))

    save(mraw, mraw_o)
    ends = doc_ends(lens)

    @loop(rows // 128)
    def _(i):
        spot = pl.ds(i * 128, 128)
        z, _r = normed(mraw[spot, :])
        result = h[spot, :] + z * gain[3:4, :]
        place = y * rows + i * 128 + lax.broadcasted_iota(jnp.int32, result.shape, 0)
        result = jnp.where(place < ends[DOCS - 2], result, 0.0)
        out[spot, :] = result.astype(jnp.bfloat16)

    for copy in saves:
        copy.wait()

    @pl.when(y == 0)
    def _():
        tok_copy.wait_send()

    for m in (gg, gq, go, gu, gd):
        m.sent()


def forward(tokens, lengths, gains_wide, w_qkv, w_out, w_up, w_down, tables):
    dp_size = lax.axis_size("dp")
    devices = dp_size * lax.axis_size("ctx")
    rows, width = tokens.shape
    row_len = rows * lax.axis_size("ctx")
    head_dim = width // HEADS
    pairs = width // 128
    ups = w_up.shape[1] // 512
    bf, f32 = jnp.bfloat16, jnp.float32
    any_spec = pl.BlockSpec(memory_space=pl.ANY)
    vm = pl.BlockSpec(memory_space=pltpu.VMEM)
    shape = jax.ShapeDtypeStruct

    def whole(w):
        return shape((w.shape[0] * devices, w.shape[1]), bf)

    outs = [
        shape((rows, width), bf),
        whole(w_qkv),
        whole(w_out),
        whole(w_up),
        whole(w_down),
        shape((8, width), f32),
        shape((pairs, rows, 128), bf),
        shape((pairs, row_len, 128), bf),
        shape((pairs, row_len, 128), bf),
        shape((pairs, 128, rows), bf),
        shape((pairs, 2, rows), f32),
        shape((rows, width), f32),
        shape((rows, width), f32),
        shape((rows, width), f32),
        shape((width, rows), bf),
        shape((ups, 2, 256, rows), bf),
        shape((ups, rows, 512), bf),
        shape((width, rows), bf),
        shape((width, rows), bf),
        shape((rows, width), bf),
    ]
    scratch = [
        pltpu.VMEM((width, 128), bf),
        pltpu.VMEM((8, width), f32),
        pltpu.VMEM((rows, width), bf),
        pltpu.VMEM((rows, width), bf),
        pltpu.VMEM((rows, width), bf),
        pltpu.VMEM((width, rows), bf),
        pltpu.VMEM((width, rows), bf),
        pltpu.VMEM((pairs, rows, 128), bf),
        pltpu.VMEM((pairs, row_len, 128), bf),
        pltpu.VMEM((pairs, row_len, 128), bf),
        pltpu.VMEM((pairs, 128, row_len), bf),
        pltpu.VMEM((1, row_len, rows), f32),
        pltpu.VMEM((pairs, 128, rows), bf),
        pltpu.VMEM((pairs, 2, rows), f32),
        pltpu.VMEM((rows, width), f32),
        pltpu.VMEM((rows, width), f32),
        pltpu.VMEM((rows, width), f32),
        pltpu.VMEM((rows, width), bf),
        pltpu.VMEM((width, rows), bf),
        pltpu.VMEM((ups, rows, 512), bf),
        pltpu.VMEM((ups, 2, 256, rows), bf),
        pltpu.VMEM((ups, rows, 512), bf),
        pltpu.VMEM((3, width, 512), bf),
        pltpu.VMEM((3, 512, width), bf),
    ]
    scratch += [pltpu.SemaphoreType.DMA((Gather.sems(dp_size // 4),))] * 10
    scratch += [pltpu.SemaphoreType.DMA((3,))] * 3 + [pltpu.SemaphoreType.DMA((19,))]
    scratch += [pltpu.VMEM((pairs, 128, rows), f32), pltpu.VMEM((rows, width), bf)]
    scratch += [pltpu.VMEM((row_len, 128), f32)] * 2
    return pl.pallas_call(
        functools.partial(forward_kernel, dp_size, head_dim),
        out_shape=outs,
        in_specs=[any_spec, pl.BlockSpec(memory_space=pltpu.SMEM), vm]
        + [any_spec] * 4
        + [any_spec] * 2,
        out_specs=[vm] + [any_spec] * (len(outs) - 1),
        scratch_shapes=scratch,
        compiler_params=pltpu.CompilerParams(
            collective_id=0, has_side_effects=True, vmem_limit_bytes=60 * 2**20
        ),
    )(tokens, lengths, gains_wide, w_qkv, w_out, w_up, w_down, *tables)


def backward_kernel(dp_size, head_dim, *refs):
    (tok_i, dout_i, lens, gain, cosine_i, sine_i, wq, wo, wu, wd) = refs[:10]
    (q_i, k_i, v_i, ob_i, lse_i, araw_i, h_i, mraw_i, bt_i, gt_i, gp_i, at_i, atx_i, tokx_i) = refs[10:24]
    (dtok, out_q, out_o, out_u, out_d, out_g) = refs[24:30]
    (gts, dus, dzs) = refs[30:33]
    (part, rec3, rec, gpart, grec3, grec) = refs[33:39]
    (f1, f2, acc, dm, dms, da, das, dz, bt, bts, obts, ats, atx, atxs) = refs[39:53]
    (q, ob, lse, dk, dv, dg, dgs, dgt, dnxs) = refs[53:62]
    (kbuf, vbuf, wbuf, dbuf, gbuf, gpbuf, sbuf) = refs[62:69]
    tsems = refs[69:79]
    usend, urecv, gsend, grecv, zsend, zrecv, osend, orecv, lsem = refs[79:88]
    dnsem = refs[88]
    gsems, rsems = refs[89:96], refs[96:103]
    tok, cosine, sine, dout = refs[103:107]
    at, xbuf, do, dnx, tokx = bt, gpbuf, dm, da, das
    g = Place(dp_size)
    Z, y, c = g.Z, g.y, g.c
    rows, width = dout_i.shape
    half = head_dim // 2
    pairs = width // 128
    scale = head_dim ** (-0.5)
    ups = gp_i.shape[0]
    per = width // 512
    bf, f32 = jnp.bfloat16, jnp.float32
    first = pl.multiple_of(y * rows, rows)

    def to_sib(src, dst, send, recv):
        return pltpu.make_async_remote_copy(
            src_ref=src,
            dst_ref=dst,
            send_sem=send,
            recv_sem=recv,
            device_id=g.sib,
            device_id_type=MESH,
        )

    def load(src, dst, i):
        return pltpu.make_async_copy(src, dst, lsem.at[i])

    h_load = load(h_i, f2, 0)
    bt_load = load(bt_i.at[:, c], bt, 1)
    atx_load = load(atx_i.at[:, c], atx, 2)
    q_load = load(q_i, q, 3)
    ob_load = load(ob_i, ob, 4)
    lse_load = load(lse_i, lse, 5)
    at_load = load(at_i.at[:, c], at, 6)
    tokx_load = load(tokx_i, tokx, 7)
    tok_load = load(tok_i, tok, 8)
    cosine_load = load(cosine_i, cosine, 9)
    sine_load = load(sine_i, sine, 10)
    dout_load = load(dout_i, dout, 11)

    def gt_send(i):
        half_z = pl.ds(pl.multiple_of(lax.rem(i, 2) * 256, 256), 256)
        return to_sib(
            gt_i.at[i, 1 - c], gts.at[lax.div(i, 2), half_z], gsend.at[i], grecv.at[i]
        )

    bt_send = to_sib(bt_i.at[:, 1 - c], bts, osend.at[0], orecv.at[0])
    ob_send = to_sib(ob_i.at[:, 1 - c], obts, osend.at[1], orecv.at[1])
    at_send = to_sib(at_i.at[:, 1 - c], ats, osend.at[2], orecv.at[2])
    atx_send = to_sib(atx_i.at[:, 1 - c], atxs, osend.at[3], orecv.at[3])

    def dm_send(i):
        spot = columns(i, 128)
        return to_sib(dm.at[spot, :], dms.at[spot, :], osend.at[7 + i], orecv.at[7 + i])

    da_send = to_sib(da, das, osend.at[5], orecv.at[5])
    dg_send = to_sib(dg, dgs, osend.at[6], orecv.at[6])
    dnx_send = pltpu.make_async_remote_copy(
        src_ref=dnx,
        dst_ref=dnxs,
        send_sem=dnsem.at[0],
        recv_sem=dnsem.at[1],
        device_id=g.device(g.z, g.x, c, 1 - y),
        device_id_type=MESH,
    )

    def du_send(t):
        return to_sib(dz.at[t], dus.at[t], usend.at[t], urecv.at[t])

    def dz_send(e, p):
        t = e * per + lax.div(p, 4)
        spot = columns(lax.div(lax.rem(p, 4), 2), 256)
        n = e * (pairs // 2) + lax.div(p, 2)
        return to_sib(dz.at[t, :, spot], dzs.at[t, :, spot], zsend.at[n], zrecv.at[n])

    landing = (rec3, rec)

    def write_d(total):
        out_d[...] = total.reshape(out_d.shape)

    def write_into(out, column):
        def write(total):
            for i in range(total.shape[0]):
                begin = column + i * width
                out[:, begin : begin + total.shape[2]] = total[i]

        return write

    def write_g(total):
        out_g[...] = total[0]

    modes = [c == 0 if m is None else m for m in SHARE_BY_Z]
    s_d = Share(
        g, part, 0, landing, 0, 4, gsems[0], rsems[0], write_d, modes[3]
    )
    s_u = Share(
        g, part, 4, landing, 4, 4, gsems[1], rsems[1], write_into(out_u, 0), modes[2]
    )
    s_o = Share(
        g, part, 8, landing, 8, 1, gsems[3], rsems[3], write_into(out_o, 0),
        modes[1],
    )
    s_q = [
        Share(
            g, part, 9, landing, 9, 3, gsems[4 + i], rsems[4 + i],
            write_into(out_q, i * 512), modes[0], pl.ds(i * 512, 512),
        )
        for i in (0, 1)
    ]
    s_g = Share(g, gpart, 0, (grec3, grec), 0, 1, gsems[6], rsems[6], write_g, False)
    groups = (s_d, s_u, s_o, s_q[0], s_q[1], s_g)

    def serve(name, i=0):
        for step in SHARE_PLAN.get(name, {}).get(i, ()):
            s, kind, j = groups[step // 100], step // 10 % 10, step % 10
            if kind < 2:
                (s.stage3, s.stage2)[kind](j)
            else:
                (s.sum_z, s.last)[kind - 2]()

    def serve_at(name, t, count):
        for i in range(count):
            if i in SHARE_PLAN.get(name, {}):
                pl.when(t == i)(functools.partial(serve, name, i))

    mraws = Tiles(lambda i: mraw_i.at[columns(i, 128), :], f1, tsems[9])
    araws = Tiles(lambda i: araw_i.at[columns(i, 128), :], f1, tsems[9])
    dout_load.start()
    mraws.first(rows // 128)
    g.barrier()
    for j in range(Z):
        for i in (0, 1):
            gt_send(g.order(j) * 2 + i).start()
    for copy in (bt_send, ob_send, at_send):
        copy.start()

    @pl.when(y == 1)
    def _():
        atx_send.start()

    def z_of(j):
        return sum(jnp.where(j == i, g.order(i), 0) for i in range(Z))

    def gt_ready(j):
        for i in (0, 1):
            gt_send(z_of(j) * 2 + i).wait_recv()

    own_g = Tiles(lambda j: gt_i.at[pl.ds(z_of(j) * 2, 2), c], gbuf, tsems[0])
    sib_g = Tiles(lambda j: gts.at[z_of(j)], sbuf, tsems[1], gt_ready)
    own_g.first(Z)
    for copy in (
        h_load, bt_load, atx_load, q_load, ob_load, lse_load, cosine_load, sine_load, tok_load
    ):
        copy.start()
    dg[...] = jnp.zeros_like(dg)
    ends = doc_ends(lens)

    def upstream(i):
        e = dout[pl.ds(i * 128, 128), :].astype(f32)
        place = y * rows + i * 128 + lax.broadcasted_iota(jnp.int32, e.shape, 0)
        return jnp.where(place < ends[DOCS - 2], e, 0.0)

    def gain_sum(index, term):
        dg[index : index + 1, :] += jnp.sum(term, axis=0, keepdims=True)

    dout_load.wait()

    @loop(rows // 128)
    def _(i):
        value, term = norm_pull(mraws.get(i, rows // 128), gain[3:4, :], upstream(i))
        dm[pl.ds(i * 128, 128), :] = value.astype(bf)
        gain_sum(3, term)
        dm_send(i).start()

    downs = Tiles(lambda t: wd.at[columns(t, 512), :], dbuf, tsems[2])
    upw = Tiles(lambda t: wu.at[:, columns(t, 512)], wbuf, tsems[3])
    slopes = Tiles(lambda t: gp_i.at[t], gpbuf, tsems[4])
    for tiles in (downs, upw, slopes):
        tiles.first(ups)
    araws.first(rows // 128)
    keys = Tiles(lambda p: k_i.at[p], kbuf, tsems[6])
    values = Tiles(lambda p: v_i.at[p], vbuf, tsems[7])
    keys.first(pairs)
    values.first(pairs)
    sib_g.first(Z)
    for i in range(rows // 128):
        dm_send(i).wait_recv()

    @loop(Z)
    def _(j):
        z = z_of(j)
        total = dot(own_g.get(j, Z).reshape(512, rows), dm[...])
        total += dot(sib_g.get(j, Z), dms[...])
        total = total.astype(bf).reshape(4, 4, 32, width)
        for a in range(4):
            for e in range(4):
                part[e, 4 * z + a] = total[a, e]
        s_d.start(z)

    def add_to(halves, value, weights):
        for j in (0, 1):
            halves[j] += dot_nt(value, weights[j * 512 : (j + 1) * 512])

    sib_du = Tiles(lambda t: dus.at[t], sbuf, tsems[5], lambda t: du_send(t).wait_recv())
    acc[...] = jnp.zeros_like(acc)

    @loop(ups)
    def _(t):
        serve_at("du", t, ups)
        du = dot_nt(dm[...], downs.get(t, ups)) * slopes.get(t, ups).astype(f32)
        du = du.astype(bf)
        dz[t] = du
        du_send(t).start()
        add_to(acc, du, upw.get(t, ups))
        pl.when(t == 3)(lambda: sib_du.first(ups))

    outs = Tiles(lambda t: wo.at[columns(t, 512), :], dbuf, tsems[2])
    outs.first(per)
    bt_load.wait()
    bt_send.wait_recv()
    @loop(ups)
    def _(t):
        serve_at("up", t, ups)
        total = dot(bt[...].reshape(-1, rows), dz[t])
        total += dot(bts[...].reshape(-1, rows), sib_du.get(t, ups))
        part[4 + lax.div(t, per), :, :, columns(lax.rem(t, per), 512)] = (
            total.astype(bf).reshape(4 * Z, 32, 512)
        )

    s_u.start_all()
    at_load.start()

    serve("norm")
    h_load.wait()

    @loop(rows // 128)
    def _(i):
        spot = pl.ds(i * 128, 128)
        e = jnp.concatenate([acc[0, spot, :], acc[1, spot, :]], axis=1)
        value, term = norm_pull(f2[spot, :], gain[2:3, :], e)
        gain_sum(2, term)
        dh = upstream(i) + value
        f2[spot, :] = dh
        value, term = norm_pull(araws.get(i, rows // 128), gain[1:2, :], dh)
        gain_sum(1, term)
        da[spot, :] = value.astype(bf)

    da_send.start()
    for i in range(rows // 128):
        dm_send(i).wait_send()
    serve("do")

    @loop(per)
    def _(t):
        do[:, columns(t, 512)] = dot_nt(da[...], outs.get(t, per)).astype(bf)

    serve("out")
    ob_load.wait()
    ob_send.wait_recv()
    da_send.wait_recv()

    @loop(per)
    def _(t):
        total = dot(ob[:, c].reshape(-1, rows), da[:, columns(t, 512)])
        total += dot(obts[...].reshape(-1, rows), das[:, columns(t, 512)])
        part[8, :, :, columns(t, 512)] = total.astype(bf).reshape(4 * Z, 32, 512)

    s_o.start_all()
    for t in range(ups):
        du_send(t).wait_send()

    qkv_w = Tiles(lambda t: wq.at[:, columns(t, 512)], wbuf, tsems[3])
    pl.when(y == 1)(lambda: qkv_w.first(3 * per, per))
    serve("mask")
    fill_bias(acc, lens, y * rows, rows)
    pl.when(y == 1)(lambda: tokx_load.start())
    for copy in (q_load, lse_load, cosine_load, sine_load, tok_load):
        copy.wait()
    blocks = rows // 256

    def turned_keys(p, base):
        kk = kbuf[lax.rem(p, 2), pl.ds(base, rows), :]
        return jnp.transpose(kk.astype(f32)).astype(bf)

    def attend(p, block, base, count, fresh, kt):
        spot = slice(block * 256, block * 256 + 256)
        slot = lax.rem(p, 2)
        kk = kbuf[slot, pl.ds(base, count), :]
        vv = vbuf[slot, pl.ds(base, count), :]
        kt = kt[:, :count]
        qs = split_heads(q[p, spot, :])
        do_pair = do[spot, columns(p, 128)]
        dos = split_heads(do_pair)
        ob_pair = ob[p, :, :, spot].astype(f32).reshape(128, -1)
        dot_o = jnp.transpose(do_pair.astype(f32)) * ob_pair
        mask = acc[lax.div(base, 512), :count, spot]
        parts, dk_, dv_ = [], [], []
        for i in (0, 1):
            delta = jnp.sum(
                dot_o[i * head_dim : (i + 1) * head_dim], axis=0, keepdims=True
            )
            s = dot_nt(kk, qs[i]) + mask
            prob = jnp.exp(s - lse[p, i : i + 1, spot])
            ds = (prob * (dot_nt(vv, dos[i]) - delta)).astype(bf)
            dv_.append(dot(prob.astype(bf), dos[i]))
            dk_.append(dot(ds, qs[i]))
            parts.append(dot(kt, ds))
        if fresh:
            dk[:count, :] = dk_[0] + dk_[1]
            dv[:count, :] = dv_[0] + dv_[1]
        else:
            dk[:count, :] += dk_[0] + dk_[1]
            dv[:count, :] += dv_[0] + dv_[1]
        upper = lax.broadcasted_iota(jnp.int32, parts[0].shape, 0) < head_dim
        dq = jnp.transpose(jnp.where(upper, parts[0], parts[1]) * scale)
        start = pl.multiple_of(first + block * 256, 256)
        return spot, turn(dq, cosine[pl.ds(start, 256), :], -sine[pl.ds(start, 256), :], half)

    def lanes(p):
        return columns(lax.rem(p, 4), 128)

    def keep(p, start, base):
        spot = pl.ds(start, rows)
        u = turn(dk[...], cosine[spot, :], -sine[spot, :], half)
        dz[base + lax.div(p, 4), :, lanes(p)] = u.astype(bf)
        dz[base + per + lax.div(p, 4), :, lanes(p)] = dv[...].astype(bf)

    def other_half():
        acc[...] = jnp.zeros_like(acc)
        da_send.wait_send()
        tokx_load.wait()

        @loop(2 * per)
        def _(t):
            add_to(acc, dz[t + 3 * per], qkv_w.get(t + per, 3 * per))

        @loop(rows // 128)
        def _(i):
            spot = pl.ds(i * 128, 128)
            e = jnp.concatenate([acc[0, spot, :], acc[1, spot, :]], axis=1)
            value, term = norm_pull(tokx[spot, :].astype(f32), gain[0:1, :], e)
            gain_sum(0, term)
            dnx[spot, :] = value.astype(bf)

        dnx_send.start()

    def qkv_gradient(h):
        at_both = (at[...].reshape(-1, rows), ats[...].reshape(-1, rows))

        def ready(i):
            for j in (1, 3):
                dz_send(i, h * 4 + j).wait_recv()

        sib_dz = Tiles(lambda i: dzs.at[i * per + h], sbuf, tsems[5], ready)
        sib_dx = Tiles(lambda i: dzs.at[i * per + h], xbuf, tsems[8], ready)
        sib_dz.first(3)
        pl.when(y == 1)(lambda: sib_dx.first(5, 3))

        @loop(3)
        def _(e):
            def total():
                return dot(at_both[0], dz[e * per + h]) + dot(at_both[1], sib_dz.get(e, 3))

            def keep_total(value):
                part[9 + e, :, :, columns(h, 512)] = value.astype(bf).reshape(4 * Z, 32, 512)

            both = (y == 1) & (e > 0)

            @pl.when(jnp.logical_not(both))
            def _():
                keep_total(total())

            @pl.when(both)
            def _():
                value = total() + dot(atx[...].reshape(-1, rows), dz[(e + 2) * per + h])
                keep_total(value + dot(atxs[...].reshape(-1, rows), sib_dx.get(e + 2, 5)))

        for i in (0, 1):
            pl.when(h == i)(lambda: s_q[i].start_all())

    @pl.when(y == 0)
    def _():
        for p in range(pairs):
            serve("more", p)
        serve("other")

    @pl.when(y == 1)
    def _():
        @loop(pairs)
        def _(p):
            serve_at("more", p, pairs)
            keys.get(p, pairs)
            values.get(p, pairs)
            kt = turned_keys(p, 0)
            for block in range(blocks):
                spot, dq = attend(p, block, 0, rows, block == 0, kt)
                dz[lax.div(p, 4), spot, lanes(p)] = dq.astype(bf)
            keep(p, 0, 3 * per)

            @pl.when(lax.rem(p, 2) == 1)
            def _():
                for e in (3, 4):
                    dz_send(e, p).start()

        serve("other")
        keys.first(pairs)
        values.first(pairs)
        other_half()
        fill_bias(acc, lens, y * rows, rows)

    @loop(pairs)
    def _(p):
        serve_at("pair", p, pairs)
        keys.get(p, pairs)
        values.get(p, pairs)
        kt = turned_keys(p, first)
        for block in reversed(range(blocks)):
            count = (block + 1) * 256
            spot, dq = attend(p, block, first, count, block == blocks - 1, kt)
            before = dz[lax.div(p, 4), spot, lanes(p)].astype(f32)
            dq += jnp.where(y == 1, before, 0.0)
            dz[lax.div(p, 4), spot, lanes(p)] = dq.astype(bf)
        keep(p, first, per)

        @pl.when(lax.rem(p, 2) == 1)
        def _():
            for e in range(3):
                dz_send(e, p).start()

        @pl.when(p == pairs // 2 - 1)
        def _():
            serve("half")
            at_load.wait()
            at_send.wait_recv()
            atx_load.wait()
            pl.when(y == 1)(lambda: atx_send.wait_recv())

        @pl.when(p == pairs - 1)
        def _():
            serve("rest")

        @pl.when(lax.rem(p, 4) == 3)
        def _():
            qkv_gradient(lax.div(p, 4))

    serve("input")
    qkv_w.first(3 * per)

    acc[...] = jnp.zeros_like(acc)

    @loop(3 * per)
    def _(t):
        add_to(acc, dz[t], qkv_w.get(t, 3 * per))

    @loop(rows // 128)
    def _(i):
        spot = pl.ds(i * 128, 128)
        e = jnp.concatenate([acc[0, spot, :], acc[1, spot, :]], axis=1)
        value, term = norm_pull(tok[spot, :].astype(f32), gain[0:1, :], e)
        gain_sum(0, term)
        f2[spot, :] += value

    dg_send.start()
    serve("gains")
    dg_send.wait_recv()
    wide = jnp.concatenate([dg[...] + dgs[...], jnp.zeros((120, width), f32)], axis=0)
    dgt[...] = jnp.transpose(wide).reshape(dgt.shape)
    gpart[0] = dgt[:, c].reshape(gpart.shape[1:])
    s_g.start_all()
    serve("end")

    @pl.when(y == 0)
    def _():
        dnx_send.wait_recv()
        dtok[...] = (f2[...] + dnxs[...].astype(f32)).astype(bf)

    @pl.when(y == 1)
    def _():
        dtok[...] = f2[...].astype(bf)

    for i in range(2 * Z):
        gt_send(jnp.int32(i)).wait_send()
    for copy in (bt_send, ob_send, at_send, dg_send):
        copy.wait_send()
    @loop(pairs // 2)
    def _(i):
        for e in range(3):
            dz_send(e, 2 * i + 1).wait_send()

    @pl.when(y == 0)
    def _():
        da_send.wait_send()

    @pl.when(y == 1)
    def _():
        atx_send.wait_send()
        dnx_send.wait_send()

        @loop(pairs // 2)
        def _(i):
            for e in (3, 4):
                dz_send(e, 2 * i + 1).wait_send()

    for s in (s_d, s_u, s_o, s_q[0], s_q[1], s_g):
        s.sent()


def backward(tokens, d_out, lengths, gain_rows, tables, weights, saved, shards):
    dp_size = lax.axis_size("dp")
    Z = dp_size // 4
    rows, width = tokens.shape
    row_len = rows * lax.axis_size("ctx")
    head_dim = width // HEADS
    pairs = width // 128
    per = width // 512
    bf, f32 = jnp.bfloat16, jnp.float32
    ups = saved[10].shape[0]
    any_spec = pl.BlockSpec(memory_space=pl.ANY)
    vm = pl.BlockSpec(memory_space=pltpu.VMEM)
    smem = pl.BlockSpec(memory_space=pltpu.SMEM)
    shape = jax.ShapeDtypeStruct
    block = 32
    saved = list(saved)
    for i in (3, 8, 11, 12):
        saved[i] = saved[i].reshape(2 * Z, 2, width // (4 * Z), rows)
    outs = [
        shape((rows, width), bf),
        shape(shards[0].shape, f32),
        shape(shards[1].shape, f32),
        shape(shards[2].shape, f32),
        shape(shards[3].shape, f32),
        shape((block, 128), f32),
        shape((Z, 512, rows), bf),
        shape((ups, rows, 512), bf),
        shape((5 * per, rows, 512), bf),
    ]
    core_rows = (2 * Z, width // (4 * Z), rows)
    scratch = [
        pltpu.VMEM((12, 4 * Z, block, width), bf),
        pltpu.VMEM((12, 2 * Z, block, width), bf),
        pltpu.VMEM((12, 2 * Z - 1, block, width), bf),
        pltpu.VMEM((1, 4 * Z, block, 128), f32),
        pltpu.VMEM((1, 2 * Z, block, 128), f32),
        pltpu.VMEM((1, 2 * Z - 1, block, 128), f32),
        pltpu.VMEM((2, 128, width), f32),
        pltpu.VMEM((rows, width), f32),
        pltpu.VMEM((2, rows, 512), f32),
        pltpu.VMEM((rows, width), bf),
        pltpu.VMEM((rows, width), bf),
        pltpu.VMEM((rows, width), bf),
        pltpu.VMEM((rows, width), bf),
        pltpu.VMEM((max(ups, 5 * per), rows, 512), bf),
    ]
    scratch += [pltpu.VMEM(core_rows, bf)] * 6
    scratch += [
        pltpu.VMEM((pairs, rows, 128), bf),
        pltpu.VMEM((2 * Z, 2, width // (4 * Z), rows), bf),
        pltpu.VMEM((pairs, 2, rows), f32),
        pltpu.VMEM((rows, 128), f32),
        pltpu.VMEM((rows, 128), f32),
        pltpu.VMEM((8, width), f32),
        pltpu.VMEM((8, width), f32),
        pltpu.VMEM((2 * Z, 2, width // (4 * Z), 128), f32),
        pltpu.VMEM((rows, width), bf),
        pltpu.VMEM((2, row_len, 128), bf),
        pltpu.VMEM((2, row_len, 128), bf),
        pltpu.VMEM((2, width, 512), bf),
        pltpu.VMEM((2, 512, width), bf),
        pltpu.VMEM((2, 2, 256, rows), bf),
        pltpu.VMEM((2, rows, 512), bf),
        pltpu.VMEM((2, rows, 512), bf),
    ]
    dma = pltpu.SemaphoreType.DMA
    scratch += [dma((3,))] * 10
    scratch += [dma((ups,))] * 2 + [dma((2 * Z,))] * 2 + [dma((5 * pairs,))] * 2
    scratch += [dma((11,))] * 2 + [dma((12,)), dma((2,))]
    scratch += [dma((Share.sems(Z),))] * 14
    scratch += [pltpu.VMEM((rows, width), bf)] + [pltpu.VMEM((row_len, 128), f32)] * 2
    scratch += [pltpu.VMEM((rows, width), bf)]
    return pl.pallas_call(
        functools.partial(backward_kernel, dp_size, head_dim),
        out_shape=outs,
        in_specs=[any_spec, any_spec, smem, vm] + [any_spec] * 20,
        out_specs=[vm] * 6 + [any_spec] * 3,
        scratch_shapes=scratch,
        compiler_params=pltpu.CompilerParams(
            collective_id=1, has_side_effects=True, vmem_limit_bytes=63 * 2**20
        ),
    )(tokens, d_out, lengths, gain_rows, *tables, *weights, *saved)


def hand_on(*arrays):
    n = len(arrays) - 1

    def kernel(*refs):
        sources, targets, sems = refs[: n + 1], refs[n + 1 : 2 * n + 2], refs[-1]
        copies = [
            pltpu.make_async_copy(sources[i], targets[i], sems.at[i]) for i in range(n)
        ]
        for copy in copies:
            copy.start()
        targets[n][...] = sources[n][:, : targets[n].shape[1]]
        for copy in copies:
            copy.wait()

    any_spec = pl.BlockSpec(memory_space=pl.ANY)
    vm = pl.BlockSpec(memory_space=pltpu.VMEM)
    shapes = [jax.ShapeDtypeStruct(a.shape, a.dtype) for a in arrays[:n]]
    shapes.append(jax.ShapeDtypeStruct((arrays[n].shape[0], 4), arrays[n].dtype))
    return pl.pallas_call(
        kernel,
        out_shape=shapes,
        in_specs=[vm] * (n + 1),
        out_specs=[any_spec] * n + [vm],
        scratch_shapes=[pltpu.SemaphoreType.DMA((n,))],
    )(*arrays)


def layer_norm(values, gain_vec):
    center = values - jnp.mean(values, axis=-1, keepdims=True)
    spread = jnp.mean(center * center, axis=-1, keepdims=True)
    return center * lax.rsqrt(spread + epsilon) * gain_vec


def norm_back(values, gain_vec, upstream):
    unused, pullback = jax.vjp(layer_norm, values, gain_vec)
    return pullback(upstream)


def rotate(values, cosine_table, sine_table, direction):
    half_dim = values.shape[-1] // 2
    first_half = values[..., :half_dim]
    second_half = values[..., half_dim:]
    return jnp.concatenate(
        [
            first_half * cosine_table - direction * second_half * sine_table,
            second_half * cosine_table + direction * first_half * sine_table,
        ],
        axis=-1,
    )


def doc_layout(lengths, row_len):
    doc_ends = jnp.cumsum(lengths, axis=-1)
    places = jnp.arange(row_len, dtype=jnp.int32)
    passed = places[None, :, None] >= doc_ends[:, None, :]
    segment = jnp.sum(passed.astype(jnp.int32), axis=-1)
    starts = jnp.sum(jnp.where(passed, lengths[:, None, :], 0), axis=-1)
    position = places[None, :] - starts
    is_valid = places[None, :] < doc_ends[:, DOCS - 2][:, None]
    return (segment[0], position[0], is_valid[0])


def allowed_keys(own_seg, own_place, seg_full, first_key, block_rows):
    key_place = first_key + jnp.arange(block_rows, dtype=jnp.int32)
    key_seg = lax.dynamic_slice_in_dim(seg_full, first_key, block_rows)
    return (own_seg[:, None] == key_seg[None, :]) & (key_place[None, :] <= own_place[:, None])


def make_fold(queries, own_seg, own_place, seg_full, score_scale):

    def fold_piece(fold_state, piece, start):
        key_piece, value_piece = piece
        piece_rows = key_piece.shape[0]
        block_rows = math.gcd(piece_rows, 256)
        block_count = piece_rows // block_rows
        key_blocks = key_piece.reshape((block_count, block_rows) + key_piece.shape[1:])
        value_blocks = value_piece.reshape((block_count, block_rows) + value_piece.shape[1:])

        def step_block(carried, block_items):
            row_max, row_sum, weighted = carried
            key_block, value_block, block_id = block_items
            allowed = allowed_keys(own_seg, own_place, seg_full, block_id * block_rows, block_rows)
            scores = (
                jnp.einsum("qhd,khd->hqk", queries, key_block, preferred_element_type=jnp.float32)
                * score_scale
            )
            scores = jnp.where(allowed[None], scores, masked_score)
            new_max = jnp.maximum(row_max, jnp.max(scores, axis=-1))
            factor = jnp.exp(row_max - new_max)
            shifted = jnp.where(allowed[None], jnp.exp(scores - new_max[..., None]), 0.0)
            row_sum = row_sum * factor + jnp.sum(shifted, axis=-1)
            weighted = weighted * factor[..., None] + jnp.einsum(
                "hqk,khd->hqd",
                shifted.astype(jnp.bfloat16),
                value_block,
                preferred_element_type=jnp.float32,
            )
            return ((new_max, row_sum, weighted), None)

        block_ids = jnp.arange(block_count, dtype=jnp.int32)
        fold_state, unused = lax.scan(step_block, fold_state, (key_blocks, value_blocks, block_ids))
        return fold_state

    return fold_piece


def per_device(tokens, lengths, w_qkv, w_out, w_up, w_down, gains, d_out):
    tok_rows, model_width = tokens.shape
    row_len = tok_rows * lax.axis_size("ctx")
    head_count = HEADS
    head_dim = model_width // head_count
    score_scale = head_dim ** (-0.5)
    head_shape = (tok_rows, head_count, head_dim)
    seg_full, pos_full, valid_full = doc_layout(lengths, row_len)
    offset = lax.axis_index("ctx") * tok_rows
    own_seg = lax.dynamic_slice_in_dim(seg_full, offset, tok_rows)
    own_pos = lax.dynamic_slice_in_dim(pos_full, offset, tok_rows)
    own_valid = lax.dynamic_slice_in_dim(valid_full.astype(jnp.float32), offset, tok_rows)
    own_place = offset + jnp.arange(tok_rows, dtype=jnp.int32)
    freq_index = jnp.arange(head_dim // 2, dtype=jnp.float32)
    angles = own_pos.astype(jnp.float32)[:, None] * 10000.0 ** (-2.0 * freq_index / head_dim)
    cosine_table = jnp.cos(angles)[:, None, :]
    sine_table = jnp.sin(angles)[:, None, :]
    qkv_full, out_full, up_full, down_full, gain_full = (
        lax.all_gather(w_qkv, ("dp", "ctx"), axis=0, tiled=True),
        lax.all_gather(w_out, ("dp", "ctx"), axis=0, tiled=True),
        lax.all_gather(w_up, ("dp", "ctx"), axis=0, tiled=True),
        lax.all_gather(w_down, ("dp", "ctx"), axis=0, tiled=True),
        lax.all_gather(gains, ("dp", "ctx"), axis=0, tiled=True),
    )
    gain_f = gain_full.astype(jnp.float32)
    stream = tokens.astype(jnp.float32)
    normed = layer_norm(stream, gain_f[:, 0]).astype(jnp.bfloat16)
    qkv_raw = jnp.dot(normed, qkv_full, preferred_element_type=jnp.float32)
    queries = rotate(
        qkv_raw[:, :model_width].reshape(head_shape), cosine_table, sine_table, 1.0
    ).astype(jnp.bfloat16)
    key_heads = rotate(
        qkv_raw[:, model_width : 2 * model_width].reshape(head_shape), cosine_table, sine_table, 1.0
    ).astype(jnp.bfloat16)
    value_heads = qkv_raw[:, 2 * model_width :].reshape(head_shape).astype(jnp.bfloat16)
    start_state = (
        jnp.full((head_count, tok_rows), masked_score, jnp.float32),
        jnp.zeros((head_count, tok_rows), jnp.float32),
        jnp.zeros((head_count, tok_rows, head_dim), jnp.float32),
    )
    fold_piece = make_fold(queries, own_seg, own_place, seg_full, score_scale)
    row_max, row_sum, weighted = fold_piece(
        start_state,
        (
            lax.all_gather(key_heads, "ctx", axis=0, tiled=True),
            lax.all_gather(value_heads, "ctx", axis=0, tiled=True),
        ),
        jnp.int32(0),
    )
    attended = jnp.transpose(weighted / row_sum[..., None], (1, 0, 2))
    attended_b = attended.reshape(tok_rows, model_width).astype(jnp.bfloat16)
    attn_raw = jnp.dot(attended_b, out_full, preferred_element_type=jnp.float32)
    hidden = stream + layer_norm(attn_raw, gain_f[:, 1])
    mlp_in = layer_norm(hidden, gain_f[:, 2]).astype(jnp.bfloat16)
    up_proj = jnp.dot(mlp_in, up_full, preferred_element_type=jnp.float32)
    activated = jax.nn.gelu(up_proj).astype(jnp.bfloat16)
    mlp_raw = jnp.dot(activated, down_full, preferred_element_type=jnp.float32)
    result = hidden + layer_norm(mlp_raw, gain_f[:, 3])
    output = (result * own_valid[:, None]).astype(jnp.bfloat16)
    qkv_back, out_back, up_back, down_back = (
        lax.all_gather(w_qkv, ("dp", "ctx"), axis=0, tiled=True),
        lax.all_gather(w_out, ("dp", "ctx"), axis=0, tiled=True),
        lax.all_gather(w_up, ("dp", "ctx"), axis=0, tiled=True),
        lax.all_gather(w_down, ("dp", "ctx"), axis=0, tiled=True),
    )
    upstream = d_out.astype(jnp.float32) * own_valid[:, None]
    d_mlp, d_gain_four = norm_back(mlp_raw, gain_f[:, 3], upstream)
    d_mlp_b = d_mlp.astype(jnp.bfloat16)
    grad_down = jnp.einsum("tf,td->fd", activated, d_mlp_b, preferred_element_type=jnp.float32)
    d_activated = jnp.einsum("td,fd->tf", d_mlp_b, down_back, preferred_element_type=jnp.float32)
    unused, gelu_pull = jax.vjp(jax.nn.gelu, up_proj)
    d_up_b = gelu_pull(d_activated)[0].astype(jnp.bfloat16)
    grad_up = jnp.einsum("td,tf->df", mlp_in, d_up_b, preferred_element_type=jnp.float32)
    d_mlp_in = jnp.einsum("tf,df->td", d_up_b, up_back, preferred_element_type=jnp.float32)
    d_hidden_part, d_gain_three = norm_back(hidden, gain_f[:, 2], d_mlp_in)
    d_hidden = upstream + d_hidden_part
    d_attn, d_gain_two = norm_back(attn_raw, gain_f[:, 1], d_hidden)
    d_attn_b = d_attn.astype(jnp.bfloat16)
    grad_out = jnp.einsum("td,te->de", attended_b, d_attn_b, preferred_element_type=jnp.float32)
    d_attended = (
        jnp.einsum("te,de->td", d_attn_b, out_back, preferred_element_type=jnp.float32)
        .astype(jnp.bfloat16)
        .reshape(head_shape)
    )
    row_dot = jnp.einsum("qhd,qhd->hq", d_attended.astype(jnp.float32), attended)
    key_all, value_all = (
        lax.all_gather(key_heads, "ctx", axis=0, tiled=True),
        lax.all_gather(value_heads, "ctx", axis=0, tiled=True),
    )
    block_rows = math.gcd(row_len, 256)
    block_count = row_len // block_rows
    key_blocks = key_all.reshape((block_count, block_rows) + key_all.shape[1:])
    value_blocks = value_all.reshape((block_count, block_rows) + value_all.shape[1:])

    def back_block(d_queries, block_items):
        key_block, value_block, block_id = block_items
        allowed = allowed_keys(own_seg, own_place, seg_full, block_id * block_rows, block_rows)
        scores = (
            jnp.einsum("qhd,khd->hqk", queries, key_block, preferred_element_type=jnp.float32)
            * score_scale
        )
        attn_prob = jnp.where(
            allowed[None], jnp.exp(scores - row_max[..., None]) / row_sum[..., None], 0.0
        )
        d_prob = jnp.einsum(
            "qhd,khd->hqk", d_attended, value_block, preferred_element_type=jnp.float32
        )
        d_scores = (attn_prob * (d_prob - row_dot[..., None])).astype(jnp.bfloat16)
        d_queries = (
            d_queries
            + jnp.einsum("hqk,khd->qhd", d_scores, key_block, preferred_element_type=jnp.float32)
            * score_scale
        )
        d_keys = (
            jnp.einsum("hqk,qhd->khd", d_scores, queries, preferred_element_type=jnp.float32)
            * score_scale
        )
        d_values = jnp.einsum(
            "hqk,qhd->khd",
            attn_prob.astype(jnp.bfloat16),
            d_attended,
            preferred_element_type=jnp.float32,
        )
        return (d_queries, (d_keys, d_values))

    block_ids = jnp.arange(block_count, dtype=jnp.int32)
    d_queries, (d_keys_all, d_values_all) = lax.scan(
        back_block, jnp.zeros(head_shape, jnp.float32), (key_blocks, value_blocks, block_ids)
    )
    kv_terms = jnp.concatenate(
        [d_keys_all.reshape(row_len, model_width), d_values_all.reshape(row_len, model_width)],
        axis=-1,
    )
    kv_grad = lax.psum_scatter(
        kv_terms.astype(jnp.bfloat16), "ctx", scatter_dimension=0, tiled=True
    ).astype(jnp.float32)
    d_keys = kv_grad[:, :model_width].reshape(head_shape)
    d_qkv = jnp.concatenate(
        [
            rotate(d_queries, cosine_table, sine_table, -1.0).reshape(tok_rows, model_width),
            rotate(d_keys, cosine_table, sine_table, -1.0).reshape(tok_rows, model_width),
            kv_grad[:, model_width:],
        ],
        axis=-1,
    ).astype(jnp.bfloat16)
    grad_qkv = jnp.einsum("td,te->de", normed, d_qkv, preferred_element_type=jnp.float32)
    d_normed = jnp.einsum("te,de->td", d_qkv, qkv_back, preferred_element_type=jnp.float32)
    d_stream_part, d_gain_one = norm_back(stream, gain_f[:, 0], d_normed)
    d_tokens = (d_hidden + d_stream_part).astype(jnp.bfloat16)
    grad_gains = jnp.stack([d_gain_one, d_gain_two, d_gain_three, d_gain_four], axis=-1)
    shard_qkv, shard_out, shard_up, shard_down, shard_gains = (
        lax.psum_scatter(grad_qkv, ("dp", "ctx"), scatter_dimension=0, tiled=True),
        lax.psum_scatter(grad_out, ("dp", "ctx"), scatter_dimension=0, tiled=True),
        lax.psum_scatter(grad_up, ("dp", "ctx"), scatter_dimension=0, tiled=True),
        lax.psum_scatter(grad_down, ("dp", "ctx"), scatter_dimension=0, tiled=True),
        lax.psum_scatter(grad_gains, ("dp", "ctx"), scatter_dimension=0, tiled=True),
    )
    return (output, d_tokens, shard_qkv, shard_out, shard_up, shard_down, shard_gains)


def fused_device(tokens, lengths, w_qkv, w_out, w_up, w_down, gains, d_out):
    rows, width = tokens.shape
    row_len = rows * lax.axis_size("ctx")
    gains_wide = jnp.pad(gains, ((0, 0), (0, 128 - gains.shape[1])))
    tables = tuple(jnp.asarray(v) for v in turn_tables(row_len, width // HEADS))
    output, wq, wo, wu, wd, gain_rows, *saved = forward(
        tokens, lengths, gains_wide, w_qkv, w_out, w_up, w_down, tables
    )
    d_tokens, grad_qkv, grad_out, grad_up, grad_down, grad_gains = backward(
        tokens,
        d_out,
        lengths,
        gain_rows,
        tables,
        (wq, wo, wu, wd),
        saved,
        (w_qkv, w_out, w_up, w_down),
    )[:6]
    return tuple(
        hand_on(output, d_tokens, grad_qkv, grad_out, grad_up, grad_down, grad_gains)
    )


def layer(mesh):
    if mesh.shape["dp"] == 16 and mesh.shape["ctx"] == 2:
        return fused_device
    return per_device


def solution(mesh):
    return jax.shard_map(
        layer(mesh),
        mesh=mesh,
        in_specs=(
            P(("dp", "ctx"), None),
            P("dp", None),
            P(("dp", "ctx"), None),
            P(("dp", "ctx"), None),
            P(("dp", "ctx"), None),
            P(("dp", "ctx"), None),
            P(("dp", "ctx"), None),
            P(("dp", "ctx"), None),
        ),
        out_specs=(
            P(("dp", "ctx"), None),
            P(("dp", "ctx"), None),
            P(("dp", "ctx"), None),
            P(("dp", "ctx"), None),
            P(("dp", "ctx"), None),
            P(("dp", "ctx"), None),
            P(("dp", "ctx"), None),
        ),
        check_vma=False,
    )
```

```python
import functools
import math

import jax
import jax.numpy as jnp
import numpy as np
from jax import lax
from jax.experimental import pallas as pl
from jax.experimental.pallas import tpu as pltpu
from jax.sharding import PartitionSpec as P

HEADS = 16
DOCS = 7

GATHER_BY_Z = (False, None, None, True)
SHARE_BY_Z = (None, None, None, None)

TOKENS = 999
GATHER_PLAN = {
    "norm": {
        0: (230, 210, 320, 10, 330, 110, 30, 130, 140, 141, 41, 150, 40, 142, 151, 152, 42, 52, 242, 50, 51, 420, 161, 310, 252, 240, 162, 60, 163, 999, 160, 61, 250, 63, 62, 340, 241, 342,),
    },
    "qkv": {
        0: (430, 410,),
    },
    "q": {
        1: (263,),
    },
    "v": {
        0: (251,),
        1: (350,),
    },
    "pair": {
        3: (360,),
        4: (260,),
        5: (352, 341,),
    },
    "other": {
        0: (440,),
    },
    "more": {
        0: (351,),
        2: (450, 261,),
        3: (441, 460,),
        4: (452,),
        5: (262,),
        7: (363, 442,),
    },
    "to up": {
        0: (361, 451, 362,),
    },
    "up": {
        1: (461,),
        3: (463,),
        5: (462,),
    },
    "start": {
        0: (300, 400, 120, 20, 220, 200, 100, 0,),
    },
}

NEAR = ((1, 2, 3), (0, 2, 3), (1, 3, 0), (2, 1, 0))
FAR = ((3, 2, 1), (3, 0, 2), (0, 1, 3), (0, 1, 2))

SHARE_PLAN = {
    "du": {
        3: (0,),
    },
    "up": {
        3: (10,),
        4: (1, 2,),
    },
    "out": {
        0: (100,),
    },
    "mask": {
        0: (12,),
    },
    "more": {
        1: (101,),
    },
    "other": {
        0: (110,),
    },
    "pair": {
        0: (200, 11,),
        1: (102,),
        2: (201,),
        3: (210, 112, 202, 212,),
        4: (111,),
        6: (3,),
    },
    "half": {
        0: (211,),
    },
    "input": {
        0: (301, 300,),
    },
    "gains": {
        0: (302, 400, 312, 311, 401, 310,),
    },
    "end": {
        0: (402, 303, 203, 412, 410, 500, 501, 502, 103, 220, 320, 403, 411, 510, 511, 512, 20, 120, 230, 330, 420, 503, 30, 130, 430, 520, 530,),
    },
}

epsilon = 1e-05
masked_score = -1e30


MESH = pl.DeviceIdType.MESH


def when(condition, body):
    if isinstance(condition, bool):
        if condition:
            body()
    else:
        pl.when(condition)(body)


def unless(condition, body):
    if isinstance(condition, bool):
        if not condition:
            body()
    else:
        pl.when(jnp.logical_not(condition))(body)


def pick(condition, one, other):
    if isinstance(condition, bool):
        return one if condition else other
    return jnp.where(condition, one, other)


class Place:
    def __init__(self, dp_size):
        dp = lax.axis_index("dp")
        self.Z = dp_size // 4
        self.z = lax.div(dp, 4)
        self.x = lax.rem(lax.div(dp, 2), 2)
        self.c = lax.rem(dp, 2)
        self.y = lax.axis_index("ctx")
        c, x, y = self.c, self.x, self.y
        self.i2 = y * (1 - c) + x * c
        self.i3 = x * (1 - c) + y * c
        self.sib = self.device(self.z, x, 1 - c, y)
        self.p2 = self.device(self.z, x * (1 - c) + (1 - x) * c, c, (1 - y) * (1 - c) + y * c)
        self.p3 = self.device(self.z, (1 - x) * (1 - c) + x * c, c, y * (1 - c) + (1 - y) * c)

    def device(self, z, x, c, y):
        return ((z * 2 + x) * 2 + c, y)

    def above(self, k):
        return lax.rem(self.z + k, self.Z)

    def below(self, k):
        return lax.rem(self.z - k + self.Z, self.Z)

    def at_z(self, z):
        return self.device(z, self.x, self.c, self.y)

    def near(self, j):
        if self.Z != 4:
            return self.below(j + 1)
        return sum(jnp.where(self.z == z, row[j], 0) for z, row in enumerate(NEAR))

    def order(self, j):
        if j == self.Z - 1:
            return self.z
        if self.Z != 4:
            return self.above(j + 1)
        return sum(jnp.where(self.z == z, row[j], 0) for z, row in enumerate(FAR))

    def far(self, z):
        return jnp.abs(z - self.z) == self.Z - 1

    def between(self, z):
        last = self.Z - 1
        return ((z == 0) & (self.z == last - 1)) | ((z == last) & (self.z == 1))

    def block(self, z, a2, a3):
        c = self.c
        return (z * 2 + a3 * (1 - c) + a2 * c) * 2 + a2 * (1 - c) + a3 * c

    def row_block(self, z, a2, a3, core):
        c = self.c
        xx = a3 * (1 - c) + a2 * c
        yy = a2 * (1 - c) + a3 * c
        return ((z * 2 + xx) * 2 + core) * 2 + yy

    def barrier(self):
        bar = pltpu.get_barrier_semaphore()
        for device in (self.sib, self.p2, self.p3):
            pl.semaphore_signal(bar, 1, device_id=device, device_id_type=MESH)
        for k in range(1, self.Z):
            pl.semaphore_signal(
                bar, 1, device_id=self.at_z(self.above(k)), device_id_type=MESH
            )
        pl.semaphore_wait(bar, 3 + self.Z - 1)


class Gather:
    def __init__(self, place, shard, full, send, recv, by_z):
        self.g, self.shard, self.full = place, shard, full
        self.send, self.recv = send, recv
        self.rows = shard.shape[0]
        self.by_z = by_z
        Z = place.Z
        self.n_z = 0
        self.n_pass = 2 * Z
        self.n_p2 = 2 * Z + 2
        self.n_p3 = self.n_p2 + Z
        self.n_sib = self.n_p3 + 2 * Z
        self.n_own = self.n_sib + 2 * Z

    @staticmethod
    def sems(Z):
        return 7 * Z + 3

    def at(self, index):
        return self.full.at[pl.ds(pl.multiple_of(index * self.rows, self.rows), self.rows)]

    def copy(self, index, send, recv, device, src=None):
        return pltpu.make_async_remote_copy(
            src_ref=self.at(index) if src is None else src,
            dst_ref=self.at(index),
            send_sem=self.send.at[send],
            recv_sem=self.recv.at[recv],
            device_id=device,
            device_id_type=MESH,
        )

    def own_copy(self):
        g = self.g
        index = g.row_block(g.z, g.i2, g.i3, g.c)
        return pltpu.make_async_copy(self.shard, self.at(index), self.recv.at[self.n_own])

    def z_copy(self, other, z, src=None):
        g = self.g
        a2 = (1 - g.i2) if other else g.i2
        return self.copy(
            g.row_block(g.z, a2, g.i3, g.c),
            self.n_z + z * 2 + int(other),
            self.n_z + g.z * 2 + int(other),
            g.at_z(z),
            src,
        )

    def pass_copy(self, other, z):
        g = self.g
        a2 = (1 - g.i2) if other else g.i2
        return self.copy(
            g.row_block(z, a2, g.i3, g.c),
            self.n_pass + int(other),
            self.n_z + z * 2 + int(other),
            g.at_z(g.Z - 1 - z),
        )

    def p2_copy(self, z, src=None):
        g = self.g
        number = self.n_p2 + z
        return self.copy(g.row_block(z, g.i2, g.i3, g.c), number, number, g.p2, src)

    def p3_copy(self, z, a2, src=None):
        g = self.g
        number = self.n_p3 + z * 2 + a2
        return self.copy(g.row_block(z, a2, g.i3, g.c), number, number, g.p3, src)

    def sib_copy(self, z, xx, core):
        rows = 2 * self.rows
        spot = pl.ds(pl.multiple_of(((z * 2 + xx) * 2 + core) * rows, rows), rows)
        number = self.n_sib + z * 2 + xx
        return pltpu.make_async_remote_copy(
            src_ref=self.full.at[spot],
            dst_ref=self.full.at[spot],
            send_sem=self.send.at[number],
            recv_sem=self.recv.at[number],
            device_id=self.g.sib,
            device_id_type=MESH,
        )

    def wait(self, number, index):
        self.copy(index, number, number, self.g.sib).wait_recv()

    def each_z(self, act):
        g = self.g
        for k in range(1, g.Z):
            z = g.above(k)
            unless(g.far(z), lambda: act(z))

    def start_z(self):
        self.each_z(lambda z: self.z_copy(False, z, self.shard).start())

    def start_p2(self):
        self.p2_copy(self.g.z, self.shard).start()

    def start_p3(self):
        self.p3_copy(self.g.z, self.g.i2, self.shard).start()
        self.own_copy().start()

    def first(self):
        g = self.g
        o2 = 1 - g.i2
        self.wait(self.n_p2 + g.z, g.row_block(g.z, o2, g.i3, g.c))
        when(self.by_z, lambda: self.each_z(lambda z: self.z_copy(True, z).start()))
        self.p3_copy(g.z, o2).start()

    def relay(self, j, z, other):
        if j == self.g.Z - 2:
            pl.when(self.g.between(z))(lambda: self.pass_copy(other, z).start())

    def from_z(self, j):
        g = self.g
        z = g.near(j)
        self.wait(self.n_z + z * 2, g.row_block(z, g.i2, g.i3, g.c))
        self.relay(j, z, False)
        unless(self.by_z, lambda: self.p2_copy(z).start())
        self.p3_copy(z, g.i2).start()

    def from_p2(self, j):
        g = self.g
        z = g.near(j)
        o2 = 1 - g.i2
        number = pick(self.by_z, self.n_z + z * 2 + 1, self.n_p2 + z)
        self.wait(number, g.row_block(z, o2, g.i3, g.c))
        when(self.by_z, lambda: self.relay(j, z, True))
        self.p3_copy(z, o2).start()

    def from_p3(self, j):
        g = self.g
        z = g.near(j - 1) if j else g.z
        for a2 in (0, 1):
            self.wait(self.n_p3 + z * 2 + a2, g.row_block(z, a2, 1 - g.i3, g.c))
        if j == 0:
            self.own_copy().wait()
        for xx in (0, 1):
            self.sib_copy(z, xx, g.c).start()

    def complete(self):
        g = self.g
        for z in range(g.Z):
            for xx in (0, 1):
                self.sib_copy(z, xx, 1 - g.c).wait_recv()

    def sent(self):
        g, src = self.g, self.shard
        self.p2_copy(g.z, src).wait_send()
        self.p3_copy(g.z, g.i2, src).wait_send()
        self.each_z(lambda z: self.z_copy(False, z, src).wait_send())
        when(self.by_z, lambda: self.each_z(lambda z: self.z_copy(True, z).wait_send()))
        end = g.near(g.Z - 2)

        def passed():
            self.pass_copy(False, end).wait_send()
            when(self.by_z, lambda: self.pass_copy(True, end).wait_send())

        pl.when(g.between(end))(passed)
        for k in range(1, g.Z):
            z = g.above(k)
            unless(self.by_z, lambda: self.p2_copy(z).wait_send())
            self.p3_copy(z, g.i2).wait_send()
        for z in range(g.Z):
            self.p3_copy(z, 1 - g.i2).wait_send()
            for xx in (0, 1):
                self.sib_copy(z, xx, g.c).wait_send()


class Share:
    def __init__(self, place, part, first, landing, unit, n, send, recv, write, by_z, cols=None):
        self.g, self.part, self.first = place, part, first
        self.rec3, self.rec = landing
        self.unit, self.n, self.send, self.recv, self.write = unit, n, send, recv, write
        self.kind, self.by_z = part.dtype, by_z
        self.cols = pl.ds(0, part.shape[-1]) if cols is None else cols

    @staticmethod
    def sems(Z):
        return 4 * Z - 1

    def copy(self, block, landing, slot, number, device):
        rows = slice(None)
        return pltpu.make_async_remote_copy(
            src_ref=self.part.at[pl.ds(self.first, self.n), block, rows, self.cols],
            dst_ref=landing.at[pl.ds(self.unit, self.n), slot, rows, self.cols],
            send_sem=self.send.at[number],
            recv_sem=self.recv.at[number],
            device_id=device,
            device_id_type=MESH,
        )

    def p3_copy(self, z, a2):
        g = self.g
        slot = z * 2 + a2
        return self.copy(g.block(z, a2, 1 - g.i3), self.rec3, slot, slot, g.p3)

    def p2_copy(self, z):
        g = self.g
        slot = pick(self.by_z, 0, z)
        block = g.block(z, 1 - g.i2, g.i3)
        return self.copy(block, self.rec, slot, 2 * g.Z + slot, g.p2)

    def z_slot(self, k, a2, by_z):
        return 1 + (k - 1) * 2 + a2 if by_z else self.g.Z + k - 1

    def z_copy(self, z, a2, by_z):
        g = self.g
        slot = self.z_slot(lax.rem(z - g.z + g.Z, g.Z), a2, by_z)
        return self.copy(g.block(z, a2, g.i3), self.rec, slot, 2 * g.Z + slot, g.at_z(z))

    def z_wait(self, k, a2, by_z):
        g = self.g
        slot = self.z_slot(k, a2, by_z)
        block = g.block(g.z, a2, g.i3)
        self.copy(block, self.rec, slot, 2 * g.Z + slot, g.sib).wait_recv()
        return self.landed(self.rec, slot)

    def landed(self, ref, slot):
        return ref[pl.ds(self.unit, self.n), slot, :, self.cols].astype(jnp.float32)

    def own(self, block):
        return self.part[pl.ds(self.first, self.n), block, :, self.cols].astype(jnp.float32)

    def add_to(self, block, ref, slot):
        spot = (pl.ds(self.first, self.n), block, slice(None), self.cols)
        self.part[spot] += ref[pl.ds(self.unit, self.n), slot, :, self.cols]

    def put(self, block, total):
        self.part[pl.ds(self.first, self.n), block, :, self.cols] = total.astype(self.kind)

    def start(self, z):
        for a2 in (0, 1):
            self.p3_copy(z, a2).start()

    def start_all(self):
        for j in range(self.g.Z):
            self.start(self.g.order(j))

    def add3(self, z, a2):
        g = self.g
        self.p3_copy(z, a2).wait_recv()
        self.add_to(g.block(z, a2, g.i3), self.rec3, z * 2 + a2)

    def stage3(self, j):
        g = self.g
        z = g.order(j)
        o2 = 1 - g.i2
        own = j == g.Z - 1
        self.add3(z, o2)
        if not own:
            when(self.by_z, lambda: self.z_copy(z, o2, True).start())
        unless(self.by_z, lambda: self.p2_copy(z).start())
        self.add3(z, g.i2)
        if not own:
            when(self.by_z, lambda: self.z_copy(z, g.i2, True).start())

    def stage2(self, j):
        g = self.g

        def with_p2():
            z = g.order(j)
            self.p2_copy(z).wait_recv()
            self.add_to(g.block(z, g.i2, g.i3), self.rec, z)
            self.z_copy(z, g.i2, False).start()

        unless(self.by_z, with_p2)

    def sum_z(self):
        g = self.g

        def along_z():
            o2 = 1 - g.i2
            block = g.block(g.z, o2, g.i3)
            total = self.own(block)
            for k in range(1, g.Z):
                total += self.z_wait(k, o2, True)
            self.put(block, total)
            self.p2_copy(g.z).start()

        when(self.by_z, along_z)

    def last(self):
        g = self.g

        def finish(by_z):
            total = self.own(g.block(g.z, g.i2, g.i3))
            for k in range(1, g.Z):
                total += self.z_wait(k, g.i2, by_z)
            self.p2_copy(g.z).wait_recv()
            total += self.landed(self.rec, 0 if by_z else g.z)
            self.write(total)

        when(self.by_z, lambda: finish(True))
        unless(self.by_z, lambda: finish(False))

    def sent(self):
        g = self.g
        for z in range(g.Z):
            for a2 in (0, 1):
                self.p3_copy(z, a2).wait_send()

        def by_z():
            self.p2_copy(g.z).wait_send()
            for k in range(1, g.Z):
                for a2 in (0, 1):
                    self.z_copy(g.above(k), a2, True).wait_send()

        def by_p2():
            for z in range(g.Z):
                self.p2_copy(z).wait_send()
            for k in range(1, g.Z):
                self.z_copy(g.above(k), g.i2, False).wait_send()

        when(self.by_z, by_z)
        unless(self.by_z, by_p2)


def loop(count):
    def run(body):
        def step(i, carry):
            body(i)
            return carry

        lax.fori_loop(0, count, step, 0)

    return run


def run_at(t, events):
    for i, event in events.items():
        pl.when(t == i)(event)


def dot(a, b):
    return jnp.dot(a, b, preferred_element_type=jnp.float32)


def dot_nt(a, b):
    return lax.dot_general(a, b, (((1,), (1,)), ((), ())), preferred_element_type=jnp.float32)


def normed(v):
    center = v - jnp.mean(v, axis=-1, keepdims=True)
    r = lax.rsqrt(jnp.mean(center * center, axis=-1, keepdims=True) + epsilon)
    return center * r, r


def norm_pull(v, gain, e):
    z, r = normed(v)
    f = e * gain
    dv = r * (
        f
        - jnp.mean(f, axis=-1, keepdims=True)
        - z * jnp.mean(f * z, axis=-1, keepdims=True)
    )
    return dv, e * z


def turn(u, cosine, sine, half):
    lane = lax.broadcasted_iota(jnp.int32, u.shape, 1)
    swapped = jnp.where(
        lax.rem(lane, 2 * half) < half,
        pltpu.roll(u, u.shape[1] - half, 1),
        pltpu.roll(u, half, 1),
    )
    return u * cosine + swapped * sine


def turn_tables(row_len, head_dim):
    half = head_dim // 2
    inverse = 10000.0 ** (-2.0 * np.arange(half) / head_dim)
    angles = np.arange(row_len)[:, None] * inverse[None, :]
    cosine = np.tile(np.cos(angles), (1, 4))
    sine = np.tile(np.concatenate([-np.sin(angles), np.sin(angles)], axis=1), (1, 2))
    return cosine.astype(np.float32), sine.astype(np.float32)


def doc_ends(lens):
    ends = [lens[0, 0]]
    for d in range(1, DOCS):
        ends.append(ends[-1] + lens[0, d])
    return ends


def fill_bias(bias, lens, first, rows):
    ends = doc_ends(lens)
    block = 128
    blocks = bias.shape[1] // block

    @loop(bias.shape[0] * blocks)
    def _(i):
        place = first + lax.broadcasted_iota(jnp.int32, (1, rows), 1)
        key = i * block + lax.broadcasted_iota(jnp.int32, (block, rows), 0)
        start = jnp.zeros((1, rows), jnp.int32)
        for d in range(DOCS):
            start = jnp.where(place >= ends[d], ends[d], start)
        fine = (key >= start) & (key <= place)
        spot = pl.ds(lax.rem(i, blocks) * block, block)
        bias[lax.div(i, blocks), spot, :] = jnp.where(fine, 0.0, masked_score)


def split_heads(v, axis=1):
    spot = lax.broadcasted_iota(jnp.int32, v.shape, axis)
    first = spot < v.shape[axis] // 2
    zero = jnp.zeros_like(v)
    return jnp.where(first, v, zero), jnp.where(first, zero, v)


class Tiles:
    def __init__(self, source, buffer, sems, ready=None):
        self.source, self.buffer, self.sems, self.ready = source, buffer, sems, ready
        self.depth = buffer.shape[0]

    def copy(self, t):
        slot = lax.rem(t, self.depth)
        return pltpu.make_async_copy(self.source(t), self.buffer.at[slot], self.sems.at[slot])

    def start(self, t):
        if self.ready is not None:
            self.ready(t)
        self.copy(t).start()

    def first(self, end, begin=0):
        for t in range(begin, min(begin + self.depth - 1, end)):
            self.start(jnp.int32(t))

    def get(self, t, end):
        later = t + self.depth - 1

        @pl.when(later < end)
        def _():
            self.start(later)

        self.copy(t).wait()
        return self.buffer[lax.rem(t, self.depth)]


def columns(t, size):
    return pl.ds(pl.multiple_of(t * size, size), size)


def forward_kernel(dp_size, head_dim, *refs):
    (tok_i, lens, gs, wq, wo, wu, wd, cosine_i, sine_i) = refs[:9]
    (out, wq_f, wo_f, wu_f, wd_f, gain_o, q_o, k_o, v_o, ob_o, lse_o) = refs[9:20]
    (araw_o, h_o, mraw_o, bt_o, gt_o, gp_o, at_o, atx_o, tokx_o) = refs[20:29]
    (g_full, gain, tokx, a, ax, at, atx, q, k, v, vt, bias, ob, lse) = refs[29:43]
    (araw, h, mraw, b, bt, act, actt, gp, wbuf, dbuf) = refs[43:53]
    sems = refs[53:63]
    wsem, dsem, xsem, osem = refs[63:67]
    o_own, tok, cosine, sine = refs[67:71]
    g = Place(dp_size)
    y = g.y
    rows, width = tok.shape
    half = head_dim // 2
    pairs = width // 128
    scale = head_dim ** (-0.5)
    modes = [g.c == 0 if m is None else m for m in GATHER_BY_Z]
    gg, gq, go, gu, gd = [
        Gather(g, s, f, sems[2 * i], sems[2 * i + 1], mode)
        for i, (s, f, mode) in enumerate(
            (
                (gs, g_full, False),
                (wq, wq_f, modes[0]),
                (wo, wo_f, modes[1]),
                (wu, wu_f, modes[2]),
                (wd, wd_f, modes[3]),
            )
        )
    ]
    Z = g.Z
    saves = []

    def save(src, dst):
        copy = pltpu.make_async_copy(src, dst, osem.at[len(saves)])
        copy.start()
        saves.append(copy)

    tok_copy = pltpu.make_async_remote_copy(
        src_ref=tok_i,
        dst_ref=tokx,
        send_sem=xsem.at[0],
        recv_sem=xsem.at[1],
        device_id=g.device(g.z, g.x, g.c, 1 - y),
        device_id_type=MESH,
    )
    matrices = (gg, gq, go, gu, gd)

    def serve(name, i=0):
        for step in GATHER_PLAN.get(name, {}).get(i, ()):
            if step == TOKENS:
                pl.when(y == 0)(lambda: tok_copy.start())
                continue
            m, kind, j = matrices[step // 100], step // 10 % 10, step % 10
            if kind < 4:
                (m.start_p2, m.start_p3, m.start_z, m.first)[kind]()
            else:
                (m.from_z, m.from_p2, m.from_p3)[kind - 4](j)

    def serve_at(name, t, count):
        for i in range(count):
            if i in GATHER_PLAN.get(name, {}):
                pl.when(t == i)(functools.partial(serve, name, i))

    loads = [
        pltpu.make_async_copy(src, dst, osem.at[16 + i])
        for i, (src, dst) in enumerate(((tok_i, tok), (cosine_i, cosine), (sine_i, sine)))
    ]
    g.barrier()
    serve("start")
    for copy in loads:
        copy.start()
    fill_bias(bias, lens, y * rows, rows)
    serve("norm")
    gg.complete()
    turned = jnp.transpose(g_full[...].astype(jnp.float32))
    gain[...] = turned[:8]
    save(gain, gain_o)

    def first_norm(src, dst, dst_t):
        @loop(rows // 128)
        def _(i):
            spot = pl.ds(i * 128, 128)
            z, _r = normed(src[spot, :].astype(jnp.float32))
            value = z * gain[0:1, :]
            dst[spot, :] = value.astype(jnp.bfloat16)
            dst_t[:, spot] = jnp.transpose(value).astype(jnp.bfloat16)

    loads[0].wait()
    first_norm(tok, a, at)
    save(at, at_o)
    serve("qkv")
    gq.complete()

    loads[1].wait()
    loads[2].wait()
    tiles = Tiles(lambda t: wq_f.at[:, columns(t, 512)], wbuf, wsem)
    per = width // 512
    first = pl.multiple_of(y * rows, rows)

    def turned_pair(u, start):
        return turn(u, cosine[pl.ds(start, rows), :], sine[pl.ds(start, rows), :], half)

    tiles.first(3 * per)

    @loop(per)
    def _(t):
        serve_at("q", t, per)
        u = dot(a[...], tiles.get(t, 3 * per))
        for j in range(4):
            part = turned_pair(u[:, j * 128 : j * 128 + 128], first) * scale
            q[4 * t + j] = part.astype(jnp.bfloat16)

    def keys(w, t, src, start):
        u = dot(src[...], w)
        for j in range(4):
            part = turned_pair(u[:, j * 128 : j * 128 + 128], start)
            k[4 * t + j, pl.ds(start, rows), :] = part.astype(jnp.bfloat16)

    def values(w, t, src, start):
        u = dot(src[...], w)
        ut = jnp.transpose(u).astype(jnp.bfloat16)
        for j in range(4):
            cols = slice(j * 128, j * 128 + 128)
            v[4 * t + j, pl.ds(start, rows), :] = u[:, cols].astype(jnp.bfloat16)
            vt[4 * t + j, :, pl.ds(start, rows)] = ut[cols]

    @loop(per)
    def _(t):
        serve_at("k", t, per)
        keys(tiles.get(t + per, 3 * per), t, a, first)

    @loop(per)
    def _(t):
        serve_at("v", t, per)
        values(tiles.get(t + 2 * per, 3 * per), t, a, first)

    def attend(p, block, keys_at):
        spot = slice(block * 256, block * 256 + 256)
        heads = split_heads(q[p, spot, :])
        kk = k[p, keys_at, :]
        vv = vt[p, :, keys_at]
        mask = bias[0, keys_at, spot]
        parts, logs = [], []
        for i in (0, 1):
            s = dot_nt(kk, heads[i]) + mask
            m = jnp.max(s, axis=0, keepdims=True)
            e = jnp.exp(s - m)
            total = jnp.sum(e, axis=0, keepdims=True)
            logs.append(m + jnp.log(total))
            parts.append(dot(vv, e.astype(jnp.bfloat16)) * (1.0 / total))
        return spot, parts, logs

    upper = lax.broadcasted_iota(jnp.int32, (128, 256), 0) < head_dim
    blocks = rows // 256

    @loop(pairs)
    def _(p):
        serve_at("pair", p, pairs)
        for block in range(blocks):
            spot, parts, logs = attend(p, block, pl.ds(first, (block + 1) * 256))
            for i in (0, 1):
                lse[p, i : i + 1, spot] = logs[i]
            o_own[p, :, spot] = jnp.where(upper, parts[0], parts[1])

    serve("other")

    @pl.when(y == 1)
    def _():
        tok_copy.wait_recv()
        first_norm(tokx, ax, atx)
        tiles.first(3 * per, per)

        @loop(per)
        def _(t):
            keys(tiles.get(t + per, 3 * per), t, ax, 0)

        @loop(per)
        def _(t):
            values(tiles.get(t + 2 * per, 3 * per), t, ax, 0)

    save(atx, atx_o)
    save(tokx, tokx_o)
    save(q, q_o)
    save(k, k_o)
    save(v, v_o)

    @pl.when(y == 0)
    def _():
        @loop(pairs)
        def _(p):
            serve_at("more", p, pairs)
            ob[p] = o_own[p].astype(jnp.bfloat16)

    @pl.when(y == 1)
    def _():
        @loop(pairs)
        def _(p):
            serve_at("more", p, pairs)
            for block in range(blocks):
                spot, parts, logs = attend(p, block, pl.ds(0, rows))
                shares = []
                for i in (0, 1):
                    old = lse[p, i : i + 1, spot]
                    top = jnp.maximum(old, logs[i])
                    both = top + jnp.log(jnp.exp(old - top) + jnp.exp(logs[i] - top))
                    lse[p, i : i + 1, spot] = both
                    shares.append((jnp.exp(old - both), jnp.exp(logs[i] - both)))
                own = o_own[p, :, spot]
                first_head = own * shares[0][0] + parts[0] * shares[0][1]
                second_head = own * shares[1][0] + parts[1] * shares[1][1]
                ob[p, :, spot] = jnp.where(upper, first_head, second_head).astype(jnp.bfloat16)

    save(ob, ob_o)
    save(lse, lse_o)

    serve("out")
    go.complete()
    tiles = Tiles(lambda t: wo_f.at[:, columns(t, 512)], wbuf, wsem)
    tiles.first(per)
    a[...] = jnp.transpose(ob[...].reshape(width, rows))

    @loop(per)
    def _(t):
        w = tiles.get(t, per)
        araw[:, columns(t, 512)] = dot(a[...], w)

    save(araw, araw_o)

    @loop(rows // 128)
    def _(i):
        spot = pl.ds(i * 128, 128)
        z, _r = normed(araw[spot, :])
        hidden = tok[spot, :].astype(jnp.float32) + z * gain[1:2, :]
        h[spot, :] = hidden
        z, _r = normed(hidden)
        value = z * gain[2:3, :]
        b[spot, :] = value.astype(jnp.bfloat16)
        bt[:, spot] = jnp.transpose(value).astype(jnp.bfloat16)

    save(h, h_o)
    save(bt, bt_o)

    serve("to up")
    gu.complete()
    tiles = Tiles(lambda t: wu_f.at[:, columns(t, 512)], wbuf, wsem)
    ups = act.shape[0]
    tiles.first(ups)
    c0 = math.sqrt(2.0 / math.pi)

    @loop(ups)
    def _(t):
        serve_at("up", t, ups)
        u = dot(b[...], tiles.get(t, ups))
        square = u * u
        th = jnp.tanh(c0 * (u + 0.044715 * (square * u)))
        value = 0.5 * u * (1.0 + th)
        slope = 0.5 * (1.0 + th) + (0.5 * c0) * u * (1.0 - th * th) * (
            1.0 + (3 * 0.044715) * square
        )
        act[t] = value.astype(jnp.bfloat16)
        actt[t] = jnp.transpose(value).astype(jnp.bfloat16).reshape(2, 256, rows)
        gp[t] = slope.astype(jnp.bfloat16)

    save(actt, gt_o)
    save(gp, gp_o)

    serve("down")
    gd.complete()
    tiles = Tiles(lambda t: wd_f.at[columns(t, 512), :], dbuf, dsem)
    tiles.first(ups)
    mraw[...] = jnp.zeros_like(mraw)

    @loop(ups)
    def _(t):
        mraw[...] += dot(act[t], tiles.get(t, ups))

    save(mraw, mraw_o)
    ends = doc_ends(lens)

    @loop(rows // 128)
    def _(i):
        spot = pl.ds(i * 128, 128)
        z, _r = normed(mraw[spot, :])
        result = h[spot, :] + z * gain[3:4, :]
        place = y * rows + i * 128 + lax.broadcasted_iota(jnp.int32, result.shape, 0)
        result = jnp.where(place < ends[DOCS - 2], result, 0.0)
        out[spot, :] = result.astype(jnp.bfloat16)

    for copy in saves:
        copy.wait()

    @pl.when(y == 0)
    def _():
        tok_copy.wait_send()

    for m in (gg, gq, go, gu, gd):
        m.sent()


def forward(tokens, lengths, gains_wide, w_qkv, w_out, w_up, w_down, tables):
    dp_size = lax.axis_size("dp")
    devices = dp_size * lax.axis_size("ctx")
    rows, width = tokens.shape
    row_len = rows * lax.axis_size("ctx")
    head_dim = width // HEADS
    pairs = width // 128
    ups = w_up.shape[1] // 512
    bf, f32 = jnp.bfloat16, jnp.float32
    any_spec = pl.BlockSpec(memory_space=pl.ANY)
    vm = pl.BlockSpec(memory_space=pltpu.VMEM)
    shape = jax.ShapeDtypeStruct

    def whole(w):
        return shape((w.shape[0] * devices, w.shape[1]), bf)

    outs = [
        shape((rows, width), bf),
        whole(w_qkv),
        whole(w_out),
        whole(w_up),
        whole(w_down),
        shape((8, width), f32),
        shape((pairs, rows, 128), bf),
        shape((pairs, row_len, 128), bf),
        shape((pairs, row_len, 128), bf),
        shape((pairs, 128, rows), bf),
        shape((pairs, 2, rows), f32),
        shape((rows, width), f32),
        shape((rows, width), f32),
        shape((rows, width), f32),
        shape((width, rows), bf),
        shape((ups, 2, 256, rows), bf),
        shape((ups, rows, 512), bf),
        shape((width, rows), bf),
        shape((width, rows), bf),
        shape((rows, width), bf),
    ]
    scratch = [
        pltpu.VMEM((width, 128), bf),
        pltpu.VMEM((8, width), f32),
        pltpu.VMEM((rows, width), bf),
        pltpu.VMEM((rows, width), bf),
        pltpu.VMEM((rows, width), bf),
        pltpu.VMEM((width, rows), bf),
        pltpu.VMEM((width, rows), bf),
        pltpu.VMEM((pairs, rows, 128), bf),
        pltpu.VMEM((pairs, row_len, 128), bf),
        pltpu.VMEM((pairs, row_len, 128), bf),
        pltpu.VMEM((pairs, 128, row_len), bf),
        pltpu.VMEM((1, row_len, rows), f32),
        pltpu.VMEM((pairs, 128, rows), bf),
        pltpu.VMEM((pairs, 2, rows), f32),
        pltpu.VMEM((rows, width), f32),
        pltpu.VMEM((rows, width), f32),
        pltpu.VMEM((rows, width), f32),
        pltpu.VMEM((rows, width), bf),
        pltpu.VMEM((width, rows), bf),
        pltpu.VMEM((ups, rows, 512), bf),
        pltpu.VMEM((ups, 2, 256, rows), bf),
        pltpu.VMEM((ups, rows, 512), bf),
        pltpu.VMEM((3, width, 512), bf),
        pltpu.VMEM((3, 512, width), bf),
    ]
    scratch += [pltpu.SemaphoreType.DMA((Gather.sems(dp_size // 4),))] * 10
    scratch += [pltpu.SemaphoreType.DMA((3,))] * 3 + [pltpu.SemaphoreType.DMA((19,))]
    scratch += [pltpu.VMEM((pairs, 128, rows), f32), pltpu.VMEM((rows, width), bf)]
    scratch += [pltpu.VMEM((row_len, 128), f32)] * 2
    return pl.pallas_call(
        functools.partial(forward_kernel, dp_size, head_dim),
        out_shape=outs,
        in_specs=[any_spec, pl.BlockSpec(memory_space=pltpu.SMEM), vm]
        + [any_spec] * 4
        + [any_spec] * 2,
        out_specs=[vm] + [any_spec] * (len(outs) - 1),
        scratch_shapes=scratch,
        compiler_params=pltpu.CompilerParams(
            collective_id=0, has_side_effects=True, vmem_limit_bytes=60 * 2**20
        ),
    )(tokens, lengths, gains_wide, w_qkv, w_out, w_up, w_down, *tables)


def backward_kernel(dp_size, head_dim, *refs):
    (tok_i, dout_i, lens, gain, cosine_i, sine_i, wq, wo, wu, wd) = refs[:10]
    (q_i, k_i, v_i, ob_i, lse_i, araw_i, h_i, mraw_i, bt_i, gt_i, gp_i, at_i, atx_i, tokx_i) = refs[10:24]
    (dtok, out_q, out_o, out_u, out_d, out_g) = refs[24:30]
    (gts, dus, dzs) = refs[30:33]
    (part, rec3, rec, gpart, grec3, grec) = refs[33:39]
    (f1, f2, acc, dm, dms, da, das, dz, bt, bts, obts, ats, atx, atxs) = refs[39:53]
    (q, ob, lse, dk, dv, dg, dgs, dgt, dnxs) = refs[53:62]
    (kbuf, vbuf, wbuf, dbuf, gbuf, gpbuf, sbuf) = refs[62:69]
    tsems = refs[69:79]
    usend, urecv, gsend, grecv, zsend, zrecv, osend, orecv, lsem = refs[79:88]
    dnsem = refs[88]
    gsems, rsems = refs[89:96], refs[96:103]
    tok, cosine, sine, dout = refs[103:107]
    at, xbuf, do, dnx, tokx = bt, gpbuf, dm, da, das
    g = Place(dp_size)
    Z, y, c = g.Z, g.y, g.c
    rows, width = dout_i.shape
    half = head_dim // 2
    pairs = width // 128
    scale = head_dim ** (-0.5)
    ups = gp_i.shape[0]
    per = width // 512
    bf, f32 = jnp.bfloat16, jnp.float32
    first = pl.multiple_of(y * rows, rows)

    def to_sib(src, dst, send, recv):
        return pltpu.make_async_remote_copy(
            src_ref=src,
            dst_ref=dst,
            send_sem=send,
            recv_sem=recv,
            device_id=g.sib,
            device_id_type=MESH,
        )

    def load(src, dst, i):
        return pltpu.make_async_copy(src, dst, lsem.at[i])

    h_load = load(h_i, f2, 0)
    bt_load = load(bt_i.at[:, c], bt, 1)
    atx_load = load(atx_i.at[:, c], atx, 2)
    q_load = load(q_i, q, 3)
    ob_load = load(ob_i, ob, 4)
    lse_load = load(lse_i, lse, 5)
    at_load = load(at_i.at[:, c], at, 6)
    tokx_load = load(tokx_i, tokx, 7)
    tok_load = load(tok_i, tok, 8)
    cosine_load = load(cosine_i, cosine, 9)
    sine_load = load(sine_i, sine, 10)
    dout_load = load(dout_i, dout, 11)

    def gt_send(i):
        half_z = pl.ds(pl.multiple_of(lax.rem(i, 2) * 256, 256), 256)
        return to_sib(
            gt_i.at[i, 1 - c], gts.at[lax.div(i, 2), half_z], gsend.at[i], grecv.at[i]
        )

    bt_send = to_sib(bt_i.at[:, 1 - c], bts, osend.at[0], orecv.at[0])
    ob_send = to_sib(ob_i.at[:, 1 - c], obts, osend.at[1], orecv.at[1])
    at_send = to_sib(at_i.at[:, 1 - c], ats, osend.at[2], orecv.at[2])
    atx_send = to_sib(atx_i.at[:, 1 - c], atxs, osend.at[3], orecv.at[3])

    def dm_send(i):
        spot = columns(i, 128)
        return to_sib(dm.at[spot, :], dms.at[spot, :], osend.at[7 + i], orecv.at[7 + i])

    da_send = to_sib(da, das, osend.at[5], orecv.at[5])
    dg_send = to_sib(dg, dgs, osend.at[6], orecv.at[6])
    dnx_send = pltpu.make_async_remote_copy(
        src_ref=dnx,
        dst_ref=dnxs,
        send_sem=dnsem.at[0],
        recv_sem=dnsem.at[1],
        device_id=g.device(g.z, g.x, c, 1 - y),
        device_id_type=MESH,
    )

    def du_send(t):
        return to_sib(dz.at[t], dus.at[t], usend.at[t], urecv.at[t])

    def dz_send(e, p):
        t = e * per + lax.div(p, 4)
        spot = columns(lax.div(lax.rem(p, 4), 2), 256)
        n = e * (pairs // 2) + lax.div(p, 2)
        return to_sib(dz.at[t, :, spot], dzs.at[t, :, spot], zsend.at[n], zrecv.at[n])

    landing = (rec3, rec)

    def write_d(total):
        out_d[...] = total.reshape(out_d.shape)

    def write_into(out, column):
        def write(total):
            for i in range(total.shape[0]):
                begin = column + i * width
                out[:, begin : begin + total.shape[2]] = total[i]

        return write

    def write_g(total):
        out_g[...] = total[0]

    modes = [c == 0 if m is None else m for m in SHARE_BY_Z]
    s_d = Share(
        g, part, 0, landing, 0, 4, gsems[0], rsems[0], write_d, modes[3]
    )
    s_u = Share(
        g, part, 4, landing, 4, 4, gsems[1], rsems[1], write_into(out_u, 0), modes[2]
    )
    s_o = Share(
        g, part, 8, landing, 8, 1, gsems[3], rsems[3], write_into(out_o, 0),
        modes[1],
    )
    s_q = [
        Share(
            g, part, 9, landing, 9, 3, gsems[4 + i], rsems[4 + i],
            write_into(out_q, i * 512), modes[0], pl.ds(i * 512, 512),
        )
        for i in (0, 1)
    ]
    s_g = Share(g, gpart, 0, (grec3, grec), 0, 1, gsems[6], rsems[6], write_g, False)
    groups = (s_d, s_u, s_o, s_q[0], s_q[1], s_g)

    def serve(name, i=0):
        for step in SHARE_PLAN.get(name, {}).get(i, ()):
            s, kind, j = groups[step // 100], step // 10 % 10, step % 10
            if kind < 2:
                (s.stage3, s.stage2)[kind](j)
            else:
                (s.sum_z, s.last)[kind - 2]()

    def serve_at(name, t, count):
        for i in range(count):
            if i in SHARE_PLAN.get(name, {}):
                pl.when(t == i)(functools.partial(serve, name, i))

    mraws = Tiles(lambda i: mraw_i.at[columns(i, 128), :], f1, tsems[9])
    araws = Tiles(lambda i: araw_i.at[columns(i, 128), :], f1, tsems[9])
    dout_load.start()
    mraws.first(rows // 128)
    g.barrier()
    for j in range(Z):
        for i in (0, 1):
            gt_send(g.order(j) * 2 + i).start()
    for copy in (bt_send, ob_send, at_send):
        copy.start()

    @pl.when(y == 1)
    def _():
        atx_send.start()

    def z_of(j):
        return sum(jnp.where(j == i, g.order(i), 0) for i in range(Z))

    def gt_ready(j):
        for i in (0, 1):
            gt_send(z_of(j) * 2 + i).wait_recv()

    own_g = Tiles(lambda j: gt_i.at[pl.ds(z_of(j) * 2, 2), c], gbuf, tsems[0])
    sib_g = Tiles(lambda j: gts.at[z_of(j)], sbuf, tsems[1], gt_ready)
    own_g.first(Z)
    for copy in (
        h_load, bt_load, atx_load, q_load, ob_load, lse_load, cosine_load, sine_load, tok_load
    ):
        copy.start()
    dg[...] = jnp.zeros_like(dg)
    ends = doc_ends(lens)

    def upstream(i):
        e = dout[pl.ds(i * 128, 128), :].astype(f32)
        place = y * rows + i * 128 + lax.broadcasted_iota(jnp.int32, e.shape, 0)
        return jnp.where(place < ends[DOCS - 2], e, 0.0)

    def gain_sum(index, term):
        dg[index : index + 1, :] += jnp.sum(term, axis=0, keepdims=True)

    dout_load.wait()

    @loop(rows // 128)
    def _(i):
        value, term = norm_pull(mraws.get(i, rows // 128), gain[3:4, :], upstream(i))
        dm[pl.ds(i * 128, 128), :] = value.astype(bf)
        gain_sum(3, term)
        dm_send(i).start()

    downs = Tiles(lambda t: wd.at[columns(t, 512), :], dbuf, tsems[2])
    upw = Tiles(lambda t: wu.at[:, columns(t, 512)], wbuf, tsems[3])
    slopes = Tiles(lambda t: gp_i.at[t], gpbuf, tsems[4])
    for tiles in (downs, upw, slopes):
        tiles.first(ups)
    araws.first(rows // 128)
    keys = Tiles(lambda p: k_i.at[p], kbuf, tsems[6])
    values = Tiles(lambda p: v_i.at[p], vbuf, tsems[7])
    keys.first(pairs)
    values.first(pairs)
    sib_g.first(Z)
    for i in range(rows // 128):
        dm_send(i).wait_recv()

    @loop(Z)
    def _(j):
        z = z_of(j)
        total = dot(own_g.get(j, Z).reshape(512, rows), dm[...])
        total += dot(sib_g.get(j, Z), dms[...])
        total = total.astype(bf).reshape(4, 4, 32, width)
        for a in range(4):
            for e in range(4):
                part[e, 4 * z + a] = total[a, e]
        s_d.start(z)

    def add_to(halves, value, weights):
        for j in (0, 1):
            halves[j] += dot_nt(value, weights[j * 512 : (j + 1) * 512])

    sib_du = Tiles(lambda t: dus.at[t], sbuf, tsems[5], lambda t: du_send(t).wait_recv())
    acc[...] = jnp.zeros_like(acc)

    @loop(ups)
    def _(t):
        serve_at("du", t, ups)
        du = dot_nt(dm[...], downs.get(t, ups)) * slopes.get(t, ups).astype(f32)
        du = du.astype(bf)
        dz[t] = du
        du_send(t).start()
        add_to(acc, du, upw.get(t, ups))
        pl.when(t == 3)(lambda: sib_du.first(ups))

    outs = Tiles(lambda t: wo.at[columns(t, 512), :], dbuf, tsems[2])
    outs.first(per)
    bt_load.wait()
    bt_send.wait_recv()
    @loop(ups)
    def _(t):
        serve_at("up", t, ups)
        total = dot(bt[...].reshape(-1, rows), dz[t])
        total += dot(bts[...].reshape(-1, rows), sib_du.get(t, ups))
        part[4 + lax.div(t, per), :, :, columns(lax.rem(t, per), 512)] = (
            total.astype(bf).reshape(4 * Z, 32, 512)
        )

    s_u.start_all()
    at_load.start()

    serve("norm")
    h_load.wait()

    @loop(rows // 128)
    def _(i):
        spot = pl.ds(i * 128, 128)
        e = jnp.concatenate([acc[0, spot, :], acc[1, spot, :]], axis=1)
        value, term = norm_pull(f2[spot, :], gain[2:3, :], e)
        gain_sum(2, term)
        dh = upstream(i) + value
        f2[spot, :] = dh
        value, term = norm_pull(araws.get(i, rows // 128), gain[1:2, :], dh)
        gain_sum(1, term)
        da[spot, :] = value.astype(bf)

    da_send.start()
    for i in range(rows // 128):
        dm_send(i).wait_send()
    serve("do")

    @loop(per)
    def _(t):
        do[:, columns(t, 512)] = dot_nt(da[...], outs.get(t, per)).astype(bf)

    serve("out")
    ob_load.wait()
    ob_send.wait_recv()
    da_send.wait_recv()

    @loop(per)
    def _(t):
        total = dot(ob[:, c].reshape(-1, rows), da[:, columns(t, 512)])
        total += dot(obts[...].reshape(-1, rows), das[:, columns(t, 512)])
        part[8, :, :, columns(t, 512)] = total.astype(bf).reshape(4 * Z, 32, 512)

    s_o.start_all()
    for t in range(ups):
        du_send(t).wait_send()

    qkv_w = Tiles(lambda t: wq.at[:, columns(t, 512)], wbuf, tsems[3])
    pl.when(y == 1)(lambda: qkv_w.first(3 * per, per))
    serve("mask")
    fill_bias(acc, lens, y * rows, rows)
    pl.when(y == 1)(lambda: tokx_load.start())
    for copy in (q_load, lse_load, cosine_load, sine_load, tok_load):
        copy.wait()
    blocks = rows // 256

    def turned_keys(p, base):
        kk = kbuf[lax.rem(p, 2), pl.ds(base, rows), :]
        return jnp.transpose(kk.astype(f32)).astype(bf)

    def attend(p, block, base, count, fresh, kt):
        spot = slice(block * 256, block * 256 + 256)
        slot = lax.rem(p, 2)
        kk = kbuf[slot, pl.ds(base, count), :]
        vv = vbuf[slot, pl.ds(base, count), :]
        kt = kt[:, :count]
        qs = split_heads(q[p, spot, :])
        do_pair = do[spot, columns(p, 128)]
        dos = split_heads(do_pair)
        ob_pair = ob[p, :, :, spot].astype(f32).reshape(128, -1)
        dot_o = jnp.transpose(do_pair.astype(f32)) * ob_pair
        mask = acc[lax.div(base, 512), :count, spot]
        parts, dk_, dv_ = [], [], []
        for i in (0, 1):
            delta = jnp.sum(
                dot_o[i * head_dim : (i + 1) * head_dim], axis=0, keepdims=True
            )
            s = dot_nt(kk, qs[i]) + mask
            prob = jnp.exp(s - lse[p, i : i + 1, spot])
            ds = (prob * (dot_nt(vv, dos[i]) - delta)).astype(bf)
            dv_.append(dot(prob.astype(bf), dos[i]))
            dk_.append(dot(ds, qs[i]))
            parts.append(dot(kt, ds))
        if fresh:
            dk[:count, :] = dk_[0] + dk_[1]
            dv[:count, :] = dv_[0] + dv_[1]
        else:
            dk[:count, :] += dk_[0] + dk_[1]
            dv[:count, :] += dv_[0] + dv_[1]
        upper = lax.broadcasted_iota(jnp.int32, parts[0].shape, 0) < head_dim
        dq = jnp.transpose(jnp.where(upper, parts[0], parts[1]) * scale)
        start = pl.multiple_of(first + block * 256, 256)
        return spot, turn(dq, cosine[pl.ds(start, 256), :], -sine[pl.ds(start, 256), :], half)

    def lanes(p):
        return columns(lax.rem(p, 4), 128)

    def keep(p, start, base):
        spot = pl.ds(start, rows)
        u = turn(dk[...], cosine[spot, :], -sine[spot, :], half)
        dz[base + lax.div(p, 4), :, lanes(p)] = u.astype(bf)
        dz[base + per + lax.div(p, 4), :, lanes(p)] = dv[...].astype(bf)

    def other_half():
        acc[...] = jnp.zeros_like(acc)
        da_send.wait_send()
        tokx_load.wait()

        @loop(2 * per)
        def _(t):
            add_to(acc, dz[t + 3 * per], qkv_w.get(t + per, 3 * per))

        @loop(rows // 128)
        def _(i):
            spot = pl.ds(i * 128, 128)
            e = jnp.concatenate([acc[0, spot, :], acc[1, spot, :]], axis=1)
            value, term = norm_pull(tokx[spot, :].astype(f32), gain[0:1, :], e)
            gain_sum(0, term)
            dnx[spot, :] = value.astype(bf)

        dnx_send.start()

    def qkv_gradient(h):
        at_both = (at[...].reshape(-1, rows), ats[...].reshape(-1, rows))

        def ready(i):
            for j in (1, 3):
                dz_send(i, h * 4 + j).wait_recv()

        sib_dz = Tiles(lambda i: dzs.at[i * per + h], sbuf, tsems[5], ready)
        sib_dx = Tiles(lambda i: dzs.at[i * per + h], xbuf, tsems[8], ready)
        sib_dz.first(3)
        pl.when(y == 1)(lambda: sib_dx.first(5, 3))

        @loop(3)
        def _(e):
            def total():
                return dot(at_both[0], dz[e * per + h]) + dot(at_both[1], sib_dz.get(e, 3))

            def keep_total(value):
                part[9 + e, :, :, columns(h, 512)] = value.astype(bf).reshape(4 * Z, 32, 512)

            both = (y == 1) & (e > 0)

            @pl.when(jnp.logical_not(both))
            def _():
                keep_total(total())

            @pl.when(both)
            def _():
                value = total() + dot(atx[...].reshape(-1, rows), dz[(e + 2) * per + h])
                keep_total(value + dot(atxs[...].reshape(-1, rows), sib_dx.get(e + 2, 5)))

        for i in (0, 1):
            pl.when(h == i)(lambda: s_q[i].start_all())

    @pl.when(y == 0)
    def _():
        for p in range(pairs):
            serve("more", p)
        serve("other")

    @pl.when(y == 1)
    def _():
        @loop(pairs)
        def _(p):
            serve_at("more", p, pairs)
            keys.get(p, pairs)
            values.get(p, pairs)
            kt = turned_keys(p, 0)
            for block in range(blocks):
                spot, dq = attend(p, block, 0, rows, block == 0, kt)
                dz[lax.div(p, 4), spot, lanes(p)] = dq.astype(bf)
            keep(p, 0, 3 * per)

            @pl.when(lax.rem(p, 2) == 1)
            def _():
                for e in (3, 4):
                    dz_send(e, p).start()

        serve("other")
        keys.first(pairs)
        values.first(pairs)
        other_half()
        fill_bias(acc, lens, y * rows, rows)

    @loop(pairs)
    def _(p):
        serve_at("pair", p, pairs)
        keys.get(p, pairs)
        values.get(p, pairs)
        kt = turned_keys(p, first)
        for block in reversed(range(blocks)):
            count = (block + 1) * 256
            spot, dq = attend(p, block, first, count, block == blocks - 1, kt)
            before = dz[lax.div(p, 4), spot, lanes(p)].astype(f32)
            dq += jnp.where(y == 1, before, 0.0)
            dz[lax.div(p, 4), spot, lanes(p)] = dq.astype(bf)
        keep(p, first, per)

        @pl.when(lax.rem(p, 2) == 1)
        def _():
            for e in range(3):
                dz_send(e, p).start()

        @pl.when(p == pairs // 2 - 1)
        def _():
            serve("half")
            at_load.wait()
            at_send.wait_recv()
            atx_load.wait()
            pl.when(y == 1)(lambda: atx_send.wait_recv())

        @pl.when(p == pairs - 1)
        def _():
            serve("rest")

        @pl.when(lax.rem(p, 4) == 3)
        def _():
            qkv_gradient(lax.div(p, 4))

    serve("input")
    qkv_w.first(3 * per)

    acc[...] = jnp.zeros_like(acc)

    @loop(3 * per)
    def _(t):
        add_to(acc, dz[t], qkv_w.get(t, 3 * per))

    @loop(rows // 128)
    def _(i):
        spot = pl.ds(i * 128, 128)
        e = jnp.concatenate([acc[0, spot, :], acc[1, spot, :]], axis=1)
        value, term = norm_pull(tok[spot, :].astype(f32), gain[0:1, :], e)
        gain_sum(0, term)
        f2[spot, :] += value

    dg_send.start()
    serve("gains")
    dg_send.wait_recv()
    wide = jnp.concatenate([dg[...] + dgs[...], jnp.zeros((120, width), f32)], axis=0)
    dgt[...] = jnp.transpose(wide).reshape(dgt.shape)
    gpart[0] = dgt[:, c].reshape(gpart.shape[1:])
    s_g.start_all()
    serve("end")

    @pl.when(y == 0)
    def _():
        dnx_send.wait_recv()
        dtok[...] = (f2[...] + dnxs[...].astype(f32)).astype(bf)

    @pl.when(y == 1)
    def _():
        dtok[...] = f2[...].astype(bf)

    for i in range(2 * Z):
        gt_send(jnp.int32(i)).wait_send()
    for copy in (bt_send, ob_send, at_send, dg_send):
        copy.wait_send()
    @loop(pairs // 2)
    def _(i):
        for e in range(3):
            dz_send(e, 2 * i + 1).wait_send()

    @pl.when(y == 0)
    def _():
        da_send.wait_send()

    @pl.when(y == 1)
    def _():
        atx_send.wait_send()
        dnx_send.wait_send()

        @loop(pairs // 2)
        def _(i):
            for e in (3, 4):
                dz_send(e, 2 * i + 1).wait_send()

    for s in (s_d, s_u, s_o, s_q[0], s_q[1], s_g):
        s.sent()


def backward(tokens, d_out, lengths, gain_rows, tables, weights, saved, shards):
    dp_size = lax.axis_size("dp")
    Z = dp_size // 4
    rows, width = tokens.shape
    row_len = rows * lax.axis_size("ctx")
    head_dim = width // HEADS
    pairs = width // 128
    per = width // 512
    bf, f32 = jnp.bfloat16, jnp.float32
    ups = saved[10].shape[0]
    any_spec = pl.BlockSpec(memory_space=pl.ANY)
    vm = pl.BlockSpec(memory_space=pltpu.VMEM)
    smem = pl.BlockSpec(memory_space=pltpu.SMEM)
    shape = jax.ShapeDtypeStruct
    block = 32
    saved = list(saved)
    for i in (3, 8, 11, 12):
        saved[i] = saved[i].reshape(2 * Z, 2, width // (4 * Z), rows)
    outs = [
        shape((rows, width), bf),
        shape(shards[0].shape, f32),
        shape(shards[1].shape, f32),
        shape(shards[2].shape, f32),
        shape(shards[3].shape, f32),
        shape((block, 128), f32),
        shape((Z, 512, rows), bf),
        shape((ups, rows, 512), bf),
        shape((5 * per, rows, 512), bf),
    ]
    core_rows = (2 * Z, width // (4 * Z), rows)
    scratch = [
        pltpu.VMEM((12, 4 * Z, block, width), bf),
        pltpu.VMEM((12, 2 * Z, block, width), bf),
        pltpu.VMEM((12, 2 * Z - 1, block, width), bf),
        pltpu.VMEM((1, 4 * Z, block, 128), f32),
        pltpu.VMEM((1, 2 * Z, block, 128), f32),
        pltpu.VMEM((1, 2 * Z - 1, block, 128), f32),
        pltpu.VMEM((2, 128, width), f32),
        pltpu.VMEM((rows, width), f32),
        pltpu.VMEM((2, rows, 512), f32),
        pltpu.VMEM((rows, width), bf),
        pltpu.VMEM((rows, width), bf),
        pltpu.VMEM((rows, width), bf),
        pltpu.VMEM((rows, width), bf),
        pltpu.VMEM((max(ups, 5 * per), rows, 512), bf),
    ]
    scratch += [pltpu.VMEM(core_rows, bf)] * 6
    scratch += [
        pltpu.VMEM((pairs, rows, 128), bf),
        pltpu.VMEM((2 * Z, 2, width // (4 * Z), rows), bf),
        pltpu.VMEM((pairs, 2, rows), f32),
        pltpu.VMEM((rows, 128), f32),
        pltpu.VMEM((rows, 128), f32),
        pltpu.VMEM((8, width), f32),
        pltpu.VMEM((8, width), f32),
        pltpu.VMEM((2 * Z, 2, width // (4 * Z), 128), f32),
        pltpu.VMEM((rows, width), bf),
        pltpu.VMEM((2, row_len, 128), bf),
        pltpu.VMEM((2, row_len, 128), bf),
        pltpu.VMEM((2, width, 512), bf),
        pltpu.VMEM((2, 512, width), bf),
        pltpu.VMEM((2, 2, 256, rows), bf),
        pltpu.VMEM((2, rows, 512), bf),
        pltpu.VMEM((2, rows, 512), bf),
    ]
    dma = pltpu.SemaphoreType.DMA
    scratch += [dma((3,))] * 10
    scratch += [dma((ups,))] * 2 + [dma((2 * Z,))] * 2 + [dma((5 * pairs,))] * 2
    scratch += [dma((11,))] * 2 + [dma((12,)), dma((2,))]
    scratch += [dma((Share.sems(Z),))] * 14
    scratch += [pltpu.VMEM((rows, width), bf)] + [pltpu.VMEM((row_len, 128), f32)] * 2
    scratch += [pltpu.VMEM((rows, width), bf)]
    return pl.pallas_call(
        functools.partial(backward_kernel, dp_size, head_dim),
        out_shape=outs,
        in_specs=[any_spec, any_spec, smem, vm] + [any_spec] * 20,
        out_specs=[vm] * 6 + [any_spec] * 3,
        scratch_shapes=scratch,
        compiler_params=pltpu.CompilerParams(
            collective_id=1, has_side_effects=True, vmem_limit_bytes=63 * 2**20
        ),
    )(tokens, d_out, lengths, gain_rows, *tables, *weights, *saved)


def hand_on(*arrays):
    n = len(arrays) - 1

    def kernel(*refs):
        sources, targets = refs[: n + 1], refs[n + 1 : 2 * n + 2]
        held, loaded, stored = refs[2 * n + 2 : 3 * n + 2], refs[-2], refs[-1]
        loads = [
            pltpu.make_async_copy(sources[i], held[i], loaded.at[i]) for i in range(n)
        ]
        stores = [
            pltpu.make_async_copy(held[i], targets[i], stored.at[i]) for i in range(n)
        ]
        for copy in loads:
            copy.start()
        targets[n][...] = jnp.transpose(sources[n][...])[: targets[n].shape[0]]
        for load, store in zip(loads, stores):
            load.wait()
            store.start()
        for copy in stores:
            copy.wait()

    any_spec = pl.BlockSpec(memory_space=pl.ANY)
    vm = pl.BlockSpec(memory_space=pltpu.VMEM)
    shapes = [jax.ShapeDtypeStruct(a.shape, a.dtype) for a in arrays[:n]]
    shapes.append(jax.ShapeDtypeStruct((4, arrays[n].shape[0]), arrays[n].dtype))
    return pl.pallas_call(
        kernel,
        out_shape=shapes,
        in_specs=[any_spec] * n + [vm],
        out_specs=[any_spec] * n + [vm],
        scratch_shapes=[pltpu.VMEM(a.shape, a.dtype) for a in arrays[:n]]
        + [pltpu.SemaphoreType.DMA((n,))] * 2,
        compiler_params=pltpu.CompilerParams(vmem_limit_bytes=16 * 2**20),
    )(*arrays)


def layer_norm(values, gain_vec):
    center = values - jnp.mean(values, axis=-1, keepdims=True)
    spread = jnp.mean(center * center, axis=-1, keepdims=True)
    return center * lax.rsqrt(spread + epsilon) * gain_vec


def norm_back(values, gain_vec, upstream):
    unused, pullback = jax.vjp(layer_norm, values, gain_vec)
    return pullback(upstream)


def rotate(values, cosine_table, sine_table, direction):
    half_dim = values.shape[-1] // 2
    first_half = values[..., :half_dim]
    second_half = values[..., half_dim:]
    return jnp.concatenate(
        [
            first_half * cosine_table - direction * second_half * sine_table,
            second_half * cosine_table + direction * first_half * sine_table,
        ],
        axis=-1,
    )


def doc_layout(lengths, row_len):
    doc_ends = jnp.cumsum(lengths, axis=-1)
    places = jnp.arange(row_len, dtype=jnp.int32)
    passed = places[None, :, None] >= doc_ends[:, None, :]
    segment = jnp.sum(passed.astype(jnp.int32), axis=-1)
    starts = jnp.sum(jnp.where(passed, lengths[:, None, :], 0), axis=-1)
    position = places[None, :] - starts
    is_valid = places[None, :] < doc_ends[:, DOCS - 2][:, None]
    return (segment[0], position[0], is_valid[0])


def allowed_keys(own_seg, own_place, seg_full, first_key, block_rows):
    key_place = first_key + jnp.arange(block_rows, dtype=jnp.int32)
    key_seg = lax.dynamic_slice_in_dim(seg_full, first_key, block_rows)
    return (own_seg[:, None] == key_seg[None, :]) & (key_place[None, :] <= own_place[:, None])


def make_fold(queries, own_seg, own_place, seg_full, score_scale):

    def fold_piece(fold_state, piece, start):
        key_piece, value_piece = piece
        piece_rows = key_piece.shape[0]
        block_rows = math.gcd(piece_rows, 256)
        block_count = piece_rows // block_rows
        key_blocks = key_piece.reshape((block_count, block_rows) + key_piece.shape[1:])
        value_blocks = value_piece.reshape((block_count, block_rows) + value_piece.shape[1:])

        def step_block(carried, block_items):
            row_max, row_sum, weighted = carried
            key_block, value_block, block_id = block_items
            allowed = allowed_keys(own_seg, own_place, seg_full, block_id * block_rows, block_rows)
            scores = (
                jnp.einsum("qhd,khd->hqk", queries, key_block, preferred_element_type=jnp.float32)
                * score_scale
            )
            scores = jnp.where(allowed[None], scores, masked_score)
            new_max = jnp.maximum(row_max, jnp.max(scores, axis=-1))
            factor = jnp.exp(row_max - new_max)
            shifted = jnp.where(allowed[None], jnp.exp(scores - new_max[..., None]), 0.0)
            row_sum = row_sum * factor + jnp.sum(shifted, axis=-1)
            weighted = weighted * factor[..., None] + jnp.einsum(
                "hqk,khd->hqd",
                shifted.astype(jnp.bfloat16),
                value_block,
                preferred_element_type=jnp.float32,
            )
            return ((new_max, row_sum, weighted), None)

        block_ids = jnp.arange(block_count, dtype=jnp.int32)
        fold_state, unused = lax.scan(step_block, fold_state, (key_blocks, value_blocks, block_ids))
        return fold_state

    return fold_piece


def per_device(tokens, lengths, w_qkv, w_out, w_up, w_down, gains, d_out):
    tok_rows, model_width = tokens.shape
    row_len = tok_rows * lax.axis_size("ctx")
    head_count = HEADS
    head_dim = model_width // head_count
    score_scale = head_dim ** (-0.5)
    head_shape = (tok_rows, head_count, head_dim)
    seg_full, pos_full, valid_full = doc_layout(lengths, row_len)
    offset = lax.axis_index("ctx") * tok_rows
    own_seg = lax.dynamic_slice_in_dim(seg_full, offset, tok_rows)
    own_pos = lax.dynamic_slice_in_dim(pos_full, offset, tok_rows)
    own_valid = lax.dynamic_slice_in_dim(valid_full.astype(jnp.float32), offset, tok_rows)
    own_place = offset + jnp.arange(tok_rows, dtype=jnp.int32)
    freq_index = jnp.arange(head_dim // 2, dtype=jnp.float32)
    angles = own_pos.astype(jnp.float32)[:, None] * 10000.0 ** (-2.0 * freq_index / head_dim)
    cosine_table = jnp.cos(angles)[:, None, :]
    sine_table = jnp.sin(angles)[:, None, :]
    qkv_full, out_full, up_full, down_full, gain_full = (
        lax.all_gather(w_qkv, ("dp", "ctx"), axis=0, tiled=True),
        lax.all_gather(w_out, ("dp", "ctx"), axis=0, tiled=True),
        lax.all_gather(w_up, ("dp", "ctx"), axis=0, tiled=True),
        lax.all_gather(w_down, ("dp", "ctx"), axis=0, tiled=True),
        lax.all_gather(gains, ("dp", "ctx"), axis=0, tiled=True),
    )
    gain_f = gain_full.astype(jnp.float32)
    stream = tokens.astype(jnp.float32)
    normed = layer_norm(stream, gain_f[:, 0]).astype(jnp.bfloat16)
    qkv_raw = jnp.dot(normed, qkv_full, preferred_element_type=jnp.float32)
    queries = rotate(
        qkv_raw[:, :model_width].reshape(head_shape), cosine_table, sine_table, 1.0
    ).astype(jnp.bfloat16)
    key_heads = rotate(
        qkv_raw[:, model_width : 2 * model_width].reshape(head_shape), cosine_table, sine_table, 1.0
    ).astype(jnp.bfloat16)
    value_heads = qkv_raw[:, 2 * model_width :].reshape(head_shape).astype(jnp.bfloat16)
    start_state = (
        jnp.full((head_count, tok_rows), masked_score, jnp.float32),
        jnp.zeros((head_count, tok_rows), jnp.float32),
        jnp.zeros((head_count, tok_rows, head_dim), jnp.float32),
    )
    fold_piece = make_fold(queries, own_seg, own_place, seg_full, score_scale)
    row_max, row_sum, weighted = fold_piece(
        start_state,
        (
            lax.all_gather(key_heads, "ctx", axis=0, tiled=True),
            lax.all_gather(value_heads, "ctx", axis=0, tiled=True),
        ),
        jnp.int32(0),
    )
    attended = jnp.transpose(weighted / row_sum[..., None], (1, 0, 2))
    attended_b = attended.reshape(tok_rows, model_width).astype(jnp.bfloat16)
    attn_raw = jnp.dot(attended_b, out_full, preferred_element_type=jnp.float32)
    hidden = stream + layer_norm(attn_raw, gain_f[:, 1])
    mlp_in = layer_norm(hidden, gain_f[:, 2]).astype(jnp.bfloat16)
    up_proj = jnp.dot(mlp_in, up_full, preferred_element_type=jnp.float32)
    activated = jax.nn.gelu(up_proj).astype(jnp.bfloat16)
    mlp_raw = jnp.dot(activated, down_full, preferred_element_type=jnp.float32)
    result = hidden + layer_norm(mlp_raw, gain_f[:, 3])
    output = (result * own_valid[:, None]).astype(jnp.bfloat16)
    qkv_back, out_back, up_back, down_back = (
        lax.all_gather(w_qkv, ("dp", "ctx"), axis=0, tiled=True),
        lax.all_gather(w_out, ("dp", "ctx"), axis=0, tiled=True),
        lax.all_gather(w_up, ("dp", "ctx"), axis=0, tiled=True),
        lax.all_gather(w_down, ("dp", "ctx"), axis=0, tiled=True),
    )
    upstream = d_out.astype(jnp.float32) * own_valid[:, None]
    d_mlp, d_gain_four = norm_back(mlp_raw, gain_f[:, 3], upstream)
    d_mlp_b = d_mlp.astype(jnp.bfloat16)
    grad_down = jnp.einsum("tf,td->fd", activated, d_mlp_b, preferred_element_type=jnp.float32)
    d_activated = jnp.einsum("td,fd->tf", d_mlp_b, down_back, preferred_element_type=jnp.float32)
    unused, gelu_pull = jax.vjp(jax.nn.gelu, up_proj)
    d_up_b = gelu_pull(d_activated)[0].astype(jnp.bfloat16)
    grad_up = jnp.einsum("td,tf->df", mlp_in, d_up_b, preferred_element_type=jnp.float32)
    d_mlp_in = jnp.einsum("tf,df->td", d_up_b, up_back, preferred_element_type=jnp.float32)
    d_hidden_part, d_gain_three = norm_back(hidden, gain_f[:, 2], d_mlp_in)
    d_hidden = upstream + d_hidden_part
    d_attn, d_gain_two = norm_back(attn_raw, gain_f[:, 1], d_hidden)
    d_attn_b = d_attn.astype(jnp.bfloat16)
    grad_out = jnp.einsum("td,te->de", attended_b, d_attn_b, preferred_element_type=jnp.float32)
    d_attended = (
        jnp.einsum("te,de->td", d_attn_b, out_back, preferred_element_type=jnp.float32)
        .astype(jnp.bfloat16)
        .reshape(head_shape)
    )
    row_dot = jnp.einsum("qhd,qhd->hq", d_attended.astype(jnp.float32), attended)
    key_all, value_all = (
        lax.all_gather(key_heads, "ctx", axis=0, tiled=True),
        lax.all_gather(value_heads, "ctx", axis=0, tiled=True),
    )
    block_rows = math.gcd(row_len, 256)
    block_count = row_len // block_rows
    key_blocks = key_all.reshape((block_count, block_rows) + key_all.shape[1:])
    value_blocks = value_all.reshape((block_count, block_rows) + value_all.shape[1:])

    def back_block(d_queries, block_items):
        key_block, value_block, block_id = block_items
        allowed = allowed_keys(own_seg, own_place, seg_full, block_id * block_rows, block_rows)
        scores = (
            jnp.einsum("qhd,khd->hqk", queries, key_block, preferred_element_type=jnp.float32)
            * score_scale
        )
        attn_prob = jnp.where(
            allowed[None], jnp.exp(scores - row_max[..., None]) / row_sum[..., None], 0.0
        )
        d_prob = jnp.einsum(
            "qhd,khd->hqk", d_attended, value_block, preferred_element_type=jnp.float32
        )
        d_scores = (attn_prob * (d_prob - row_dot[..., None])).astype(jnp.bfloat16)
        d_queries = (
            d_queries
            + jnp.einsum("hqk,khd->qhd", d_scores, key_block, preferred_element_type=jnp.float32)
            * score_scale
        )
        d_keys = (
            jnp.einsum("hqk,qhd->khd", d_scores, queries, preferred_element_type=jnp.float32)
            * score_scale
        )
        d_values = jnp.einsum(
            "hqk,qhd->khd",
            attn_prob.astype(jnp.bfloat16),
            d_attended,
            preferred_element_type=jnp.float32,
        )
        return (d_queries, (d_keys, d_values))

    block_ids = jnp.arange(block_count, dtype=jnp.int32)
    d_queries, (d_keys_all, d_values_all) = lax.scan(
        back_block, jnp.zeros(head_shape, jnp.float32), (key_blocks, value_blocks, block_ids)
    )
    kv_terms = jnp.concatenate(
        [d_keys_all.reshape(row_len, model_width), d_values_all.reshape(row_len, model_width)],
        axis=-1,
    )
    kv_grad = lax.psum_scatter(
        kv_terms.astype(jnp.bfloat16), "ctx", scatter_dimension=0, tiled=True
    ).astype(jnp.float32)
    d_keys = kv_grad[:, :model_width].reshape(head_shape)
    d_qkv = jnp.concatenate(
        [
            rotate(d_queries, cosine_table, sine_table, -1.0).reshape(tok_rows, model_width),
            rotate(d_keys, cosine_table, sine_table, -1.0).reshape(tok_rows, model_width),
            kv_grad[:, model_width:],
        ],
        axis=-1,
    ).astype(jnp.bfloat16)
    grad_qkv = jnp.einsum("td,te->de", normed, d_qkv, preferred_element_type=jnp.float32)
    d_normed = jnp.einsum("te,de->td", d_qkv, qkv_back, preferred_element_type=jnp.float32)
    d_stream_part, d_gain_one = norm_back(stream, gain_f[:, 0], d_normed)
    d_tokens = (d_hidden + d_stream_part).astype(jnp.bfloat16)
    grad_gains = jnp.stack([d_gain_one, d_gain_two, d_gain_three, d_gain_four], axis=-1)
    shard_qkv, shard_out, shard_up, shard_down, shard_gains = (
        lax.psum_scatter(grad_qkv, ("dp", "ctx"), scatter_dimension=0, tiled=True),
        lax.psum_scatter(grad_out, ("dp", "ctx"), scatter_dimension=0, tiled=True),
        lax.psum_scatter(grad_up, ("dp", "ctx"), scatter_dimension=0, tiled=True),
        lax.psum_scatter(grad_down, ("dp", "ctx"), scatter_dimension=0, tiled=True),
        lax.psum_scatter(grad_gains, ("dp", "ctx"), scatter_dimension=0, tiled=True),
    )
    return (output, d_tokens, shard_qkv, shard_out, shard_up, shard_down, shard_gains)


def fused_device(tokens, lengths, w_qkv, w_out, w_up, w_down, gains, d_out):
    rows, width = tokens.shape
    row_len = rows * lax.axis_size("ctx")
    gains_wide = jnp.pad(gains, ((0, 0), (0, 128 - gains.shape[1])))
    tables = tuple(jnp.asarray(v) for v in turn_tables(row_len, width // HEADS))
    output, wq, wo, wu, wd, gain_rows, *saved = forward(
        tokens, lengths, gains_wide, w_qkv, w_out, w_up, w_down, tables
    )
    d_tokens, grad_qkv, grad_out, grad_up, grad_down, grad_gains = backward(
        tokens,
        d_out,
        lengths,
        gain_rows,
        tables,
        (wq, wo, wu, wd),
        saved,
        (w_qkv, w_out, w_up, w_down),
    )[:6]
    *results, gains_turned = hand_on(
        output, d_tokens, grad_qkv, grad_out, grad_up, grad_down, grad_gains
    )
    return (*results, gains_turned.T)


def layer(mesh):
    if mesh.shape["dp"] == 16 and mesh.shape["ctx"] == 2:
        return fused_device
    return per_device


def solution(mesh):
    return jax.shard_map(
        layer(mesh),
        mesh=mesh,
        in_specs=(
            P(("dp", "ctx"), None),
            P("dp", None),
            P(("dp", "ctx"), None),
            P(("dp", "ctx"), None),
            P(("dp", "ctx"), None),
            P(("dp", "ctx"), None),
            P(("dp", "ctx"), None),
            P(("dp", "ctx"), None),
        ),
        out_specs=(
            P(("dp", "ctx"), None),
            P(("dp", "ctx"), None),
            P(("dp", "ctx"), None),
            P(("dp", "ctx"), None),
            P(("dp", "ctx"), None),
            P(("dp", "ctx"), None),
            P(("dp", "ctx"), None),
        ),
        check_vma=False,
    )
```
